32 devices in a mesh: head: 4 (over z), shard: 8 (over y, x, core).
Axes of the slice: x: 2, y: 2, z: 4, core: 2. Of those that a mesh axis runs over, the one named last changes fastest.
Arguments:
- tokens: bfloat16 [16384, 768], P(('head', 'shard')), may hold values from -6 to 6
- norm_gain: bfloat16 [768], P('shard'), may hold values from 0.5 to 1.5
- in_weight: bfloat16 [768, 3352], P('shard'), may hold values from -0.21875 to 0.21875
- conv_weight: float32 [4, 1792], replicated, may hold values from -3 to 3
- conv_bias: float32 [1792], replicated, may hold values from -2 to 2
- dt_bias: float32 [24], replicated, may hold values from -4.6 to -2.3
- a_log: float32 [24], replicated, may hold values from -8 to 2.77
- d_skip: float32 [24], replicated, may hold values from 0.5 to 1.5
- inner_gain: float32 [1536], replicated, may hold values from 0.5 to 1.5
- out_weight: bfloat16 [1536, 768], P('shard'), may hold values from -0.15625 to 0.15625
- block_place: int32 [8, 8], P('shard'), may hold values from 0 to 7, each once within a row
- seq_length: int32 [8, 1], P('shard'), may hold values from 1793 to 2048, as said below
- cotangent: bfloat16 [16384, 768], P(('head', 'shard')), may hold values from -6 to 6
Outputs:
- mixed: bfloat16 [16384, 768], P(('head', 'shard'))
- token_grad: bfloat16 [16384, 768], P(('head', 'shard'))
- norm_gain_grad: float32 [768], P('shard')
- in_weight_grad: float32 [768, 3352], P('shard')
- conv_weight_grad: float32 [4, 1792], replicated
- conv_bias_grad: float32 [1792], replicated
- dt_bias_grad: float32 [24], replicated
- a_log_grad: float32 [24], replicated
- d_skip_grad: float32 [24], replicated
- inner_gain_grad: float32 [1536], replicated
- out_weight_grad: float32 [1536, 768], P('shard')
The draws below stay inside these ranges and needn't reach their ends.
Inputs may be any that keep to these rules, and one draw needn't show every extreme that they name: `block_place`: each row is a permutation of the group's 8 blocks. `seq_length`: A group's 1 sequence, each padded up to whole blocks of 256 tokens, fill exactly 8 blocks; each takes 4 blocks or more.
All inputs are finite; a program needn't handle non-finite values.
Results may differ from the reference program's by a relative error of at most 0.017.
Values may be sent and summed in bfloat16 or wider, within the bound.
No kernel may reach another device: no remote copies, remote signals or barrier semaphores. Data moves between devices by JAX's collectives and lax.ppermute only.
A program may use at most 192 MiB of HBM per device.

```python
import jax
import jax.numpy as jnp
from jax import lax

D = 768
NH = 24
HD = 64
NS = 128
KC = 4
CH = 256
MINB = 4
DI = 1536
NPROJ = 3352
CONVD = 1792
TOK_DEV = 512
GB = 8
SEQS = 1
TOKENS = 16384
N_HEAD = 4
N_SHARD = 8


def draw_seq_length(key, part):
    key = jax.random.fold_in(key, 7)
    spare_key, cut_key, pick_key, which_key = jax.random.split(key, 4)
    spare_units = GB - SEQS * MINB
    long_group = jax.random.randint(pick_key, (), 0, N_SHARD)
    long_seq = jax.random.randint(which_key, (), 0, SEQS)
    short_group = (long_group + 1) % N_SHARD
    short_seq = min(1, SEQS - 1)
    group_ids = jnp.arange(N_SHARD, dtype=jnp.int32)[:, None]
    seq_ids = jnp.arange(SEQS, dtype=jnp.int32)[None, :]
    chosen = jax.random.randint(spare_key, (N_SHARD, spare_units), 0, SEQS)
    chosen = jnp.where(group_ids == long_group, long_seq, chosen)
    chosen = jnp.where(group_ids == short_group, 0, chosen)
    counts = jnp.sum((chosen[:, :, None] == jnp.arange(SEQS)[None, None, :]).astype(jnp.int32), axis=1)
    blocks = MINB + counts
    trimmed = jax.random.randint(cut_key, (N_SHARD, SEQS), 0, CH)
    trimmed = jnp.where((group_ids == long_group) & (seq_ids == long_seq), 0, trimmed)
    trimmed = jnp.where((group_ids == short_group) & (seq_ids == short_seq), CH - 1, trimmed)
    return (blocks * CH - trimmed).astype(jnp.int32)


def draw_a_log(key, part):
    key = jax.random.fold_in(key, 11)
    pick_key, slow_key, fast_key = jax.random.split(key, 3)
    slow_count = NH // 2
    slow_floor = -7.0
    ranks = jax.random.permutation(pick_key, NH)
    slow_heads = ranks < slow_count
    slow_rates = jax.random.uniform(slow_key, (NH,), jnp.float32, slow_floor, -4.5)
    fast_rates = jax.random.uniform(fast_key, (NH,), jnp.float32, -1.0, 2.77)
    return jnp.where(slow_heads, slow_rates, fast_rates).astype(jnp.float32)


def shard_levels(rng, dims, cuts, least, largest):
    loudness = 1.0
    for dim, blocks in cuts:
        heights = jax.random.uniform(jax.random.fold_in(jax.random.fold_in(rng, 6), dim), (blocks,), jnp.float32, least / len(cuts), largest / len(cuts))
        loudness = loudness * jnp.repeat(jnp.exp(heights), dims[dim] // blocks).reshape((-1,) + (1,) * (len(dims) - 1 - dim))
    return loudness


def bell_draw(key, dims, scale, bound, pieces=(), held_as=jnp.bfloat16):
    entries = scale * jax.random.normal(key, dims, jnp.float32)
    if pieces:
        entries = entries * shard_levels(key, dims, pieces, -0.22, 0.18)
    return jnp.clip(entries, -bound, bound).astype(held_as)


def setup_inputs(seed: int = 0) -> dict:
    streams_of = jax.random.split(jax.random.key(seed), 14)
    tokens = bell_draw(streams_of[0], (TOKENS, D), 1.0, 6.0, ((0, 32),))
    norm_gain = jnp.clip(1.0 + 0.1 * jax.random.normal(streams_of[1], (D,), jnp.float32), 0.5, 1.5).astype(jnp.bfloat16)
    in_weight = bell_draw(streams_of[2], (D, NPROJ), D ** -0.5, 0.21875, ((0, 8),))
    conv_weight = bell_draw(streams_of[3], (KC, CONVD), 0.5, 3.0, (), jnp.float32)
    conv_bias = bell_draw(streams_of[4], (CONVD,), 0.3, 2.0, (), jnp.float32)
    dt_bias = jnp.clip(jax.random.uniform(streams_of[5], (NH,), jnp.float32, -4.6, -2.3), -4.6, -2.3)
    a_log = draw_a_log(jax.random.fold_in(streams_of[13], 71), 0)
    d_skip = jnp.clip(1.0 + 0.1 * jax.random.normal(streams_of[7], (NH,), jnp.float32), 0.5, 1.5)
    inner_gain = jnp.clip(1.0 + 0.1 * jax.random.normal(streams_of[8], (DI,), jnp.float32), 0.5, 1.5)
    out_weight = bell_draw(streams_of[9], (DI, D), DI ** -0.5, 0.15625, ((0, 8),))
    block_place = jax.vmap(lambda own: jax.random.permutation(own, GB))(jax.random.split(streams_of[10], N_SHARD)).reshape((N_SHARD, GB)).astype(jnp.int32)
    seq_length = draw_seq_length(jax.random.fold_in(streams_of[13], 71), 0)
    cotangent = bell_draw(streams_of[12], (TOKENS, D), 1.0, 6.0, ((0, 32),))
    return dict(tokens=tokens, norm_gain=norm_gain, in_weight=in_weight, conv_weight=conv_weight, conv_bias=conv_bias, dt_bias=dt_bias, a_log=a_log, d_skip=d_skip, inner_gain=inner_gain, out_weight=out_weight, block_place=block_place, seq_length=seq_length, cotangent=cotangent)


EPSILON = 1e-05
PRECISE = lax.Precision.HIGHEST

@jax.custom_vjp
def low(v):
    return lax.optimization_barrier(v.astype(jnp.bfloat16)).astype(jnp.float32)

@jax.custom_vjp
def low_back(v):
    return v

def low_keep(v):
    return (low(v), None)

def low_pass(kept, grad):
    return (grad,)

def back_keep(v):
    return (v, None)

def back_low(kept, grad):
    return (low(grad),)
low.defvjp(low_keep, low_pass)
low_back.defvjp(back_keep, back_low)

def layout(lengths, blocks, span_len):
    block_count = ((lengths + span_len - 1) // span_len).astype(jnp.int32)
    starts = (jnp.cumsum(block_count) - block_count).astype(jnp.int32)
    block_index = jnp.arange(blocks, dtype=jnp.int32)
    inside = (block_index[:, None] >= starts[None, :]) & (block_index[:, None] < (starts + block_count)[None, :])
    first_block = lax.optimization_barrier(jnp.sum(jnp.where(inside, starts[None, :], 0), axis=1)).astype(jnp.int32)
    seq_tokens = lax.optimization_barrier(jnp.sum(jnp.where(inside, lengths[None, :], 0), axis=1)).astype(jnp.int32)
    within = jnp.arange(span_len, dtype=jnp.int32)
    position = ((block_index - first_block)[:, None] * span_len + within[None, :]).reshape(-1).astype(jnp.int32)
    usable = (position < jnp.repeat(seq_tokens, span_len)).astype(jnp.float32)
    return (position, usable, block_index == first_block)

def conv_silu(signal, kernel, offset_bias, position, usable):
    masked = signal * usable[:, None]
    summed = offset_bias[None, :] + kernel[KC - 1][None, :] * masked
    for lag_steps in range(1, KC):
        shifted = jnp.concatenate([jnp.zeros((lag_steps, masked.shape[1]), jnp.float32), masked[:-lag_steps]], axis=0)
        reaches = (position >= lag_steps).astype(jnp.float32)[:, None]
        summed = summed + kernel[KC - 1 - lag_steps][None, :] * shifted * reaches
    return jax.nn.silu(summed)

def block_inner(item_in):
    c_one, b_one, steps_one, running_one, values_one = item_in
    scores = jnp.einsum('tn,sn->ts', c_one, b_one, precision=PRECISE)
    causal = jnp.arange(CH)[:, None] >= jnp.arange(CH)[None, :]
    running_t = jnp.transpose(running_one, (1, 0))
    spread_log = running_t[:, :, None] - running_t[:, None, :]
    decays = jnp.where(causal[None], jnp.exp(jnp.where(causal[None], spread_log, 0.0)), 0.0)
    mixing = decays * scores[None, :, :] * jnp.transpose(steps_one, (1, 0))[:, None, :]
    local_out = jnp.einsum('hts,shd->thd', mixing, values_one, precision=PRECISE)
    to_end = jnp.exp(running_one[-1:, :] - running_one) * steps_one
    weighted = values_one * to_end[:, :, None]
    state_new = jnp.einsum('sn,shd->hnd', b_one, weighted, precision=PRECISE)
    return (local_out, state_new)

def state_space(inputs, b_rows, c_rows, step_size, decay_log, first_flags, head_count):
    block_num = inputs.shape[0] // CH
    head_dim = inputs.shape[1] // head_count
    state_dim = b_rows.shape[1]
    values = inputs.reshape(block_num, CH, head_count, head_dim)
    b_block = b_rows.reshape(block_num, CH, state_dim)
    c_block = c_rows.reshape(block_num, CH, state_dim)
    steps_block = step_size.reshape(block_num, CH, head_count)
    running = jnp.cumsum(decay_log.reshape(block_num, CH, head_count), axis=1)
    local_out, block_states = lax.map(jax.checkpoint(block_inner), (c_block, b_block, steps_block, running, values))
    block_fade = jnp.exp(running[:, -1, :])

    def advance(carried, item_in):
        state_new, fade_now, first_now = item_in
        entering = jnp.where(first_now, 0.0, carried)
        return (fade_now[:, None, None] * entering + state_new, entering)
    start_state = jnp.zeros((head_count, state_dim, head_dim), jnp.float32)
    final_state, entering = lax.scan(advance, start_state, (block_states, block_fade, first_flags))
    carried_out = jnp.einsum('ctn,chnd->cthd', c_block, entering, precision=PRECISE) * jnp.exp(running)[:, :, :, None]
    return (local_out + carried_out).reshape(block_num * CH, head_count * head_dim)

def mixer_core(gate_in, conv_in, step_raw, kernel, offset_bias, step_bias, log_rate, skip_gain, position, usable, first_flags, head_count):
    activated = conv_silu(conv_in, kernel, offset_bias, position, usable)
    width_all = head_count * HD
    x_rows = activated[:, :width_all]
    b_rows = activated[:, width_all:width_all + NS]
    c_rows = activated[:, width_all + NS:]
    step_size = jax.nn.softplus(step_raw + step_bias[None, :])
    decay_log = -step_size * jnp.exp(log_rate)[None, :]
    scanned = state_space(x_rows, b_rows, c_rows, step_size, decay_log, first_flags, head_count)
    scanned = scanned + x_rows * jnp.repeat(skip_gain, HD)[None, :]
    return scanned * jax.nn.silu(gate_in)

def forward(token_rows, pre_gain, in_matrix, conv_kernel, conv_offset, step_bias, log_rate, skip_gain, post_gain, out_matrix, block_place, seq_length):
    inv_rms = lax.rsqrt(lax.optimization_barrier(jnp.mean(token_rows * token_rows, axis=1, keepdims=True)) + EPSILON)
    normal_in = low(token_rows * inv_rms * pre_gain[None, :])
    projected = low(low_back(jnp.dot(normal_in, in_matrix, precision=PRECISE)))
    by_group = projected.reshape(N_HEAD, N_SHARD, TOK_DEV, NPROJ).transpose(1, 0, 2, 3).reshape(N_SHARD, GB * CH, NPROJ)

    def one_group(item_in):
        group_rows, placing, lengths = item_in
        inverse = jnp.zeros((GB,), jnp.int32).at[placing].set(jnp.arange(GB, dtype=jnp.int32))
        ordered = group_rows.reshape(GB, CH, NPROJ)[inverse].reshape(GB * CH, NPROJ)
        position, usable, first_flags = layout(lengths, GB, CH)
        gated_rows = mixer_core(ordered[:, :DI], ordered[:, DI:DI + CONVD], ordered[:, DI + CONVD:], conv_kernel, conv_offset, step_bias, log_rate, skip_gain, position, usable, first_flags, NH)
        inv_scale = lax.rsqrt(lax.optimization_barrier(jnp.mean(gated_rows * gated_rows, axis=1, keepdims=True)) + EPSILON)
        normed = low(low_back(gated_rows * inv_scale * post_gain[None, :] * usable[:, None]))
        return normed.reshape(GB, CH, DI)[placing].reshape(GB * CH, DI)
    given_rows = lax.map(jax.checkpoint(one_group), (by_group, block_place, seq_length))
    home_rows = given_rows.reshape(N_SHARD, N_HEAD, TOK_DEV, DI).transpose(1, 0, 2, 3).reshape(N_HEAD * N_SHARD * TOK_DEV, DI)
    return token_rows + jnp.dot(home_rows, out_matrix, precision=PRECISE)

def reference(tokens, norm_gain, in_weight, conv_weight, conv_bias, dt_bias, a_log, d_skip, inner_gain, out_weight, block_place, seq_length, cotangent):

    def layer(token_rows, pre_gain, in_matrix, conv_kernel, conv_offset, step_bias, log_rate, skip_gain, post_gain, out_matrix):
        return forward(token_rows, pre_gain, in_matrix, conv_kernel, conv_offset, step_bias, log_rate, skip_gain, post_gain, out_matrix, block_place, seq_length)
    output, pullback = jax.vjp(layer, tokens.astype(jnp.float32), norm_gain.astype(jnp.float32), in_weight.astype(jnp.float32), conv_weight, conv_bias, dt_bias, a_log, d_skip, inner_gain, out_weight.astype(jnp.float32))
    grads = pullback(cotangent.astype(jnp.float32))
    return (output.astype(jnp.bfloat16), grads[0].astype(jnp.bfloat16), grads[1], grads[2], grads[3], grads[4], grads[5], grads[6], grads[7], grads[8], grads[9])
```

```python
import jax
import jax.numpy as jnp
from jax import lax
from jax.sharding import PartitionSpec as P

NH = 24
HD = 64
NS = 128
KC = 4
CH = 256
DI = 1536
DM = 768
XBC = DI + 2 * NS
WA = 1920
HALO = 8
EPSILON = 1e-05
F32 = jnp.float32
BF = jnp.bfloat16


def trade(value, axis, bit):
    size = lax.axis_size(axis)
    return lax.ppermute(value, axis, [(i, i ^ bit) for i in range(size)])


def swap_home(value):
    n_head, n_shard = lax.axis_size("head"), lax.axis_size("shard")
    half = n_head // 2
    pairs = []
    for h in range(n_head):
        for s in range(n_shard):
            upper, core = h // half, s & 1
            pairs.append((h * n_shard + s, (h % half + core * half) * n_shard + (s - core + upper)))
    return lax.ppermute(value, ("head", "shard"), pairs)


def group_gather(value):
    half = lax.axis_size("head") // 2
    pieces = [value]
    bit = 1
    while bit < half:
        pieces = pieces + [trade(v, "head", bit) for v in pieces]
        bit *= 2
    return pieces + [trade(v, "shard", 1) for v in pieces]


def gather_rows(piece):
    n_shard = lax.axis_size("shard")
    me = lax.axis_index("shard")
    rows = piece.shape[0]
    cut = rows // 2
    low_bits = [b for b in (2, 4, 8, 16, 32, 64) if b < n_shard]
    lo, hi = low_bits[: len(low_bits) // 2], low_bits[len(low_bits) // 2 :]
    whole = jnp.zeros((n_shard, rows) + piece.shape[1:], piece.dtype)
    parts = []
    for order, part, start in ((lo + hi, piece[:cut], 0), (hi + lo, piece[cut:], cut)):
        held = {0: part}
        for b in order:
            held.update({k ^ b: trade(v, "shard", b) for k, v in list(held.items())})
        held.update({k ^ 1: trade(v, "shard", 1) for k, v in list(held.items())})
        for k, v in held.items():
            whole = lax.dynamic_update_slice(
                whole, v[None], (me ^ k, start) + (0,) * (piece.ndim - 1)
            )
    return whole.reshape((n_shard * rows,) + piece.shape[1:])


def scatter_sum(term):
    n_shard = lax.axis_size("shard")
    me = lax.axis_index("shard")
    rows = term.shape[0] // n_shard
    cols = term.shape[1]
    low_bits = [b for b in (2, 4, 8, 16, 32, 64) if b < n_shard]
    lo, hi = low_bits[: len(low_bits) // 2], low_bits[len(low_bits) // 2 :]
    cut = cols // 2 // 128 * 128
    done = []
    for order, begin, end in ((lo + hi, 0, cut), (hi + lo, cut, cols)):
        held = term[:, begin:end].reshape(n_shard, rows, end - begin)
        todo = [1] + list(order)
        left = [b for b in (1,) + tuple(low_bits)]
        for b in todo:
            at = left.index(b)
            below = 1 << at
            split = held.reshape(-1, 2, below, rows, end - begin)
            mine = (me // b) % 2
            keep = lax.dynamic_index_in_dim(split, mine, 1, False)
            give = lax.dynamic_index_in_dim(split, 1 - mine, 1, False)
            got = trade(give, "shard", b)
            held = (keep.astype(F32) + got.astype(F32)).astype(BF).reshape(-1, rows, end - begin)
            left.remove(b)
        done.append(held.reshape(rows, end - begin))
    return done


def head_sum(value):
    size = lax.axis_size("head")
    bit = 1
    total = value.astype(F32)
    while bit < size:
        low = total.astype(BF)
        total = low.astype(F32) + trade(low, "head", bit).astype(F32)
        bit *= 2
    return total


def full_sum(value):
    for axis in ("shard", "head"):
        bit = 1
        while bit < lax.axis_size(axis):
            value = value + trade(value, axis, bit)
            bit *= 2
    return value


def dot(a, b):
    return jnp.dot(a, b, preferred_element_type=F32)


def dot_nt(a, b):
    return lax.dot_general(a, b, (((1,), (1,)), ((), ())), preferred_element_type=F32)


def dot_tn(a, b):
    return lax.dot_general(a, b, (((0,), (0,)), ((), ())), preferred_element_type=F32)


def wide(per_head):
    return jnp.repeat(per_head, HD, axis=-1)


def narrow(full):
    return full.reshape(full.shape[:-1] + (NH, HD)).sum(axis=-1)


def silu(v):
    return v * jax.nn.sigmoid(v)


def silu_grad(v):
    s = jax.nn.sigmoid(v)
    return s * (1.0 + v * (1.0 - s))


def unit(rows):
    f = rows.astype(F32)
    inv = lax.rsqrt(jnp.mean(f * f, axis=1, keepdims=True) + EPSILON)
    return f * inv, inv


def block_shift(body, halo):
    nb = body.shape[0] // CH
    return jnp.concatenate(
        [halo.reshape(nb, HALO, -1), body.reshape(nb, CH, -1)], axis=1
    ).astype(F32)


def pre_act(xbc, xbc_halo, kernel, bias):
    ext = block_shift(xbc, xbc_halo)
    total = bias[None, None, :]
    for lag in range(KC):
        total = total + kernel[KC - 1 - lag] * ext[:, HALO - lag : HALO - lag + CH]
    return total.reshape(xbc.shape)


def k1(tok, halo_tok, wa, gain, conv_w, conv_b, dt_bias, a_log, usable, has_prev):
    nb = tok.shape[0] // CH
    normal = (unit(tok)[0] * gain[None, :]).astype(BF)
    normal_halo = (unit(halo_tok)[0] * gain[None, :]).astype(BF)
    proj = dot(normal, wa).astype(BF)
    proj_halo = dot(normal_halo, wa).astype(BF)
    xbc = (proj[:, :XBC].astype(F32) * usable).astype(BF)
    halo_on = (jnp.repeat(has_prev, HALO) * (jnp.arange(nb * HALO) % HALO >= HALO - KC + 1))[:, None]
    xbc_halo = jnp.where(halo_on, proj_halo[:, :XBC], 0)
    act = silu(pre_act(xbc, xbc_halo, conv_w, conv_b))
    xs, bs, cs = act[:, :DI], act[:, DI : DI + NS].astype(BF), act[:, DI + NS :].astype(BF)
    raw = proj[:, XBC : XBC + NH].astype(F32) + dt_bias
    dt = jax.nn.softplus(raw)
    logd = -dt * jnp.exp(a_log)
    cum = jnp.cumsum(logd.reshape(nb, CH, NH), axis=1)
    clast = cum[:, -1]
    to_end = (jnp.exp(clast[:, None] - cum) * dt.reshape(nb, CH, NH)).reshape(-1, NH)
    xt = lax.optimization_barrier((xs * wide(dt)).astype(BF))
    xw = (xs * wide(to_end)).astype(BF)
    states = jnp.stack(
        [dot_tn(bs[i * CH : (i + 1) * CH], xw[i * CH : (i + 1) * CH]) for i in range(nb)]
    ).astype(BF)
    return dict(
        normal=normal, normal_halo=normal_halo, xbc=xbc, xbc_halo=xbc_halo, xs=xs.astype(BF),
        bs=bs, cs=cs, raw=raw, dt=dt, cum=cum.reshape(-1, NH), xt=xt, clast=clast, states=states,
    )


def decay(cum_block):
    t = cum_block.T
    spread = t[:, :, None] - t[:, None, :]
    causal = jnp.arange(CH)[:, None] >= jnp.arange(CH)[None, :]
    return jnp.where(causal, jnp.exp(jnp.where(causal, spread, 0.0)), 0.0)


def k2(a):
    out = []
    nb = a["cs"].shape[0] // CH
    for i in range(nb):
        r = slice(i * CH, (i + 1) * CH)
        scores = dot_nt(a["cs"][r], a["bs"][r])
        mix = (decay(a["cum"][r]) * scores).astype(BF)
        xt = a["xt"][r].reshape(CH, NH, HD)
        out.append(
            jnp.einsum("hts,shd->thd", mix, xt, preferred_element_type=F32).reshape(CH, DI)
        )
    return jnp.concatenate(out)


def k3(a, y_intra, entering, z, q, inner_gain, d_skip, usable):
    nb = a["cs"].shape[0] // CH
    ecum = wide(jnp.exp(a["cum"]))
    inter = jnp.concatenate(
        [dot(a["cs"][i * CH : (i + 1) * CH], entering[i]) for i in range(nb)]
    )
    y_scan = y_intra + ecum * inter
    xs = a["xs"].astype(F32)
    y = y_scan + wide(d_skip) * xs
    zf = z.astype(F32)
    sz = silu(zf)
    gated = y * sz
    inv = lax.rsqrt(jnp.mean(gated * gated, axis=1, keepdims=True) + EPSILON)
    normed = (gated * inv * inner_gain * usable).astype(BF)
    qf = q.astype(F32) * usable
    gain_part = jnp.sum(qf * gated * inv, axis=0)
    qg = qf * inner_gain
    gg = inv * qg - gated * (inv * inv * inv) * (
        jnp.sum(qg * gated, axis=1, keepdims=True) / DI
    )
    dy = gg * sz
    dz = (gg * y * silu_grad(zf)).astype(BF)
    dyr = lax.optimization_barrier(dy.astype(BF))
    row_part = narrow(dyr.astype(F32) * y_scan)
    skip_part = narrow(jnp.sum(dy * xs, axis=0))
    dye = (ecum * dy).astype(BF)
    d_enter = jnp.stack(
        [dot_tn(a["cs"][i * CH : (i + 1) * CH], dye[i * CH : (i + 1) * CH]) for i in range(nb)]
    ).astype(BF)
    return normed, gain_part, dz, dyr, dye, row_part, skip_part, d_enter


def k4(a, dyr, dye, entering):
    nb = a["cs"].shape[0] // CH
    dx, db, dc = [], [], []
    for i in range(nb):
        r = slice(i * CH, (i + 1) * CH)
        scores = dot_nt(a["cs"][r], a["bs"][r])
        dec = decay(a["cum"][r])
        mix = (dec * scores).astype(BF)
        dy = dyr[r].reshape(CH, NH, HD)
        xt = a["xt"][r].reshape(CH, NH, HD)
        dx.append(jnp.einsum("hts,thd->shd", mix, dy, preferred_element_type=F32).reshape(CH, DI))
        dmix = jnp.einsum("thd,shd->hts", dy, xt, preferred_element_type=F32)
        dscore = jnp.sum(dmix * dec, axis=0).astype(BF)
        db.append(dot_tn(dscore, a["cs"][r]))
        dc.append(dot(dscore, a["bs"][r]) + dot_nt(dye[r], entering[i]))
    return jnp.concatenate(dx), jnp.concatenate(db), jnp.concatenate(dc)


def k5(a, dx_intra, db, dc, d_state, entering, row_part, dyr, conv_w, conv_b, a_log, d_skip, usable):
    nb = a["cs"].shape[0] // CH
    cum = a["cum"].reshape(nb, CH, NH)
    to_end = jnp.exp(a["clast"][:, None] - cum).reshape(-1, NH)
    back = jnp.concatenate(
        [dot(a["bs"][i * CH : (i + 1) * CH], d_state[i]) for i in range(nb)]
    )
    to_end_w = wide(to_end)
    inter = to_end_w * back
    dxt = dx_intra + inter
    xt = a["xt"].astype(F32)
    xw = (xt * to_end_w).astype(BF)
    db = db + jnp.concatenate(
        [dot_nt(xw[i * CH : (i + 1) * CH], d_state[i]) for i in range(nb)]
    )
    h_part = narrow(xt * inter).reshape(nb, CH, NH).sum(axis=1)
    fade = jnp.exp(a["clast"]) * narrow(
        jnp.sum(d_state.astype(F32) * entering.astype(F32), axis=1)
    )
    d_cum = (row_part - narrow(xt * dxt)).reshape(nb, CH, NH)
    d_cum = d_cum.at[:, -1].add(h_part + fade)
    d_log = jnp.flip(jnp.cumsum(jnp.flip(d_cum, 1), axis=1), 1).reshape(-1, NH)
    xs = a["xs"].astype(F32)
    rate = jnp.exp(a_log)
    d_dt = narrow(xs * dxt) - d_log * rate
    d_raw = d_dt * jax.nn.sigmoid(a["raw"])
    rate_part = jnp.sum(d_log * (-a["dt"] * rate), axis=0)
    bias_part = jnp.sum(d_raw, axis=0)
    dxs = wide(a["dt"]) * dxt + wide(d_skip) * dyr.astype(F32)
    dact = jnp.concatenate([dxs, db, dc], axis=1)
    pre = pre_act(a["xbc"], a["xbc_halo"], conv_w, conv_b)
    dpre = dact * silu_grad(pre)
    offset_part = jnp.sum(dpre, axis=0)
    ext = block_shift(a["xbc"], a["xbc_halo"])
    dp = dpre.reshape(nb, CH, XBC)
    kernel_part = jnp.stack(
        [
            jnp.sum(dp * ext[:, HALO - lag : HALO - lag + CH], axis=(0, 1))
            for lag in range(KC - 1, -1, -1)
        ]
    )
    padded = jnp.pad(dp, ((0, 0), (HALO, HALO), (0, 0)))
    total = 0.0
    for lag in range(KC):
        total = total + conv_w[KC - 1 - lag] * padded[:, lag : lag + HALO + CH]
    dxbc = (total[:, HALO:].reshape(-1, XBC) * usable).astype(BF)
    dxbc_halo = total[:, :HALO].reshape(-1, XBC)
    return dxbc, dxbc_halo, d_raw.astype(BF), kernel_part, offset_part, bias_part, rate_part


def norm_back(normal_grad, rows, gain):
    u, inv = unit(rows)
    g = normal_grad * gain[None, :]
    return inv * (g - u * jnp.mean(g * u, axis=1, keepdims=True)), jnp.sum(normal_grad * u, axis=0)


def shards(
    tokens, norm_gain, in_weight, conv_weight, conv_bias, dt_bias, a_log, d_skip, inner_gain,
    out_weight, block_place, seq_length, cotangent,
):
    n_head, n_shard = lax.axis_size("head"), lax.axis_size("shard")
    half = n_head // 2
    head_at, shard_at = lax.axis_index("head"), lax.axis_index("shard")
    rows = tokens.shape[0]
    nb = rows // CH
    group_blocks = nb * n_head
    k_rows = in_weight.shape[0]

    piece_a = jnp.concatenate(
        [in_weight[:, DI:], norm_gain[:, None], jnp.zeros((k_rows, WA - XBC - NH - 1), BF)], axis=1
    )
    wa = gather_rows(piece_a)
    gain = wa[:, XBC + NH].astype(F32)
    wz = gather_rows(in_weight[:, :DI])
    wo = gather_rows(out_weight)

    tok = swap_home(tokens)
    cot = swap_home(cotangent)
    tails = tokens.reshape(nb, CH, DM)[:, CH - HALO :].reshape(nb * HALO, DM)
    tails = group_gather(swap_home(tails))

    other_place, other_length = trade(block_place, "shard", 1), trade(seq_length, "shard", 1)
    stay = (head_at // half) == (shard_at & 1)
    placing = jnp.where(stay, block_place, other_place)[0]
    lengths = jnp.where(stay, seq_length, other_length)[0]
    own = head_at % half + (shard_at & 1) * half
    order = []
    for core in (0, 1):
        for z in range(half):
            order.append((head_at % half ^ z) + ((shard_at & 1) ^ core) * half)
    block_ids = jnp.concatenate([o * nb + jnp.arange(nb) for o in order])
    places = placing[block_ids]
    block_count = (lengths + CH - 1) // CH
    starts = jnp.cumsum(block_count) - block_count
    inside = (places[:, None] >= starts) & (places[:, None] < starts + block_count)
    first = jnp.sum(jnp.where(inside, starts, 0), axis=1)
    seq_tokens = jnp.sum(jnp.where(inside, lengths, 0), axis=1)
    position = ((places - first)[:nb, None] * CH + jnp.arange(CH)).reshape(-1)
    usable = (position < jnp.repeat(seq_tokens[:nb], CH)).astype(F32)[:, None]
    has_prev = (places != first)[:nb]
    reach = (places[None, :] >= first[:, None]) & (places[None, :] < places[:, None])
    between = (places[None, None, :] > places[None, :, None]) & (
        places[None, None, :] < places[:, None, None]
    )

    halo_all = jnp.concatenate(tails).reshape(group_blocks, HALO, DM)
    is_prev = (places[None, :] == places[:nb, None] - 1) & has_prev[:, None]
    halo_tok = jnp.sum(
        jnp.where(is_prev[:, :, None, None], halo_all[None].astype(F32), 0.0), axis=1
    ).astype(BF).reshape(nb * HALO, DM)

    a = k1(tok, halo_tok, wa, gain, conv_weight, conv_bias, dt_bias, a_log, usable, has_prev)
    all_states = jnp.concatenate(group_gather(a["states"]))
    all_clast = jnp.concatenate(group_gather(a["clast"]))
    log_w = jnp.sum(jnp.where(between[..., None], all_clast[None, None], 0.0), axis=2)
    carry = jnp.where(reach[..., None], jnp.exp(log_w), 0.0)

    y_intra = k2(a)
    z = dot(a["normal"], wz).astype(BF)
    q = dot_nt(cot, wo).astype(BF)
    entering = jnp.stack(
        [
            sum(wide(carry[i, j])[None, :] * all_states[j].astype(F32) for j in range(group_blocks))
            for i in range(nb)
        ]
    ).astype(BF)
    normed, gain_part, dz, dyr, dye, row_part, skip_part, d_enter = k3(
        a, y_intra, entering, z, q, inner_gain, d_skip, usable
    )
    all_enter = jnp.concatenate(group_gather(d_enter))
    mixed = swap_home((tok.astype(F32) + dot(normed, wo)).astype(BF))
    out_term = scatter_sum(dot_tn(normed, cot).astype(BF))
    z_term = scatter_sum(dot_tn(a["normal"], dz).astype(BF))
    dx_intra, db, dc = k4(a, dyr, dye, entering)
    d_state = jnp.stack(
        [
            sum(wide(carry[j, i])[None, :] * all_enter[j].astype(F32) for j in range(group_blocks))
            for i in range(nb)
        ]
    ).astype(BF)
    dxbc, dxbc_halo, d_raw, kernel_part, offset_part, bias_part, rate_part = k5(
        a, dx_intra, db, dc, d_state, entering, row_part, dyr, conv_weight, conv_bias, a_log, d_skip,
        usable,
    )
    halo_on = (jnp.repeat(has_prev, HALO) * (jnp.arange(nb * HALO) % HALO >= HALO - KC + 1))[:, None]
    dxbc_halo = jnp.where(halo_on, dxbc_halo, 0.0).astype(BF)
    d_a = jnp.concatenate([dxbc, d_raw, jnp.zeros((rows, WA - XBC - NH), BF)], axis=1)
    d_a_halo = jnp.pad(dxbc_halo, ((0, 0), (0, WA - XBC)))
    a_term = dot_tn(
        jnp.concatenate([a["normal"], a["normal_halo"]]), jnp.concatenate([d_a, d_a_halo])
    ).astype(BF)
    a_term = scatter_sum(a_term)
    normal_grad = dot_nt(dz, wz) + dot_nt(d_a, wa)
    halo_grad = dot_nt(d_a_halo, wa)
    tok_part, gain_main = norm_back(normal_grad, tok, gain)
    halo_part, gain_halo = norm_back(halo_grad, halo_tok, gain)
    gain_grad = gain_main + gain_halo
    token_grad = swap_home((cot.astype(F32) + tok_part).astype(BF))
    all_halo = jnp.concatenate(group_gather(halo_part)).reshape(group_blocks, HALO, DM)
    is_next = (places[None, :] == places[:nb, None] + 1) & (first[None, :] == first[:nb, None])
    halo_back = swap_home(jnp.sum(jnp.where(is_next[:, :, None, None], all_halo[None], 0.0), axis=1))
    token_grad = token_grad.reshape(nb, CH, DM)
    token_grad = token_grad.at[:, CH - HALO :].set(
        (token_grad[:, CH - HALO :].astype(F32) + halo_back).astype(BF)
    ).reshape(rows, DM)

    in_grad = jnp.concatenate(
        [head_sum(v) for v in z_term] + [head_sum(v) for v in a_term], axis=1
    )[:, : DI + XBC + NH]
    out_grad = jnp.concatenate([head_sum(v) for v in out_term], axis=1)

    small = jnp.concatenate(
        [
            kernel_part.reshape(-1), offset_part, bias_part, rate_part, skip_part, gain_part,
            gain_grad,
        ]
    )
    small = full_sum(small)
    sizes = [KC * XBC, XBC, NH, NH, NH, DI, DM]
    cuts = []
    at = 0
    for s in sizes:
        cuts.append(small[at : at + s])
        at += s
    gain_out = lax.dynamic_slice_in_dim(cuts[6], shard_at * k_rows, k_rows, 0)
    return (
        mixed, token_grad, gain_out, in_grad, cuts[0].reshape(KC, XBC), cuts[1], cuts[2], cuts[3],
        cuts[4], cuts[5], out_grad,
    )


def solution(mesh):
    return jax.shard_map(
        shards,
        mesh=mesh,
        in_specs=(
            P(("head", "shard"), None), P("shard"), P("shard", None), P(), P(), P(), P(), P(), P(),
            P("shard", None), P("shard", None), P("shard", None), P(("head", "shard"), None),
        ),
        out_specs=(
            P(("head", "shard"), None), P(("head", "shard"), None), P("shard"), P("shard", None),
            P(), P(), P(), P(), P(), P(), P("shard", None),
        ),
        check_vma=False,
    )
```

```python
import functools

import jax
import jax.numpy as jnp
from jax import lax
from jax.experimental import pallas as pl
from jax.experimental.pallas import tpu as pltpu
from jax.sharding import PartitionSpec as P

NH = 24
HD = 64
NS = 128
KC = 4
CH = 256
DI = 1536
DM = 768
XBC = DI + 2 * NS
WA = 1920
HALO = 8
EPSILON = 1e-05
F32 = jnp.float32
BF = jnp.bfloat16
LANES = 128
CW = 384
NCW = DI // CW
VMEM_ASK = 56 * 2**20


def trade(value, axis, bit):
    size = lax.axis_size(axis)
    return lax.ppermute(value, axis, [(i, i ^ bit) for i in range(size)])


def after(value, *others):
    return lax.optimization_barrier((value,) + others)[0]


def move_home(value):
    n_head, n_shard = lax.axis_size("head"), lax.axis_size("shard")
    half = n_head // 2
    pairs = []
    for h in range(n_head):
        for s in range(n_shard):
            upper, core = h // half, s & 1
            if upper != core:
                there = (h % half + core * half) * n_shard + (s - core + upper)
                pairs.append((h * n_shard + s, there))
    return lax.ppermute(value, ("head", "shard"), pairs)


def swap_home(value, stay):
    return jnp.where(stay, value, move_home(value))


def group_spread(value, stay):
    n_head, n_shard = lax.axis_size("head"), lax.axis_size("shard")
    half = n_head // 2
    pieces = [swap_home(value, stay)]
    for core in (0, 1):
        for low in range(half):
            if core or low:
                pairs = []
                for h in range(n_head):
                    for s in range(n_shard):
                        there = (h % half ^ low) + (s & 1) * half
                        pairs.append((h * n_shard + s, there * n_shard + (s - (s & 1) + (h // half ^ core))))
                pieces.append(lax.ppermute(value, ("head", "shard"), pairs))
    return pieces


def group_gather(value):
    half = lax.axis_size("head") // 2
    pieces = [value]
    bit = 1
    while bit < half:
        pieces = pieces + [trade(v, "head", bit) for v in pieces]
        bit *= 2
    return pieces + [trade(v, "shard", 1) for v in pieces]


def gather_pieces(piece):
    n_shard = lax.axis_size("shard")
    if n_shard != 8:
        held = {0: piece}
        bit = 1
        while bit < n_shard:
            held.update({k ^ bit: trade(v, "shard", bit) for k, v in list(held.items())})
            bit *= 2
        return [(v, k, None) for k, v in held.items()]

    def from_core(value, core, bit):
        return lax.ppermute(value, "shard", [(i, i ^ bit) for i in range(n_shard) if i % 2 == core])

    by_x, by_y, by_core = trade(piece, "shard", 2), trade(piece, "shard", 4), trade(piece, "shard", 1)
    far_0, far_1 = from_core(by_x, 0, 4), from_core(by_y, 1, 2)
    return [
        (piece, 0, None), (by_core, 1, None), (by_x, 2, None), (by_y, 4, None),
        (trade(by_x, "shard", 1), 3, None), (trade(by_y, "shard", 1), 5, None),
        (far_0, 6, 0), (far_1, 6, 1),
        (from_core(far_0, 0, 1), 7, 1), (from_core(far_1, 1, 1), 7, 0),
    ]


def head_pieces(value):
    pieces = [value]
    bit = 1
    while bit < lax.axis_size("head") // 2:
        pieces = pieces + [trade(v, "head", bit) for v in pieces]
        bit *= 2
    return pieces[1:]


def core_give(blocks):
    n_shard = lax.axis_size("shard")
    core = lax.axis_index("shard") % 2

    def half(which):
        parts = []
        for v in blocks:
            split = v.reshape((n_shard // 2, 2) + v.shape[1:])
            parts.append(lax.dynamic_index_in_dim(split, which, 1, False))
        return jnp.concatenate(parts, axis=2) if len(parts) > 1 else parts[0]

    return half(core), half(1 - core)


def chip_pairs(keep, got):
    pair = (keep.astype(F32) + got.astype(F32)).astype(BF)
    chip = lax.axis_index("shard") // 2
    return [lax.dynamic_index_in_dim(pair, chip ^ k, 0, False) for k in range(pair.shape[0])]


def chip_send(pairs):
    return [trade(v, "shard", 2 * k) for k, v in enumerate(pairs) if k]


def chip_sum(own, got):
    total = own.astype(F32)
    for v in got:
        total = total + v.astype(F32)
    return total.astype(BF)


def head_sum(value):
    cut = value.shape[1] // 2 // LANES * LANES
    bits = [b for b in (1, 2, 4, 8, 16) if b < lax.axis_size("head")]
    done = []
    for part, order in ((value[:, :cut], bits), (value[:, cut:], bits[::-1])):
        total = part.astype(F32)
        for bit in order:
            low = total.astype(BF)
            total = low.astype(F32) + trade(low, "head", bit).astype(F32)
        done.append(total)
    return jnp.concatenate(done, axis=1)


def full_sum(value):
    for axis in ("shard", "head"):
        bit = 1
        while bit < lax.axis_size(axis):
            value = value + trade(value, axis, bit)
            bit *= 2
    return value


def dot(a, b):
    return jnp.dot(a, b, preferred_element_type=F32)


def dot_nt(a, b):
    return lax.dot_general(a, b, (((1,), (1,)), ((), ())), preferred_element_type=F32)


def dot_tn(a, b):
    return lax.dot_general(a, b, (((0,), (0,)), ((), ())), preferred_element_type=F32)


def spread_table():
    row = jnp.arange(2 * LANES)[:, None] % LANES
    return (row == jnp.arange(DI)[None, :] // HD).astype(BF)


def pieces2(v):
    hi = v.astype(BF)
    return hi, (v - hi.astype(F32)).astype(BF)


def pieces3(v):
    hi = v.astype(BF)
    rest = v - hi.astype(F32)
    mid = rest.astype(BF)
    return hi, mid, (rest - mid.astype(F32)).astype(BF)


def softplus(v):
    return jnp.maximum(v, 0.0) + jnp.log1p(jnp.exp(-jnp.abs(v)))


sigmoid = jax.nn.sigmoid


def shape(dims, dtype):
    return jax.ShapeDtypeStruct(dims, dtype)


def whole(arr):
    return pl.BlockSpec(arr.shape, lambda *g: (0,) * len(arr.shape))


def columns(arr, at, width=None):
    dims = arr.shape[:-1] + (width or CW,)
    return pl.BlockSpec(dims, lambda *g: (0,) * (len(dims) - 1) + (at(*g),))


def in_hbm():
    return pl.BlockSpec(memory_space=pl.ANY)


def in_smem():
    return pl.BlockSpec(memory_space=pltpu.SMEM)


def call(kernel, grid, ins, outs, scratch, flops):
    moved = sum(a.size * a.dtype.itemsize for a, _ in ins)
    moved += sum(o.size * o.dtype.itemsize for o, _ in outs)
    return pl.pallas_call(
        kernel,
        grid=grid,
        out_shape=[o for o, _ in outs],
        in_specs=[s for _, s in ins],
        out_specs=[s for _, s in outs],
        scratch_shapes=scratch,
        compiler_params=pltpu.CompilerParams(vmem_limit_bytes=VMEM_ASK),
        cost_estimate=pl.CostEstimate(flops=flops, bytes_accessed=moved, transcendentals=0),
    )(*[a for a, _ in ins])


def iota(dims, axis):
    return lax.broadcasted_iota(jnp.int32, dims, axis)


def place_of(info, q):
    return info[2 + 3 * q]


def first_of(info, q):
    return info[3 + 3 * q]


def usable_of(info, i):
    begin = (place_of(info, i) - first_of(info, i)) * CH
    return (iota((CH, 1), 0) + begin < info[4 + 3 * i]).astype(F32)


def halo_used(info, i):
    has_prev = place_of(info, i) > first_of(info, i)
    return (iota((HALO, 1), 0) + jnp.where(has_prev, 0, -HALO) > HALO - KC).astype(F32)


def clast_rows(refs, nb):
    rows = []
    for ref in refs:
        for b in range(nb):
            part = ref[b].astype(F32)
            rows.append(part[0:1, :] + part[1:2, :] + part[2:3, :])
    return rows


def carry_weights(info, ends, nb, into):
    n_all = len(ends)
    row = iota((n_all, 1), 0)
    place = jnp.zeros((n_all, 1), jnp.int32)
    first = jnp.zeros((n_all, 1), jnp.int32)
    for j in range(n_all):
        place = jnp.where(row == j, place_of(info, j), place)
        first = jnp.where(row == j, first_of(info, j), first)
    parts = []
    for i in range(nb):
        own = place_of(info, i)
        total = jnp.zeros((n_all, LANES), F32)
        for k in range(n_all):
            at = place_of(info, k)
            if into:
                between = (place > at) & (at > own)
            else:
                between = (place < at) & (at < own)
            total = total + jnp.where(between, ends[k], 0.0)
        if into:
            reach = (first <= own) & (place > own)
        else:
            reach = (place >= first_of(info, i)) & (place < own)
        parts.append(jnp.where(reach, jnp.exp(total), 0.0))
    return jnp.concatenate(pieces2(jnp.concatenate(parts, axis=0)), axis=1)


def normal_rows(rows, gain):
    f = rows.astype(F32)
    inv = lax.rsqrt(jnp.sum(f * f, axis=1, keepdims=True) / DM + EPSILON)
    return (f * inv * gain).astype(BF)


def project_kernel(layout, n_halo, *refs):
    info = refs[0]
    pieces = refs[1 : 1 + len(layout)]
    halos = refs[1 + len(layout) : 1 + len(layout) + n_halo]
    (
        tok_own, tok_got, conv_w, conv_b, dt_bias, a_log, table,
        wa_out, tok, tok_halo, normal, xbc, slope, xs, xt, bs, cs, raw, cum, cum_t, states,
        wa, ext, small, sems, out_sem,
    ) = refs[1 + len(layout) + n_halo :]
    step = pl.program_id(0)
    rows = tok_own.shape[0]
    nb = rows // CH
    me = info[0]

    def project(at, width):
        proj = dot(normal[...], wa[:, pl.ds(at, width)]).astype(BF).astype(F32)
        acts, heads = [], []
        for i in range(nb):
            head = proj[rows + i * HALO : rows + (i + 1) * HALO, :] * halo_used(info, i)
            body = proj[i * CH : (i + 1) * CH, :] * usable_of(info, i)
            heads.append(head)
            ext[i, :HALO, :width] = head
            ext[i, HALO:, :width] = body
            xbc[i * CH : (i + 1) * CH, :width] = body.astype(BF)
            pre = conv_b[:, pl.ds(at, width)]
            for lag in range(KC):
                tap = conv_w[KC - 1 - lag : KC - lag, pl.ds(at, width)]
                pre = pre + tap * ext[i, HALO - lag : HALO - lag + CH, :width]
            sg = sigmoid(pre)
            act = pre * sg
            slope[i * CH : (i + 1) * CH, :width] = (sg + act * (1.0 - sg)).astype(BF)
            acts.append(act)
        xbc[rows:, :width] = jnp.concatenate(heads, axis=0).astype(BF)
        return acts

    def out_copy():
        return pltpu.make_async_copy(wa, wa_out, out_sem)

    @pl.when(step == 0)
    def _():
        def copy_of(n):
            offset, core = layout[n]
            at = pl.multiple_of((me ^ offset) * pieces[n].shape[0], 16)
            return pltpu.make_async_copy(
                pieces[n], wa.at[pl.ds(at, pieces[n].shape[0]), :], sems.at[n]
            )

        for n, (offset, core) in enumerate(layout):
            if core is None:
                copy_of(n).start()
            else:
                pl.when(me % 2 == core)(lambda n=n: copy_of(n).start())
        stay = info[1] > 0
        tok[...] = jnp.where(stay, tok_own[...], tok_got[...])
        found = []
        for i in range(nb):
            own, has_prev = place_of(info, i), place_of(info, i) > first_of(info, i)
            total = jnp.zeros((HALO, DM), F32)
            for o in range(n_halo):
                part = halos[o][...].astype(F32)
                for b in range(nb):
                    hit = (place_of(info, o * nb + b) == own - 1) & has_prev
                    total = total + jnp.where(hit, part[b * HALO : (b + 1) * HALO, :], 0.0)
            found.append(total)
        tok_halo[...] = jnp.concatenate(found, axis=0).astype(BF)
        for n, (offset, core) in enumerate(layout):
            if core is None:
                copy_of(n).wait()
            else:
                pl.when(me % 2 == core)(lambda n=n: copy_of(n).wait())
        out_copy().start()
        gain = wa[:, XBC : XBC + LANES].astype(F32).T[NH : NH + 1, :]
        normal[:rows, :] = normal_rows(tok[...], gain)
        normal[rows:, :] = normal_rows(tok_halo[...], gain)
        for i, act in enumerate(project(DI, 2 * NS)):
            bs[i * CH : (i + 1) * CH, :] = act[:, :NS].astype(BF)
            cs[i * CH : (i + 1) * CH, :] = act[:, NS:].astype(BF)
        xbc[:, 2 * NS :] = jnp.zeros((xbc.shape[0], CW - 2 * NS), BF)
        slope[:, 2 * NS :] = jnp.zeros((rows, CW - 2 * NS), BF)
        first = dot(normal[:rows, :], wa[:, XBC : XBC + LANES]).astype(BF).astype(F32) + dt_bias[...]
        raw[...] = first
        dt_all = softplus(first)
        rate = jnp.exp(a_log[...])
        causal = (iota((CH, CH), 0) >= iota((CH, CH), 1)).astype(F32).astype(BF)
        states[:, :, DI:] = jnp.zeros((nb, NS, LANES), BF)
        for i in range(nb):
            dt = dt_all[i * CH : (i + 1) * CH, :]
            parts = dot(causal, jnp.concatenate(pieces3(-dt * rate), axis=1))
            run = parts[:, :LANES] + parts[:, LANES : 2 * LANES] + parts[:, 2 * LANES :]
            cum[i * CH : (i + 1) * CH, :] = run
            cum_t[:, i * CH : (i + 1) * CH] = run.T
            last = run[CH - 1 : CH, :]
            ends = jnp.concatenate(pieces3(last) + (jnp.zeros((13, LANES), BF),), axis=0)
            states[i, :16, DI:] = ends
            small[i, 0] = jnp.concatenate(pieces2(dt), axis=1)
            small[i, 1] = jnp.concatenate(pieces2(jnp.exp(last - run) * dt), axis=1)

    @pl.when(step > 0)
    def _():
        at = pl.multiple_of((step - 1) * CW, CW)
        for i, act in enumerate(project(at, CW)):
            r = slice(i * CH, (i + 1) * CH)
            xs[r, :] = act.astype(BF)
            xt[r, :] = (act * dot(small[i, 0], table[...])).astype(BF)
            weighted = (act * dot(small[i, 1], table[...])).astype(BF)
            states[i, :, pl.ds(at, CW)] = dot_tn(bs[r, :], weighted).astype(BF)

    @pl.when(step == NCW)
    def _():
        out_copy().wait()


def run_project(info, parts, halos, tok_own, tok_got, conv_w, conv_b, dt_bias, a_log, table):
    rows = tok_own.shape[0]
    nb = rows // CH
    ext_rows = rows + nb * HALO
    layout = [(offset, core) for _, offset, core in parts]

    def before(s):
        return jnp.maximum(s - 1, 0)

    def tail_first(s):
        return jnp.where(s == 0, NCW, s - 1)

    ins = [(info, in_smem())] + [(v, in_hbm()) for v, _, _ in parts]
    ins += [(v, whole(v)) for v in halos]
    ins += [(v, whole(v)) for v in (tok_own, tok_got, conv_w, conv_b, dt_bias, a_log)]
    ins += [(table, columns(table, before))]
    outs = {
        "wa": (shape((DM, WA), BF), in_hbm()),
        "tok": (shape((rows, DM), BF), whole),
        "tok_halo": (shape((nb * HALO, DM), BF), whole),
        "normal": (shape((ext_rows, DM), BF), whole),
        "xbc": (shape((ext_rows, WA), BF), lambda v: columns(v, tail_first)),
        "slope": (shape((rows, WA), BF), lambda v: columns(v, tail_first)),
        "xs": (shape((rows, DI), BF), lambda v: columns(v, before)),
        "xt": (shape((rows, DI), BF), lambda v: columns(v, before)),
        "bs": (shape((rows, NS), BF), whole),
        "cs": (shape((rows, NS), BF), whole),
        "raw": (shape((rows, LANES), F32), whole),
        "cum": (shape((rows, LANES), F32), whole),
        "cum_t": (shape((LANES, rows), F32), whole),
        "states": (shape((nb, NS, DI + LANES), BF), whole),
    }
    out_list = [(o, s(o) if callable(s) else s) for o, s in outs.values()]
    scratch = [
        pltpu.VMEM((DM, WA), BF), pltpu.VMEM((nb, HALO + CH, CW), F32),
        pltpu.VMEM((nb, 2, CH, 2 * LANES), BF), pltpu.SemaphoreType.DMA((len(parts),)),
        pltpu.SemaphoreType.DMA,
    ]
    got = call(
        functools.partial(project_kernel, layout, len(halos)), (NCW + 1,), ins, out_list, scratch,
        2 * ext_rows * DM * WA * 2,
    )
    return dict(zip(outs, got))


PER = CW // HD
HALF = CH // 2


def chunk_heads(cum, first):
    return pltpu.roll(cum, lax.rem(LANES - first, LANES), axis=1)


def intra_kernel(bs, cs, xt, cum, cum_t, out, scores):
    c = pl.program_id(0)
    nb = bs.shape[0] // CH
    low = iota((CH, LANES), 1) < HD
    keep = iota((HALF, HALF), 0) >= iota((HALF, HALF), 1)

    @pl.when(c == 0)
    def _():
        for i in range(nb):
            r = slice(i * CH, (i + 1) * CH)
            scores[i] = dot_nt(cs[r, :], bs[r, :])

    for i in range(nb):
        r = slice(i * CH, (i + 1) * CH)
        cols = chunk_heads(cum[r, :], c * PER)
        for p in range(PER // 2):
            lanes = slice(p * LANES, (p + 1) * LANES)
            both = xt[r, lanes]
            got = []
            for k in range(2):
                h = 2 * p + k
                col = cols[:, h : h + 1]
                row = cum_t[pl.ds(c * PER + h, 1), r]
                a, b = col[:HALF], col[HALF:]
                s, t = row[:, :HALF], row[:, HALF:]
                upper = jnp.where(keep, jnp.exp(a - s), 0.0) * scores[i, :HALF, :HALF]
                left = jnp.exp(b - s) * scores[i, HALF:, :HALF]
                right = jnp.where(keep, jnp.exp(b - t), 0.0) * scores[i, HALF:, HALF:]
                lower = jnp.concatenate([left.astype(BF), right.astype(BF)], axis=1)
                got.append(
                    jnp.concatenate([dot(upper.astype(BF), both[:HALF, :]), dot(lower, both)], axis=0)
                )
            out[r, lanes] = jnp.where(low, got[0], got[1])


def middle_kernel(
    bs, cs, xt, cum, cum_t, normal, cot, zo_z, zo_o, out, z, q, wz, wo, scores
):
    wz[...] = zo_z[...]
    z[...] = dot(normal[...], zo_z[...]).astype(BF)
    unit_rows = zo_o.shape[0] // 2
    parts = []
    for k in range(2):
        block = zo_o[k * unit_rows : (k + 1) * unit_rows, :]
        parts += [block[:, :DM], block[:, DM:]]
    rows_o = jnp.concatenate(parts, axis=0)
    wo[...] = rows_o
    q[...] = dot_nt(cot[...], rows_o).astype(BF)
    intra_kernel(bs, cs, xt, cum, cum_t, out, scores)


def run_middle(a, cot, zo):
    rows = cot.shape[0]
    nb = rows // CH

    def same(c):
        return c

    ins = [(a[k], whole(a[k])) for k in ("bs", "cs")]
    ins += [(a["xt"], columns(a["xt"], same))]
    ins += [(a[k], whole(a[k])) for k in ("cum", "cum_t")]
    ins += [(a["normal"], pl.BlockSpec((rows, DM), lambda c: (0, 0))), (cot, whole(cot))]
    ins += [(zo, columns(zo, same)), (zo, pl.BlockSpec((DM // NCW, DI), lambda c: (c, 1)))]
    wide, wide_f = shape((rows, DI), BF), shape((rows, DI), F32)
    wz, wo = shape((DM, DI), BF), shape((DI, DM), BF)
    outs = [(v, columns(v, same)) for v in (wide_f, wide, wide, wz)]
    outs += [(wo, pl.BlockSpec((CW, DM), lambda c: (c, 0)))]
    return call(
        middle_kernel, (NCW,), ins, outs, [pltpu.VMEM((nb, CH, CH), F32)],
        2 * rows * CH * DI * 2 + 4 * rows * DM * DI,
    )


def run_intra(a):
    rows = a["bs"].shape[0]
    nb = rows // CH
    ins = [(a[k], whole(a[k])) for k in ("bs", "cs")]
    ins += [(a["xt"], columns(a["xt"], lambda c: c))]
    ins += [(a[k], whole(a[k])) for k in ("cum", "cum_t")]
    out = shape((rows, DI), F32)
    return call(
        intra_kernel, (NCW,), ins, [(out, columns(out, lambda c: c))],
        [pltpu.VMEM((nb, CH, CH), F32)], 2 * rows * CH * DI * 2,
    )[0]


def terms_kernel(normal, dz, normed, cot, out):
    c = pl.program_id(0)
    out[:, pl.ds(pl.multiple_of(c * CW, CW), CW)] = dot_tn(normal[...], dz[...]).astype(BF)
    part = dot_tn(normed[...], cot[...]).astype(BF)
    unit_rows = CW // 4
    for k in range(2):
        at = pl.multiple_of((2 * c + k) * unit_rows, unit_rows)
        for j in range(2):
            rows = part[(2 * k + j) * unit_rows : (2 * k + j + 1) * unit_rows, :]
            out[pl.ds(at, unit_rows), DI + j * DM : DI + (j + 1) * DM] = rows


def run_terms(normal, dz, normed, cot):
    rows = dz.shape[0]

    def same(c):
        return c

    out = shape((DM, DI + 2 * DM), BF)
    return call(
        terms_kernel, (NCW,),
        [
            (normal, pl.BlockSpec((rows, DM), lambda c: (0, 0))), (dz, columns(dz, same)),
            (normed, columns(normed, same)), (cot, whole(cot)),
        ],
        [(out, whole(out))], [], 8 * rows * DM * DI,
    )[0]


def gate_kernel(n_pieces, *refs):
    info = refs[0]
    pieces = refs[1 : 1 + n_pieces]
    ends = refs[1 + n_pieces : 1 + 2 * n_pieces]
    (
        y_intra, cs, cum, xs, z, q, inner_gain, d_skip, table,
        enter, normed, gain_part, dz, dyr, dye, product, skip_part, d_enter,
        y_scan, small, weights, squares, dots,
    ) = refs[1 + 2 * n_pieces :]
    phase, c = pl.program_id(0), pl.program_id(1)
    rows = cs.shape[0]
    nb = rows // CH
    n_all = n_pieces * nb
    here = pl.ds(pl.multiple_of(c * CW, CW), CW)

    @pl.when((phase == 0) & (c == 0))
    def _():
        weights[...] = carry_weights(info, clast_rows(ends, nb), nb, False)
        squares[...] = jnp.zeros_like(squares)
        dots[...] = jnp.zeros_like(dots)
        for i in range(nb):
            r = slice(i * CH, (i + 1) * CH)
            small[r, :] = jnp.concatenate(pieces2(jnp.exp(cum[r, :])), axis=1)

    @pl.when(phase == 0)
    def _():
        wide_w = dot(weights[...], table[...])
        totals = [jnp.zeros((NS, CW), F32) for _ in range(nb)]
        for j in range(n_all):
            piece = pieces[j // nb][j % nb].astype(F32)
            for i in range(nb):
                totals[i] = totals[i] + wide_w[i * n_all + j : i * n_all + j + 1, :] * piece
        for i in range(nb):
            r = slice(i * CH, (i + 1) * CH)
            low = totals[i].astype(BF)
            enter[i, :, here] = low
            scan = y_intra[r, :] + dot(small[r, :], table[...]) * dot(cs[r, :], low)
            y_scan[r, here] = scan
            y = scan + d_skip[...] * xs[r, :].astype(F32)
            zf = z[r, :].astype(F32)
            gated = y * (zf * sigmoid(zf))
            qg = q[r, :].astype(F32) * inner_gain[...] * usable_of(info, i)
            squares[r, :] += jnp.sum(gated * gated, axis=1, keepdims=True)
            dots[r, :] += jnp.sum(qg * gated, axis=1, keepdims=True)

    @pl.when(phase == 1)
    def _():
        gain_sum = jnp.zeros((1, CW), F32)
        skip_sum = jnp.zeros((1, CW), F32)
        for i in range(nb):
            r = slice(i * CH, (i + 1) * CH)
            inv = lax.rsqrt(squares[r, :] / DI + EPSILON)
            slope = inv * inv * inv * dots[r, :] / DI
            use = usable_of(info, i)
            scan = y_scan[r, here]
            x = xs[r, :].astype(F32)
            y = scan + d_skip[...] * x
            zf = z[r, :].astype(F32)
            sg = sigmoid(zf)
            sz = zf * sg
            gated = y * sz
            qf = q[r, :].astype(F32) * use
            scaled = gated * inv
            normed[r, :] = (scaled * inner_gain[...] * use).astype(BF)
            gain_sum = gain_sum + jnp.sum(qf * scaled, axis=0, keepdims=True)
            gg = inv * qf * inner_gain[...] - gated * slope
            dz[r, :] = (gg * y * (sg + sz * (1.0 - sg))).astype(BF)
            dy = gg * sz
            low = dy.astype(BF)
            dyr[r, :] = low
            product[r, :] = low.astype(F32) * scan
            skip_sum = skip_sum + jnp.sum(dy * x, axis=0, keepdims=True)
            back = (dot(small[r, :], table[...]) * dy).astype(BF)
            dye[r, :] = back
            d_enter[i] = dot_tn(cs[r, :], back).astype(BF)
        gain_part[...] = gain_sum
        skip_part[...] = skip_sum


def run_gate(info, a, pieces, y_intra, z, q, inner_gain, d_skip, table):
    rows = z.shape[0]
    nb = rows // CH

    def early(p, c):
        return jnp.where(p == 0, c, NCW - 1)

    def both(p, c):
        return c

    def late(p, c):
        return jnp.where(p == 0, 0, c)

    ins = [(info, in_smem())]
    ins += [(v, columns(v, early)) for v in pieces]
    ins += [(v, pl.BlockSpec((nb, 16, LANES), lambda p, c: (0, 0, DI // LANES))) for v in pieces]
    ins += [(y_intra, columns(y_intra, early))]
    ins += [(a[k], whole(a[k])) for k in ("cs", "cum")]
    ins += [(v, columns(v, both)) for v in (a["xs"], z, q, inner_gain, d_skip, table)]
    wide = shape((rows, DI), BF)
    wide_f = shape((rows, DI), F32)
    row = shape((1, DI), F32)
    state = shape((nb, NS, DI), BF)
    outs = [(state, whole(state))]
    outs += [(v, columns(v, late)) for v in (wide, row, wide, wide, wide, wide_f, row, state)]
    scratch = [
        pltpu.VMEM((rows, DI), F32), pltpu.VMEM((rows, 2 * LANES), BF),
        pltpu.VMEM((nb * nb * len(pieces), 2 * LANES), BF), pltpu.VMEM((rows, 1), F32),
        pltpu.VMEM((rows, 1), F32),
    ]
    return call(
        functools.partial(gate_kernel, len(pieces)), (2, NCW), ins, outs, scratch,
        2 * rows * NS * DI * 8,
    )


def intra_back_kernel(bs, cs, xt, cum, cum_t, dyr, dye, enter, dxt, db, dc, scores, top, bottom):
    c = pl.program_id(0)
    nb = bs.shape[0] // CH
    low = iota((CH, LANES), 1) < HD
    keep = iota((HALF, HALF), 1) >= iota((HALF, HALF), 0)

    @pl.when(c == 0)
    def _():
        for i in range(nb):
            r = slice(i * CH, (i + 1) * CH)
            scores[i] = dot_nt(bs[r, :], cs[r, :])
        top[...] = jnp.zeros_like(top)
        bottom[...] = jnp.zeros_like(bottom)
        dc[...] = jnp.zeros_like(dc)

    for i in range(nb):
        r = slice(i * CH, (i + 1) * CH)
        cols = chunk_heads(cum[r, :], c * PER)
        dc[r, :] += dot_nt(dye[r, :], enter[i])
        top_sum, bottom_sum = top[i], bottom[i]
        for p in range(PER // 2):
            lanes = slice(p * LANES, (p + 1) * LANES)
            x, dy = xt[r, lanes], dyr[r, lanes]
            got = []
            for k in range(2):
                h = 2 * p + k
                col = cols[:, h : h + 1]
                row = cum_t[pl.ds(c * PER + h, 1), r]
                a, b = col[:HALF], col[HALF:]
                s, t = row[:, :HALF], row[:, HALF:]
                left = jnp.where(keep, jnp.exp(s - a), 0.0)
                right = jnp.exp(t - a)
                last = jnp.where(keep, jnp.exp(t - b), 0.0)
                dec = jnp.concatenate([left, right], axis=1)
                got.append(
                    jnp.concatenate(
                        [
                            dot((dec * scores[i, :HALF, :]).astype(BF), dy),
                            dot((last * scores[i, HALF:, HALF:]).astype(BF), dy[HALF:, :]),
                        ],
                        axis=0,
                    )
                )
                own = jnp.where(low, x, 0) if k == 0 else jnp.where(low, 0, x)
                top_sum = top_sum + dot_nt(own[:HALF, :], dy) * dec
                bottom_sum = bottom_sum + dot_nt(own[HALF:, :], dy[HALF:, :]) * last
            dxt[r, lanes] = jnp.where(low, got[0], got[1])
        top[i], bottom[i] = top_sum, bottom_sum

    @pl.when(c == NCW - 1)
    def _():
        for i in range(nb):
            r = slice(i * CH, (i + 1) * CH)
            up, down = top[i].astype(BF), bottom[i].astype(BF)
            down = jnp.concatenate([jnp.zeros((HALF, HALF), BF), down], axis=1)
            both = jnp.concatenate([up, down], axis=0)
            db[r, :] = dot(both, cs[r, :])
            dc[r, :] += dot_tn(both, bs[r, :])


def run_intra_back(a, dyr, dye, enter):
    rows = dyr.shape[0]
    nb = rows // CH

    def same(c):
        return c

    ins = [(a[k], whole(a[k])) for k in ("bs", "cs")]
    ins += [(a["xt"], columns(a["xt"], same))]
    ins += [(a[k], whole(a[k])) for k in ("cum", "cum_t")]
    ins += [(v, columns(v, same)) for v in (dyr, dye, enter)]
    full, small = shape((rows, DI), F32), shape((rows, NS), F32)
    return call(
        intra_back_kernel, (NCW,), ins,
        [(full, columns(full, same)), (small, whole(small)), (small, whole(small))],
        [
            pltpu.VMEM((nb, CH, CH), F32), pltpu.VMEM((nb, HALF, CH), F32),
            pltpu.VMEM((nb, HALF, HALF), F32),
        ],
        2 * rows * CH * DI * 4,
    )


def back_kernel(n_pieces, *refs):
    info = refs[0]
    pieces = refs[1 : 1 + n_pieces]
    ends = refs[1 + n_pieces : 1 + 2 * n_pieces]
    (
        dx_intra, db_in, dc_in, xbc, slope, xs, xt, bs, raw, cum, enter, product, dyr, conv_w,
        a_log, d_skip, table, narrow,
        d_a, kernel_part, offset_part, bias_part, rate_part,
        grad, small, d_bs, heads, weights,
    ) = refs[1 + 2 * n_pieces :]
    step = pl.program_id(0)
    rows = xs.shape[0]
    nb = rows // CH
    n_all = n_pieces * nb

    @pl.when(step == 0)
    def _():
        weights[...] = carry_weights(info, clast_rows(ends, nb), nb, True)
        dt_all = softplus(raw[...])
        for i in range(nb):
            r = slice(i * CH, (i + 1) * CH)
            last = cum[(i + 1) * CH - 1 : (i + 1) * CH, :]
            small[i, 0] = jnp.concatenate(pieces2(dt_all[r, :]), axis=1)
            small[i, 1] = jnp.concatenate(pieces2(jnp.exp(last - cum[r, :])), axis=1)
            grad[i, :HALO, :] = jnp.zeros((HALO, CW), F32)
            grad[i, HALO + CH :, :] = jnp.zeros((HALO, CW), F32)
        d_bs[...] = db_in[...]
        heads[...] = jnp.zeros_like(heads)

    def convolve_back(dacts, width):
        offset_sum = jnp.zeros((1, width), F32)
        tap_sums = [jnp.zeros((1, width), F32) for _ in range(KC)]
        all_heads = xbc[rows:, :width].astype(F32)
        head_grads = []
        for i in range(nb):
            r = slice(i * CH, (i + 1) * CH)
            dpre = dacts[i] * slope[r, :width].astype(F32)
            offset_sum = offset_sum + jnp.sum(dpre, axis=0, keepdims=True)
            grad[i, HALO : HALO + CH, :width] = dpre
            body = xbc[r, :width].astype(F32)
            head = all_heads[i * HALO : (i + 1) * HALO, :]
            total = jnp.zeros((CH, width), F32)
            total_head = jnp.zeros((HALO, width), F32)
            for lag in range(KC):
                tap = conv_w[KC - 1 - lag : KC - lag, :width]
                later = grad[i, HALO + lag : HALO + lag + CH, :width]
                later_head = grad[i, lag : lag + HALO, :width]
                total = total + tap * later
                total_head = total_head + tap * later_head
                tap_sums[KC - 1 - lag] = (
                    tap_sums[KC - 1 - lag]
                    + jnp.sum(later * body, axis=0, keepdims=True)
                    + jnp.sum(later_head * head, axis=0, keepdims=True)
                )
            d_a[r, :width] = (total * usable_of(info, i)).astype(BF)
            head_grads.append(total_head * halo_used(info, i))
        d_a[rows:, :width] = jnp.concatenate(head_grads, axis=0).astype(BF)
        offset_part[:, :width] = offset_sum
        for k in range(KC):
            kernel_part[k : k + 1, :width] = tap_sums[k]

    @pl.when(step < NCW)
    def _():
        wide_w = dot(weights[...], table[...])
        totals = [jnp.zeros((NS, CW), F32) for _ in range(nb)]
        for j in range(n_all):
            piece = pieces[j // nb][j % nb].astype(F32)
            for i in range(nb):
                totals[i] = totals[i] + wide_w[i * n_all + j : i * n_all + j + 1, :] * piece
        select = narrow[...]
        dacts = []
        for i in range(nb):
            r = slice(i * CH, (i + 1) * CH)
            low = totals[i].astype(BF)
            fade = jnp.sum(low.astype(F32) * enter[i].astype(F32), axis=0, keepdims=True)
            end_w = dot(small[i, 1], table[...])
            x_dt = xt[r, :].astype(F32)
            inter = end_w * dot(bs[r, :], low)
            d_bs[r, :] += dot_nt((x_dt * end_w).astype(BF), low)
            dxt = dx_intra[r, :] + inter
            flow = jnp.sum(x_dt * inter, axis=0, keepdims=True)
            hi, mid, lo = pieces3(product[r, :] - x_dt * dxt)
            heads[0, r, :] += dot(hi, select) + dot(mid, select) + dot(lo, select)
            heads[1, r, :] += dot((xs[r, :].astype(F32) * dxt).astype(BF), select)
            hi, mid, lo = pieces3(jnp.concatenate([flow, fade, jnp.zeros((6, CW), F32)], axis=0))
            heads[2, i * 8 : (i + 1) * 8, :] += dot(hi, select) + dot(mid, select) + dot(lo, select)
            dacts.append(
                dot(small[i, 0], table[...]) * dxt + d_skip[...] * dyr[r, :].astype(F32)
            )
        convolve_back(dacts, CW)

    @pl.when(step == NCW)
    def _():
        dacts = []
        for i in range(nb):
            r = slice(i * CH, (i + 1) * CH)
            dacts.append(jnp.concatenate([d_bs[r, :], dc_in[r, :]], axis=1))
        convolve_back(dacts, 2 * NS)
        rate = jnp.exp(a_log[...])
        anti = (iota((CH, CH), 0) <= iota((CH, CH), 1)).astype(F32).astype(BF)
        bias_sum = jnp.zeros((1, LANES), F32)
        rate_sum = jnp.zeros((1, LANES), F32)
        for i in range(nb):
            r = slice(i * CH, (i + 1) * CH)
            last = cum[(i + 1) * CH - 1 : (i + 1) * CH, :]
            flow, fade = heads[2, i * 8 : i * 8 + 1, :], heads[2, i * 8 + 1 : i * 8 + 2, :]
            parts = dot(anti, jnp.concatenate(pieces3(heads[0, r, :]), axis=1))
            d_log = parts[:, :LANES] + parts[:, LANES : 2 * LANES] + parts[:, 2 * LANES :]
            d_log = d_log + (flow + jnp.exp(last) * fade)
            start = raw[r, :]
            d_raw = (heads[1, r, :] - d_log * rate) * sigmoid(start)
            d_raw = jnp.where(iota((CH, LANES), 1) < NH, d_raw, 0.0)
            bias_sum = bias_sum + jnp.sum(d_raw, axis=0, keepdims=True)
            rate_sum = rate_sum - jnp.sum(d_log * softplus(start), axis=0, keepdims=True) * rate
            d_a[r, 2 * NS :] = d_raw.astype(BF)
        d_a[rows:, 2 * NS :] = jnp.zeros((nb * HALO, CW - 2 * NS), BF)
        bias_part[...] = bias_sum
        rate_part[...] = rate_sum


def run_back(
    info, a, pieces, ends, dx_intra, db, dc, enter, product, dyr, conv_w, a_log, d_skip, table
):
    rows = dyr.shape[0]
    nb = rows // CH
    ext_rows = rows + nb * HALO

    def chunk(s):
        return jnp.minimum(s, NCW - 1)

    def same(s):
        return s

    narrow = table[:LANES].T
    ins = [(info, in_smem())]
    ins += [(v, columns(v, chunk)) for v in pieces]
    ins += [(v, pl.BlockSpec((nb, 16, LANES), lambda s: (0, 0, DI // LANES))) for v in ends]
    ins += [(dx_intra, columns(dx_intra, chunk)), (db, whole(db)), (dc, whole(dc))]
    ins += [(a["xbc"], columns(a["xbc"], same)), (a["slope"], columns(a["slope"], same))]
    ins += [(a["xs"], columns(a["xs"], chunk)), (a["xt"], columns(a["xt"], chunk))]
    ins += [(a[k], whole(a[k])) for k in ("bs", "raw", "cum")]
    ins += [(v, columns(v, chunk)) for v in (enter, product, dyr)]
    ins += [(conv_w, columns(conv_w, same)), (a_log, whole(a_log)), (d_skip, columns(d_skip, chunk))]
    ins += [(table, columns(table, chunk))]
    ins += [(narrow, pl.BlockSpec((CW, LANES), lambda s: (chunk(s), 0)))]
    wide, taps, row = shape((ext_rows, WA), BF), shape((KC, WA), F32), shape((1, WA), F32)
    lane = shape((1, LANES), F32)
    outs = [(v, columns(v, same)) for v in (wide, taps, row)]
    outs += [(lane, whole(lane)), (lane, whole(lane))]
    scratch = [
        pltpu.VMEM((nb, CH + 2 * HALO, CW), F32), pltpu.VMEM((nb, 2, CH, 2 * LANES), BF),
        pltpu.VMEM((rows, NS), F32), pltpu.VMEM((3, rows, LANES), F32),
        pltpu.VMEM((nb * nb * len(pieces), 2 * LANES), BF),
    ]
    return call(
        functools.partial(back_kernel, len(pieces)), (NCW + 1,), ins, outs, scratch,
        2 * rows * NS * DI * 16,
    )


def unit(rows):
    f = rows.astype(F32)
    inv = lax.rsqrt(jnp.mean(f * f, axis=1, keepdims=True) + EPSILON)
    return f * inv, inv


def norm_back(normal_grad, rows, gain):
    u, inv = unit(rows)
    g = normal_grad * gain[None, :]
    return inv * (g - u * jnp.mean(g * u, axis=1, keepdims=True))


def shards(
    tokens, norm_gain, in_weight, conv_weight, conv_bias, dt_bias, a_log, d_skip, inner_gain,
    out_weight, block_place, seq_length, cotangent,
):
    n_head, n_shard = lax.axis_size("head"), lax.axis_size("shard")
    half = n_head // 2
    head_at, shard_at = lax.axis_index("head"), lax.axis_index("shard")
    rows = tokens.shape[0]
    nb = rows // CH
    group_blocks = nb * n_head
    k_rows = in_weight.shape[0]
    stay = (head_at // half) == (shard_at & 1)

    piece_a = jnp.concatenate(
        [in_weight[:, DI:], norm_gain[:, None], jnp.zeros((k_rows, WA - XBC - NH - 1), BF)], axis=1
    )
    parts_a = gather_pieces(piece_a)
    me = shard_at.astype(jnp.int32)
    if k_rows % 32:
        joined = jnp.zeros((n_shard, k_rows, WA), BF)
        for v, k, _ in parts_a:
            joined = lax.dynamic_update_slice(joined, v[None], (shard_at ^ k, 0, 0))
        parts_a, me = [(joined.reshape(DM, WA), 0, None)], jnp.int32(0)
    piece_zo = jnp.concatenate(
        [in_weight[:, :DI], out_weight[:k_rows], out_weight[k_rows:]], axis=1
    )
    zo = lax.all_gather(piece_zo, "shard", axis=0, tiled=True)

    tails = tokens.reshape(nb, CH, DM)[:, CH - HALO :].reshape(nb * HALO, DM)
    tails = group_spread(tails, stay)
    tok_got = move_home(after(tokens, tails[0]))
    cot_got = move_home(after(cotangent, tok_got))

    numbers = jnp.concatenate([block_place, seq_length], axis=1)
    numbers = jnp.where(stay, numbers, trade(numbers, "shard", 1))[0]
    lengths = [numbers[group_blocks + k] for k in range(seq_length.shape[1])]
    ids = []
    for core in (0, 1):
        for z in range(half):
            device = (head_at % half ^ z) + ((shard_at & 1) ^ core) * half
            ids += [device * nb + b for b in range(nb)]
    ids = jnp.stack(ids)
    places = jnp.sum(
        jnp.where(ids[:, None] == jnp.arange(group_blocks)[None, :], numbers[None, :group_blocks], 0),
        axis=1,
    )
    first, in_seq, begin = jnp.zeros_like(places), jnp.zeros_like(places), 0
    for length in lengths:
        first = jnp.where(places >= begin, begin, first)
        in_seq = jnp.where(places >= begin, length, in_seq)
        begin = begin + (length + CH - 1) // CH
    info = jnp.concatenate(
        [
            jnp.stack([me, stay.astype(jnp.int32)]),
            jnp.stack([places, first, in_seq], axis=1).reshape(-1),
        ]
    ).astype(jnp.int32)

    table = spread_table()

    def head_row(v):
        return jnp.pad(v, (0, LANES - NH))[None]

    taps = jnp.pad(conv_weight, ((0, 0), (0, WA - XBC)))
    rate_row = head_row(a_log)
    skip_row = jnp.repeat(d_skip, HD)[None]
    a = run_project(
        info, parts_a, tails, tokens, tok_got, taps, jnp.pad(conv_bias, (0, WA - XBC))[None],
        head_row(dt_bias), rate_row, table,
    )
    wa, tok, normal = a["wa"], a["tok"], a["normal"]
    state_by_head = head_pieces(a["states"])
    state_by_core = trade(a["states"], "shard", 1)
    cot = jnp.where(stay, cotangent, after(cot_got, a["cum"]))
    if k_rows % 32:
        wz = zo[:, :DI]
        wo = zo[:, DI:].reshape(n_shard, k_rows, 2, DM).swapaxes(1, 2).reshape(DI, DM)
        z, q, y_intra = dot(normal[:rows], wz).astype(BF), dot_nt(cot, wo).astype(BF), run_intra(a)
    else:
        y_intra, z, q, wz, wo = run_middle(a, cot, zo)
    state_by_head = [after(v, y_intra) for v in state_by_head]
    all_states = (
        [a["states"]] + state_by_head + [state_by_core] + [trade(v, "shard", 1) for v in state_by_head]
    )
    enter, normed, gain_part, dz, dyr, dye, product, skip_part, d_enter = run_gate(
        info, a, all_states, y_intra, z, q, inner_gain[None], skip_row, table
    )
    enter_by_head = head_pieces(d_enter)
    enter_by_core = trade(d_enter, "shard", 1)
    if k_rows % 32:
        z_term = dot_tn(normal[:rows], dz).astype(BF)
        out_term = dot_tn(normed, cot).astype(BF).reshape(n_shard, 2, k_rows, DM)
        out_term = out_term.swapaxes(1, 2).reshape(DM, 2 * DM)
        zo_term = jnp.concatenate([z_term, out_term], axis=1)
    else:
        zo_term = run_terms(normal, dz, normed, cot)
    zo_own = lax.psum_scatter(zo_term, "shard", scatter_dimension=0, tiled=True)
    dx_intra, db, dc = run_intra_back(a, after(dyr, zo_term), dye, enter)
    mixed = (tok.astype(F32) + dot(after(normed, dx_intra), wo)).astype(BF)
    enter_by_head = [after(v, mixed) for v in enter_by_head]
    all_enter = (
        [d_enter] + enter_by_head + [enter_by_core] + [trade(v, "shard", 1) for v in enter_by_head]
    )
    mixed_got = move_home(after(mixed, all_enter[-1]))
    d_a_all, kernel_part, offset_part, bias_part, rate_part = run_back(
        info, a, all_enter, all_states, dx_intra, db, dc, enter, product, dyr, taps, rate_row,
        skip_row, table,
    )
    a_term = dot_tn(normal, d_a_all).astype(BF).reshape(n_shard, k_rows, WA)
    a_keep, a_give = core_give([a_term])
    a_got = trade(a_give, "shard", 1)

    small = jnp.concatenate(
        [
            kernel_part[:, :XBC].reshape(-1), offset_part[0, :XBC], bias_part[0, :NH],
            rate_part[0, :NH], jnp.sum(skip_part.reshape(NH, HD), axis=1), gain_part[0],
        ]
    )
    small = full_sum(after(small, a_give))

    d_a_all = after(d_a_all, a_give)
    normal_grad = dot_nt(dz, wz) + dot_nt(d_a_all[:rows], wa)
    halo_grad = dot_nt(d_a_all[rows:], wa)
    gain = wa[:, XBC + NH].astype(F32)
    token_grad = (cot.astype(F32) + norm_back(normal_grad, tok, gain)).astype(BF)
    halo_part = norm_back(halo_grad, a["tok_halo"], gain)

    a_pairs = chip_pairs(a_keep, a_got)
    a_far = chip_send(a_pairs)
    token_got = move_home(after(token_grad, a_pairs[0]))
    token_grad = jnp.where(stay, token_grad, token_got)
    all_halo = jnp.concatenate(group_gather(halo_part)).reshape(group_blocks, HALO, DM)
    is_next = (places[None, :] == places[:nb, None] + 1) & (first[None, :] == first[:nb, None])
    halo_back = swap_home(
        jnp.sum(jnp.where(is_next[:, :, None, None], all_halo[None], 0.0), axis=1), stay
    )
    token_grad = token_grad.reshape(nb, CH, DM)
    token_grad = token_grad.at[:, CH - HALO :].set(
        (token_grad[:, CH - HALO :].astype(F32) + halo_back).astype(BF)
    ).reshape(rows, DM)
    mixed = jnp.where(stay, mixed, after(mixed_got, a_give))

    zo_grad = head_sum(after(zo_own, a_pairs[0]))
    a_grad = head_sum(chip_sum(a_pairs[0], a_far))
    in_grad = jnp.concatenate([zo_grad[:, :DI], a_grad[:, : XBC + NH]], axis=1)
    out_grad = jnp.concatenate([zo_grad[:, DI : DI + DM], zo_grad[:, DI + DM :]], axis=0)
    gain_grad = jnp.sum(in_grad * in_weight.astype(F32), axis=1) / norm_gain.astype(F32)

    sizes = [KC * XBC, XBC, NH, NH, NH, DI]
    cuts = []
    at = 0
    for s in sizes:
        cuts.append(small[at : at + s])
        at += s
    return (
        mixed, token_grad, gain_grad, in_grad, cuts[0].reshape(KC, XBC), cuts[1], cuts[2], cuts[3],
        cuts[4], cuts[5], out_grad,
    )


def solution(mesh):
    return jax.shard_map(
        shards,
        mesh=mesh,
        in_specs=(
            P(("head", "shard"), None), P("shard"), P("shard", None), P(), P(), P(), P(), P(), P(),
            P("shard", None), P("shard", None), P("shard", None), P(("head", "shard"), None),
        ),
        out_specs=(
            P(("head", "shard"), None), P(("head", "shard"), None), P("shard"), P("shard", None),
            P(), P(), P(), P(), P(), P(), P("shard", None),
        ),
        check_vma=False,
    )
```

```python
import functools

import jax
import jax.numpy as jnp
from jax import lax
from jax.experimental import pallas as pl
from jax.experimental.pallas import tpu as pltpu
from jax.sharding import PartitionSpec as P

NH = 24
HD = 64
NS = 128
KC = 4
CH = 256
DI = 1536
DM = 768
XBC = DI + 2 * NS
WA = 1920
HALO = 8
EPSILON = 1e-05
F32 = jnp.float32
BF = jnp.bfloat16
LANES = 128
CW = 384
NCW = DI // CW
VMEM_ASK = 56 * 2**20
VMEM_ROOM = 56 * 2**20
COST_SCALE = 0.4


def trade(value, axis, bit):
    size = lax.axis_size(axis)
    return lax.ppermute(value, axis, [(i, i ^ bit) for i in range(size)])


def after(value, *others):
    return lax.optimization_barrier((value,) + others)[0]


def move_home(value):
    n_head, n_shard = lax.axis_size("head"), lax.axis_size("shard")
    half = n_head // 2
    pairs = []
    for h in range(n_head):
        for s in range(n_shard):
            upper, core = h // half, s & 1
            if upper != core:
                there = (h % half + core * half) * n_shard + (s - core + upper)
                pairs.append((h * n_shard + s, there))
    return lax.ppermute(value, ("head", "shard"), pairs)


def swap_home(value, stay):
    return jnp.where(stay, value, move_home(value))


def group_spread(value):
    n_head, n_shard = lax.axis_size("head"), lax.axis_size("shard")
    pieces = [value]
    for core in (0, 1):
        for low in range(n_head // 2):
            if core or low:
                pairs = [
                    (h * n_shard + s, (h ^ low) * n_shard + (s ^ core))
                    for h in range(n_head)
                    for s in range(n_shard)
                ]
                pieces.append(lax.ppermute(value, ("head", "shard"), pairs))
    return pieces


def group_gather(value):
    half = lax.axis_size("head") // 2
    pieces = [value]
    bit = 1
    while bit < half:
        pieces = pieces + [trade(v, "head", bit) for v in pieces]
        bit *= 2
    return pieces + [trade(v, "shard", 1) for v in pieces]


def gather_pieces(piece, *first):
    n_shard = lax.axis_size("shard")
    if n_shard != 8:
        held = {0: piece}
        bit = 1
        while bit < n_shard:
            held.update({k ^ bit: trade(v, "shard", bit) for k, v in list(held.items())})
            bit *= 2
        return [(v, k) for k, v in held.items()]

    far = [trade(piece, "shard", bit) for bit in (6, 2, 4)]
    near = [trade(v, "shard", 1) for v in after_all([piece] + far, *first)]
    return [(v, k) for v, k in zip([piece] + far + near, (0, 6, 2, 4, 1, 7, 3, 5))]


def head_pieces(value):
    pieces = [value]
    bit = 1
    while bit < lax.axis_size("head") // 2:
        pieces = pieces + [trade(v, "head", bit) for v in pieces]
        bit *= 2
    return pieces[1:]


def core_give(blocks):
    n_shard = lax.axis_size("shard")
    core = lax.axis_index("shard") % 2

    def half(which):
        parts = []
        for v in blocks:
            split = v.reshape((n_shard // 2, 2) + v.shape[1:])
            parts.append(lax.dynamic_index_in_dim(split, which, 1, False))
        return jnp.concatenate(parts, axis=2) if len(parts) > 1 else parts[0]

    return half(core), half(1 - core)


def chip_pairs(keep, got):
    pair = (keep.astype(F32) + got.astype(F32)).astype(BF)
    chip = lax.axis_index("shard") // 2
    return [lax.dynamic_index_in_dim(pair, chip ^ k, 0, False) for k in range(pair.shape[0])]


def after_all(values, *others):
    return list(lax.optimization_barrier((*values, *others)))[: len(values)]


def chip_send(pairs):
    return [trade(v, "shard", 2 * k) for k, v in enumerate(pairs) if k]


def chip_sum(own, got):
    total = own.astype(F32)
    for v in got:
        total = total + v.astype(F32)
    return total.astype(BF)


def split2(v):
    high = lax.reduce_precision(v, 8, 7)
    return jnp.concatenate([high.astype(BF), (v - high).astype(BF)], axis=1)


def join2(parts):
    high, low = jnp.split(parts, 2, axis=1)
    return high.astype(F32) + low.astype(F32)


def head_split(value):
    cut = value.shape[1] // 2
    odd = lax.axis_index("head") % 2
    return [lax.dynamic_slice_in_dim(value, at * cut, cut, 1) for at in (odd, 1 - odd)]


def head_add(keep, got):
    return (keep.astype(F32) + got.astype(F32)).astype(BF)


def head_join(half, other):
    odd = lax.axis_index("head") % 2
    return jnp.concatenate([jnp.where(odd, other, half), jnp.where(odd, half, other)], axis=1)


def dot(a, b):
    return jnp.dot(a, b, preferred_element_type=F32)


def dot_nt(a, b):
    return lax.dot_general(a, b, (((1,), (1,)), ((), ())), preferred_element_type=F32)


def dot_tn(a, b):
    return lax.dot_general(a, b, (((0,), (0,)), ((), ())), preferred_element_type=F32)


def spread_table():
    row = jnp.arange(2 * LANES)[:, None] % LANES
    return (row == jnp.arange(DI)[None, :] // HD).astype(BF)


def narrow_table():
    return (jnp.arange(DI)[:, None] // HD == jnp.arange(LANES)[None, :]).astype(BF)


def pieces2(v):
    hi = v.astype(BF)
    return hi, (v - hi.astype(F32)).astype(BF)


def pieces3(v):
    hi = v.astype(BF)
    rest = v - hi.astype(F32)
    mid = rest.astype(BF)
    return hi, mid, (rest - mid.astype(F32)).astype(BF)


def softplus(v):
    return jnp.maximum(v, 0.0) + jnp.log1p(jnp.exp(-jnp.abs(v)))


sigmoid = jax.nn.sigmoid


def shape(dims, dtype):
    return jax.ShapeDtypeStruct(dims, dtype)


def whole(arr):
    return pl.BlockSpec(arr.shape, lambda *g: (0,) * len(arr.shape))


def columns(arr, at, width=None):
    dims = arr.shape[:-1] + (width or CW,)
    return pl.BlockSpec(dims, lambda *g: (0,) * (len(dims) - 1) + (at(*g),))


def in_hbm():
    return pl.BlockSpec(memory_space=pl.ANY)


def in_smem():
    return pl.BlockSpec(memory_space=pltpu.SMEM)


def call(kernel, micros, grid, ins, outs, scratch, room=VMEM_ROOM):
    return pl.pallas_call(
        kernel,
        grid=grid,
        out_shape=[o for o, _ in outs],
        in_specs=[s for _, s in ins],
        out_specs=[s for _, s in outs],
        scratch_shapes=scratch,
        compiler_params=pltpu.CompilerParams(vmem_limit_bytes=room),
        cost_estimate=pl.CostEstimate(
            flops=1, bytes_accessed=int(micros * COST_SCALE * 3.7e6), transcendentals=0
        ),
    )(*[a for a, _ in ins])


def iota(dims, axis):
    return lax.broadcasted_iota(jnp.int32, dims, axis)


def place_of(info, q):
    return info[2 + 3 * q]


def first_of(info, q):
    return info[3 + 3 * q]


def usable_of(info, i):
    begin = (place_of(info, i) - first_of(info, i)) * CH
    return (iota((CH, 1), 0) + begin < info[4 + 3 * i]).astype(F32)


def halo_used(info, i):
    has_prev = place_of(info, i) > first_of(info, i)
    return (iota((HALO, 1), 0) + jnp.where(has_prev, 0, -HALO) > HALO - KC).astype(F32)


def clast_rows(refs, nb):
    rows = []
    for ref in refs:
        for b in range(nb):
            part = ref[b].astype(F32)
            rows.append(part[0:1, :] + part[1:2, :] + part[2:3, :])
    return rows


def carry_weights(info, ends, nb, into):
    n_all = len(ends)
    row = iota((n_all, 1), 0)
    place = jnp.zeros((n_all, 1), jnp.int32)
    first = jnp.zeros((n_all, 1), jnp.int32)
    for j in range(n_all):
        place = jnp.where(row == j, place_of(info, j), place)
        first = jnp.where(row == j, first_of(info, j), first)
    parts = []
    for i in range(nb):
        own = place_of(info, i)
        total = jnp.zeros((n_all, LANES), F32)
        for k in range(n_all):
            at = place_of(info, k)
            if into:
                between = (place > at) & (at > own)
            else:
                between = (place < at) & (at < own)
            total = total + jnp.where(between, ends[k], 0.0)
        if into:
            reach = (first <= own) & (place > own)
        else:
            reach = (place >= first_of(info, i)) & (place < own)
        parts.append(jnp.where(reach, jnp.exp(total), 0.0))
    return jnp.concatenate(pieces2(jnp.concatenate(parts, axis=0)), axis=1)


def normal_rows(rows, gain):
    f = rows.astype(F32)
    inv = lax.rsqrt(jnp.sum(f * f, axis=1, keepdims=True) / DM + EPSILON)
    return (f * inv * gain).astype(BF)


def project_kernel(layout, n_halo, *refs):
    info = refs[0]
    pieces = refs[1 : 1 + len(layout)]
    halos = refs[1 + len(layout) : 1 + len(layout) + n_halo]
    (
        tok_own, tok_got, conv_w, conv_b, dt_bias, a_log, table,
        wa_out, tok, tok_halo, normal, normal_t, xbc, slope, xs, xt, bs, cs, raw, cum, cum_t, states,
        wa, ext, small, sems, out_sem,
    ) = refs[1 + len(layout) + n_halo :]
    step = pl.program_id(0)
    rows = tok_own.shape[0]
    nb = rows // CH
    me = info[0]

    def project(at, width):
        proj = dot(normal[...], wa[:, pl.ds(at, width)]).astype(BF).astype(F32)
        acts, heads = [], []
        for i in range(nb):
            head = proj[rows + i * HALO : rows + (i + 1) * HALO, :] * halo_used(info, i)
            body = proj[i * CH : (i + 1) * CH, :] * usable_of(info, i)
            heads.append(head)
            ext[i, :HALO, :width] = head
            ext[i, HALO:, :width] = body
            xbc[i * CH : (i + 1) * CH, :width] = body.astype(BF)
            pre = conv_b[:, pl.ds(at, width)]
            for lag in range(KC):
                tap = conv_w[KC - 1 - lag : KC - lag, pl.ds(at, width)]
                pre = pre + tap * ext[i, HALO - lag : HALO - lag + CH, :width]
            sg = sigmoid(pre)
            act = pre * sg
            slope[i * CH : (i + 1) * CH, :width] = (sg + act * (1.0 - sg)).astype(BF)
            acts.append(act)
        xbc[rows:, :width] = jnp.concatenate(heads, axis=0).astype(BF)
        return acts

    def out_copy():
        return pltpu.make_async_copy(wa, wa_out, out_sem)

    @pl.when(step == 0)
    def _():
        def copy_of(n):
            at = pl.multiple_of((me ^ layout[n]) * pieces[n].shape[0], 16)
            return pltpu.make_async_copy(
                pieces[n], wa.at[pl.ds(at, pieces[n].shape[0]), :], sems.at[n]
            )

        for n in range(len(layout)):
            copy_of(n).start()
        stay = info[1] > 0
        tok[...] = jnp.where(stay, tok_own[...], tok_got[...])
        found = []
        for i in range(nb):
            own, has_prev = place_of(info, i), place_of(info, i) > first_of(info, i)
            total = jnp.zeros((HALO, DM), F32)
            for o in range(n_halo):
                part = halos[o][...].astype(F32)
                for b in range(nb):
                    hit = (place_of(info, o * nb + b) == own - 1) & has_prev
                    total = total + jnp.where(hit, part[b * HALO : (b + 1) * HALO, :], 0.0)
            found.append(total)
        tok_halo[...] = jnp.concatenate(found, axis=0).astype(BF)
        for n in range(len(layout)):
            copy_of(n).wait()
        out_copy().start()
        gain = wa[:, XBC : XBC + LANES].astype(F32).T[NH : NH + 1, :]
        normal[:rows, :] = normal_rows(tok[...], gain)
        normal_t[...] = normal[:rows, :].T
        normal[rows:, :] = normal_rows(tok_halo[...], gain)
        for i, act in enumerate(project(DI, 2 * NS)):
            bs[i * CH : (i + 1) * CH, :] = act[:, :NS].astype(BF)
            cs[i * CH : (i + 1) * CH, :] = act[:, NS:].astype(BF)
        xbc[:, 2 * NS :] = jnp.zeros((xbc.shape[0], CW - 2 * NS), BF)
        slope[:, 2 * NS :] = jnp.zeros((rows, CW - 2 * NS), BF)
        first = dot(normal[:rows, :], wa[:, XBC : XBC + LANES]).astype(BF).astype(F32) + dt_bias[...]
        raw[...] = first
        dt_all = softplus(first)
        rate = jnp.exp(a_log[...])
        causal = (iota((CH, CH), 0) >= iota((CH, CH), 1)).astype(F32).astype(BF)
        states[:, :, DI:] = jnp.zeros((nb, NS, LANES), BF)
        for i in range(nb):
            dt = dt_all[i * CH : (i + 1) * CH, :]
            parts = dot(causal, jnp.concatenate(pieces3(-dt * rate), axis=1))
            run = parts[:, :LANES] + parts[:, LANES : 2 * LANES] + parts[:, 2 * LANES :]
            cum[i * CH : (i + 1) * CH, :] = run
            cum_t[:, i * CH : (i + 1) * CH] = run.T
            last = run[CH - 1 : CH, :]
            ends = jnp.concatenate(pieces3(last) + (jnp.zeros((13, LANES), BF),), axis=0)
            states[i, :16, DI:] = ends
            small[i, 0] = jnp.concatenate(pieces2(dt), axis=1)
            small[i, 1] = jnp.concatenate(pieces2(jnp.exp(last - run) * dt), axis=1)

    @pl.when(step > 0)
    def _():
        at = pl.multiple_of((step - 1) * CW, CW)
        for i, act in enumerate(project(at, CW)):
            r = slice(i * CH, (i + 1) * CH)
            xs[r, :] = act.astype(BF)
            xt[r, :] = (act * dot(small[i, 0], table[...])).astype(BF)
            weighted = (act * dot(small[i, 1], table[...])).astype(BF)
            states[i, :, pl.ds(at, CW)] = dot_tn(bs[r, :], weighted).astype(BF)

    @pl.when(step == NCW)
    def _():
        out_copy().wait()


def run_project(info, parts, halos, tok_own, tok_got, conv_w, conv_b, dt_bias, a_log, table):
    rows = tok_own.shape[0]
    nb = rows // CH
    ext_rows = rows + nb * HALO
    layout = [offset for _, offset in parts]

    def before(s):
        return jnp.maximum(s - 1, 0)

    def tail_first(s):
        return jnp.where(s == 0, NCW, s - 1)

    ins = [(info, in_smem())] + [(v, in_hbm()) for v, _ in parts]
    ins += [(v, whole(v)) for v in halos]
    ins += [(v, whole(v)) for v in (tok_own, tok_got, conv_w, conv_b, dt_bias, a_log)]
    ins += [(table, columns(table, before))]
    outs = {
        "wa": (shape((DM, WA), BF), in_hbm()),
        "tok": (shape((rows, DM), BF), whole),
        "tok_halo": (shape((nb * HALO, DM), BF), whole),
        "normal": (shape((ext_rows, DM), BF), whole),
        "normal_t": (shape((DM, rows), BF), whole),
        "xbc": (shape((ext_rows, WA), BF), lambda v: columns(v, tail_first)),
        "slope": (shape((rows, WA), BF), lambda v: columns(v, tail_first)),
        "xs": (shape((rows, DI), BF), lambda v: columns(v, before)),
        "xt": (shape((rows, DI), BF), lambda v: columns(v, before)),
        "bs": (shape((rows, NS), BF), whole),
        "cs": (shape((rows, NS), BF), whole),
        "raw": (shape((rows, LANES), F32), whole),
        "cum": (shape((rows, LANES), F32), whole),
        "cum_t": (shape((LANES, rows), F32), whole),
        "states": (shape((nb, NS, DI + LANES), BF), whole),
    }
    out_list = [(o, s(o) if callable(s) else s) for o, s in outs.values()]
    scratch = [
        pltpu.VMEM((DM, WA), BF), pltpu.VMEM((nb, HALO + CH, CW), F32),
        pltpu.VMEM((nb, 2, CH, 2 * LANES), BF), pltpu.SemaphoreType.DMA((len(parts),)),
        pltpu.SemaphoreType.DMA,
    ]
    got = call(
        functools.partial(project_kernel, layout, len(halos)), 14, (NCW + 1,), ins, out_list, scratch, VMEM_ASK,
    )
    return dict(zip(outs, got))


SUM_GAIN = (KC + 1) * XBC // LANES
SUM_SKIP = SUM_GAIN + DI // LANES
SUM_HEADS = SUM_SKIP + DI // LANES
SUM_ROWS = SUM_HEADS + 2
OUT_ROWS = CW // 4
PER = CW // HD
HALF = CH // 2


def chunk_heads(cum, first):
    return pltpu.roll(cum, lax.rem(LANES - first, LANES), axis=1)


def intra_kernel(bs, cs, xt, cum, cum_t, out, scores):
    c = pl.program_id(0)
    nb = bs.shape[0] // CH
    low = iota((CH, LANES), 1) < HD
    keep = iota((HALF, HALF), 0) >= iota((HALF, HALF), 1)

    @pl.when(c == 0)
    def _():
        for i in range(nb):
            r = slice(i * CH, (i + 1) * CH)
            scores[i] = dot_nt(cs[r, :], bs[r, :])

    for i in range(nb):
        r = slice(i * CH, (i + 1) * CH)
        cols = chunk_heads(cum[r, :], c * PER)
        for p in range(PER // 2):
            lanes = slice(p * LANES, (p + 1) * LANES)
            both = xt[r, lanes]
            got = []
            for k in range(2):
                h = 2 * p + k
                col = cols[:, h : h + 1]
                row = cum_t[pl.ds(c * PER + h, 1), r]
                a, b = col[:HALF], col[HALF:]
                s, t = row[:, :HALF], row[:, HALF:]
                upper = jnp.where(keep, jnp.exp(a - s), 0.0) * scores[i, :HALF, :HALF]
                left = jnp.exp(b - s) * scores[i, HALF:, :HALF]
                right = jnp.where(keep, jnp.exp(b - t), 0.0) * scores[i, HALF:, HALF:]
                lower = jnp.concatenate([left.astype(BF), right.astype(BF)], axis=1)
                got.append(
                    jnp.concatenate([dot(upper.astype(BF), both[:HALF, :]), dot(lower, both)], axis=0)
                )
            out[r, lanes] = jnp.where(low, got[0], got[1])


def run_intra(a):
    rows = a["bs"].shape[0]
    nb = rows // CH
    ins = [(a[k], whole(a[k])) for k in ("bs", "cs")]
    ins += [(a["xt"], columns(a["xt"], lambda c: c))]
    ins += [(a[k], whole(a[k])) for k in ("cum", "cum_t")]
    out = shape((rows, DI), F32)
    return call(
        intra_kernel, 6, (NCW,), ins, [(out, columns(out, lambda c: c))],
        [pltpu.VMEM((nb, CH, CH), F32)],
    )[0]


def terms_kernel(normal_t, dz, normed, cot, out):
    out[:, :DI] = dot(normal_t[...], dz[...]).astype(BF)
    part = dot_tn(normed[...], cot[...]).astype(BF)
    for k in range(2):
        for j in range(2):
            rows = part[(2 * k + j) * OUT_ROWS : (2 * k + j + 1) * OUT_ROWS, :]
            out[k * OUT_ROWS : (k + 1) * OUT_ROWS, DI + j * DM : DI + (j + 1) * DM] = rows


def run_terms(normal_t, dz, normed, cot):
    rows = dz.shape[0]
    out = shape((DM, DI + 2 * DM), BF)
    return call(
        terms_kernel, 1, (NCW,),
        [
            (normal_t, pl.BlockSpec((2 * OUT_ROWS, rows), lambda c: (c, 0))), (dz, whole(dz)),
            (normed, columns(normed, lambda c: c)), (cot, whole(cot)),
        ],
        [(out, pl.BlockSpec((2 * OUT_ROWS, DI + 2 * DM), lambda c: (c, 0)))], [],
    )[0]


def pair_small_kernel(at, keep, got, small, small_got, *outs):
    n, _, cols = keep.shape
    chip = at[0] // 2
    total = small[...] + small_got[...]
    parts = jnp.concatenate(pieces2(total), axis=1)
    for k, out in enumerate(outs):
        out[:, :cols] = (keep[chip ^ k].astype(F32) + got[chip ^ k].astype(F32)).astype(BF)
        out[:, cols:] = parts


def run_pair_small(at, keep, got, small, small_got):
    n, rows, cols = keep.shape
    out = shape((rows, cols + 2 * small.shape[1]), BF)
    args = [keep, got, small, small_got]
    return call(
        pair_small_kernel, 1, (1,), [(at, in_smem())] + [(v, whole(v)) for v in args],
        [(out, whole(out))] * n, [],
    )


GW = 768
GNW = DI // GW


def columns_g(arr, at):
    return columns(arr, at, GW)


def gate_kernel(n_pieces, *refs):
    info = refs[0]
    pieces = refs[1 : 1 + n_pieces]
    ends = refs[1 + n_pieces : 1 + 2 * n_pieces]
    (
        y_intra, cs, cum, xs, z, q, inner_gain, d_skip, table,
        enter, normed, gain_part, dz, dyr, dye, product, skip_part, d_enter,
        y_scan, small, weights, squares, dots,
    ) = refs[1 + 2 * n_pieces :]
    phase, c = pl.program_id(0), pl.program_id(1)
    rows = cs.shape[0]
    nb = rows // CH
    n_all = n_pieces * nb
    here = pl.ds(pl.multiple_of(c * GW, GW), GW)

    @pl.when((phase == 0) & (c == 0))
    def _():
        weights[...] = carry_weights(info, clast_rows(ends, nb), nb, False)
        squares[...] = jnp.zeros_like(squares)
        dots[...] = jnp.zeros_like(dots)
        for i in range(nb):
            r = slice(i * CH, (i + 1) * CH)
            small[r, :] = jnp.concatenate(pieces2(jnp.exp(cum[r, :])), axis=1)

    @pl.when(phase == 0)
    def _():
        wide_w = dot(weights[...], table[...])
        totals = [jnp.zeros((NS, GW), F32) for _ in range(nb)]
        for j in range(n_all):
            piece = pieces[j // nb][j % nb].astype(F32)
            for i in range(nb):
                totals[i] = totals[i] + wide_w[i * n_all + j : i * n_all + j + 1, :] * piece
        for i in range(nb):
            r = slice(i * CH, (i + 1) * CH)
            low = totals[i].astype(BF)
            enter[i, :, here] = low
            scan = y_intra[r, :] + dot(small[r, :], table[...]) * dot(cs[r, :], low)
            y_scan[r, here] = scan
            y = scan + d_skip[...] * xs[r, :].astype(F32)
            zf = z[r, :].astype(F32)
            gated = y * (zf * sigmoid(zf))
            qg = q[r, :].astype(F32) * inner_gain[...] * usable_of(info, i)
            squares[r, :] += jnp.sum(gated * gated, axis=1, keepdims=True)
            dots[r, :] += jnp.sum(qg * gated, axis=1, keepdims=True)

    @pl.when(phase == 1)
    def _():
        gain_sum = jnp.zeros((1, GW), F32)
        skip_sum = jnp.zeros((1, GW), F32)
        for i in range(nb):
            r = slice(i * CH, (i + 1) * CH)
            inv = lax.rsqrt(squares[r, :] / DI + EPSILON)
            slope = inv * inv * inv * dots[r, :] / DI
            use = usable_of(info, i)
            scan = y_scan[r, here]
            x = xs[r, :].astype(F32)
            y = scan + d_skip[...] * x
            zf = z[r, :].astype(F32)
            sg = sigmoid(zf)
            sz = zf * sg
            gated = y * sz
            qf = q[r, :].astype(F32) * use
            scaled = gated * inv
            normed[r, :] = (scaled * inner_gain[...] * use).astype(BF)
            gain_sum = gain_sum + jnp.sum(qf * scaled, axis=0, keepdims=True)
            gg = inv * qf * inner_gain[...] - gated * slope
            dz[r, :] = (gg * y * (sg + sz * (1.0 - sg))).astype(BF)
            dy = gg * sz
            low = dy.astype(BF)
            dyr[r, :] = low
            product[r, :] = low.astype(F32) * scan
            skip_sum = skip_sum + jnp.sum(dy * x, axis=0, keepdims=True)
            back = (dot(small[r, :], table[...]) * dy).astype(BF)
            dye[r, :] = back
            d_enter[i] = dot_tn(cs[r, :], back).astype(BF)
        gain_part[...] = gain_sum
        skip_part[...] = skip_sum


def run_gate(info, a, pieces, y_intra, z, q, inner_gain, d_skip, table):
    rows = z.shape[0]
    nb = rows // CH

    def early(p, c):
        return jnp.where(p == 0, c, GNW - 1)

    def both(p, c):
        return c

    def late(p, c):
        return jnp.where(p == 0, 0, c)

    ins = [(info, in_smem())]
    ins += [(v, columns_g(v, early)) for v in pieces]
    ins += [(v, pl.BlockSpec((nb, 16, LANES), lambda p, c: (0, 0, DI // LANES))) for v in pieces]
    ins += [(y_intra, columns_g(y_intra, early))]
    ins += [(a[k], whole(a[k])) for k in ("cs", "cum")]
    ins += [(v, columns_g(v, both)) for v in (a["xs"], z, q, inner_gain, d_skip, table)]
    wide = shape((rows, DI), BF)
    wide_f = shape((rows, DI), F32)
    row = shape((1, DI), F32)
    state = shape((nb, NS, DI), BF)
    outs = [(state, whole(state))]
    outs += [(v, columns_g(v, late)) for v in (wide, row, wide, wide, wide, wide_f, row, state)]
    scratch = [
        pltpu.VMEM((rows, DI), F32), pltpu.VMEM((rows, 2 * LANES), BF),
        pltpu.VMEM((nb * nb * len(pieces), 2 * LANES), BF), pltpu.VMEM((rows, 1), F32),
        pltpu.VMEM((rows, 1), F32),
    ]
    return call(
        functools.partial(gate_kernel, len(pieces)), 16, (2, GNW), ins, outs, scratch, VMEM_ASK,
    )


def intra_back_kernel(
    bs, cs, xt, cum, cum_t, dyr, dye, enter, normed, wo, tok, dxt, db, dc, mixed, scores, top, bottom,
    total,
):
    c = pl.program_id(0)
    nb = bs.shape[0] // CH
    low = iota((CH, LANES), 1) < HD
    keep = iota((HALF, HALF), 1) >= iota((HALF, HALF), 0)

    @pl.when(c == 0)
    def _():
        for i in range(nb):
            r = slice(i * CH, (i + 1) * CH)
            scores[i] = dot_nt(bs[r, :], cs[r, :])
        top[...] = jnp.zeros_like(top)
        bottom[...] = jnp.zeros_like(bottom)
        dc[...] = jnp.zeros_like(dc)
        total[...] = tok[...].astype(F32)

    total[...] += dot(normed[...], wo[...])

    for i in range(nb):
        r = slice(i * CH, (i + 1) * CH)
        cols = chunk_heads(cum[r, :], c * PER)
        dc[r, :] += dot_nt(dye[r, :], enter[i])
        top_sum, bottom_sum = top[i], bottom[i]
        for p in range(PER // 2):
            lanes = slice(p * LANES, (p + 1) * LANES)
            x, dy = xt[r, lanes], dyr[r, lanes]
            got = []
            for k in range(2):
                h = 2 * p + k
                col = cols[:, h : h + 1]
                row = cum_t[pl.ds(c * PER + h, 1), r]
                a, b = col[:HALF], col[HALF:]
                s, t = row[:, :HALF], row[:, HALF:]
                left = jnp.where(keep, jnp.exp(s - a), 0.0)
                right = jnp.exp(t - a)
                last = jnp.where(keep, jnp.exp(t - b), 0.0)
                dec = jnp.concatenate([left, right], axis=1)
                got.append(
                    jnp.concatenate(
                        [
                            dot((dec * scores[i, :HALF, :]).astype(BF), dy),
                            dot((last * scores[i, HALF:, HALF:]).astype(BF), dy[HALF:, :]),
                        ],
                        axis=0,
                    )
                )
                own = jnp.where(low, x, 0) if k == 0 else jnp.where(low, 0, x)
                top_sum = top_sum + dot_nt(own[:HALF, :], dy) * dec
                bottom_sum = bottom_sum + dot_nt(own[HALF:, :], dy[HALF:, :]) * last
            dxt[r, lanes] = jnp.where(low, got[0], got[1])
        top[i], bottom[i] = top_sum, bottom_sum

    @pl.when(c == NCW - 1)
    def _():
        for i in range(nb):
            r = slice(i * CH, (i + 1) * CH)
            up, down = top[i].astype(BF), bottom[i].astype(BF)
            down = jnp.concatenate([jnp.zeros((HALF, HALF), BF), down], axis=1)
            both = jnp.concatenate([up, down], axis=0)
            db[r, :] = dot(both, cs[r, :])
            dc[r, :] += dot_tn(both, bs[r, :])
        mixed[...] = total[...].astype(BF)


def run_intra_back(a, dyr, dye, enter, normed, wo, tok):
    rows = dyr.shape[0]
    nb = rows // CH

    def same(c):
        return c

    ins = [(a[k], whole(a[k])) for k in ("bs", "cs")]
    ins += [(a["xt"], columns(a["xt"], same))]
    ins += [(a[k], whole(a[k])) for k in ("cum", "cum_t")]
    ins += [(v, columns(v, same)) for v in (dyr, dye, enter, normed)]
    ins += [(wo, pl.BlockSpec((CW, DM), lambda c: (c, 0))), (tok, whole(tok))]
    full, small, mixed = shape((rows, DI), F32), shape((rows, NS), F32), shape((rows, DM), BF)
    return call(
        intra_back_kernel, 1, (NCW,), ins,
        [(full, columns(full, same))] + [(v, whole(v)) for v in (small, small, mixed)],
        [
            pltpu.VMEM((nb, CH, CH), F32), pltpu.VMEM((nb, HALF, CH), F32),
            pltpu.VMEM((nb, HALF, HALF), F32), pltpu.VMEM((rows, DM), F32),
        ],
    )


def back_kernel(n_pieces, *refs):
    info = refs[0]
    pieces = refs[1 : 1 + n_pieces]
    ends = refs[1 + n_pieces : 1 + 2 * n_pieces]
    (
        dx_intra, db_in, dc_in, xbc, slope, xs, xt, bs, raw, cum, enter, product, dyr, conv_w,
        a_log, d_skip, table, narrow, gain_part, skip_part,
        d_a, sums,
        grad, small, d_bs, heads, weights,
    ) = refs[1 + 2 * n_pieces :]
    step = pl.program_id(0)
    rows = xs.shape[0]
    nb = rows // CH
    n_all = n_pieces * nb

    @pl.when(step == 0)
    def _():
        weights[...] = carry_weights(info, clast_rows(ends, nb), nb, True)
        dt_all = softplus(raw[...])
        for i in range(nb):
            r = slice(i * CH, (i + 1) * CH)
            last = cum[(i + 1) * CH - 1 : (i + 1) * CH, :]
            small[i, 0] = jnp.concatenate(pieces2(dt_all[r, :]), axis=1)
            small[i, 1] = jnp.concatenate(pieces2(jnp.exp(last - cum[r, :])), axis=1)
            grad[i, :HALO, :] = jnp.zeros((HALO, CW), F32)
            grad[i, HALO + CH :, :] = jnp.zeros((HALO, CW), F32)
        d_bs[...] = db_in[...]
        heads[...] = jnp.zeros_like(heads)

    def put_rows(at, row):
        for j in range(row.shape[1] // LANES):
            sums[pl.ds(at + j, 1), :] = row[:, j * LANES : (j + 1) * LANES]

    def convolve_back(dacts, width):
        offset_sum = jnp.zeros((1, width), F32)
        tap_sums = [jnp.zeros((1, width), F32) for _ in range(KC)]
        all_heads = xbc[rows:, :width].astype(F32)
        head_grads = []
        for i in range(nb):
            r = slice(i * CH, (i + 1) * CH)
            dpre = dacts[i] * slope[r, :width].astype(F32)
            offset_sum = offset_sum + jnp.sum(dpre, axis=0, keepdims=True)
            grad[i, HALO : HALO + CH, :width] = dpre
            body = xbc[r, :width].astype(F32)
            head = all_heads[i * HALO : (i + 1) * HALO, :]
            total = jnp.zeros((CH, width), F32)
            total_head = jnp.zeros((HALO, width), F32)
            for lag in range(KC):
                tap = conv_w[KC - 1 - lag : KC - lag, :width]
                later = grad[i, HALO + lag : HALO + lag + CH, :width]
                later_head = grad[i, lag : lag + HALO, :width]
                total = total + tap * later
                total_head = total_head + tap * later_head
                tap_sums[KC - 1 - lag] = (
                    tap_sums[KC - 1 - lag]
                    + jnp.sum(later * body, axis=0, keepdims=True)
                    + jnp.sum(later_head * head, axis=0, keepdims=True)
                )
            d_a[r, :width] = (total * usable_of(info, i)).astype(BF)
            head_grads.append(total_head * halo_used(info, i))
        d_a[rows:, :width] = jnp.concatenate(head_grads, axis=0).astype(BF)
        for k, row in enumerate(tap_sums + [offset_sum]):
            put_rows(k * (XBC // LANES) + step * (CW // LANES), row)

    @pl.when(step < NCW)
    def _():
        wide_w = dot(weights[...], table[...])
        totals = [jnp.zeros((NS, CW), F32) for _ in range(nb)]
        for j in range(n_all):
            piece = pieces[j // nb][j % nb].astype(F32)
            for i in range(nb):
                totals[i] = totals[i] + wide_w[i * n_all + j : i * n_all + j + 1, :] * piece
        select = narrow[...]
        dacts = []
        for i in range(nb):
            r = slice(i * CH, (i + 1) * CH)
            low = totals[i].astype(BF)
            fade = jnp.sum(low.astype(F32) * enter[i].astype(F32), axis=0, keepdims=True)
            end_w = dot(small[i, 1], table[...])
            x_dt = xt[r, :].astype(F32)
            inter = end_w * dot(bs[r, :], low)
            d_bs[r, :] += dot_nt((x_dt * end_w).astype(BF), low)
            dxt = dx_intra[r, :] + inter
            flow = jnp.sum(x_dt * inter, axis=0, keepdims=True)
            hi, mid, lo = pieces3(product[r, :] - x_dt * dxt)
            heads[0, r, :] += dot(hi, select) + dot(mid, select) + dot(lo, select)
            heads[1, r, :] += dot((xs[r, :].astype(F32) * dxt).astype(BF), select)
            hi, mid, lo = pieces3(jnp.concatenate([flow, fade, jnp.zeros((6, CW), F32)], axis=0))
            heads[2, i * 8 : (i + 1) * 8, :] += dot(hi, select) + dot(mid, select) + dot(lo, select)
            dacts.append(
                dot(small[i, 0], table[...]) * dxt + d_skip[...] * dyr[r, :].astype(F32)
            )
        convolve_back(dacts, CW)
        put_rows(SUM_GAIN + step * (CW // LANES), gain_part[...])
        put_rows(SUM_SKIP + step * (CW // LANES), skip_part[...])

    @pl.when(step == NCW)
    def _():
        dacts = []
        for i in range(nb):
            r = slice(i * CH, (i + 1) * CH)
            dacts.append(jnp.concatenate([d_bs[r, :], dc_in[r, :]], axis=1))
        convolve_back(dacts, 2 * NS)
        rate = jnp.exp(a_log[...])
        anti = (iota((CH, CH), 0) <= iota((CH, CH), 1)).astype(F32).astype(BF)
        bias_sum = jnp.zeros((1, LANES), F32)
        rate_sum = jnp.zeros((1, LANES), F32)
        for i in range(nb):
            r = slice(i * CH, (i + 1) * CH)
            last = cum[(i + 1) * CH - 1 : (i + 1) * CH, :]
            flow, fade = heads[2, i * 8 : i * 8 + 1, :], heads[2, i * 8 + 1 : i * 8 + 2, :]
            parts = dot(anti, jnp.concatenate(pieces3(heads[0, r, :]), axis=1))
            d_log = parts[:, :LANES] + parts[:, LANES : 2 * LANES] + parts[:, 2 * LANES :]
            d_log = d_log + (flow + jnp.exp(last) * fade)
            start = raw[r, :]
            d_raw = (heads[1, r, :] - d_log * rate) * sigmoid(start)
            d_raw = jnp.where(iota((CH, LANES), 1) < NH, d_raw, 0.0)
            bias_sum = bias_sum + jnp.sum(d_raw, axis=0, keepdims=True)
            rate_sum = rate_sum - jnp.sum(d_log * softplus(start), axis=0, keepdims=True) * rate
            d_a[r, 2 * NS :] = d_raw.astype(BF)
        d_a[rows:, 2 * NS :] = jnp.zeros((nb * HALO, CW - 2 * NS), BF)
        put_rows(SUM_HEADS, bias_sum)
        put_rows(SUM_HEADS + 1, rate_sum)


def run_back(
    info, a, pieces, ends, dx_intra, db, dc, enter, product, dyr, conv_w, a_log, d_skip, table,
    narrow, gain_part, skip_part,
):
    rows = dyr.shape[0]
    nb = rows // CH
    ext_rows = rows + nb * HALO

    def chunk(s):
        return jnp.minimum(s, NCW - 1)

    def same(s):
        return s

    ins = [(info, in_smem())]
    ins += [(v, columns(v, chunk)) for v in pieces]
    ins += [(v, pl.BlockSpec((nb, 16, LANES), lambda s: (0, 0, DI // LANES))) for v in ends]
    ins += [(dx_intra, columns(dx_intra, chunk)), (db, whole(db)), (dc, whole(dc))]
    ins += [(a["xbc"], columns(a["xbc"], same)), (a["slope"], columns(a["slope"], same))]
    ins += [(a["xs"], columns(a["xs"], chunk)), (a["xt"], columns(a["xt"], chunk))]
    ins += [(a[k], whole(a[k])) for k in ("bs", "raw", "cum")]
    ins += [(v, columns(v, chunk)) for v in (enter, product, dyr)]
    ins += [(conv_w, columns(conv_w, same)), (a_log, whole(a_log)), (d_skip, columns(d_skip, chunk))]
    ins += [(table, columns(table, chunk))]
    ins += [(narrow, pl.BlockSpec((CW, LANES), lambda s: (chunk(s), 0)))]
    ins += [(v, columns(v, chunk)) for v in (gain_part, skip_part)]
    wide, sums = shape((ext_rows, WA), BF), shape((SUM_ROWS, LANES), F32)
    outs = [(wide, columns(wide, same)), (sums, whole(sums))]
    scratch = [
        pltpu.VMEM((nb, CH + 2 * HALO, CW), F32), pltpu.VMEM((nb, 2, CH, 2 * LANES), BF),
        pltpu.VMEM((rows, NS), F32), pltpu.VMEM((3, rows, LANES), F32),
        pltpu.VMEM((nb * nb * len(pieces), 2 * LANES), BF),
    ]
    return call(
        functools.partial(back_kernel, len(pieces)), 2, (NCW + 1,), ins, outs, scratch, VMEM_ASK,
    )


def unit(rows):
    f = rows.astype(F32)
    inv = lax.rsqrt(jnp.mean(f * f, axis=1, keepdims=True) + EPSILON)
    return f * inv, inv


def norm_back(normal_grad, rows, gain):
    u, inv = unit(rows)
    g = normal_grad * gain[None, :]
    return inv * (g - u * jnp.mean(g * u, axis=1, keepdims=True))


def shards(
    tokens, norm_gain, in_weight, conv_weight, conv_bias, dt_bias, a_log, d_skip, inner_gain,
    out_weight, block_place, seq_length, cotangent,
):
    n_head, n_shard = lax.axis_size("head"), lax.axis_size("shard")
    half = n_head // 2
    head_at, shard_at = lax.axis_index("head"), lax.axis_index("shard")
    rows = tokens.shape[0]
    nb = rows // CH
    group_blocks = nb * n_head
    k_rows = in_weight.shape[0]
    stay = (head_at // half) == (shard_at & 1)

    piece_a = jnp.concatenate(
        [in_weight[:, DI:], norm_gain[:, None], jnp.zeros((k_rows, WA - XBC - NH - 1), BF)], axis=1
    )
    table = spread_table()

    def head_row(v):
        return jnp.pad(v, (0, LANES - NH))[None]

    narrow = narrow_table()
    gain_row = inner_gain[None]
    at = shard_at.astype(jnp.int32).reshape(1)
    taps = jnp.pad(conv_weight, ((0, 0), (0, WA - XBC)))
    rate_row = head_row(a_log)
    skip_row = jnp.repeat(d_skip, HD)[None]
    taps, rate_row, skip_row, bias_row, step_row, gain_row, narrow, table = after_all(
        [
            taps, rate_row, skip_row, jnp.pad(conv_bias, (0, WA - XBC))[None], head_row(dt_bias),
            gain_row, narrow, table,
        ]
    )
    prepared = [taps, rate_row, skip_row, bias_row, step_row, gain_row, narrow, table]
    numbers = jnp.concatenate([block_place, seq_length], axis=1)
    numbers_got = trade(numbers, "shard", 1)
    me = jnp.int32(0) if k_rows % 32 else shard_at.astype(jnp.int32)
    def block_tails(v):
        return v.reshape(nb, CH, DM)[:, CH - HALO :].reshape(nb * HALO, DM)

    tok_got = move_home(tokens)
    tails = jnp.where(stay, block_tails(tokens), block_tails(tok_got))

    numbers = jnp.where(stay, numbers, numbers_got)[0]
    lengths = [numbers[group_blocks + k] for k in range(seq_length.shape[1])]

    def order_from(core_at):
        ids = []
        for core in (0, 1):
            for z in range(half):
                device = (head_at % half ^ z) + (core_at ^ core) * half
                ids += [device * nb + b for b in range(nb)]
        return jnp.stack(ids)

    ids, home_order = order_from(shard_at & 1), order_from(head_at // half)
    places = jnp.sum(
        jnp.where(ids[:, None] == jnp.arange(group_blocks)[None, :], numbers[None, :group_blocks], 0),
        axis=1,
    )
    first, in_seq, begin = jnp.zeros_like(places), jnp.zeros_like(places), 0
    for length in lengths:
        first = jnp.where(places >= begin, begin, first)
        in_seq = jnp.where(places >= begin, length, in_seq)
        begin = begin + (length + CH - 1) // CH
    info = jnp.concatenate(
        [
            jnp.stack([me, stay.astype(jnp.int32)]),
            jnp.stack([places, first, in_seq], axis=1).reshape(-1),
        ]
    ).astype(jnp.int32)

    parts_a = gather_pieces(piece_a, info, *prepared)
    if k_rows % 32:
        joined = jnp.zeros((n_shard, k_rows, WA), BF)
        for v, k in parts_a:
            joined = lax.dynamic_update_slice(joined, v[None], (shard_at ^ k, 0, 0))
        parts_a = [(joined.reshape(DM, WA), 0)]
    wo = lax.all_gather(out_weight, "shard", axis=0, tiled=True)
    wz = lax.all_gather(in_weight[:, :DI], "shard", axis=0, tiled=True)

    tails = group_spread(after(tails, *[v for v, _ in parts_a[1:]]))
    cot_got = move_home(after(cotangent, *tails))
    a = run_project(info, parts_a, tails, tokens, tok_got, taps, bias_row, step_row, rate_row, table)
    wa, tok, normal = a["wa"], a["tok"], a["normal"]
    state_by_head = head_pieces(a["states"])
    state_by_core = trade(a["states"], "shard", 1)
    y_intra = run_intra(a)
    cot = jnp.where(stay, cotangent, after(cot_got, y_intra))
    q = dot_nt(cot, wo).astype(BF)
    z = dot(after(normal, q)[:rows], wz).astype(BF)
    state_by_head = [after(v, z) for v in state_by_head]
    all_states = (
        [a["states"]] + state_by_head + [state_by_core] + [trade(v, "shard", 1) for v in state_by_head]
    )
    enter, normed, gain_part, dz, dyr, dye, product, skip_part, d_enter = run_gate(
        info, a, all_states, y_intra, z, q, gain_row, skip_row, table
    )
    enter_by_head = head_pieces(d_enter)
    enter_by_core = trade(d_enter, "shard", 1)
    zo_term = run_terms(a["normal_t"], dz, normed, cot)
    zo_own = lax.psum_scatter(zo_term, "shard", scatter_dimension=0, tiled=True)
    dx_intra, db, dc, mixed = run_intra_back(a, after(dyr, zo_term), dye, enter, normed, wo, tok)
    enter_by_head = [after(v, dx_intra) for v in enter_by_head]
    all_enter = (
        [d_enter] + enter_by_head + [enter_by_core] + [trade(v, "shard", 1) for v in enter_by_head]
    )
    mixed_got = move_home(after(mixed, all_enter[-1]))
    d_a_all, small = run_back(
        info, a, all_enter, all_states, dx_intra, db, dc, enter, product, dyr, taps,
        rate_row, skip_row, table, narrow, gain_part, skip_part,
    )
    d_a_all = after(d_a_all, mixed_got)
    a_term = dot_tn(normal, d_a_all).astype(BF).reshape(n_shard, k_rows, WA)
    a_keep, a_give = core_give([a_term])
    a_got = trade(a_give, "shard", 1)

    small_got = trade(after(small, a_give), "shard", 1)
    d_a_all, dz, tok, tok_halo, wa = after_all([d_a_all, dz, tok, a["tok_halo"], wa], a_give)
    gain = wa[:, XBC + NH].astype(F32)
    halo_part = norm_back(dot_nt(d_a_all[rows:], wa), tok_halo, gain)
    halo_part = halo_part.reshape(nb, HALO, DM)[:, HALO - KC :].astype(BF).reshape(k_rows, -1)
    halos = [halo_part, trade(halo_part, "shard", 1)]
    normal_grad = dot_nt(dz, wz) + dot_nt(d_a_all[:rows], wa)
    token_grad = (cot.astype(F32) + norm_back(normal_grad, tok, gain)).astype(BF)

    a_got, small_got, halos[1], zo_own = after_all([a_got, small_got, halos[1], zo_own], token_grad)
    zo_sum = lax.psum(zo_own, "head")
    if k_rows % 32:
        parts = split2((small + small_got).reshape(k_rows, -1))
        a_pairs = [jnp.concatenate([v, parts], axis=1) for v in chip_pairs(a_keep, a_got)]
    else:
        a_pairs = run_pair_small(at, a_keep, a_got, small, small_got)
    a_far = chip_send(a_pairs)
    token_got = move_home(after(token_grad, a_pairs[0]))
    *a_far, token_got = after_all(a_far + [token_got])
    a_own = chip_sum(a_pairs[0][:, :WA], [v[:, :WA] for v in a_far])
    sums = [join2(v[:, WA:]) for v in [a_pairs[0]] + a_far]
    while len(sums) > 1:
        sums = [sums[k] + sums[k + 1] for k in range(0, len(sums), 2)]
    small = sums[0]
    a_keep, a_give = head_split(a_own)
    small_keep, small_give = head_split(small)
    cut, edge = a_keep.shape[1], a_keep.shape[1] + 2 * small_keep.shape[1]
    total, small = a_keep.astype(F32), small_keep
    bits = [b for b in (1, 2, 4, 8, 16) if b < n_head]
    for bit in bits:
        if bit > 1:
            a_give, small_give = total.astype(BF), small
            total = a_give.astype(F32)
        parts = split2(small_give)
        sent = jnp.concatenate([a_give, parts] + (halos if bit < half else []), axis=1)
        sent = trade(sent, "head", bit)
        if bit < half:
            halos = halos + jnp.split(sent[:, edge:], len(halos), axis=1)
        total = total + sent[:, :cut].astype(F32)
        small = (small if bit == 1 else join2(parts)) + join2(sent[:, cut:edge])
    low, parts = total.astype(BF), split2(small)
    other = trade(jnp.concatenate([low, parts], axis=1), "head", 1)
    halos = jnp.concatenate(halos, axis=1)
    halos = jnp.where(stay, halos, move_home(halos))
    halos = jnp.split(halos, group_blocks // nb, axis=1)
    other = after(other, *halos)
    zo_grad = after(zo_sum, other).astype(F32)
    a_grad = head_join(low, other[:, :cut]).astype(F32)
    small = head_join(join2(parts), join2(other[:, cut:])).reshape(SUM_ROWS, LANES)

    all_halo = jnp.concatenate(halos[0::2] + halos[1::2]).reshape(group_blocks, KC, DM).astype(F32)
    own_numbers = jnp.concatenate([block_place, seq_length], axis=1)[0]
    own_places = jnp.sum(
        jnp.where(
            home_order[:, None] == jnp.arange(group_blocks), own_numbers[None, :group_blocks], 0
        ),
        axis=1,
    )
    home_ids = head_at * nb + jnp.arange(nb)
    home_places = jnp.sum(
        jnp.where(
            home_ids[:, None] == jnp.arange(group_blocks), own_numbers[None, :group_blocks], 0
        ),
        axis=1,
    )
    goes_on, begin = home_places < 0, 0
    for k in range(seq_length.shape[1]):
        end = begin + (own_numbers[group_blocks + k] + CH - 1) // CH
        goes_on = goes_on | ((home_places >= begin) & (home_places + 1 < end))
        begin = end
    is_next = (own_places[None, :] == home_places[:, None] + 1) & goes_on[:, None]
    halo_back = jnp.sum(jnp.where(is_next[:, :, None, None], all_halo[None], 0.0), axis=1)
    token_grad = jnp.where(stay, token_grad, token_got).reshape(nb, CH, DM)
    token_grad = token_grad.at[:, CH - KC :].set(
        (token_grad[:, CH - KC :].astype(F32) + halo_back).astype(BF)
    ).reshape(rows, DM)
    mixed = jnp.where(stay, mixed, after(mixed_got, a_own))

    in_grad = jnp.concatenate([zo_grad[:, :DI], a_grad[:, : XBC + NH]], axis=1)
    out_grad = jnp.concatenate([zo_grad[:, DI : DI + DM], zo_grad[:, DI + DM :]], axis=0)
    gain_grad = jnp.sum(in_grad * in_weight.astype(F32), axis=1) / norm_gain.astype(F32)

    return (
        mixed, token_grad, gain_grad, in_grad, small[: KC * XBC // LANES].reshape(KC, XBC),
        small[KC * XBC // LANES : SUM_GAIN].reshape(XBC), small[SUM_HEADS, :NH],
        small[SUM_HEADS + 1, :NH], jnp.sum(small[SUM_SKIP:SUM_HEADS].reshape(NH, HD), axis=1),
        small[SUM_GAIN:SUM_SKIP].reshape(DI), out_grad,
    )


def solution(mesh):
    return jax.shard_map(
        shards,
        mesh=mesh,
        in_specs=(
            P(("head", "shard"), None), P("shard"), P("shard", None), P(), P(), P(), P(), P(), P(),
            P("shard", None), P("shard", None), P("shard", None), P(("head", "shard"), None),
        ),
        out_specs=(
            P(("head", "shard"), None), P(("head", "shard"), None), P("shard"), P("shard", None),
            P(), P(), P(), P(), P(), P(), P("shard", None),
        ),
        check_vma=False,
    )
```

```python
import functools

import jax
import jax.numpy as jnp
from jax import lax
from jax.experimental import pallas as pl
from jax.experimental.pallas import tpu as pltpu
from jax.sharding import PartitionSpec as P

NH = 24
HD = 64
NS = 128
KC = 4
CH = 256
DI = 1536
DM = 768
XBC = DI + 2 * NS
WA = 1920
HALO = 8
EPSILON = 1e-05
F32 = jnp.float32
BF = jnp.bfloat16
LANES = 128
CW = 384
NCW = DI // CW
VMEM_ASK = 56 * 2**20
VMEM_ROOM = 56 * 2**20
COST_SCALE = 0.4


def trade(value, axis, bit):
    size = lax.axis_size(axis)
    return lax.ppermute(value, axis, [(i, i ^ bit) for i in range(size)])


def after(value, *others):
    return lax.optimization_barrier((value,) + others)[0]


def move_home(value):
    n_head, n_shard = lax.axis_size("head"), lax.axis_size("shard")
    half = n_head // 2
    pairs = []
    for h in range(n_head):
        for s in range(n_shard):
            upper, core = h // half, s & 1
            if upper != core:
                there = (h % half + core * half) * n_shard + (s - core + upper)
                pairs.append((h * n_shard + s, there))
    return lax.ppermute(value, ("head", "shard"), pairs)


def swap_home(value, stay):
    return jnp.where(stay, value, move_home(value))


def group_spread(value):
    n_head, n_shard = lax.axis_size("head"), lax.axis_size("shard")
    pieces = [value]
    for core in (0, 1):
        for low in range(n_head // 2):
            if core or low:
                pairs = [
                    (h * n_shard + s, (h ^ low) * n_shard + (s ^ core))
                    for h in range(n_head)
                    for s in range(n_shard)
                ]
                pieces.append(lax.ppermute(value, ("head", "shard"), pairs))
    return pieces


def group_gather(value):
    half = lax.axis_size("head") // 2
    pieces = [value]
    bit = 1
    while bit < half:
        pieces = pieces + [trade(v, "head", bit) for v in pieces]
        bit *= 2
    return pieces + [trade(v, "shard", 1) for v in pieces]


def gather_far(piece):
    bits = range(2, lax.axis_size("shard"), 2)
    return [trade(piece, "shard", bit) for bit in sorted(bits, reverse=True)]


def gather_near(piece, far):
    held = [piece] + far
    offsets = [0] + sorted(range(2, lax.axis_size("shard"), 2), reverse=True)
    near = [trade(v, "shard", 1) for v in held]
    return list(zip(held + near, offsets + [k ^ 1 for k in offsets]))


def join_pieces(parts):
    me, n_shard = lax.axis_index("shard"), lax.axis_size("shard")
    joined = jnp.zeros((n_shard,) + parts[0][0].shape, parts[0][0].dtype)
    for v, k in parts:
        joined = lax.dynamic_update_slice(joined, v[None], (me ^ k, 0, 0))
    return joined


def head_pieces(value):
    pieces = [value]
    bit = 1
    while bit < lax.axis_size("head") // 2:
        pieces = pieces + [trade(v, "head", bit) for v in pieces]
        bit *= 2
    return pieces[1:]


def core_give(blocks):
    n_shard = lax.axis_size("shard")
    core = lax.axis_index("shard") % 2

    def half(which):
        parts = []
        for v in blocks:
            split = v.reshape((n_shard // 2, 2) + v.shape[1:])
            parts.append(lax.dynamic_index_in_dim(split, which, 1, False))
        return jnp.concatenate(parts, axis=2) if len(parts) > 1 else parts[0]

    return half(core), half(1 - core)


def chip_pairs(keep, got):
    pair = (keep.astype(F32) + got.astype(F32)).astype(BF)
    chip = lax.axis_index("shard") // 2
    return [lax.dynamic_index_in_dim(pair, chip ^ k, 0, False) for k in range(pair.shape[0])]


def after_all(values, *others):
    return list(lax.optimization_barrier((*values, *others)))[: len(values)]


def chip_send(pairs):
    return [trade(v, "shard", 2 * k) for k, v in enumerate(pairs) if k]


def chip_sum(own, got):
    total = own.astype(F32)
    for v in got:
        total = total + v.astype(F32)
    return total.astype(BF)


def split2(v):
    high = lax.reduce_precision(v, 8, 7)
    return jnp.concatenate([high.astype(BF), (v - high).astype(BF)], axis=1)


def join2(parts):
    high, low = jnp.split(parts, 2, axis=1)
    return high.astype(F32) + low.astype(F32)


def head_split(value):
    cut = value.shape[1] // 2
    odd = lax.axis_index("head") % 2
    return [lax.dynamic_slice_in_dim(value, at * cut, cut, 1) for at in (odd, 1 - odd)]


def head_add(keep, got):
    return (keep.astype(F32) + got.astype(F32)).astype(BF)


def head_join(half, other):
    odd = lax.axis_index("head") % 2
    return jnp.concatenate([jnp.where(odd, other, half), jnp.where(odd, half, other)], axis=1)


def dot(a, b):
    return jnp.dot(a, b, preferred_element_type=F32)


def dot_nt(a, b):
    return lax.dot_general(a, b, (((1,), (1,)), ((), ())), preferred_element_type=F32)


def dot_tn(a, b):
    return lax.dot_general(a, b, (((0,), (0,)), ((), ())), preferred_element_type=F32)


def spread_table(none):
    row = jnp.arange(2 * LANES)[:, None] % LANES + none
    return (row == jnp.arange(DI)[None, :] // HD).astype(BF)


def narrow_table(none):
    return (jnp.arange(DI)[:, None] // HD == jnp.arange(LANES)[None, :] + none).astype(BF)


def pieces2(v):
    hi = v.astype(BF)
    return hi, (v - hi.astype(F32)).astype(BF)


def pieces3(v):
    hi = v.astype(BF)
    rest = v - hi.astype(F32)
    mid = rest.astype(BF)
    return hi, mid, (rest - mid.astype(F32)).astype(BF)


def softplus(v):
    return jnp.maximum(v, 0.0) + jnp.log1p(jnp.exp(-jnp.abs(v)))


sigmoid = jax.nn.sigmoid


def shape(dims, dtype):
    return jax.ShapeDtypeStruct(dims, dtype)


def whole(arr):
    return pl.BlockSpec(arr.shape, lambda *g: (0,) * len(arr.shape))


def columns(arr, at, width=None):
    dims = arr.shape[:-1] + (width or CW,)
    return pl.BlockSpec(dims, lambda *g: (0,) * (len(dims) - 1) + (at(*g),))


def in_hbm():
    return pl.BlockSpec(memory_space=pl.ANY)


def in_smem():
    return pl.BlockSpec(memory_space=pltpu.SMEM)


def call(kernel, micros, grid, ins, outs, scratch, room=VMEM_ROOM):
    return pl.pallas_call(
        kernel,
        grid=grid,
        out_shape=[o for o, _ in outs],
        in_specs=[s for _, s in ins],
        out_specs=[s for _, s in outs],
        scratch_shapes=scratch,
        compiler_params=pltpu.CompilerParams(vmem_limit_bytes=room),
        cost_estimate=pl.CostEstimate(
            flops=1, bytes_accessed=int(micros * COST_SCALE * 3.7e6), transcendentals=0
        ),
    )(*[a for a, _ in ins])


def iota(dims, axis):
    return lax.broadcasted_iota(jnp.int32, dims, axis)


def place_of(info, q):
    return info[2 + 3 * q]


def first_of(info, q):
    return info[3 + 3 * q]


def usable_of(info, i):
    begin = (place_of(info, i) - first_of(info, i)) * CH
    return (iota((CH, 1), 0) + begin < info[4 + 3 * i]).astype(F32)


def halo_used(info, i):
    has_prev = place_of(info, i) > first_of(info, i)
    return (iota((HALO, 1), 0) + jnp.where(has_prev, 0, -HALO) > HALO - KC).astype(F32)


def clast_rows(refs, nb):
    rows = []
    for ref in refs:
        for b in range(nb):
            part = ref[b].astype(F32)
            rows.append(part[0:1, :] + part[1:2, :] + part[2:3, :])
    return rows


def carry_weights(info, ends, nb, into):
    n_all = len(ends)
    row = iota((n_all, 1), 0)
    place = jnp.zeros((n_all, 1), jnp.int32)
    first = jnp.zeros((n_all, 1), jnp.int32)
    for j in range(n_all):
        place = jnp.where(row == j, place_of(info, j), place)
        first = jnp.where(row == j, first_of(info, j), first)
    parts = []
    for i in range(nb):
        own = place_of(info, i)
        total = jnp.zeros((n_all, LANES), F32)
        for k in range(n_all):
            at = place_of(info, k)
            if into:
                between = (place > at) & (at > own)
            else:
                between = (place < at) & (at < own)
            total = total + jnp.where(between, ends[k], 0.0)
        if into:
            reach = (first <= own) & (place > own)
        else:
            reach = (place >= first_of(info, i)) & (place < own)
        parts.append(jnp.where(reach, jnp.exp(total), 0.0))
    return jnp.concatenate(pieces2(jnp.concatenate(parts, axis=0)), axis=1)


def normal_rows(rows, gain):
    f = rows.astype(F32)
    inv = lax.rsqrt(jnp.sum(f * f, axis=1, keepdims=True) / DM + EPSILON)
    return (f * inv * gain).astype(BF)


def project_kernel(layout, n_halo, *refs):
    info = refs[0]
    pieces = refs[1 : 1 + len(layout)]
    halos = refs[1 + len(layout) : 1 + len(layout) + n_halo]
    (
        tok_own, tok_got, conv_w, conv_b, dt_bias, a_log, table,
        wa_out, tok, tok_halo, normal, normal_t, xbc, slope, xs, xt, bs, cs, raw, cum, cum_t, states,
        wa, ext, small, sems, out_sem,
    ) = refs[1 + len(layout) + n_halo :]
    step = pl.program_id(0)
    rows = tok_own.shape[0]
    nb = rows // CH
    me = info[0]

    def project(at, width):
        proj = dot(normal[...], wa[:, pl.ds(at, width)]).astype(BF).astype(F32)
        acts, heads = [], []
        for i in range(nb):
            head = proj[rows + i * HALO : rows + (i + 1) * HALO, :] * halo_used(info, i)
            body = proj[i * CH : (i + 1) * CH, :] * usable_of(info, i)
            heads.append(head)
            ext[i, :HALO, :width] = head
            ext[i, HALO:, :width] = body
            xbc[i * CH : (i + 1) * CH, :width] = body.astype(BF)
            pre = conv_b[:, pl.ds(at, width)]
            for lag in range(KC):
                tap = conv_w[KC - 1 - lag : KC - lag, pl.ds(at, width)]
                pre = pre + tap * ext[i, HALO - lag : HALO - lag + CH, :width]
            sg = sigmoid(pre)
            act = pre * sg
            slope[i * CH : (i + 1) * CH, :width] = (sg + act * (1.0 - sg)).astype(BF)
            acts.append(act)
        xbc[rows:, :width] = jnp.concatenate(heads, axis=0).astype(BF)
        return acts

    def out_copy():
        return pltpu.make_async_copy(wa, wa_out, out_sem)

    @pl.when(step == 0)
    def _():
        def copy_of(n):
            at = pl.multiple_of((me ^ layout[n]) * pieces[n].shape[0], 16)
            return pltpu.make_async_copy(
                pieces[n], wa.at[pl.ds(at, pieces[n].shape[0]), :], sems.at[n]
            )

        for n in range(len(layout)):
            copy_of(n).start()
        stay = info[1] > 0
        tok[...] = jnp.where(stay, tok_own[...], tok_got[...])
        found = []
        for i in range(nb):
            own, has_prev = place_of(info, i), place_of(info, i) > first_of(info, i)
            total = jnp.zeros((HALO, DM), F32)
            for o in range(n_halo):
                part = halos[o][...].astype(F32)
                for b in range(nb):
                    hit = (place_of(info, o * nb + b) == own - 1) & has_prev
                    total = total + jnp.where(hit, part[b * HALO : (b + 1) * HALO, :], 0.0)
            found.append(total)
        tok_halo[...] = jnp.concatenate(found, axis=0).astype(BF)
        for n in range(len(layout)):
            copy_of(n).wait()
        out_copy().start()
        gain = wa[:, XBC : XBC + LANES].astype(F32).T[NH : NH + 1, :]
        normal[:rows, :] = normal_rows(tok[...], gain)
        normal_t[...] = normal[:rows, :].T
        normal[rows:, :] = normal_rows(tok_halo[...], gain)
        for i, act in enumerate(project(DI, 2 * NS)):
            bs[i * CH : (i + 1) * CH, :] = act[:, :NS].astype(BF)
            cs[i * CH : (i + 1) * CH, :] = act[:, NS:].astype(BF)
        xbc[:, 2 * NS :] = jnp.zeros((xbc.shape[0], CW - 2 * NS), BF)
        slope[:, 2 * NS :] = jnp.zeros((rows, CW - 2 * NS), BF)
        first = dot(normal[:rows, :], wa[:, XBC : XBC + LANES]).astype(BF).astype(F32) + dt_bias[...]
        raw[...] = first
        dt_all = softplus(first)
        rate = jnp.exp(a_log[...])
        causal = (iota((CH, CH), 0) >= iota((CH, CH), 1)).astype(F32).astype(BF)
        states[:, :, DI:] = jnp.zeros((nb, NS, LANES), BF)
        for i in range(nb):
            dt = dt_all[i * CH : (i + 1) * CH, :]
            parts = dot(causal, jnp.concatenate(pieces3(-dt * rate), axis=1))
            run = parts[:, :LANES] + parts[:, LANES : 2 * LANES] + parts[:, 2 * LANES :]
            cum[i * CH : (i + 1) * CH, :] = run
            cum_t[:, i * CH : (i + 1) * CH] = run.T
            last = run[CH - 1 : CH, :]
            ends = jnp.concatenate(pieces3(last) + (jnp.zeros((13, LANES), BF),), axis=0)
            states[i, :16, DI:] = ends
            small[i, 0] = jnp.concatenate(pieces2(dt), axis=1)
            small[i, 1] = jnp.concatenate(pieces2(jnp.exp(last - run) * dt), axis=1)

    @pl.when(step > 0)
    def _():
        at = pl.multiple_of((step - 1) * CW, CW)
        for i, act in enumerate(project(at, CW)):
            r = slice(i * CH, (i + 1) * CH)
            xs[r, :] = act.astype(BF)
            xt[r, :] = (act * dot(small[i, 0], table[...])).astype(BF)
            weighted = (act * dot(small[i, 1], table[...])).astype(BF)
            states[i, :, pl.ds(at, CW)] = dot_tn(bs[r, :], weighted).astype(BF)

    @pl.when(step == NCW)
    def _():
        out_copy().wait()


def run_project(info, parts, halos, tok_own, tok_got, conv_w, conv_b, dt_bias, a_log, table):
    rows = tok_own.shape[0]
    nb = rows // CH
    ext_rows = rows + nb * HALO
    layout = [offset for _, offset in parts]

    def before(s):
        return jnp.maximum(s - 1, 0)

    def tail_first(s):
        return jnp.where(s == 0, NCW, s - 1)

    ins = [(info, in_smem())] + [(v, in_hbm()) for v, _ in parts]
    ins += [(v, whole(v)) for v in halos]
    ins += [(v, whole(v)) for v in (tok_own, tok_got, conv_w, conv_b, dt_bias, a_log)]
    ins += [(table, columns(table, before))]
    outs = {
        "wa": (shape((DM, WA), BF), in_hbm()),
        "tok": (shape((rows, DM), BF), whole),
        "tok_halo": (shape((nb * HALO, DM), BF), whole),
        "normal": (shape((ext_rows, DM), BF), whole),
        "normal_t": (shape((DM, rows), BF), whole),
        "xbc": (shape((ext_rows, WA), BF), lambda v: columns(v, tail_first)),
        "slope": (shape((rows, WA), BF), lambda v: columns(v, tail_first)),
        "xs": (shape((rows, DI), BF), lambda v: columns(v, before)),
        "xt": (shape((rows, DI), BF), lambda v: columns(v, before)),
        "bs": (shape((rows, NS), BF), whole),
        "cs": (shape((rows, NS), BF), whole),
        "raw": (shape((rows, LANES), F32), whole),
        "cum": (shape((rows, LANES), F32), whole),
        "cum_t": (shape((LANES, rows), F32), whole),
        "states": (shape((nb, NS, DI + LANES), BF), whole),
    }
    out_list = [(o, s(o) if callable(s) else s) for o, s in outs.values()]
    scratch = [
        pltpu.VMEM((DM, WA), BF), pltpu.VMEM((nb, HALO + CH, CW), F32),
        pltpu.VMEM((nb, 2, CH, 2 * LANES), BF), pltpu.SemaphoreType.DMA((len(parts),)),
        pltpu.SemaphoreType.DMA,
    ]
    got = call(
        functools.partial(project_kernel, layout, len(halos)), 14, (NCW + 1,), ins, out_list, scratch, VMEM_ASK,
    )
    return dict(zip(outs, got))


SUM_GAIN = (KC + 1) * XBC // LANES
SUM_SKIP = SUM_GAIN + DI // LANES
SUM_HEADS = SUM_SKIP + DI // LANES
SUM_ROWS = SUM_HEADS + 2
OUT_ROWS = CW // 4
PER = CW // HD
HALF = CH // 2


def chunk_heads(cum, first):
    return pltpu.roll(cum, lax.rem(LANES - first, LANES), axis=1)


def intra_kernel(bs, cs, xt, cum, cum_t, out, scores):
    c = pl.program_id(0)
    nb = bs.shape[0] // CH
    low = iota((CH, LANES), 1) < HD
    keep = iota((HALF, HALF), 0) >= iota((HALF, HALF), 1)

    @pl.when(c == 0)
    def _():
        for i in range(nb):
            r = slice(i * CH, (i + 1) * CH)
            scores[i] = dot_nt(cs[r, :], bs[r, :])

    for i in range(nb):
        r = slice(i * CH, (i + 1) * CH)
        cols = chunk_heads(cum[r, :], c * PER)
        for p in range(PER // 2):
            lanes = slice(p * LANES, (p + 1) * LANES)
            both = xt[r, lanes]
            got = []
            for k in range(2):
                h = 2 * p + k
                col = cols[:, h : h + 1]
                row = cum_t[pl.ds(c * PER + h, 1), r]
                a, b = col[:HALF], col[HALF:]
                s, t = row[:, :HALF], row[:, HALF:]
                upper = jnp.where(keep, jnp.exp(a - s), 0.0) * scores[i, :HALF, :HALF]
                left = jnp.exp(b - s) * scores[i, HALF:, :HALF]
                right = jnp.where(keep, jnp.exp(b - t), 0.0) * scores[i, HALF:, HALF:]
                lower = jnp.concatenate([left.astype(BF), right.astype(BF)], axis=1)
                got.append(
                    jnp.concatenate([dot(upper.astype(BF), both[:HALF, :]), dot(lower, both)], axis=0)
                )
            out[r, lanes] = jnp.where(low, got[0], got[1])


def run_intra(a):
    rows = a["bs"].shape[0]
    nb = rows // CH
    ins = [(a[k], whole(a[k])) for k in ("bs", "cs")]
    ins += [(a["xt"], columns(a["xt"], lambda c: c))]
    ins += [(a[k], whole(a[k])) for k in ("cum", "cum_t")]
    out = shape((rows, DI), F32)
    return call(
        intra_kernel, 6, (NCW,), ins, [(out, columns(out, lambda c: c))],
        [pltpu.VMEM((nb, CH, CH), F32)],
    )[0]


def open_kernel(layout, at, *refs):
    pieces = refs[: len(layout)]
    normal, cot_own, cot_got, stay, z, q, cot, wz, wo, sems = refs[len(layout) :]
    c = pl.program_id(0)
    k_rows = pieces[0].shape[0]

    def copies(n):
        shard = at[0] ^ layout[n]
        parts = [(wz, shard * k_rows, slice(0, DI))]
        for j in range(2):
            lanes = slice(DI + j * DM, DI + (j + 1) * DM)
            parts.append((wo, (2 * shard + j) * k_rows, lanes))
        return [
            pltpu.make_async_copy(
                pieces[n].at[:, lanes],
                ref.at[pl.ds(pl.multiple_of(begin, 16), k_rows), :],
                sems.at[3 * n + k],
            )
            for k, (ref, begin, lanes) in enumerate(parts)
        ]

    @pl.when(c == 0)
    def _():
        for n in range(len(layout)):
            for copy in copies(n):
                copy.start()
        cot[...] = jnp.where(stay[0] > 0, cot_own[...], cot_got[...])
        for n in range(len(layout)):
            for copy in copies(n):
                copy.wait()

    here = pl.ds(pl.multiple_of(c * CW, CW), CW)
    z[...] = dot(normal[...], wz[:, here]).astype(BF)
    q[...] = dot_nt(cot[...], wo[here, :]).astype(BF)


def run_open(at, parts, normal, cot_own, cot_got, stay):
    rows = cot_own.shape[0]
    layout = [offset for _, offset in parts]
    ins = [(at, in_smem())] + [(v, in_hbm()) for v, _ in parts]
    ins += [(normal, pl.BlockSpec((rows, DM), lambda c: (0, 0)))]
    ins += [(cot_own, whole(cot_own)), (cot_got, whole(cot_got)), (stay, in_smem())]
    wide = shape((rows, DI), BF)
    outs = [(wide, columns(wide, lambda c: c))] * 2
    outs += [(v, whole(v)) for v in (shape((rows, DM), BF), shape((DM, DI), BF), shape((DI, DM), BF))]
    return call(
        functools.partial(open_kernel, layout), 1, (NCW,), ins, outs,
        [pltpu.SemaphoreType.DMA((3 * len(parts),))],
    )


def terms_kernel(at, normal_t, dz, normed, cot, keep, *refs):
    *give, z_part, o_part = refs
    p = pl.program_id(0)
    unit = give[0].shape[0]
    even = at[0] % 2 == 0
    z_part[...] = dot(normal_t[...], dz[...])
    o_part[...] = dot_tn(normed[...], cot[...])

    def rows_of(which):
        parts = [(z_part[which * unit : (which + 1) * unit, :], slice(0, DI))]
        for j in range(2):
            rows = o_part[(2 * which + j) * unit : (2 * which + j + 1) * unit, :]
            parts.append((rows, slice(DI + j * DM, DI + (j + 1) * DM)))
        return parts

    for (first, lanes), (second, _) in zip(rows_of(0), rows_of(1)):
        keep[0, :, lanes] = jnp.where(even, first, second).astype(BF)
        other = jnp.where(even, second, first).astype(BF)
        for k, ref in enumerate(give):

            @pl.when(p == k)
            def _(ref=ref, other=other, lanes=lanes):
                ref[:, lanes] = other


def run_terms(at, normal_t, dz, normed, cot, n_shard):
    rows = dz.shape[0]
    n, unit = n_shard // 2, DM // n_shard
    give = shape((unit, DI + 2 * DM), BF)
    keep = shape((n,) + give.shape, BF)
    got = call(
        terms_kernel, 1, (n,),
        [
            (at, in_smem()), (normal_t, pl.BlockSpec((2 * unit, rows), lambda p: (p, 0))),
            (dz, whole(dz)), (normed, columns(normed, lambda p: p, 4 * unit)), (cot, whole(cot)),
        ],
        [(keep, pl.BlockSpec((1,) + give.shape, lambda p: (p, 0, 0)))] + [(give, whole(give))] * n,
        [pltpu.VMEM((2 * unit, DI), F32), pltpu.VMEM((4 * unit, DM), F32)],
    )
    return got[0], list(got[1:])


def pair_small_kernel(at, keep, got, small, small_got, *outs):
    n, _, cols = keep.shape
    chip = at[0] // 2
    total = small[...] + small_got[...]
    parts = jnp.concatenate(pieces2(total), axis=1)
    for k, out in enumerate(outs):
        out[:, :cols] = (keep[chip ^ k].astype(F32) + got[chip ^ k].astype(F32)).astype(BF)
        out[:, cols:] = parts


def run_pair_small(at, keep, got, small, small_got):
    n, rows, cols = keep.shape
    out = shape((rows, cols + 2 * small.shape[1]), BF)
    args = [keep, got, small, small_got]
    return call(
        pair_small_kernel, 1, (1,), [(at, in_smem())] + [(v, whole(v)) for v in args],
        [(out, whole(out))] * n, [],
    )


GW = 768
GNW = DI // GW


def columns_g(arr, at):
    return columns(arr, at, GW)


def gate_kernel(n_pieces, *refs):
    info = refs[0]
    pieces = refs[1 : 1 + n_pieces]
    ends = refs[1 + n_pieces : 1 + 2 * n_pieces]
    (
        y_intra, cs, cum, xs, z, q, inner_gain, d_skip, table,
        enter, normed, gain_part, dz, dyr, dye, product, skip_part, d_enter,
        y_scan, small, weights, squares, dots,
    ) = refs[1 + 2 * n_pieces :]
    phase, c = pl.program_id(0), pl.program_id(1)
    rows = cs.shape[0]
    nb = rows // CH
    n_all = n_pieces * nb
    here = pl.ds(pl.multiple_of(c * GW, GW), GW)

    @pl.when((phase == 0) & (c == 0))
    def _():
        weights[...] = carry_weights(info, clast_rows(ends, nb), nb, False)
        squares[...] = jnp.zeros_like(squares)
        dots[...] = jnp.zeros_like(dots)
        for i in range(nb):
            r = slice(i * CH, (i + 1) * CH)
            small[r, :] = jnp.concatenate(pieces2(jnp.exp(cum[r, :])), axis=1)

    @pl.when(phase == 0)
    def _():
        wide_w = dot(weights[...], table[...])
        totals = [jnp.zeros((NS, GW), F32) for _ in range(nb)]
        for j in range(n_all):
            piece = pieces[j // nb][j % nb].astype(F32)
            for i in range(nb):
                totals[i] = totals[i] + wide_w[i * n_all + j : i * n_all + j + 1, :] * piece
        for i in range(nb):
            r = slice(i * CH, (i + 1) * CH)
            low = totals[i].astype(BF)
            enter[i, :, here] = low
            scan = y_intra[r, :] + dot(small[r, :], table[...]) * dot(cs[r, :], low)
            y_scan[r, here] = scan
            y = scan + d_skip[...] * xs[r, :].astype(F32)
            zf = z[r, :].astype(F32)
            gated = y * (zf * sigmoid(zf))
            qg = q[r, :].astype(F32) * inner_gain[...] * usable_of(info, i)
            squares[r, :] += jnp.sum(gated * gated, axis=1, keepdims=True)
            dots[r, :] += jnp.sum(qg * gated, axis=1, keepdims=True)

    @pl.when(phase == 1)
    def _():
        gain_sum = jnp.zeros((1, GW), F32)
        skip_sum = jnp.zeros((1, GW), F32)
        for i in range(nb):
            r = slice(i * CH, (i + 1) * CH)
            inv = lax.rsqrt(squares[r, :] / DI + EPSILON)
            slope = inv * inv * inv * dots[r, :] / DI
            use = usable_of(info, i)
            scan = y_scan[r, here]
            x = xs[r, :].astype(F32)
            y = scan + d_skip[...] * x
            zf = z[r, :].astype(F32)
            sg = sigmoid(zf)
            sz = zf * sg
            gated = y * sz
            qf = q[r, :].astype(F32) * use
            scaled = gated * inv
            normed[r, :] = (scaled * inner_gain[...] * use).astype(BF)
            gain_sum = gain_sum + jnp.sum(qf * scaled, axis=0, keepdims=True)
            gg = inv * qf * inner_gain[...] - gated * slope
            dz[r, :] = (gg * y * (sg + sz * (1.0 - sg))).astype(BF)
            dy = gg * sz
            low = dy.astype(BF)
            dyr[r, :] = low
            product[r, :] = low.astype(F32) * scan
            skip_sum = skip_sum + jnp.sum(dy * x, axis=0, keepdims=True)
            back = (dot(small[r, :], table[...]) * dy).astype(BF)
            dye[r, :] = back
            d_enter[i] = dot_tn(cs[r, :], back).astype(BF)
        gain_part[...] = gain_sum
        skip_part[...] = skip_sum


def run_gate(info, a, pieces, y_intra, z, q, inner_gain, d_skip, table):
    rows = z.shape[0]
    nb = rows // CH

    def early(p, c):
        return jnp.where(p == 0, c, GNW - 1)

    def both(p, c):
        return c

    def late(p, c):
        return jnp.where(p == 0, 0, c)

    ins = [(info, in_smem())]
    ins += [(v, columns_g(v, early)) for v in pieces]
    ins += [(v, pl.BlockSpec((nb, 16, LANES), lambda p, c: (0, 0, DI // LANES))) for v in pieces]
    ins += [(y_intra, columns_g(y_intra, early))]
    ins += [(a[k], whole(a[k])) for k in ("cs", "cum")]
    ins += [(v, columns_g(v, both)) for v in (a["xs"], z, q, inner_gain, d_skip, table)]
    wide = shape((rows, DI), BF)
    wide_f = shape((rows, DI), F32)
    row = shape((1, DI), F32)
    state = shape((nb, NS, DI), BF)
    outs = [(state, whole(state))]
    outs += [(v, columns_g(v, late)) for v in (wide, row, wide, wide, wide, wide_f, row, state)]
    scratch = [
        pltpu.VMEM((rows, DI), F32), pltpu.VMEM((rows, 2 * LANES), BF),
        pltpu.VMEM((nb * nb * len(pieces), 2 * LANES), BF), pltpu.VMEM((rows, 1), F32),
        pltpu.VMEM((rows, 1), F32),
    ]
    return call(
        functools.partial(gate_kernel, len(pieces)), 16, (2, GNW), ins, outs, scratch, VMEM_ASK,
    )


def intra_back_kernel(
    bs, cs, xt, cum, cum_t, dyr, dye, enter, normed, wo, tok, dxt, db, dc, mixed, scores, top, bottom,
    total,
):
    c = pl.program_id(0)
    nb = bs.shape[0] // CH
    low = iota((CH, LANES), 1) < HD
    keep = iota((HALF, HALF), 1) >= iota((HALF, HALF), 0)

    @pl.when(c == 0)
    def _():
        for i in range(nb):
            r = slice(i * CH, (i + 1) * CH)
            scores[i] = dot_nt(bs[r, :], cs[r, :])
        top[...] = jnp.zeros_like(top)
        bottom[...] = jnp.zeros_like(bottom)
        dc[...] = jnp.zeros_like(dc)
        total[...] = tok[...].astype(F32)

    total[...] += dot(normed[...], wo[...])

    for i in range(nb):
        r = slice(i * CH, (i + 1) * CH)
        cols = chunk_heads(cum[r, :], c * PER)
        dc[r, :] += dot_nt(dye[r, :], enter[i])
        top_sum, bottom_sum = top[i], bottom[i]
        for p in range(PER // 2):
            lanes = slice(p * LANES, (p + 1) * LANES)
            x, dy = xt[r, lanes], dyr[r, lanes]
            got = []
            for k in range(2):
                h = 2 * p + k
                col = cols[:, h : h + 1]
                row = cum_t[pl.ds(c * PER + h, 1), r]
                a, b = col[:HALF], col[HALF:]
                s, t = row[:, :HALF], row[:, HALF:]
                left = jnp.where(keep, jnp.exp(s - a), 0.0)
                right = jnp.exp(t - a)
                last = jnp.where(keep, jnp.exp(t - b), 0.0)
                dec = jnp.concatenate([left, right], axis=1)
                got.append(
                    jnp.concatenate(
                        [
                            dot((dec * scores[i, :HALF, :]).astype(BF), dy),
                            dot((last * scores[i, HALF:, HALF:]).astype(BF), dy[HALF:, :]),
                        ],
                        axis=0,
                    )
                )
                own = jnp.where(low, x, 0) if k == 0 else jnp.where(low, 0, x)
                top_sum = top_sum + dot_nt(own[:HALF, :], dy) * dec
                bottom_sum = bottom_sum + dot_nt(own[HALF:, :], dy[HALF:, :]) * last
            dxt[r, lanes] = jnp.where(low, got[0], got[1])
        top[i], bottom[i] = top_sum, bottom_sum

    @pl.when(c == NCW - 1)
    def _():
        for i in range(nb):
            r = slice(i * CH, (i + 1) * CH)
            up, down = top[i].astype(BF), bottom[i].astype(BF)
            down = jnp.concatenate([jnp.zeros((HALF, HALF), BF), down], axis=1)
            both = jnp.concatenate([up, down], axis=0)
            db[r, :] = dot(both, cs[r, :])
            dc[r, :] += dot_tn(both, bs[r, :])
        mixed[...] = total[...].astype(BF)


def run_intra_back(a, dyr, dye, enter, normed, wo, tok):
    rows = dyr.shape[0]
    nb = rows // CH

    def same(c):
        return c

    ins = [(a[k], whole(a[k])) for k in ("bs", "cs")]
    ins += [(a["xt"], columns(a["xt"], same))]
    ins += [(a[k], whole(a[k])) for k in ("cum", "cum_t")]
    ins += [(v, columns(v, same)) for v in (dyr, dye, enter, normed)]
    ins += [(wo, pl.BlockSpec((CW, DM), lambda c: (c, 0))), (tok, whole(tok))]
    full, small, mixed = shape((rows, DI), F32), shape((rows, NS), F32), shape((rows, DM), BF)
    return call(
        intra_back_kernel, 1, (NCW,), ins,
        [(full, columns(full, same))] + [(v, whole(v)) for v in (small, small, mixed)],
        [
            pltpu.VMEM((nb, CH, CH), F32), pltpu.VMEM((nb, HALF, CH), F32),
            pltpu.VMEM((nb, HALF, HALF), F32), pltpu.VMEM((rows, DM), F32),
        ],
    )


def back_kernel(n_pieces, *refs):
    info = refs[0]
    pieces = refs[1 : 1 + n_pieces]
    ends = refs[1 + n_pieces : 1 + 2 * n_pieces]
    (
        dx_intra, db_in, dc_in, xbc, slope, xs, xt, bs, raw, cum, enter, product, dyr, conv_w,
        a_log, d_skip, table, narrow, gain_part, skip_part,
        d_a, sums,
        grad, small, d_bs, heads, weights,
    ) = refs[1 + 2 * n_pieces :]
    step = pl.program_id(0)
    rows = xs.shape[0]
    nb = rows // CH
    n_all = n_pieces * nb

    @pl.when(step == 0)
    def _():
        weights[...] = carry_weights(info, clast_rows(ends, nb), nb, True)
        dt_all = softplus(raw[...])
        for i in range(nb):
            r = slice(i * CH, (i + 1) * CH)
            last = cum[(i + 1) * CH - 1 : (i + 1) * CH, :]
            small[i, 0] = jnp.concatenate(pieces2(dt_all[r, :]), axis=1)
            small[i, 1] = jnp.concatenate(pieces2(jnp.exp(last - cum[r, :])), axis=1)
            grad[i, :HALO, :] = jnp.zeros((HALO, CW), F32)
            grad[i, HALO + CH :, :] = jnp.zeros((HALO, CW), F32)
        d_bs[...] = db_in[...]
        heads[...] = jnp.zeros_like(heads)

    def put_rows(at, row):
        for j in range(row.shape[1] // LANES):
            sums[pl.ds(at + j, 1), :] = row[:, j * LANES : (j + 1) * LANES]

    def convolve_back(dacts, width):
        offset_sum = jnp.zeros((1, width), F32)
        tap_sums = [jnp.zeros((1, width), F32) for _ in range(KC)]
        all_heads = xbc[rows:, :width].astype(F32)
        head_grads = []
        for i in range(nb):
            r = slice(i * CH, (i + 1) * CH)
            dpre = dacts[i] * slope[r, :width].astype(F32)
            offset_sum = offset_sum + jnp.sum(dpre, axis=0, keepdims=True)
            grad[i, HALO : HALO + CH, :width] = dpre
            body = xbc[r, :width].astype(F32)
            head = all_heads[i * HALO : (i + 1) * HALO, :]
            total = jnp.zeros((CH, width), F32)
            total_head = jnp.zeros((HALO, width), F32)
            for lag in range(KC):
                tap = conv_w[KC - 1 - lag : KC - lag, :width]
                later = grad[i, HALO + lag : HALO + lag + CH, :width]
                later_head = grad[i, lag : lag + HALO, :width]
                total = total + tap * later
                total_head = total_head + tap * later_head
                tap_sums[KC - 1 - lag] = (
                    tap_sums[KC - 1 - lag]
                    + jnp.sum(later * body, axis=0, keepdims=True)
                    + jnp.sum(later_head * head, axis=0, keepdims=True)
                )
            d_a[r, :width] = (total * usable_of(info, i)).astype(BF)
            head_grads.append(total_head * halo_used(info, i))
        d_a[rows:, :width] = jnp.concatenate(head_grads, axis=0).astype(BF)
        for k, row in enumerate(tap_sums + [offset_sum]):
            put_rows(k * (XBC // LANES) + step * (CW // LANES), row)

    @pl.when(step < NCW)
    def _():
        wide_w = dot(weights[...], table[...])
        totals = [jnp.zeros((NS, CW), F32) for _ in range(nb)]
        for j in range(n_all):
            piece = pieces[j // nb][j % nb].astype(F32)
            for i in range(nb):
                totals[i] = totals[i] + wide_w[i * n_all + j : i * n_all + j + 1, :] * piece
        select = narrow[...]
        dacts = []
        for i in range(nb):
            r = slice(i * CH, (i + 1) * CH)
            low = totals[i].astype(BF)
            fade = jnp.sum(low.astype(F32) * enter[i].astype(F32), axis=0, keepdims=True)
            end_w = dot(small[i, 1], table[...])
            x_dt = xt[r, :].astype(F32)
            inter = end_w * dot(bs[r, :], low)
            d_bs[r, :] += dot_nt((x_dt * end_w).astype(BF), low)
            dxt = dx_intra[r, :] + inter
            flow = jnp.sum(x_dt * inter, axis=0, keepdims=True)
            hi, mid, lo = pieces3(product[r, :] - x_dt * dxt)
            heads[0, r, :] += dot(hi, select) + dot(mid, select) + dot(lo, select)
            heads[1, r, :] += dot((xs[r, :].astype(F32) * dxt).astype(BF), select)
            hi, mid, lo = pieces3(jnp.concatenate([flow, fade, jnp.zeros((6, CW), F32)], axis=0))
            heads[2, i * 8 : (i + 1) * 8, :] += dot(hi, select) + dot(mid, select) + dot(lo, select)
            dacts.append(
                dot(small[i, 0], table[...]) * dxt + d_skip[...] * dyr[r, :].astype(F32)
            )
        convolve_back(dacts, CW)
        put_rows(SUM_GAIN + step * (CW // LANES), gain_part[...])
        put_rows(SUM_SKIP + step * (CW // LANES), skip_part[...])

    @pl.when(step == NCW)
    def _():
        dacts = []
        for i in range(nb):
            r = slice(i * CH, (i + 1) * CH)
            dacts.append(jnp.concatenate([d_bs[r, :], dc_in[r, :]], axis=1))
        convolve_back(dacts, 2 * NS)
        rate = jnp.exp(a_log[...])
        anti = (iota((CH, CH), 0) <= iota((CH, CH), 1)).astype(F32).astype(BF)
        bias_sum = jnp.zeros((1, LANES), F32)
        rate_sum = jnp.zeros((1, LANES), F32)
        for i in range(nb):
            r = slice(i * CH, (i + 1) * CH)
            last = cum[(i + 1) * CH - 1 : (i + 1) * CH, :]
            flow, fade = heads[2, i * 8 : i * 8 + 1, :], heads[2, i * 8 + 1 : i * 8 + 2, :]
            parts = dot(anti, jnp.concatenate(pieces3(heads[0, r, :]), axis=1))
            d_log = parts[:, :LANES] + parts[:, LANES : 2 * LANES] + parts[:, 2 * LANES :]
            d_log = d_log + (flow + jnp.exp(last) * fade)
            start = raw[r, :]
            d_raw = (heads[1, r, :] - d_log * rate) * sigmoid(start)
            d_raw = jnp.where(iota((CH, LANES), 1) < NH, d_raw, 0.0)
            bias_sum = bias_sum + jnp.sum(d_raw, axis=0, keepdims=True)
            rate_sum = rate_sum - jnp.sum(d_log * softplus(start), axis=0, keepdims=True) * rate
            d_a[r, 2 * NS :] = d_raw.astype(BF)
        d_a[rows:, 2 * NS :] = jnp.zeros((nb * HALO, CW - 2 * NS), BF)
        put_rows(SUM_HEADS, bias_sum)
        put_rows(SUM_HEADS + 1, rate_sum)


def run_back(
    info, a, pieces, ends, dx_intra, db, dc, enter, product, dyr, conv_w, a_log, d_skip, table,
    narrow, gain_part, skip_part,
):
    rows = dyr.shape[0]
    nb = rows // CH
    ext_rows = rows + nb * HALO

    def chunk(s):
        return jnp.minimum(s, NCW - 1)

    def same(s):
        return s

    ins = [(info, in_smem())]
    ins += [(v, columns(v, chunk)) for v in pieces]
    ins += [(v, pl.BlockSpec((nb, 16, LANES), lambda s: (0, 0, DI // LANES))) for v in ends]
    ins += [(dx_intra, columns(dx_intra, chunk)), (db, whole(db)), (dc, whole(dc))]
    ins += [(a["xbc"], columns(a["xbc"], same)), (a["slope"], columns(a["slope"], same))]
    ins += [(a["xs"], columns(a["xs"], chunk)), (a["xt"], columns(a["xt"], chunk))]
    ins += [(a[k], whole(a[k])) for k in ("bs", "raw", "cum")]
    ins += [(v, columns(v, chunk)) for v in (enter, product, dyr)]
    ins += [(conv_w, columns(conv_w, same)), (a_log, whole(a_log)), (d_skip, columns(d_skip, chunk))]
    ins += [(table, columns(table, chunk))]
    ins += [(narrow, pl.BlockSpec((CW, LANES), lambda s: (chunk(s), 0)))]
    ins += [(v, columns(v, chunk)) for v in (gain_part, skip_part)]
    wide, sums = shape((ext_rows, WA), BF), shape((SUM_ROWS, LANES), F32)
    outs = [(wide, columns(wide, same)), (sums, whole(sums))]
    scratch = [
        pltpu.VMEM((nb, CH + 2 * HALO, CW), F32), pltpu.VMEM((nb, 2, CH, 2 * LANES), BF),
        pltpu.VMEM((rows, NS), F32), pltpu.VMEM((3, rows, LANES), F32),
        pltpu.VMEM((nb * nb * len(pieces), 2 * LANES), BF),
    ]
    return call(
        functools.partial(back_kernel, len(pieces)), 2, (NCW + 1,), ins, outs, scratch, VMEM_ASK,
    )


def unit(rows):
    f = rows.astype(F32)
    inv = lax.rsqrt(jnp.mean(f * f, axis=1, keepdims=True) + EPSILON)
    return f * inv, inv


def norm_back(normal_grad, rows, gain):
    u, inv = unit(rows)
    g = normal_grad * gain[None, :]
    return inv * (g - u * jnp.mean(g * u, axis=1, keepdims=True))


def shards(
    tokens, norm_gain, in_weight, conv_weight, conv_bias, dt_bias, a_log, d_skip, inner_gain,
    out_weight, block_place, seq_length, cotangent,
):
    n_head, n_shard = lax.axis_size("head"), lax.axis_size("shard")
    half = n_head // 2
    head_at, shard_at = lax.axis_index("head"), lax.axis_index("shard")
    rows = tokens.shape[0]
    nb = rows // CH
    group_blocks = nb * n_head
    k_rows = in_weight.shape[0]
    stay = (head_at // half) == (shard_at & 1)

    piece_a = jnp.concatenate(
        [in_weight[:, DI:], norm_gain[:, None], jnp.zeros((k_rows, WA - XBC - NH - 1), BF)], axis=1
    )
    numbers = jnp.concatenate([block_place, seq_length], axis=1)
    numbers_got = trade(numbers, "shard", 1)
    me = jnp.int32(0) if k_rows % 32 else shard_at.astype(jnp.int32)
    def block_tails(v):
        return v.reshape(nb, CH, DM)[:, CH - HALO :].reshape(nb * HALO, DM)

    tok_got = move_home(tokens)
    tails = jnp.where(stay, block_tails(tokens), block_tails(tok_got))

    numbers = jnp.where(stay, numbers, numbers_got)[0]
    lengths = [numbers[group_blocks + k] for k in range(seq_length.shape[1])]

    def order_from(core_at):
        ids = []
        for core in (0, 1):
            for z in range(half):
                device = (head_at % half ^ z) + (core_at ^ core) * half
                ids += [device * nb + b for b in range(nb)]
        return jnp.stack(ids)

    ids, home_order = order_from(shard_at & 1), order_from(head_at // half)
    places = jnp.sum(
        jnp.where(ids[:, None] == jnp.arange(group_blocks)[None, :], numbers[None, :group_blocks], 0),
        axis=1,
    )
    first, in_seq, begin = jnp.zeros_like(places), jnp.zeros_like(places), 0
    for length in lengths:
        first = jnp.where(places >= begin, begin, first)
        in_seq = jnp.where(places >= begin, length, in_seq)
        begin = begin + (length + CH - 1) // CH
    info = jnp.concatenate(
        [
            jnp.stack([me, stay.astype(jnp.int32)]),
            jnp.stack([places, first, in_seq], axis=1).reshape(-1),
        ]
    ).astype(jnp.int32)

    far_a = gather_far(piece_a)
    conv_weight, conv_bias, dt_bias, a_log, d_skip, inner_gain, none = after_all(
        [conv_weight, conv_bias, dt_bias, a_log, d_skip, inner_gain, jnp.int32(0)], far_a[0]
    )
    table = spread_table(none)

    def head_row(v):
        return jnp.pad(v, (0, LANES - NH))[None]

    narrow = narrow_table(none)
    gain_row = inner_gain[None]
    at = shard_at.astype(jnp.int32).reshape(1)
    taps = jnp.pad(conv_weight, ((0, 0), (0, WA - XBC)))
    rate_row = head_row(a_log)
    skip_row = jnp.repeat(d_skip, HD)[None]
    taps, rate_row, skip_row, bias_row, step_row, gain_row, narrow, table = after_all(
        [
            taps, rate_row, skip_row, jnp.pad(conv_bias, (0, WA - XBC))[None], head_row(dt_bias),
            gain_row, narrow, table,
        ]
    )
    prepared = [taps, rate_row, skip_row, bias_row, step_row, gain_row, narrow, table]
    parts_a = gather_near(piece_a, far_a)
    if k_rows % 32:
        parts_a = [(join_pieces(parts_a).reshape(DM, WA), 0)]
    z_own, o_own = after_all([in_weight[:, :DI], out_weight], numbers_got)
    piece_zo = jnp.concatenate([z_own, o_own[:k_rows], o_own[k_rows:]], axis=1)
    far_zo = gather_far(piece_zo)
    tails = group_spread(after(tails, info, *[v for v, _ in parts_a[1:]], *prepared))
    cot_got = move_home(after(cotangent, *tails))
    a = run_project(info, parts_a, tails, tokens, tok_got, taps, bias_row, step_row, rate_row, table)
    wa, tok, normal = a["wa"], a["tok"], a["normal"]
    state_by_head = head_pieces(a["states"])
    state_by_core = trade(a["states"], "shard", 1)
    y_intra = run_intra(a)
    parts_zo = gather_near(after(piece_zo, y_intra), after_all(far_zo, y_intra))
    if k_rows % 32:
        zo = join_pieces(parts_zo)
        wz, wo = zo[:, :, :DI].reshape(DM, DI), zo[:, :, DI:]
        wo = wo.reshape(n_shard, k_rows, 2, DM).swapaxes(1, 2).reshape(DI, DM)
        cot = jnp.where(stay, cotangent, cot_got)
        z, q = dot(normal[:rows], wz).astype(BF), dot_nt(cot, wo).astype(BF)
    else:
        cot_got = after(cot_got, y_intra)
        z, q, cot, wz, wo = run_open(
            at, parts_zo, normal, cotangent, cot_got, stay.astype(jnp.int32).reshape(1)
        )
    state_by_head = [after(v, z) for v in state_by_head]
    all_states = (
        [a["states"]] + state_by_head + [state_by_core] + [trade(v, "shard", 1) for v in state_by_head]
    )
    enter, normed, gain_part, dz, dyr, dye, product, skip_part, d_enter = run_gate(
        info, a, all_states, y_intra, z, q, gain_row, skip_row, table
    )
    enter_by_head = head_pieces(d_enter)
    enter_by_core = trade(d_enter, "shard", 1)
    if k_rows % 32:
        z_term = dot_tn(normal[:rows], dz).astype(BF).reshape(n_shard, k_rows, DI)
        out_term = dot_tn(normed, cot).astype(BF).reshape(n_shard, 2, k_rows, DM)
        zo_keep, zo_give = core_give([z_term, out_term[:, 0], out_term[:, 1]])
        zo_give = [zo_give[p] for p in range(n_shard // 2)]
    else:
        zo_keep, zo_give = run_terms(at, a["normal_t"], dz, normed, cot, n_shard)
    zo_got = [trade(v, "shard", 1) for v in zo_give]
    dx_intra, db, dc, mixed = run_intra_back(a, after(dyr, *zo_give), dye, enter, normed, wo, tok)
    arrived = after_all(enter_by_head + zo_got, dx_intra)
    enter_by_head, zo_got = arrived[: len(enter_by_head)], arrived[len(enter_by_head) :]
    zo_pairs = chip_pairs(zo_keep, jnp.stack(zo_got))
    zo_far = chip_send(zo_pairs)
    enter_by_head = [after(v, *zo_pairs) for v in enter_by_head]
    all_enter = (
        [d_enter] + enter_by_head + [enter_by_core] + [trade(v, "shard", 1) for v in enter_by_head]
    )
    mixed_got = move_home(after(mixed, all_enter[-1]))
    d_a_all, small = run_back(
        info, a, all_enter, all_states, dx_intra, db, dc, enter, product, dyr, taps,
        rate_row, skip_row, table, narrow, gain_part, skip_part,
    )
    d_a_all = after(d_a_all, mixed_got)
    a_term = dot_tn(normal, d_a_all).astype(BF).reshape(n_shard, k_rows, WA)
    a_keep, a_give = core_give([a_term])
    a_got = trade(a_give, "shard", 1)

    small_got = trade(after(small, a_give), "shard", 1)
    zo_own = chip_sum(zo_pairs[0], after_all(zo_far, a_give))
    zo_keep, zo_give = head_split(zo_own)
    zo_got = trade(zo_give, "head", 1)
    d_a_all, dz, tok, tok_halo, wa = after_all(
        [d_a_all, dz, tok, a["tok_halo"], wa], a_give, zo_give
    )
    gain = wa[:, XBC + NH].astype(F32)
    halo_part = norm_back(dot_nt(d_a_all[rows:], wa), tok_halo, gain)
    halo_part = halo_part.reshape(nb, HALO, DM)[:, HALO - KC :].astype(BF).reshape(k_rows, -1)
    halos = [halo_part, trade(halo_part, "shard", 1)]
    normal_grad = dot_nt(dz, wz) + dot_nt(d_a_all[:rows], wa)
    token_grad = (cot.astype(F32) + norm_back(normal_grad, tok, gain)).astype(BF)

    a_got, small_got, halos[1], zo_got = after_all([a_got, small_got, halos[1], zo_got], token_grad)
    if k_rows % 32:
        parts = split2((small + small_got).reshape(k_rows, -1))
        a_pairs = [jnp.concatenate([v, parts], axis=1) for v in chip_pairs(a_keep, a_got)]
    else:
        a_pairs = run_pair_small(at, a_keep, a_got, small, small_got)
    a_far = chip_send(a_pairs)
    token_got = move_home(after(token_grad, a_pairs[0]))
    zo_half = head_add(zo_keep, after(zo_got, a_pairs[0]))
    zo_got = trade(zo_half, "head", 2)
    *a_far, token_got = after_all(a_far + [token_got])
    a_own = chip_sum(a_pairs[0][:, :WA], [v[:, :WA] for v in a_far])
    sums = [join2(v[:, WA:]) for v in [a_pairs[0]] + a_far]
    while len(sums) > 1:
        sums = [sums[k] + sums[k + 1] for k in range(0, len(sums), 2)]
    small = sums[0]
    a_keep, a_give = head_split(a_own)
    cut, edge = a_keep.shape[1], a_keep.shape[1] + 2 * small.shape[1]
    total = a_keep.astype(F32)
    bits = [b for b in (1, 2, 4, 8, 16) if b < n_head]
    for bit in bits:
        if bit > 1:
            a_give = total.astype(BF)
            total = a_give.astype(F32)
        parts = split2(small)
        sent = jnp.concatenate([a_give, parts] + (halos if bit < half else []), axis=1)
        sent = trade(sent, "head", bit)
        if bit == 1:
            sent, zo_got = after_all([sent, zo_got])
            zo_half = head_add(zo_half, zo_got)
            for more in bits[2:]:
                zo_half = head_add(zo_half, trade(zo_half, "head", more))
            zo_other = trade(zo_half, "head", 1)
        elif bit == bits[-1]:
            sent, zo_other = after_all([sent, zo_other])
            zo_grad = head_join(zo_half, zo_other).astype(F32)
        if bit < half:
            halos = halos + jnp.split(sent[:, edge:], len(halos), axis=1)
        total = total + sent[:, :cut].astype(F32)
        small = join2(parts) + join2(sent[:, cut:edge])
    low = total.astype(BF)
    other = trade(low, "head", 1)
    halos = after(jnp.concatenate(halos, axis=1), low)
    halos = jnp.where(stay, halos, move_home(halos))
    halos = jnp.split(halos, group_blocks // nb, axis=1)
    other = after(other, *halos)
    a_grad = head_join(low, other).astype(F32)
    small = small.reshape(SUM_ROWS, LANES)

    all_halo = jnp.concatenate(halos[0::2] + halos[1::2]).reshape(group_blocks, KC, DM).astype(F32)
    own_numbers = jnp.concatenate([block_place, seq_length], axis=1)[0]
    own_places = jnp.sum(
        jnp.where(
            home_order[:, None] == jnp.arange(group_blocks), own_numbers[None, :group_blocks], 0
        ),
        axis=1,
    )
    home_ids = head_at * nb + jnp.arange(nb)
    home_places = jnp.sum(
        jnp.where(
            home_ids[:, None] == jnp.arange(group_blocks), own_numbers[None, :group_blocks], 0
        ),
        axis=1,
    )
    goes_on, begin = home_places < 0, 0
    for k in range(seq_length.shape[1]):
        end = begin + (own_numbers[group_blocks + k] + CH - 1) // CH
        goes_on = goes_on | ((home_places >= begin) & (home_places + 1 < end))
        begin = end
    is_next = (own_places[None, :] == home_places[:, None] + 1) & goes_on[:, None]
    halo_back = jnp.sum(jnp.where(is_next[:, :, None, None], all_halo[None], 0.0), axis=1)
    token_grad = jnp.where(stay, token_grad, token_got).reshape(nb, CH, DM)
    token_grad = token_grad.at[:, CH - KC :].set(
        (token_grad[:, CH - KC :].astype(F32) + halo_back).astype(BF)
    ).reshape(rows, DM)
    mixed = jnp.where(stay, mixed, after(mixed_got, a_own))

    in_grad = jnp.concatenate([zo_grad[:, :DI], a_grad[:, : XBC + NH]], axis=1)
    out_grad = jnp.concatenate([zo_grad[:, DI : DI + DM], zo_grad[:, DI + DM :]], axis=0)
    gain_grad = jnp.sum(in_grad * in_weight.astype(F32), axis=1) / norm_gain.astype(F32)

    return (
        mixed, token_grad, gain_grad, in_grad, small[: KC * XBC // LANES].reshape(KC, XBC),
        small[KC * XBC // LANES : SUM_GAIN].reshape(XBC), small[SUM_HEADS, :NH],
        small[SUM_HEADS + 1, :NH], jnp.sum(small[SUM_SKIP:SUM_HEADS].reshape(NH, HD), axis=1),
        small[SUM_GAIN:SUM_SKIP].reshape(DI), out_grad,
    )


def solution(mesh):
    return jax.shard_map(
        shards,
        mesh=mesh,
        in_specs=(
            P(("head", "shard"), None), P("shard"), P("shard", None), P(), P(), P(), P(), P(), P(),
            P("shard", None), P("shard", None), P("shard", None), P(("head", "shard"), None),
        ),
        out_specs=(
            P(("head", "shard"), None), P(("head", "shard"), None), P("shard"), P("shard", None),
            P(), P(), P(), P(), P(), P(), P("shard", None),
        ),
        check_vma=False,
    )
```

```python
import functools

import jax
import jax.numpy as jnp
from jax import lax
from jax.experimental import pallas as pl
from jax.experimental.pallas import tpu as pltpu
from jax.sharding import PartitionSpec as P

NH = 24
HD = 64
NS = 128
KC = 4
CH = 256
DI = 1536
DM = 768
XBC = DI + 2 * NS
WA = 1920
HALO = 8
EPSILON = 1e-05
F32 = jnp.float32
BF = jnp.bfloat16
LANES = 128
CW = 384
NCW = DI // CW
VMEM_ASK = 56 * 2**20
VMEM_ROOM = 56 * 2**20
VMEM_LESS = 44 * 2**20
COST_SCALE = 0.4


def trade(value, axis, bit):
    size = lax.axis_size(axis)
    return lax.ppermute(value, axis, [(i, i ^ bit) for i in range(size)])


def after(value, *others):
    return lax.optimization_barrier((value,) + others)[0]


def move_home(value):
    n_head, n_shard = lax.axis_size("head"), lax.axis_size("shard")
    half = n_head // 2
    pairs = []
    for h in range(n_head):
        for s in range(n_shard):
            upper, core = h // half, s & 1
            if upper != core:
                there = (h % half + core * half) * n_shard + (s - core + upper)
                pairs.append((h * n_shard + s, there))
    return lax.ppermute(value, ("head", "shard"), pairs)


def swap_home(value, stay):
    return jnp.where(stay, value, move_home(value))


def group_spread(value):
    n_head, n_shard = lax.axis_size("head"), lax.axis_size("shard")
    pieces = [value]
    for core in (0, 1):
        for low in range(n_head // 2):
            if core or low:
                pairs = [
                    (h * n_shard + s, (h ^ low) * n_shard + (s ^ core))
                    for h in range(n_head)
                    for s in range(n_shard)
                ]
                pieces.append(lax.ppermute(value, ("head", "shard"), pairs))
    return pieces


def group_gather(value):
    half = lax.axis_size("head") // 2
    pieces = [value]
    bit = 1
    while bit < half:
        pieces = pieces + [trade(v, "head", bit) for v in pieces]
        bit *= 2
    return pieces + [trade(v, "shard", 1) for v in pieces]


def gather_far(piece):
    bits = range(2, lax.axis_size("shard"), 2)
    return [trade(piece, "shard", bit) for bit in sorted(bits, reverse=True)]


def gather_near(piece, far):
    held = [piece] + far
    offsets = [0] + sorted(range(2, lax.axis_size("shard"), 2), reverse=True)
    near = [trade(v, "shard", 1) for v in held]
    return list(zip(held + near, offsets + [k ^ 1 for k in offsets]))


def join_pieces(parts):
    me, n_shard = lax.axis_index("shard"), lax.axis_size("shard")
    joined = jnp.zeros((n_shard,) + parts[0][0].shape, parts[0][0].dtype)
    for v, k in parts:
        joined = lax.dynamic_update_slice(joined, v[None], (me ^ k, 0, 0))
    return joined


def head_pieces(value):
    pieces = [value]
    bit = 1
    while bit < lax.axis_size("head") // 2:
        pieces = pieces + [trade(v, "head", bit) for v in pieces]
        bit *= 2
    return pieces[1:]


def core_give(blocks):
    n_shard = lax.axis_size("shard")
    core = lax.axis_index("shard") % 2

    def half(which):
        parts = []
        for v in blocks:
            split = v.reshape((n_shard // 2, 2) + v.shape[1:])
            parts.append(lax.dynamic_index_in_dim(split, which, 1, False))
        return jnp.concatenate(parts, axis=2) if len(parts) > 1 else parts[0]

    return half(core), half(1 - core)


def chip_pairs(keep, got):
    pair = (keep.astype(F32) + got.astype(F32)).astype(BF)
    chip = lax.axis_index("shard") // 2
    return [lax.dynamic_index_in_dim(pair, chip ^ k, 0, False) for k in range(pair.shape[0])]


def after_all(values, *others):
    return list(lax.optimization_barrier((*values, *others)))[: len(values)]


def chip_send(pairs):
    return [trade(v, "shard", 2 * k) for k, v in enumerate(pairs) if k]


def chip_sum(own, got):
    total = own.astype(F32)
    for v in got:
        total = total + v.astype(F32)
    return total.astype(BF)


def split2(v):
    high = lax.reduce_precision(v, 8, 7)
    return jnp.concatenate([high.astype(BF), (v - high).astype(BF)], axis=1)


def join2(parts):
    high, low = jnp.split(parts, 2, axis=1)
    return high.astype(F32) + low.astype(F32)


def head_split(value):
    cut = value.shape[1] // 2
    odd = lax.axis_index("head") % 2
    return [lax.dynamic_slice_in_dim(value, at * cut, cut, 1) for at in (odd, 1 - odd)]


def head_add(keep, got):
    return (keep.astype(F32) + got.astype(F32)).astype(BF)


def head_join(half, other):
    odd = lax.axis_index("head") % 2
    return jnp.concatenate([jnp.where(odd, other, half), jnp.where(odd, half, other)], axis=1)


def dot(a, b):
    return jnp.dot(a, b, preferred_element_type=F32)


def dot_nt(a, b):
    return lax.dot_general(a, b, (((1,), (1,)), ((), ())), preferred_element_type=F32)


def dot_tn(a, b):
    return lax.dot_general(a, b, (((0,), (0,)), ((), ())), preferred_element_type=F32)


def spread_table(none):
    row = jnp.arange(2 * LANES)[:, None] % LANES + none
    return (row == jnp.arange(DI)[None, :] // HD).astype(BF)


def narrow_table(none):
    return (jnp.arange(DI)[:, None] // HD == jnp.arange(LANES)[None, :] + none).astype(BF)


def pieces2(v):
    hi = v.astype(BF)
    return hi, (v - hi.astype(F32)).astype(BF)


def pieces3(v):
    hi = v.astype(BF)
    rest = v - hi.astype(F32)
    mid = rest.astype(BF)
    return hi, mid, (rest - mid.astype(F32)).astype(BF)


def softplus(v):
    return jnp.maximum(v, 0.0) + jnp.log1p(jnp.exp(-jnp.abs(v)))


sigmoid = jax.nn.sigmoid


def shape(dims, dtype):
    return jax.ShapeDtypeStruct(dims, dtype)


def whole(arr):
    return pl.BlockSpec(arr.shape, lambda *g: (0,) * len(arr.shape))


def columns(arr, at, width=None):
    dims = arr.shape[:-1] + (width or CW,)
    return pl.BlockSpec(dims, lambda *g: (0,) * (len(dims) - 1) + (at(*g),))


def in_hbm():
    return pl.BlockSpec(memory_space=pl.ANY)


def in_smem():
    return pl.BlockSpec(memory_space=pltpu.SMEM)


def call(kernel, micros, grid, ins, outs, scratch, room=VMEM_ROOM):
    return pl.pallas_call(
        kernel,
        grid=grid,
        out_shape=[o for o, _ in outs],
        in_specs=[s for _, s in ins],
        out_specs=[s for _, s in outs],
        scratch_shapes=scratch,
        compiler_params=pltpu.CompilerParams(vmem_limit_bytes=room),
        cost_estimate=pl.CostEstimate(
            flops=1, bytes_accessed=int(micros * COST_SCALE * 3.7e6), transcendentals=0
        ),
    )(*[a for a, _ in ins])


def iota(dims, axis):
    return lax.broadcasted_iota(jnp.int32, dims, axis)


def place_of(info, q):
    return info[2 + 3 * q]


def first_of(info, q):
    return info[3 + 3 * q]


def usable_of(info, i):
    begin = (place_of(info, i) - first_of(info, i)) * CH
    return (iota((CH, 1), 0) + begin < info[4 + 3 * i]).astype(F32)


def halo_used(info, i):
    has_prev = place_of(info, i) > first_of(info, i)
    return (iota((HALO, 1), 0) + jnp.where(has_prev, 0, -HALO) > HALO - KC).astype(F32)


def clast_rows(refs, nb):
    rows = []
    for ref in refs:
        for b in range(nb):
            part = ref[b].astype(F32)
            rows.append(part[0:1, :] + part[1:2, :] + part[2:3, :])
    return rows


def carry_weights(info, ends, nb, into):
    n_all = len(ends)
    row = iota((n_all, 1), 0)
    place = jnp.zeros((n_all, 1), jnp.int32)
    first = jnp.zeros((n_all, 1), jnp.int32)
    for j in range(n_all):
        place = jnp.where(row == j, place_of(info, j), place)
        first = jnp.where(row == j, first_of(info, j), first)
    parts = []
    for i in range(nb):
        own = place_of(info, i)
        total = jnp.zeros((n_all, LANES), F32)
        for k in range(n_all):
            at = place_of(info, k)
            if into:
                between = (place > at) & (at > own)
            else:
                between = (place < at) & (at < own)
            total = total + jnp.where(between, ends[k], 0.0)
        if into:
            reach = (first <= own) & (place > own)
        else:
            reach = (place >= first_of(info, i)) & (place < own)
        parts.append(jnp.where(reach, jnp.exp(total), 0.0))
    return jnp.concatenate(pieces2(jnp.concatenate(parts, axis=0)), axis=1)


def normal_rows(rows, gain):
    f = rows.astype(F32)
    inv = lax.rsqrt(jnp.sum(f * f, axis=1, keepdims=True) / DM + EPSILON)
    return (f * inv * gain).astype(BF)


def project_kernel(layout, n_halo, *refs):
    info = refs[0]
    pieces = refs[1 : 1 + len(layout)]
    halos = refs[1 + len(layout) : 1 + len(layout) + n_halo]
    (
        tok_own, tok_got, conv_w, conv_b, dt_bias, a_log, table,
        wa_out, tok_out, tok_halo, normal_out, normal_t_out, xbc, slope, xs, xt, bs_out, cs_out,
        raw_out, cum_out, cum_t_out, states,
        wa, ext, small, sems, out_sems, tok, normal, normal_t, bs, cs, raw, cum, cum_t,
    ) = refs[1 + len(layout) + n_halo :]
    step = pl.program_id(0)
    rows = tok_own.shape[0]
    nb = rows // CH
    me = info[0]

    def project(at, width):
        proj = dot(normal[...], wa[:, pl.ds(at, width)]).astype(BF).astype(F32)
        acts, heads = [], []
        for i in range(nb):
            head = proj[rows + i * HALO : rows + (i + 1) * HALO, :] * halo_used(info, i)
            body = proj[i * CH : (i + 1) * CH, :] * usable_of(info, i)
            heads.append(head)
            ext[i, :HALO, :width] = head
            ext[i, HALO:, :width] = body
            xbc[i * CH : (i + 1) * CH, :width] = body.astype(BF)
            pre = conv_b[:, pl.ds(at, width)]
            for lag in range(KC):
                tap = conv_w[KC - 1 - lag : KC - lag, pl.ds(at, width)]
                pre = pre + tap * ext[i, HALO - lag : HALO - lag + CH, :width]
            sg = sigmoid(pre)
            act = pre * sg
            slope[i * CH : (i + 1) * CH, :width] = (sg + act * (1.0 - sg)).astype(BF)
            acts.append(act)
        xbc[rows:, :width] = jnp.concatenate(heads, axis=0).astype(BF)
        return acts

    def leaving():
        moves = [(wa, wa_out), (tok, tok_out), (normal, normal_out), (normal_t, normal_t_out)]
        moves += [(bs, bs_out), (cs, cs_out), (raw, raw_out), (cum, cum_out), (cum_t, cum_t_out)]
        return [pltpu.make_async_copy(v, there, out_sems.at[n]) for n, (v, there) in enumerate(moves)]

    @pl.when(step == 0)
    def _():
        def copy_of(n):
            at = pl.multiple_of((me ^ layout[n]) * pieces[n].shape[0], 16)
            return pltpu.make_async_copy(
                pieces[n], wa.at[pl.ds(at, pieces[n].shape[0]), :], sems.at[n]
            )

        for n in range(len(layout)):
            copy_of(n).start()
        stay = info[1] > 0
        tok[...] = jnp.where(stay, tok_own[...], tok_got[...])
        found = []
        for i in range(nb):
            own, has_prev = place_of(info, i), place_of(info, i) > first_of(info, i)
            total = jnp.zeros((HALO, DM), F32)
            for o in range(n_halo):
                part = halos[o][...].astype(F32)
                for b in range(nb):
                    hit = (place_of(info, o * nb + b) == own - 1) & has_prev
                    total = total + jnp.where(hit, part[b * HALO : (b + 1) * HALO, :], 0.0)
            found.append(total)
        tok_halo[...] = jnp.concatenate(found, axis=0).astype(BF)
        for n in range(len(layout)):
            copy_of(n).wait()
        for copy in leaving()[:2]:
            copy.start()
        gain = wa[:, XBC : XBC + LANES].astype(F32).T[NH : NH + 1, :]
        normal[:rows, :] = normal_rows(tok[...], gain)
        normal_t[...] = normal[:rows, :].T
        normal[rows:, :] = normal_rows(tok_halo[...], gain)
        for i, act in enumerate(project(DI, 2 * NS)):
            bs[i * CH : (i + 1) * CH, :] = act[:, :NS].astype(BF)
            cs[i * CH : (i + 1) * CH, :] = act[:, NS:].astype(BF)
        xbc[:, 2 * NS :] = jnp.zeros((xbc.shape[0], CW - 2 * NS), BF)
        slope[:, 2 * NS :] = jnp.zeros((rows, CW - 2 * NS), BF)
        first = dot(normal[:rows, :], wa[:, XBC : XBC + LANES]).astype(BF).astype(F32) + dt_bias[...]
        raw[...] = first
        dt_all = softplus(first)
        rate = jnp.exp(a_log[...])
        causal = (iota((CH, CH), 0) >= iota((CH, CH), 1)).astype(F32).astype(BF)
        states[:, :, DI:] = jnp.zeros((nb, NS, LANES), BF)
        for i in range(nb):
            dt = dt_all[i * CH : (i + 1) * CH, :]
            parts = dot(causal, jnp.concatenate(pieces3(-dt * rate), axis=1))
            run = parts[:, :LANES] + parts[:, LANES : 2 * LANES] + parts[:, 2 * LANES :]
            cum[i * CH : (i + 1) * CH, :] = run
            cum_t[:, i * CH : (i + 1) * CH] = run.T
            last = run[CH - 1 : CH, :]
            ends = jnp.concatenate(pieces3(last) + (jnp.zeros((13, LANES), BF),), axis=0)
            states[i, :16, DI:] = ends
            small[i, 0] = jnp.concatenate(pieces2(dt), axis=1)
            small[i, 1] = jnp.concatenate(pieces2(jnp.exp(last - run) * dt), axis=1)
        for copy in leaving()[2:]:
            copy.start()

    @pl.when(step > 0)
    def _():
        at = pl.multiple_of((step - 1) * CW, CW)
        for i, act in enumerate(project(at, CW)):
            r = slice(i * CH, (i + 1) * CH)
            xs[r, :] = act.astype(BF)
            xt[r, :] = (act * dot(small[i, 0], table[...])).astype(BF)
            weighted = (act * dot(small[i, 1], table[...])).astype(BF)
            states[i, :, pl.ds(at, CW)] = dot_tn(bs[r, :], weighted).astype(BF)

    @pl.when(step == NCW)
    def _():
        for copy in leaving():
            copy.wait()


def run_project(info, parts, halos, tok_own, tok_got, conv_w, conv_b, dt_bias, a_log, table):
    rows = tok_own.shape[0]
    nb = rows // CH
    ext_rows = rows + nb * HALO
    layout = [offset for _, offset in parts]

    def before(s):
        return jnp.maximum(s - 1, 0)

    def tail_first(s):
        return jnp.where(s == 0, NCW, s - 1)

    ins = [(info, in_smem())] + [(v, in_hbm()) for v, _ in parts]
    ins += [(v, whole(v)) for v in halos]
    ins += [(v, whole(v)) for v in (tok_own, tok_got, conv_w, conv_b, dt_bias, a_log)]
    ins += [(table, columns(table, before))]
    outs = {
        "wa": (shape((DM, WA), BF), in_hbm()),
        "tok": (shape((rows, DM), BF), in_hbm()),
        "tok_halo": (shape((nb * HALO, DM), BF), whole),
        "normal": (shape((ext_rows, DM), BF), in_hbm()),
        "normal_t": (shape((DM, rows), BF), in_hbm()),
        "xbc": (shape((ext_rows, WA), BF), lambda v: columns(v, tail_first)),
        "slope": (shape((rows, WA), BF), lambda v: columns(v, tail_first)),
        "xs": (shape((rows, DI), BF), lambda v: columns(v, before)),
        "xt": (shape((rows, DI), BF), lambda v: columns(v, before)),
        "bs": (shape((rows, NS), BF), in_hbm()),
        "cs": (shape((rows, NS), BF), in_hbm()),
        "raw": (shape((rows, LANES), F32), in_hbm()),
        "cum": (shape((rows, LANES), F32), in_hbm()),
        "cum_t": (shape((LANES, rows), F32), in_hbm()),
        "states": (shape((nb, NS, DI + LANES), BF), whole),
    }
    out_list = [(o, s(o) if callable(s) else s) for o, s in outs.values()]
    scratch = [
        pltpu.VMEM((DM, WA), BF), pltpu.VMEM((nb, HALO + CH, CW), F32),
        pltpu.VMEM((nb, 2, CH, 2 * LANES), BF), pltpu.SemaphoreType.DMA((len(parts),)),
        pltpu.SemaphoreType.DMA((9,)),
    ]
    kept = ("tok", "normal", "normal_t", "bs", "cs", "raw", "cum", "cum_t")
    scratch += [pltpu.VMEM(outs[k][0].shape, outs[k][0].dtype) for k in kept]
    got = call(
        functools.partial(project_kernel, layout, len(halos)), 14, (NCW + 1,), ins, out_list, scratch, VMEM_ASK,
    )
    return dict(zip(outs, got))


SUM_GAIN = (KC + 1) * XBC // LANES
SUM_SKIP = SUM_GAIN + DI // LANES
SUM_HEADS = SUM_SKIP + DI // LANES
SUM_ROWS = SUM_HEADS + 2
OUT_ROWS = CW // 4
PER = CW // HD
HALF = CH // 2


def chunk_heads(cum, first):
    return pltpu.roll(cum, lax.rem(LANES - first, LANES), axis=1)


def intra_kernel(bs, cs, xt, cum, cum_t, out, scores):
    c = pl.program_id(0)
    nb = bs.shape[0] // CH
    low = iota((CH, LANES), 1) < HD
    keep = iota((HALF, HALF), 0) >= iota((HALF, HALF), 1)

    @pl.when(c == 0)
    def _():
        for i in range(nb):
            r = slice(i * CH, (i + 1) * CH)
            scores[i] = dot_nt(cs[r, :], bs[r, :])

    for i in range(nb):
        r = slice(i * CH, (i + 1) * CH)
        cols = chunk_heads(cum[r, :], c * PER)
        for p in range(PER // 2):
            lanes = slice(p * LANES, (p + 1) * LANES)
            both = xt[r, lanes]
            got = []
            for k in range(2):
                h = 2 * p + k
                col = cols[:, h : h + 1]
                row = cum_t[pl.ds(c * PER + h, 1), r]
                a, b = col[:HALF], col[HALF:]
                s, t = row[:, :HALF], row[:, HALF:]
                upper = jnp.where(keep, jnp.exp(a - s), 0.0) * scores[i, :HALF, :HALF]
                left = jnp.exp(b - s) * scores[i, HALF:, :HALF]
                right = jnp.where(keep, jnp.exp(b - t), 0.0) * scores[i, HALF:, HALF:]
                lower = jnp.concatenate([left.astype(BF), right.astype(BF)], axis=1)
                got.append(
                    jnp.concatenate([dot(upper.astype(BF), both[:HALF, :]), dot(lower, both)], axis=0)
                )
            out[r, lanes] = jnp.where(low, got[0], got[1])


def run_intra(a):
    rows = a["bs"].shape[0]
    nb = rows // CH
    ins = [(a[k], whole(a[k])) for k in ("bs", "cs")]
    ins += [(a["xt"], columns(a["xt"], lambda c: c))]
    ins += [(a[k], whole(a[k])) for k in ("cum", "cum_t")]
    out = shape((rows, DI), F32)
    return call(
        intra_kernel, 6, (NCW,), ins, [(out, columns(out, lambda c: c))],
        [pltpu.VMEM((nb, CH, CH), F32)],
    )[0]


OW = 768
ONW = DI // OW


def open_kernel(layout, at, *refs):
    pieces = refs[: len(layout)]
    normal, cot_own, cot_got, stay, z, q, cot, wz_out, wo_out, wz, wo, sems, out_sems = refs[
        len(layout) :
    ]
    c = pl.program_id(0)
    k_rows = pieces[0].shape[0]

    def copies(n):
        shard = at[0] ^ layout[n]
        parts = [(wz, shard * k_rows, slice(0, DI))]
        for j in range(2):
            lanes = slice(DI + j * DM, DI + (j + 1) * DM)
            parts.append((wo, (2 * shard + j) * k_rows, lanes))
        return [
            pltpu.make_async_copy(
                pieces[n].at[:, lanes],
                ref.at[pl.ds(pl.multiple_of(begin, 16), k_rows), :],
                sems.at[3 * n + k],
            )
            for k, (ref, begin, lanes) in enumerate(parts)
        ]

    def leaving():
        return [
            pltpu.make_async_copy(wz, wz_out, out_sems.at[0]),
            pltpu.make_async_copy(wo, wo_out, out_sems.at[1]),
        ]

    @pl.when(c == 0)
    def _():
        for n in range(len(layout)):
            for copy in copies(n):
                copy.start()
        cot[...] = jnp.where(stay[0] > 0, cot_own[...], cot_got[...])
        for n in range(len(layout)):
            for copy in copies(n):
                copy.wait()
        for copy in leaving():
            copy.start()

    here = pl.ds(pl.multiple_of(c * OW, OW), OW)
    z[...] = dot(normal[...], wz[:, here]).astype(BF)
    q[...] = dot_nt(cot[...], wo[here, :]).astype(BF)

    @pl.when(c == ONW - 1)
    def _():
        for copy in leaving():
            copy.wait()


def run_open(at, parts, normal, cot_own, cot_got, stay):
    rows = cot_own.shape[0]
    layout = [offset for _, offset in parts]
    ins = [(at, in_smem())] + [(v, in_hbm()) for v, _ in parts]
    ins += [(normal, pl.BlockSpec((rows, DM), lambda c: (0, 0)))]
    ins += [(cot_own, whole(cot_own)), (cot_got, whole(cot_got)), (stay, in_smem())]
    wide = shape((rows, DI), BF)
    outs = [(wide, columns(wide, lambda c: c, OW))] * 2
    outs += [(v, whole(v)) for v in (shape((rows, DM), BF),)]
    outs += [(v, in_hbm()) for v in (shape((DM, DI), BF), shape((DI, DM), BF))]
    return call(
        functools.partial(open_kernel, layout), 1, (ONW,), ins, outs,
        [
            pltpu.VMEM((DM, DI), BF), pltpu.VMEM((DI, DM), BF),
            pltpu.SemaphoreType.DMA((3 * len(parts),)), pltpu.SemaphoreType.DMA((2,)),
        ],
        VMEM_LESS,
    )


def terms_kernel(at, normal_t, dz, normed, cot, keep, *refs):
    *give, z_part, o_part = refs
    p = pl.program_id(0)
    unit = give[0].shape[0]
    even = at[0] % 2 == 0
    z_part[...] = dot(normal_t[...], dz[...])
    o_part[...] = dot_tn(normed[...], cot[...])

    def rows_of(which):
        parts = [(z_part[which * unit : (which + 1) * unit, :], slice(0, DI))]
        for j in range(2):
            rows = o_part[(2 * which + j) * unit : (2 * which + j + 1) * unit, :]
            parts.append((rows, slice(DI + j * DM, DI + (j + 1) * DM)))
        return parts

    for (first, lanes), (second, _) in zip(rows_of(0), rows_of(1)):
        keep[0, :, lanes] = jnp.where(even, first, second).astype(BF)
        other = jnp.where(even, second, first).astype(BF)
        for k, ref in enumerate(give):

            @pl.when(p == k)
            def _(ref=ref, other=other, lanes=lanes):
                ref[:, lanes] = other


def run_terms(at, normal_t, dz, normed, cot, n_shard):
    rows = dz.shape[0]
    n, unit = n_shard // 2, DM // n_shard
    give = shape((unit, DI + 2 * DM), BF)
    keep = shape((n,) + give.shape, BF)
    got = call(
        terms_kernel, 1, (n,),
        [
            (at, in_smem()), (normal_t, pl.BlockSpec((2 * unit, rows), lambda p: (p, 0))),
            (dz, whole(dz)), (normed, columns(normed, lambda p: p, 4 * unit)), (cot, whole(cot)),
        ],
        [(keep, pl.BlockSpec((1,) + give.shape, lambda p: (p, 0, 0)))] + [(give, whole(give))] * n,
        [pltpu.VMEM((2 * unit, DI), F32), pltpu.VMEM((4 * unit, DM), F32)],
    )
    return got[0], list(got[1:])


def pair_small_kernel(at, keep, got, small, small_got, *outs):
    n, _, cols = keep.shape
    chip = at[0] // 2
    total = small[...] + small_got[...]
    parts = jnp.concatenate(pieces2(total), axis=1)
    for k, out in enumerate(outs):
        out[:, :cols] = (keep[chip ^ k].astype(F32) + got[chip ^ k].astype(F32)).astype(BF)
        out[:, cols:] = parts


def run_pair_small(at, keep, got, small, small_got):
    n, rows, cols = keep.shape
    out = shape((rows, cols + 2 * small.shape[1]), BF)
    args = [keep, got, small, small_got]
    return call(
        pair_small_kernel, 1, (1,), [(at, in_smem())] + [(v, whole(v)) for v in args],
        [(out, whole(out))] * n, [],
    )


GW = 768
GNW = DI // GW


def columns_g(arr, at):
    return columns(arr, at, GW)


def gate_kernel(n_pieces, *refs):
    info = refs[0]
    pieces = refs[1 : 1 + n_pieces]
    ends = refs[1 + n_pieces : 1 + 2 * n_pieces]
    (
        y_intra, cs, cum, xs, z, q, inner_gain, d_skip, table,
        enter, normed, gain_part, dz, dyr, dye, product, skip_part, d_enter,
        y_scan, small, weights, squares, dots,
    ) = refs[1 + 2 * n_pieces :]
    phase, c = pl.program_id(0), pl.program_id(1)
    rows = cs.shape[0]
    nb = rows // CH
    n_all = n_pieces * nb
    here = pl.ds(pl.multiple_of(c * GW, GW), GW)

    @pl.when((phase == 0) & (c == 0))
    def _():
        weights[...] = carry_weights(info, clast_rows(ends, nb), nb, False)
        squares[...] = jnp.zeros_like(squares)
        dots[...] = jnp.zeros_like(dots)
        for i in range(nb):
            r = slice(i * CH, (i + 1) * CH)
            small[r, :] = jnp.concatenate(pieces2(jnp.exp(cum[r, :])), axis=1)

    @pl.when(phase == 0)
    def _():
        wide_w = dot(weights[...], table[...])
        totals = [jnp.zeros((NS, GW), F32) for _ in range(nb)]
        for j in range(n_all):
            piece = pieces[j // nb][j % nb].astype(F32)
            for i in range(nb):
                totals[i] = totals[i] + wide_w[i * n_all + j : i * n_all + j + 1, :] * piece
        for i in range(nb):
            r = slice(i * CH, (i + 1) * CH)
            low = totals[i].astype(BF)
            enter[i] = low
            scan = y_intra[r, :] + dot(small[r, :], table[...]) * dot(cs[r, :], low)
            y_scan[r, here] = scan
            y = scan + d_skip[...] * xs[r, :].astype(F32)
            zf = z[r, :].astype(F32)
            gated = y * (zf * sigmoid(zf))
            qg = q[r, :].astype(F32) * inner_gain[...] * usable_of(info, i)
            squares[r, :] += jnp.sum(gated * gated, axis=1, keepdims=True)
            dots[r, :] += jnp.sum(qg * gated, axis=1, keepdims=True)

    @pl.when(phase == 1)
    def _():
        gain_sum = jnp.zeros((1, GW), F32)
        skip_sum = jnp.zeros((1, GW), F32)
        for i in range(nb):
            r = slice(i * CH, (i + 1) * CH)
            inv = lax.rsqrt(squares[r, :] / DI + EPSILON)
            slope = inv * inv * inv * dots[r, :] / DI
            use = usable_of(info, i)
            scan = y_scan[r, here]
            x = xs[r, :].astype(F32)
            y = scan + d_skip[...] * x
            zf = z[r, :].astype(F32)
            sg = sigmoid(zf)
            sz = zf * sg
            gated = y * sz
            qf = q[r, :].astype(F32) * use
            scaled = gated * inv
            normed[r, :] = (scaled * inner_gain[...] * use).astype(BF)
            gain_sum = gain_sum + jnp.sum(qf * scaled, axis=0, keepdims=True)
            gg = inv * qf * inner_gain[...] - gated * slope
            dz[r, :] = (gg * y * (sg + sz * (1.0 - sg))).astype(BF)
            dy = gg * sz
            low = dy.astype(BF)
            dyr[r, :] = low
            product[r, :] = low.astype(F32) * scan
            skip_sum = skip_sum + jnp.sum(dy * x, axis=0, keepdims=True)
            back = (dot(small[r, :], table[...]) * dy).astype(BF)
            dye[r, :] = back
            d_enter[i] = dot_tn(cs[r, :], back).astype(BF)
        gain_part[...] = gain_sum
        skip_part[...] = skip_sum


def run_gate(info, a, pieces, y_intra, z, q, inner_gain, d_skip, table):
    rows = z.shape[0]
    nb = rows // CH

    def early(p, c):
        return jnp.where(p == 0, c, GNW - 1)

    def both(p, c):
        return c

    def late(p, c):
        return jnp.where(p == 0, 0, c)

    ins = [(info, in_smem())]
    ins += [(v, columns_g(v, early)) for v in pieces]
    ins += [(v, pl.BlockSpec((nb, 16, LANES), lambda p, c: (0, 0, DI // LANES))) for v in pieces]
    ins += [(y_intra, columns_g(y_intra, early))]
    ins += [(a[k], whole(a[k])) for k in ("cs", "cum")]
    ins += [(v, columns_g(v, both)) for v in (a["xs"], z, q, inner_gain, d_skip, table)]
    wide = shape((rows, DI), BF)
    wide_f = shape((rows, DI), F32)
    row = shape((1, DI), F32)
    state = shape((nb, NS, DI), BF)
    outs = [(state, columns_g(state, early))]
    outs += [(v, columns_g(v, late)) for v in (wide, row, wide, wide, wide, wide_f, row, state)]
    scratch = [
        pltpu.VMEM((rows, DI), F32), pltpu.VMEM((rows, 2 * LANES), BF),
        pltpu.VMEM((nb * nb * len(pieces), 2 * LANES), BF), pltpu.VMEM((rows, 1), F32),
        pltpu.VMEM((rows, 1), F32),
    ]
    return call(
        functools.partial(gate_kernel, len(pieces)), 16, (2, GNW), ins, outs, scratch, VMEM_ASK,
    )


def intra_back_kernel(
    bs, cs, xt, cum, cum_t, dyr, dye, enter, normed, wo, tok, dxt, db, dc, mixed, scores, top, bottom,
    total,
):
    c = pl.program_id(0)
    nb = bs.shape[0] // CH
    low = iota((CH, LANES), 1) < HD
    keep = iota((HALF, HALF), 1) >= iota((HALF, HALF), 0)

    @pl.when(c == 0)
    def _():
        for i in range(nb):
            r = slice(i * CH, (i + 1) * CH)
            scores[i] = dot_nt(bs[r, :], cs[r, :])
        top[...] = jnp.zeros_like(top)
        bottom[...] = jnp.zeros_like(bottom)
        dc[...] = jnp.zeros_like(dc)
        total[...] = tok[...].astype(F32)

    total[...] += dot(normed[...], wo[...])

    for i in range(nb):
        r = slice(i * CH, (i + 1) * CH)
        cols = chunk_heads(cum[r, :], c * PER)
        dc[r, :] += dot_nt(dye[r, :], enter[i])
        top_sum, bottom_sum = top[i], bottom[i]
        for p in range(PER // 2):
            lanes = slice(p * LANES, (p + 1) * LANES)
            x, dy = xt[r, lanes], dyr[r, lanes]
            got = []
            for k in range(2):
                h = 2 * p + k
                col = cols[:, h : h + 1]
                row = cum_t[pl.ds(c * PER + h, 1), r]
                a, b = col[:HALF], col[HALF:]
                s, t = row[:, :HALF], row[:, HALF:]
                left = jnp.where(keep, jnp.exp(s - a), 0.0)
                right = jnp.exp(t - a)
                last = jnp.where(keep, jnp.exp(t - b), 0.0)
                dec = jnp.concatenate([left, right], axis=1)
                got.append(
                    jnp.concatenate(
                        [
                            dot((dec * scores[i, :HALF, :]).astype(BF), dy),
                            dot((last * scores[i, HALF:, HALF:]).astype(BF), dy[HALF:, :]),
                        ],
                        axis=0,
                    )
                )
                own = jnp.where(low, x, 0) if k == 0 else jnp.where(low, 0, x)
                top_sum = top_sum + dot_nt(own[:HALF, :], dy) * dec
                bottom_sum = bottom_sum + dot_nt(own[HALF:, :], dy[HALF:, :]) * last
            dxt[r, lanes] = jnp.where(low, got[0], got[1])
        top[i], bottom[i] = top_sum, bottom_sum

    @pl.when(c == NCW - 1)
    def _():
        for i in range(nb):
            r = slice(i * CH, (i + 1) * CH)
            up, down = top[i].astype(BF), bottom[i].astype(BF)
            down = jnp.concatenate([jnp.zeros((HALF, HALF), BF), down], axis=1)
            both = jnp.concatenate([up, down], axis=0)
            db[r, :] = dot(both, cs[r, :])
            dc[r, :] += dot_tn(both, bs[r, :])
        mixed[...] = total[...].astype(BF)


def run_intra_back(a, dyr, dye, enter, normed, wo, tok):
    rows = dyr.shape[0]
    nb = rows // CH

    def same(c):
        return c

    ins = [(a[k], whole(a[k])) for k in ("bs", "cs")]
    ins += [(a["xt"], columns(a["xt"], same))]
    ins += [(a[k], whole(a[k])) for k in ("cum", "cum_t")]
    ins += [(v, columns(v, same)) for v in (dyr, dye, enter, normed)]
    ins += [(wo, pl.BlockSpec((CW, DM), lambda c: (c, 0))), (tok, whole(tok))]
    full, small, mixed = shape((rows, DI), F32), shape((rows, NS), F32), shape((rows, DM), BF)
    return call(
        intra_back_kernel, 1, (NCW,), ins,
        [(full, columns(full, same))] + [(v, whole(v)) for v in (small, small, mixed)],
        [
            pltpu.VMEM((nb, CH, CH), F32), pltpu.VMEM((nb, HALF, CH), F32),
            pltpu.VMEM((nb, HALF, HALF), F32), pltpu.VMEM((rows, DM), F32),
        ],
    )


def back_kernel(n_pieces, *refs):
    info = refs[0]
    pieces = refs[1 : 1 + n_pieces]
    ends = refs[1 + n_pieces : 1 + 2 * n_pieces]
    (
        dx_intra, db_in, dc_in, xbc, slope, xs, xt, bs, raw, cum, enter, product, dyr, conv_w,
        a_log, d_skip, table, narrow, gain_part, skip_part,
        d_a, sums,
        grad, small, d_bs, heads, weights,
    ) = refs[1 + 2 * n_pieces :]
    step = pl.program_id(0)
    rows = xs.shape[0]
    nb = rows // CH
    n_all = n_pieces * nb

    @pl.when(step == 0)
    def _():
        weights[...] = carry_weights(info, clast_rows(ends, nb), nb, True)
        dt_all = softplus(raw[...])
        for i in range(nb):
            r = slice(i * CH, (i + 1) * CH)
            last = cum[(i + 1) * CH - 1 : (i + 1) * CH, :]
            small[i, 0] = jnp.concatenate(pieces2(dt_all[r, :]), axis=1)
            small[i, 1] = jnp.concatenate(pieces2(jnp.exp(last - cum[r, :])), axis=1)
            grad[i, :HALO, :] = jnp.zeros((HALO, CW), F32)
            grad[i, HALO + CH :, :] = jnp.zeros((HALO, CW), F32)
        d_bs[...] = db_in[...]
        heads[...] = jnp.zeros_like(heads)

    def put_rows(at, row):
        for j in range(row.shape[1] // LANES):
            sums[pl.ds(at + j, 1), :] = row[:, j * LANES : (j + 1) * LANES]

    def convolve_back(dacts, width):
        offset_sum = jnp.zeros((1, width), F32)
        tap_sums = [jnp.zeros((1, width), F32) for _ in range(KC)]
        all_heads = xbc[rows:, :width].astype(F32)
        head_grads = []
        for i in range(nb):
            r = slice(i * CH, (i + 1) * CH)
            dpre = dacts[i] * slope[r, :width].astype(F32)
            offset_sum = offset_sum + jnp.sum(dpre, axis=0, keepdims=True)
            grad[i, HALO : HALO + CH, :width] = dpre
            body = xbc[r, :width].astype(F32)
            head = all_heads[i * HALO : (i + 1) * HALO, :]
            total = jnp.zeros((CH, width), F32)
            total_head = jnp.zeros((HALO, width), F32)
            for lag in range(KC):
                tap = conv_w[KC - 1 - lag : KC - lag, :width]
                later = grad[i, HALO + lag : HALO + lag + CH, :width]
                later_head = grad[i, lag : lag + HALO, :width]
                total = total + tap * later
                total_head = total_head + tap * later_head
                tap_sums[KC - 1 - lag] = (
                    tap_sums[KC - 1 - lag]
                    + jnp.sum(later * body, axis=0, keepdims=True)
                    + jnp.sum(later_head * head, axis=0, keepdims=True)
                )
            d_a[r, :width] = (total * usable_of(info, i)).astype(BF)
            head_grads.append(total_head * halo_used(info, i))
        d_a[rows:, :width] = jnp.concatenate(head_grads, axis=0).astype(BF)
        for k, row in enumerate(tap_sums + [offset_sum]):
            put_rows(k * (XBC // LANES) + step * (CW // LANES), row)

    @pl.when(step < NCW)
    def _():
        wide_w = dot(weights[...], table[...])
        totals = [jnp.zeros((NS, CW), F32) for _ in range(nb)]
        for j in range(n_all):
            piece = pieces[j // nb][j % nb].astype(F32)
            for i in range(nb):
                totals[i] = totals[i] + wide_w[i * n_all + j : i * n_all + j + 1, :] * piece
        select = narrow[...]
        dacts = []
        for i in range(nb):
            r = slice(i * CH, (i + 1) * CH)
            low = totals[i].astype(BF)
            fade = jnp.sum(low.astype(F32) * enter[i].astype(F32), axis=0, keepdims=True)
            end_w = dot(small[i, 1], table[...])
            x_dt = xt[r, :].astype(F32)
            inter = end_w * dot(bs[r, :], low)
            d_bs[r, :] += dot_nt((x_dt * end_w).astype(BF), low)
            dxt = dx_intra[r, :] + inter
            flow = jnp.sum(x_dt * inter, axis=0, keepdims=True)
            hi, mid, lo = pieces3(product[r, :] - x_dt * dxt)
            heads[0, r, :] += dot(hi, select) + dot(mid, select) + dot(lo, select)
            heads[1, r, :] += dot((xs[r, :].astype(F32) * dxt).astype(BF), select)
            hi, mid, lo = pieces3(jnp.concatenate([flow, fade, jnp.zeros((6, CW), F32)], axis=0))
            heads[2, i * 8 : (i + 1) * 8, :] += dot(hi, select) + dot(mid, select) + dot(lo, select)
            dacts.append(
                dot(small[i, 0], table[...]) * dxt + d_skip[...] * dyr[r, :].astype(F32)
            )
        convolve_back(dacts, CW)
        put_rows(SUM_GAIN + step * (CW // LANES), gain_part[...])
        put_rows(SUM_SKIP + step * (CW // LANES), skip_part[...])

    @pl.when(step == NCW)
    def _():
        dacts = []
        for i in range(nb):
            r = slice(i * CH, (i + 1) * CH)
            dacts.append(jnp.concatenate([d_bs[r, :], dc_in[r, :]], axis=1))
        convolve_back(dacts, 2 * NS)
        rate = jnp.exp(a_log[...])
        anti = (iota((CH, CH), 0) <= iota((CH, CH), 1)).astype(F32).astype(BF)
        bias_sum = jnp.zeros((1, LANES), F32)
        rate_sum = jnp.zeros((1, LANES), F32)
        for i in range(nb):
            r = slice(i * CH, (i + 1) * CH)
            last = cum[(i + 1) * CH - 1 : (i + 1) * CH, :]
            flow, fade = heads[2, i * 8 : i * 8 + 1, :], heads[2, i * 8 + 1 : i * 8 + 2, :]
            parts = dot(anti, jnp.concatenate(pieces3(heads[0, r, :]), axis=1))
            d_log = parts[:, :LANES] + parts[:, LANES : 2 * LANES] + parts[:, 2 * LANES :]
            d_log = d_log + (flow + jnp.exp(last) * fade)
            start = raw[r, :]
            d_raw = (heads[1, r, :] - d_log * rate) * sigmoid(start)
            d_raw = jnp.where(iota((CH, LANES), 1) < NH, d_raw, 0.0)
            bias_sum = bias_sum + jnp.sum(d_raw, axis=0, keepdims=True)
            rate_sum = rate_sum - jnp.sum(d_log * softplus(start), axis=0, keepdims=True) * rate
            d_a[r, 2 * NS :] = d_raw.astype(BF)
        d_a[rows:, 2 * NS :] = jnp.zeros((nb * HALO, CW - 2 * NS), BF)
        put_rows(SUM_HEADS, bias_sum)
        put_rows(SUM_HEADS + 1, rate_sum)


def run_back(
    info, a, pieces, ends, dx_intra, db, dc, enter, product, dyr, conv_w, a_log, d_skip, table,
    narrow, gain_part, skip_part,
):
    rows = dyr.shape[0]
    nb = rows // CH
    ext_rows = rows + nb * HALO

    def chunk(s):
        return jnp.minimum(s, NCW - 1)

    def same(s):
        return s

    ins = [(info, in_smem())]
    ins += [(v, columns(v, chunk)) for v in pieces]
    ins += [(v, pl.BlockSpec((nb, 16, LANES), lambda s: (0, 0, DI // LANES))) for v in ends]
    ins += [(dx_intra, columns(dx_intra, chunk)), (db, whole(db)), (dc, whole(dc))]
    ins += [(a["xbc"], columns(a["xbc"], same)), (a["slope"], columns(a["slope"], same))]
    ins += [(a["xs"], columns(a["xs"], chunk)), (a["xt"], columns(a["xt"], chunk))]
    ins += [(a[k], whole(a[k])) for k in ("bs", "raw", "cum")]
    ins += [(v, columns(v, chunk)) for v in (enter, product, dyr)]
    ins += [(conv_w, columns(conv_w, same)), (a_log, whole(a_log)), (d_skip, columns(d_skip, chunk))]
    ins += [(table, columns(table, chunk))]
    ins += [(narrow, pl.BlockSpec((CW, LANES), lambda s: (chunk(s), 0)))]
    ins += [(v, columns(v, chunk)) for v in (gain_part, skip_part)]
    wide, sums = shape((ext_rows, WA), BF), shape((SUM_ROWS, LANES), F32)
    outs = [(wide, columns(wide, same)), (sums, whole(sums))]
    scratch = [
        pltpu.VMEM((nb, CH + 2 * HALO, CW), F32), pltpu.VMEM((nb, 2, CH, 2 * LANES), BF),
        pltpu.VMEM((rows, NS), F32), pltpu.VMEM((3, rows, LANES), F32),
        pltpu.VMEM((nb * nb * len(pieces), 2 * LANES), BF),
    ]
    return call(
        functools.partial(back_kernel, len(pieces)), 2, (NCW + 1,), ins, outs, scratch, VMEM_ASK,
    )


def unit(rows):
    f = rows.astype(F32)
    inv = lax.rsqrt(jnp.mean(f * f, axis=1, keepdims=True) + EPSILON)
    return f * inv, inv


def norm_back(normal_grad, rows, gain):
    u, inv = unit(rows)
    g = normal_grad * gain[None, :]
    return inv * (g - u * jnp.mean(g * u, axis=1, keepdims=True))


def shards(
    tokens, norm_gain, in_weight, conv_weight, conv_bias, dt_bias, a_log, d_skip, inner_gain,
    out_weight, block_place, seq_length, cotangent,
):
    n_head, n_shard = lax.axis_size("head"), lax.axis_size("shard")
    half = n_head // 2
    head_at, shard_at = lax.axis_index("head"), lax.axis_index("shard")
    rows = tokens.shape[0]
    nb = rows // CH
    group_blocks = nb * n_head
    k_rows = in_weight.shape[0]
    stay = (head_at // half) == (shard_at & 1)

    piece_a = jnp.concatenate(
        [in_weight[:, DI:], norm_gain[:, None], jnp.zeros((k_rows, WA - XBC - NH - 1), BF)], axis=1
    )
    numbers = jnp.concatenate([block_place, seq_length], axis=1)
    numbers_got = trade(numbers, "shard", 1)
    me = jnp.int32(0) if k_rows % 32 else shard_at.astype(jnp.int32)
    def block_tails(v):
        return v.reshape(nb, CH, DM)[:, CH - HALO :].reshape(nb * HALO, DM)

    tok_got = move_home(tokens)
    tails = jnp.where(stay, block_tails(tokens), block_tails(tok_got))

    numbers = jnp.where(stay, numbers, numbers_got)[0]
    lengths = [numbers[group_blocks + k] for k in range(seq_length.shape[1])]

    def order_from(core_at):
        ids = []
        for core in (0, 1):
            for z in range(half):
                device = (head_at % half ^ z) + (core_at ^ core) * half
                ids += [device * nb + b for b in range(nb)]
        return jnp.stack(ids)

    ids, home_order = order_from(shard_at & 1), order_from(head_at // half)
    places = jnp.sum(
        jnp.where(ids[:, None] == jnp.arange(group_blocks)[None, :], numbers[None, :group_blocks], 0),
        axis=1,
    )
    first, in_seq, begin = jnp.zeros_like(places), jnp.zeros_like(places), 0
    for length in lengths:
        first = jnp.where(places >= begin, begin, first)
        in_seq = jnp.where(places >= begin, length, in_seq)
        begin = begin + (length + CH - 1) // CH
    info = jnp.concatenate(
        [
            jnp.stack([me, stay.astype(jnp.int32)]),
            jnp.stack([places, first, in_seq], axis=1).reshape(-1),
        ]
    ).astype(jnp.int32)

    far_a = gather_far(piece_a)
    conv_weight, conv_bias, dt_bias, a_log, d_skip, inner_gain, none = after_all(
        [conv_weight, conv_bias, dt_bias, a_log, d_skip, inner_gain, jnp.int32(0)], far_a[0]
    )
    table = spread_table(none)

    def head_row(v):
        return jnp.pad(v, (0, LANES - NH))[None]

    narrow = narrow_table(none)
    gain_row = inner_gain[None]
    at = shard_at.astype(jnp.int32).reshape(1)
    taps = jnp.pad(conv_weight, ((0, 0), (0, WA - XBC)))
    rate_row = head_row(a_log)
    skip_row = jnp.repeat(d_skip, HD)[None]
    taps, rate_row, skip_row, bias_row, step_row, gain_row, narrow, table = after_all(
        [
            taps, rate_row, skip_row, jnp.pad(conv_bias, (0, WA - XBC))[None], head_row(dt_bias),
            gain_row, narrow, table,
        ]
    )
    prepared = [taps, rate_row, skip_row, bias_row, step_row, gain_row, narrow, table]
    parts_a = gather_near(piece_a, far_a)
    if k_rows % 32:
        parts_a = [(join_pieces(parts_a).reshape(DM, WA), 0)]
    z_own, o_own = after_all([in_weight[:, :DI], out_weight], numbers_got)
    piece_zo = jnp.concatenate([z_own, o_own[:k_rows], o_own[k_rows:]], axis=1)
    far_zo = gather_far(piece_zo)
    tails = group_spread(after(tails, info, *[v for v, _ in parts_a[1:]], *prepared))
    cot_got = move_home(after(cotangent, *tails))
    a = run_project(info, parts_a, tails, tokens, tok_got, taps, bias_row, step_row, rate_row, table)
    wa, tok, normal = a["wa"], a["tok"], a["normal"]
    state_by_head = head_pieces(a["states"])
    state_by_core = trade(a["states"], "shard", 1)
    y_intra = run_intra(a)
    parts_zo = gather_near(after(piece_zo, y_intra), after_all(far_zo, y_intra))
    if k_rows % 32:
        zo = join_pieces(parts_zo)
        wz, wo = zo[:, :, :DI].reshape(DM, DI), zo[:, :, DI:]
        wo = wo.reshape(n_shard, k_rows, 2, DM).swapaxes(1, 2).reshape(DI, DM)
        cot = jnp.where(stay, cotangent, cot_got)
        z, q = dot(normal[:rows], wz).astype(BF), dot_nt(cot, wo).astype(BF)
    else:
        cot_got = after(cot_got, y_intra)
        z, q, cot, wz, wo = run_open(
            at, parts_zo, normal, cotangent, cot_got, stay.astype(jnp.int32).reshape(1)
        )
    state_by_head = [after(v, z) for v in state_by_head]
    all_states = (
        [a["states"]] + state_by_head + [state_by_core] + [trade(v, "shard", 1) for v in state_by_head]
    )
    enter, normed, gain_part, dz, dyr, dye, product, skip_part, d_enter = run_gate(
        info, a, all_states, y_intra, z, q, gain_row, skip_row, table
    )
    enter_by_head = head_pieces(d_enter)
    enter_by_core = trade(d_enter, "shard", 1)
    if k_rows % 32:
        z_term = dot_tn(normal[:rows], dz).astype(BF).reshape(n_shard, k_rows, DI)
        out_term = dot_tn(normed, cot).astype(BF).reshape(n_shard, 2, k_rows, DM)
        zo_keep, zo_give = core_give([z_term, out_term[:, 0], out_term[:, 1]])
        zo_give = [zo_give[p] for p in range(n_shard // 2)]
    else:
        zo_keep, zo_give = run_terms(at, a["normal_t"], dz, normed, cot, n_shard)
    zo_got = [trade(v, "shard", 1) for v in zo_give]
    dx_intra, db, dc, mixed = run_intra_back(a, after(dyr, *zo_give), dye, enter, normed, wo, tok)
    arrived = after_all(enter_by_head + zo_got, dx_intra)
    enter_by_head, zo_got = arrived[: len(enter_by_head)], arrived[len(enter_by_head) :]
    zo_pairs = chip_pairs(zo_keep, jnp.stack(zo_got))
    zo_far = chip_send(zo_pairs)
    enter_by_head = [after(v, *zo_pairs) for v in enter_by_head]
    all_enter = (
        [d_enter] + enter_by_head + [enter_by_core] + [trade(v, "shard", 1) for v in enter_by_head]
    )
    mixed_got = move_home(after(mixed, all_enter[-1]))
    d_a_all, small = run_back(
        info, a, all_enter, all_states, dx_intra, db, dc, enter, product, dyr, taps,
        rate_row, skip_row, table, narrow, gain_part, skip_part,
    )
    d_a_all = after(d_a_all, mixed_got)
    a_term = dot_tn(normal, d_a_all).astype(BF).reshape(n_shard, k_rows, WA)
    a_keep, a_give = core_give([a_term])
    a_got = trade(a_give, "shard", 1)

    small_got = trade(after(small, a_give), "shard", 1)
    zo_own = chip_sum(zo_pairs[0], after_all(zo_far, a_give))
    zo_keep, zo_give = head_split(zo_own)
    zo_got = trade(zo_give, "head", 1)
    d_a_all, dz, tok, tok_halo, wa = after_all(
        [d_a_all, dz, tok, a["tok_halo"], wa], a_give, zo_give
    )
    gain = wa[:, XBC + NH].astype(F32)
    from_a = dot_nt(d_a_all, wa)
    halo_part = norm_back(from_a[rows:], tok_halo, gain)
    halo_part = halo_part.reshape(nb, HALO, DM)[:, HALO - KC :].astype(BF).reshape(k_rows, -1)
    halos = [halo_part, trade(halo_part, "shard", 1)]
    normal_grad = dot_nt(dz, wz) + from_a[:rows]
    token_grad = (cot.astype(F32) + norm_back(normal_grad, tok, gain)).astype(BF)

    a_got, small_got, halos[1], zo_got = after_all([a_got, small_got, halos[1], zo_got], token_grad)
    if k_rows % 32:
        parts = split2((small + small_got).reshape(k_rows, -1))
        a_pairs = [jnp.concatenate([v, parts], axis=1) for v in chip_pairs(a_keep, a_got)]
    else:
        a_pairs = run_pair_small(at, a_keep, a_got, small, small_got)
    a_far = chip_send(a_pairs)
    token_got = move_home(after(token_grad, a_pairs[0]))
    zo_half = head_add(zo_keep, after(zo_got, a_pairs[0]))
    zo_got = trade(zo_half, "head", 2)
    *a_far, zo_got = after_all(a_far + [zo_got])
    a_own = chip_sum(a_pairs[0][:, :WA], [v[:, :WA] for v in a_far])
    sums = [join2(v[:, WA:]) for v in [a_pairs[0]] + a_far]
    while len(sums) > 1:
        sums = [sums[k] + sums[k + 1] for k in range(0, len(sums), 2)]
    small = sums[0]
    a_keep, a_give = head_split(a_own)
    cut, edge = a_keep.shape[1], a_keep.shape[1] + 2 * small.shape[1]
    total = a_keep.astype(F32)
    bits = [b for b in (1, 2, 4, 8, 16) if b < n_head]
    for bit in bits:
        if bit > 1:
            a_give = total.astype(BF)
            total = a_give.astype(F32)
        parts = split2(small)
        sent = jnp.concatenate([a_give, parts] + (halos if bit < half else []), axis=1)
        sent = trade(sent, "head", bit)
        if bit == 1:
            sent, token_got, zo_got = after_all([sent, token_got, zo_got])
            zo_half = head_add(zo_half, zo_got)
            for more in bits[2:]:
                zo_half = head_add(zo_half, trade(zo_half, "head", more))
            zo_other = trade(zo_half, "head", 1)
        elif bit == bits[-1]:
            sent, zo_other = after_all([sent, zo_other])
            zo_grad = head_join(zo_half, zo_other).astype(F32)
        if bit < half:
            halos = halos + jnp.split(sent[:, edge:], len(halos), axis=1)
        total = total + sent[:, :cut].astype(F32)
        small = join2(parts) + join2(sent[:, cut:edge])
    low = total.astype(BF)
    other = trade(low, "head", 1)
    halos = after(jnp.concatenate(halos, axis=1), low)
    halos = jnp.where(stay, halos, move_home(halos))
    halos = jnp.split(halos, group_blocks // nb, axis=1)
    other = after(other, *halos)
    a_grad = head_join(low, other).astype(F32)
    small = small.reshape(SUM_ROWS, LANES)

    all_halo = jnp.concatenate(halos[0::2] + halos[1::2]).reshape(group_blocks, KC, DM).astype(F32)
    own_numbers = jnp.concatenate([block_place, seq_length], axis=1)[0]
    own_places = jnp.sum(
        jnp.where(
            home_order[:, None] == jnp.arange(group_blocks), own_numbers[None, :group_blocks], 0
        ),
        axis=1,
    )
    home_ids = head_at * nb + jnp.arange(nb)
    home_places = jnp.sum(
        jnp.where(
            home_ids[:, None] == jnp.arange(group_blocks), own_numbers[None, :group_blocks], 0
        ),
        axis=1,
    )
    goes_on, begin = home_places < 0, 0
    for k in range(seq_length.shape[1]):
        end = begin + (own_numbers[group_blocks + k] + CH - 1) // CH
        goes_on = goes_on | ((home_places >= begin) & (home_places + 1 < end))
        begin = end
    is_next = (own_places[None, :] == home_places[:, None] + 1) & goes_on[:, None]
    halo_back = jnp.sum(jnp.where(is_next[:, :, None, None], all_halo[None], 0.0), axis=1)
    token_grad = jnp.where(stay, token_grad, token_got).reshape(nb, CH, DM)
    token_grad = token_grad.at[:, CH - KC :].set(
        (token_grad[:, CH - KC :].astype(F32) + halo_back).astype(BF)
    ).reshape(rows, DM)
    mixed = jnp.where(stay, mixed, after(mixed_got, a_own))

    in_grad = jnp.concatenate([zo_grad[:, :DI], a_grad[:, : XBC + NH]], axis=1)
    out_grad = jnp.concatenate([zo_grad[:, DI : DI + DM], zo_grad[:, DI + DM :]], axis=0)
    gain_grad = jnp.sum(in_grad * in_weight.astype(F32), axis=1) / norm_gain.astype(F32)

    return (
        mixed, token_grad, gain_grad, in_grad, small[: KC * XBC // LANES].reshape(KC, XBC),
        small[KC * XBC // LANES : SUM_GAIN].reshape(XBC), small[SUM_HEADS, :NH],
        small[SUM_HEADS + 1, :NH], jnp.sum(small[SUM_SKIP:SUM_HEADS].reshape(NH, HD), axis=1),
        small[SUM_GAIN:SUM_SKIP].reshape(DI), out_grad,
    )


def solution(mesh):
    return jax.shard_map(
        shards,
        mesh=mesh,
        in_specs=(
            P(("head", "shard"), None), P("shard"), P("shard", None), P(), P(), P(), P(), P(), P(),
            P("shard", None), P("shard", None), P("shard", None), P(("head", "shard"), None),
        ),
        out_specs=(
            P(("head", "shard"), None), P(("head", "shard"), None), P("shard"), P("shard", None),
            P(), P(), P(), P(), P(), P(), P("shard", None),
        ),
        check_vma=False,
    )
```

```python
import functools

import jax
import jax.numpy as jnp
from jax import lax
from jax.experimental import pallas as pl
from jax.experimental.pallas import tpu as pltpu
from jax.sharding import PartitionSpec as P

NH = 24
HD = 64
NS = 128
KC = 4
CH = 256
DI = 1536
DM = 768
XBC = DI + 2 * NS
WA = 1920
HALO = 8
EPSILON = 1e-05
F32 = jnp.float32
BF = jnp.bfloat16
LANES = 128
CW = 384
NCW = DI // CW
VMEM_ASK = 56 * 2**20
VMEM_ROOM = 56 * 2**20
VMEM_LESS = 44 * 2**20
COST_SCALE = 0.4


def trade(value, axis, bit):
    size = lax.axis_size(axis)
    return lax.ppermute(value, axis, [(i, i ^ bit) for i in range(size)])


def after(value, *others):
    return lax.optimization_barrier((value,) + others)[0]


def move_home(value):
    n_head, n_shard = lax.axis_size("head"), lax.axis_size("shard")
    half = n_head // 2
    pairs = []
    for h in range(n_head):
        for s in range(n_shard):
            upper, core = h // half, s & 1
            if upper != core:
                there = (h % half + core * half) * n_shard + (s - core + upper)
                pairs.append((h * n_shard + s, there))
    return lax.ppermute(value, ("head", "shard"), pairs)


def swap_home(value, stay):
    return jnp.where(stay, value, move_home(value))


def group_spread(value):
    n_head, n_shard = lax.axis_size("head"), lax.axis_size("shard")
    pieces = [value]
    for core in (0, 1):
        for low in range(n_head // 2):
            if core or low:
                pairs = [
                    (h * n_shard + s, (h ^ low) * n_shard + (s ^ core))
                    for h in range(n_head)
                    for s in range(n_shard)
                ]
                pieces.append(lax.ppermute(value, ("head", "shard"), pairs))
    return pieces


def group_gather(value):
    half = lax.axis_size("head") // 2
    pieces = [value]
    bit = 1
    while bit < half:
        pieces = pieces + [trade(v, "head", bit) for v in pieces]
        bit *= 2
    return pieces + [trade(v, "shard", 1) for v in pieces]


def gather_far(piece):
    bits = range(2, lax.axis_size("shard"), 2)
    return [trade(piece, "shard", bit) for bit in sorted(bits, reverse=True)]


def gather_near(piece, far):
    held = [piece] + far
    offsets = [0] + sorted(range(2, lax.axis_size("shard"), 2), reverse=True)
    near = [trade(v, "shard", 1) for v in held]
    return list(zip(held + near, offsets + [k ^ 1 for k in offsets]))


def join_pieces(parts):
    me, n_shard = lax.axis_index("shard"), lax.axis_size("shard")
    joined = jnp.zeros((n_shard,) + parts[0][0].shape, parts[0][0].dtype)
    for v, k in parts:
        joined = lax.dynamic_update_slice(joined, v[None], (me ^ k, 0, 0))
    return joined


def head_pieces(value):
    pieces = [value]
    bit = 1
    while bit < lax.axis_size("head") // 2:
        pieces = pieces + [trade(v, "head", bit) for v in pieces]
        bit *= 2
    return pieces[1:]


def core_give(blocks):
    n_shard = lax.axis_size("shard")
    core = lax.axis_index("shard") % 2

    def half(which):
        parts = []
        for v in blocks:
            split = v.reshape((n_shard // 2, 2) + v.shape[1:])
            parts.append(lax.dynamic_index_in_dim(split, which, 1, False))
        return jnp.concatenate(parts, axis=2) if len(parts) > 1 else parts[0]

    return half(core), half(1 - core)


def chip_pairs(keep, got):
    pair = (keep.astype(F32) + got.astype(F32)).astype(BF)
    chip = lax.axis_index("shard") // 2
    return [lax.dynamic_index_in_dim(pair, chip ^ k, 0, False) for k in range(pair.shape[0])]


def after_all(values, *others):
    return list(lax.optimization_barrier((*values, *others)))[: len(values)]


def chip_send(pairs):
    return [trade(v, "shard", 2 * k) for k, v in enumerate(pairs) if k]


def chip_sum(own, got):
    total = own.astype(F32)
    for v in got:
        total = total + v.astype(F32)
    return total.astype(BF)


def split2(v):
    high = lax.reduce_precision(v, 8, 7)
    return jnp.concatenate([high.astype(BF), (v - high).astype(BF)], axis=1)


def join2(parts):
    high, low = jnp.split(parts, 2, axis=1)
    return high.astype(F32) + low.astype(F32)


def head_split(value):
    cut = value.shape[1] // 2
    odd = lax.axis_index("head") % 2
    return [lax.dynamic_slice_in_dim(value, at * cut, cut, 1) for at in (odd, 1 - odd)]


def head_add(keep, got):
    return (keep.astype(F32) + got.astype(F32)).astype(BF)


def head_join(half, other):
    odd = lax.axis_index("head") % 2
    return jnp.concatenate([jnp.where(odd, other, half), jnp.where(odd, half, other)], axis=1)


def dot(a, b):
    return jnp.dot(a, b, preferred_element_type=F32)


def dot_nt(a, b):
    return lax.dot_general(a, b, (((1,), (1,)), ((), ())), preferred_element_type=F32)


def dot_tn(a, b):
    return lax.dot_general(a, b, (((0,), (0,)), ((), ())), preferred_element_type=F32)


def spread_table(none):
    row = jnp.arange(2 * LANES)[:, None] % LANES + none
    return (row == jnp.arange(DI)[None, :] // HD).astype(BF)


def narrow_table(none):
    return (jnp.arange(DI)[:, None] // HD == jnp.arange(LANES)[None, :] + none).astype(BF)


def pieces2(v):
    hi = v.astype(BF)
    return hi, (v - hi.astype(F32)).astype(BF)


def pieces3(v):
    hi = v.astype(BF)
    rest = v - hi.astype(F32)
    mid = rest.astype(BF)
    return hi, mid, (rest - mid.astype(F32)).astype(BF)


def softplus(v):
    return jnp.maximum(v, 0.0) + jnp.log1p(jnp.exp(-jnp.abs(v)))


sigmoid = jax.nn.sigmoid


def shape(dims, dtype):
    return jax.ShapeDtypeStruct(dims, dtype)


def whole(arr):
    return pl.BlockSpec(arr.shape, lambda *g: (0,) * len(arr.shape))


def columns(arr, at, width=None):
    dims = arr.shape[:-1] + (width or CW,)
    return pl.BlockSpec(dims, lambda *g: (0,) * (len(dims) - 1) + (at(*g),))


def in_hbm():
    return pl.BlockSpec(memory_space=pl.ANY)


def in_smem():
    return pl.BlockSpec(memory_space=pltpu.SMEM)


def call(kernel, micros, grid, ins, outs, scratch, room=VMEM_ROOM):
    return pl.pallas_call(
        kernel,
        grid=grid,
        out_shape=[o for o, _ in outs],
        in_specs=[s for _, s in ins],
        out_specs=[s for _, s in outs],
        scratch_shapes=scratch,
        compiler_params=pltpu.CompilerParams(vmem_limit_bytes=room),
        cost_estimate=pl.CostEstimate(
            flops=1, bytes_accessed=int(micros * COST_SCALE * 3.7e6), transcendentals=0
        ),
    )(*[a for a, _ in ins])


def iota(dims, axis):
    return lax.broadcasted_iota(jnp.int32, dims, axis)


def place_of(info, q):
    return info[2 + 3 * q]


def first_of(info, q):
    return info[3 + 3 * q]


def usable_of(info, i):
    begin = (place_of(info, i) - first_of(info, i)) * CH
    return (iota((CH, 1), 0) + begin < info[4 + 3 * i]).astype(F32)


def halo_used(info, i):
    has_prev = place_of(info, i) > first_of(info, i)
    return (iota((HALO, 1), 0) + jnp.where(has_prev, 0, -HALO) > HALO - KC).astype(F32)


def clast_rows(refs, nb):
    rows = []
    for ref in refs:
        for b in range(nb):
            part = ref[b].astype(F32)
            rows.append(part[0:1, :] + part[1:2, :] + part[2:3, :])
    return rows


def carry_weights(info, ends, nb, into):
    n_all = len(ends)
    row = iota((n_all, 1), 0)
    place = jnp.zeros((n_all, 1), jnp.int32)
    first = jnp.zeros((n_all, 1), jnp.int32)
    for j in range(n_all):
        place = jnp.where(row == j, place_of(info, j), place)
        first = jnp.where(row == j, first_of(info, j), first)
    parts = []
    for i in range(nb):
        own = place_of(info, i)
        total = jnp.zeros((n_all, LANES), F32)
        for k in range(n_all):
            at = place_of(info, k)
            if into:
                between = (place > at) & (at > own)
            else:
                between = (place < at) & (at < own)
            total = total + jnp.where(between, ends[k], 0.0)
        if into:
            reach = (first <= own) & (place > own)
        else:
            reach = (place >= first_of(info, i)) & (place < own)
        parts.append(jnp.where(reach, jnp.exp(total), 0.0))
    return jnp.concatenate(pieces2(jnp.concatenate(parts, axis=0)), axis=1)


def normal_rows(rows, gain):
    f = rows.astype(F32)
    inv = lax.rsqrt(jnp.sum(f * f, axis=1, keepdims=True) / DM + EPSILON)
    return (f * inv * gain).astype(BF)


def project_kernel(layout, n_halo, *refs):
    info = refs[0]
    pieces = refs[1 : 1 + len(layout)]
    halos = refs[1 + len(layout) : 1 + len(layout) + n_halo]
    (
        tok_own, tok_got, conv_w, conv_b, dt_bias, a_log, table,
        wa_out, tok_out, tok_halo, normal_out, normal_t_out, xbc, slope, xs, xt, bs_out, cs_out,
        raw_out, cum_out, cum_t_out, states,
        wa, ext, small, sems, out_sems, tok, normal, normal_t, bs, cs, raw, cum, cum_t,
    ) = refs[1 + len(layout) + n_halo :]
    step = pl.program_id(0)
    rows = tok_own.shape[0]
    nb = rows // CH
    me = info[0]

    def project(at, width):
        proj = dot(normal[...], wa[:, pl.ds(at, width)]).astype(BF).astype(F32)
        acts, heads = [], []
        for i in range(nb):
            head = proj[rows + i * HALO : rows + (i + 1) * HALO, :] * halo_used(info, i)
            body = proj[i * CH : (i + 1) * CH, :] * usable_of(info, i)
            heads.append(head)
            ext[i, :HALO, :width] = head
            ext[i, HALO:, :width] = body
            xbc[i * CH : (i + 1) * CH, :width] = body.astype(BF)
            pre = conv_b[:, pl.ds(at, width)]
            for lag in range(KC):
                tap = conv_w[KC - 1 - lag : KC - lag, pl.ds(at, width)]
                pre = pre + tap * ext[i, HALO - lag : HALO - lag + CH, :width]
            sg = sigmoid(pre)
            act = pre * sg
            slope[i * CH : (i + 1) * CH, :width] = (sg + act * (1.0 - sg)).astype(BF)
            acts.append(act)
        xbc[rows:, :width] = jnp.concatenate(heads, axis=0).astype(BF)
        return acts

    def leaving():
        moves = [(wa, wa_out), (tok, tok_out), (normal, normal_out), (normal_t, normal_t_out)]
        moves += [(bs, bs_out), (cs, cs_out), (raw, raw_out), (cum, cum_out), (cum_t, cum_t_out)]
        return [pltpu.make_async_copy(v, there, out_sems.at[n]) for n, (v, there) in enumerate(moves)]

    @pl.when(step == 0)
    def _():
        def copy_of(n):
            at = pl.multiple_of((me ^ layout[n]) * pieces[n].shape[0], 16)
            return pltpu.make_async_copy(
                pieces[n], wa.at[pl.ds(at, pieces[n].shape[0]), :], sems.at[n]
            )

        for n in range(len(layout)):
            copy_of(n).start()
        stay = info[1] > 0
        tok[...] = jnp.where(stay, tok_own[...], tok_got[...])
        found = []
        for i in range(nb):
            own, has_prev = place_of(info, i), place_of(info, i) > first_of(info, i)
            total = jnp.zeros((HALO, DM), F32)
            for o in range(n_halo):
                part = halos[o][...].astype(F32)
                for b in range(nb):
                    hit = (place_of(info, o * nb + b) == own - 1) & has_prev
                    total = total + jnp.where(hit, part[b * HALO : (b + 1) * HALO, :], 0.0)
            found.append(total)
        tok_halo[...] = jnp.concatenate(found, axis=0).astype(BF)
        for n in range(len(layout)):
            copy_of(n).wait()
        for copy in leaving()[:2]:
            copy.start()
        gain = wa[:, XBC : XBC + LANES].astype(F32).T[NH : NH + 1, :]
        normal[:rows, :] = normal_rows(tok[...], gain)
        normal_t[...] = normal[:rows, :].T
        normal[rows:, :] = normal_rows(tok_halo[...], gain)
        for i, act in enumerate(project(DI, 2 * NS)):
            bs[i * CH : (i + 1) * CH, :] = act[:, :NS].astype(BF)
            cs[i * CH : (i + 1) * CH, :] = act[:, NS:].astype(BF)
        xbc[:, 2 * NS :] = jnp.zeros((xbc.shape[0], CW - 2 * NS), BF)
        slope[:, 2 * NS :] = jnp.zeros((rows, CW - 2 * NS), BF)
        first = dot(normal[:rows, :], wa[:, XBC : XBC + LANES]).astype(BF).astype(F32) + dt_bias[...]
        raw[...] = first
        dt_all = softplus(first)
        rate = jnp.exp(a_log[...])
        causal = (iota((CH, CH), 0) >= iota((CH, CH), 1)).astype(F32).astype(BF)
        states[:, :, DI:] = jnp.zeros((nb, NS, LANES), BF)
        for i in range(nb):
            dt = dt_all[i * CH : (i + 1) * CH, :]
            parts = dot(causal, jnp.concatenate(pieces3(-dt * rate), axis=1))
            run = parts[:, :LANES] + parts[:, LANES : 2 * LANES] + parts[:, 2 * LANES :]
            cum[i * CH : (i + 1) * CH, :] = run
            cum_t[:, i * CH : (i + 1) * CH] = run.T
            last = run[CH - 1 : CH, :]
            ends = jnp.concatenate(pieces3(last) + (jnp.zeros((13, LANES), BF),), axis=0)
            states[i, :16, DI:] = ends
            small[i, 0] = jnp.concatenate(pieces2(dt), axis=1)
            small[i, 1] = jnp.concatenate(pieces2(jnp.exp(last - run) * dt), axis=1)
        for copy in leaving()[2:]:
            copy.start()

    @pl.when(step > 0)
    def _():
        at = pl.multiple_of((step - 1) * CW, CW)
        for i, act in enumerate(project(at, CW)):
            r = slice(i * CH, (i + 1) * CH)
            xs[r, :] = act.astype(BF)
            xt[r, :] = (act * dot(small[i, 0], table[...])).astype(BF)
            weighted = (act * dot(small[i, 1], table[...])).astype(BF)
            states[i, :, pl.ds(at, CW)] = dot_tn(bs[r, :], weighted).astype(BF)

    @pl.when(step == NCW)
    def _():
        for copy in leaving():
            copy.wait()


def run_project(info, parts, halos, tok_own, tok_got, conv_w, conv_b, dt_bias, a_log, table):
    rows = tok_own.shape[0]
    nb = rows // CH
    ext_rows = rows + nb * HALO
    layout = [offset for _, offset in parts]

    def before(s):
        return jnp.maximum(s - 1, 0)

    def tail_first(s):
        return jnp.where(s == 0, NCW, s - 1)

    ins = [(info, in_smem())] + [(v, in_hbm()) for v, _ in parts]
    ins += [(v, whole(v)) for v in halos]
    ins += [(v, whole(v)) for v in (tok_own, tok_got, conv_w, conv_b, dt_bias, a_log)]
    ins += [(table, columns(table, before))]
    outs = {
        "wa": (shape((DM, WA), BF), in_hbm()),
        "tok": (shape((rows, DM), BF), in_hbm()),
        "tok_halo": (shape((nb * HALO, DM), BF), whole),
        "normal": (shape((ext_rows, DM), BF), in_hbm()),
        "normal_t": (shape((DM, rows), BF), in_hbm()),
        "xbc": (shape((ext_rows, WA), BF), lambda v: columns(v, tail_first)),
        "slope": (shape((rows, WA), BF), lambda v: columns(v, tail_first)),
        "xs": (shape((rows, DI), BF), lambda v: columns(v, before)),
        "xt": (shape((rows, DI), BF), lambda v: columns(v, before)),
        "bs": (shape((rows, NS), BF), in_hbm()),
        "cs": (shape((rows, NS), BF), in_hbm()),
        "raw": (shape((rows, LANES), F32), in_hbm()),
        "cum": (shape((rows, LANES), F32), in_hbm()),
        "cum_t": (shape((LANES, rows), F32), in_hbm()),
        "states": (shape((nb, NS, DI + LANES), BF), whole),
    }
    out_list = [(o, s(o) if callable(s) else s) for o, s in outs.values()]
    scratch = [
        pltpu.VMEM((DM, WA), BF), pltpu.VMEM((nb, HALO + CH, CW), F32),
        pltpu.VMEM((nb, 2, CH, 2 * LANES), BF), pltpu.SemaphoreType.DMA((len(parts),)),
        pltpu.SemaphoreType.DMA((9,)),
    ]
    kept = ("tok", "normal", "normal_t", "bs", "cs", "raw", "cum", "cum_t")
    scratch += [pltpu.VMEM(outs[k][0].shape, outs[k][0].dtype) for k in kept]
    got = call(
        functools.partial(project_kernel, layout, len(halos)), 14, (NCW + 1,), ins, out_list, scratch, VMEM_ASK,
    )
    return dict(zip(outs, got))


SUM_GAIN = (KC + 1) * XBC // LANES
SUM_SKIP = SUM_GAIN + DI // LANES
SUM_HEADS = SUM_SKIP + DI // LANES
SUM_ROWS = SUM_HEADS + 2
OUT_ROWS = CW // 4
PER = CW // HD
HALF = CH // 2


def chunk_heads(cum, first):
    return pltpu.roll(cum, lax.rem(LANES - first, LANES), axis=1)


def intra_kernel(bs, cs, xt, cum, cum_t, out, scores):
    c = pl.program_id(0)
    nb = bs.shape[0] // CH
    low = iota((CH, LANES), 1) < HD
    keep = iota((HALF, HALF), 0) >= iota((HALF, HALF), 1)

    @pl.when(c == 0)
    def _():
        for i in range(nb):
            r = slice(i * CH, (i + 1) * CH)
            scores[i] = dot_nt(cs[r, :], bs[r, :])

    for i in range(nb):
        r = slice(i * CH, (i + 1) * CH)
        cols = chunk_heads(cum[r, :], c * PER)
        for p in range(PER // 2):
            lanes = slice(p * LANES, (p + 1) * LANES)
            both = xt[r, lanes]
            got = []
            for k in range(2):
                h = 2 * p + k
                col = cols[:, h : h + 1]
                row = cum_t[pl.ds(c * PER + h, 1), r]
                a, b = col[:HALF], col[HALF:]
                s, t = row[:, :HALF], row[:, HALF:]
                upper = jnp.where(keep, jnp.exp(a - s), 0.0) * scores[i, :HALF, :HALF]
                left = jnp.exp(b - s) * scores[i, HALF:, :HALF]
                right = jnp.where(keep, jnp.exp(b - t), 0.0) * scores[i, HALF:, HALF:]
                lower = jnp.concatenate([left.astype(BF), right.astype(BF)], axis=1)
                got.append(
                    jnp.concatenate([dot(upper.astype(BF), both[:HALF, :]), dot(lower, both)], axis=0)
                )
            out[r, lanes] = jnp.where(low, got[0], got[1])


def run_intra(a):
    rows = a["bs"].shape[0]
    nb = rows // CH
    ins = [(a[k], whole(a[k])) for k in ("bs", "cs")]
    ins += [(a["xt"], columns(a["xt"], lambda c: c))]
    ins += [(a[k], whole(a[k])) for k in ("cum", "cum_t")]
    out = shape((rows, DI), F32)
    return call(
        intra_kernel, 6, (NCW,), ins, [(out, columns(out, lambda c: c))],
        [pltpu.VMEM((nb, CH, CH), F32)],
    )[0]


OW = 768
ONW = DI // OW


def open_kernel(layout, at, *refs):
    pieces = refs[: len(layout)]
    normal, cot_own, cot_got, stay, z, q, cot, wz_out, wo_out, wz, wo, sems, out_sems = refs[
        len(layout) :
    ]
    c = pl.program_id(0)
    k_rows = pieces[0].shape[0]

    def copies(n):
        shard = at[0] ^ layout[n]
        parts = [(wz, shard * k_rows, slice(0, DI))]
        for j in range(2):
            lanes = slice(DI + j * DM, DI + (j + 1) * DM)
            parts.append((wo, (2 * shard + j) * k_rows, lanes))
        return [
            pltpu.make_async_copy(
                pieces[n].at[:, lanes],
                ref.at[pl.ds(pl.multiple_of(begin, 16), k_rows), :],
                sems.at[3 * n + k],
            )
            for k, (ref, begin, lanes) in enumerate(parts)
        ]

    def leaving():
        return [
            pltpu.make_async_copy(wz, wz_out, out_sems.at[0]),
            pltpu.make_async_copy(wo, wo_out, out_sems.at[1]),
        ]

    @pl.when(c == 0)
    def _():
        for n in range(len(layout)):
            for copy in copies(n):
                copy.start()
        cot[...] = jnp.where(stay[0] > 0, cot_own[...], cot_got[...])
        for n in range(len(layout)):
            for copy in copies(n):
                copy.wait()
        for copy in leaving():
            copy.start()

    here = pl.ds(pl.multiple_of(c * OW, OW), OW)
    z[...] = dot(normal[...], wz[:, here]).astype(BF)
    q[...] = dot_nt(cot[...], wo[here, :]).astype(BF)

    @pl.when(c == ONW - 1)
    def _():
        for copy in leaving():
            copy.wait()


def run_open(at, parts, normal, cot_own, cot_got, stay):
    rows = cot_own.shape[0]
    layout = [offset for _, offset in parts]
    ins = [(at, in_smem())] + [(v, in_hbm()) for v, _ in parts]
    ins += [(normal, pl.BlockSpec((rows, DM), lambda c: (0, 0)))]
    ins += [(cot_own, whole(cot_own)), (cot_got, whole(cot_got)), (stay, in_smem())]
    wide = shape((rows, DI), BF)
    outs = [(wide, columns(wide, lambda c: c, OW))] * 2
    outs += [(v, whole(v)) for v in (shape((rows, DM), BF),)]
    outs += [(v, in_hbm()) for v in (shape((DM, DI), BF), shape((DI, DM), BF))]
    return call(
        functools.partial(open_kernel, layout), 1, (ONW,), ins, outs,
        [
            pltpu.VMEM((DM, DI), BF), pltpu.VMEM((DI, DM), BF),
            pltpu.SemaphoreType.DMA((3 * len(parts),)), pltpu.SemaphoreType.DMA((2,)),
        ],
        VMEM_LESS,
    )


def terms_kernel(at, normal_t, dz, normed, cot, keep, *refs):
    *give, z_part, o_part = refs
    p = pl.program_id(0)
    unit = give[0].shape[0]
    even = at[0] % 2 == 0
    z_part[...] = dot(normal_t[...], dz[...])
    o_part[...] = dot_tn(normed[...], cot[...])

    def rows_of(which):
        parts = [(z_part[which * unit : (which + 1) * unit, :], slice(0, DI))]
        for j in range(2):
            rows = o_part[(2 * which + j) * unit : (2 * which + j + 1) * unit, :]
            parts.append((rows, slice(DI + j * DM, DI + (j + 1) * DM)))
        return parts

    for (first, lanes), (second, _) in zip(rows_of(0), rows_of(1)):
        keep[0, :, lanes] = jnp.where(even, first, second).astype(BF)
        other = jnp.where(even, second, first).astype(BF)
        for k, ref in enumerate(give):

            @pl.when(p == k)
            def _(ref=ref, other=other, lanes=lanes):
                ref[:, lanes] = other


def run_terms(at, normal_t, dz, normed, cot, n_shard):
    rows = dz.shape[0]
    n, unit = n_shard // 2, DM // n_shard
    give = shape((unit, DI + 2 * DM), BF)
    keep = shape((n,) + give.shape, BF)
    got = call(
        terms_kernel, 1, (n,),
        [
            (at, in_smem()), (normal_t, pl.BlockSpec((2 * unit, rows), lambda p: (p, 0))),
            (dz, whole(dz)), (normed, columns(normed, lambda p: p, 4 * unit)), (cot, whole(cot)),
        ],
        [(keep, pl.BlockSpec((1,) + give.shape, lambda p: (p, 0, 0)))] + [(give, whole(give))] * n,
        [pltpu.VMEM((2 * unit, DI), F32), pltpu.VMEM((4 * unit, DM), F32)],
    )
    return got[0], list(got[1:])


def pair_small_kernel(at, term, got, small, small_got, *outs):
    cols = got.shape[-1]
    chip, core = at[0] // 2, at[0] % 2
    total = small[...] + small_got[...]
    parts = jnp.concatenate(pieces2(total), axis=1)
    for k, out in enumerate(outs):
        kept = term[2 * (chip ^ k) + core]
        out[:, :cols] = (kept.astype(F32) + got[chip ^ k].astype(F32)).astype(BF)
        out[:, cols:] = parts


def run_pair_small(at, term, got, small, small_got):
    n, rows, cols = got.shape
    out = shape((rows, cols + 2 * small.shape[1]), BF)
    args = [term, got, small, small_got]
    return call(
        pair_small_kernel, 1, (1,), [(at, in_smem())] + [(v, whole(v)) for v in args],
        [(out, whole(out))] * n, [],
    )


GW = 768
GNW = DI // GW


def columns_g(arr, at):
    return columns(arr, at, GW)


def gate_kernel(n_pieces, *refs):
    info = refs[0]
    pieces = refs[1 : 1 + n_pieces]
    ends = refs[1 + n_pieces : 1 + 2 * n_pieces]
    (
        y_intra, cs, cum, xs, z, q, inner_gain, d_skip, table,
        enter, normed, gain_part, dz, dyr, dye, product, skip_part, d_enter,
        y_scan, small, weights, squares, dots,
    ) = refs[1 + 2 * n_pieces :]
    phase, c = pl.program_id(0), pl.program_id(1)
    rows = cs.shape[0]
    nb = rows // CH
    n_all = n_pieces * nb
    here = pl.ds(pl.multiple_of(c * GW, GW), GW)

    @pl.when((phase == 0) & (c == 0))
    def _():
        weights[...] = carry_weights(info, clast_rows(ends, nb), nb, False)
        squares[...] = jnp.zeros_like(squares)
        dots[...] = jnp.zeros_like(dots)
        for i in range(nb):
            r = slice(i * CH, (i + 1) * CH)
            small[r, :] = jnp.concatenate(pieces2(jnp.exp(cum[r, :])), axis=1)

    @pl.when(phase == 0)
    def _():
        wide_w = dot(weights[...], table[...])
        totals = [jnp.zeros((NS, GW), F32) for _ in range(nb)]
        for j in range(n_all):
            piece = pieces[j // nb][j % nb].astype(F32)
            for i in range(nb):
                totals[i] = totals[i] + wide_w[i * n_all + j : i * n_all + j + 1, :] * piece
        for i in range(nb):
            r = slice(i * CH, (i + 1) * CH)
            low = totals[i].astype(BF)
            enter[i] = low
            scan = y_intra[r, :] + dot(small[r, :], table[...]) * dot(cs[r, :], low)
            y_scan[r, here] = scan
            y = scan + d_skip[...] * xs[r, :].astype(F32)
            zf = z[r, :].astype(F32)
            gated = y * (zf * sigmoid(zf))
            qg = q[r, :].astype(F32) * inner_gain[...] * usable_of(info, i)
            squares[r, :] += jnp.sum(gated * gated, axis=1, keepdims=True)
            dots[r, :] += jnp.sum(qg * gated, axis=1, keepdims=True)

    @pl.when(phase == 1)
    def _():
        gain_sum = jnp.zeros((1, GW), F32)
        skip_sum = jnp.zeros((1, GW), F32)
        for i in range(nb):
            r = slice(i * CH, (i + 1) * CH)
            inv = lax.rsqrt(squares[r, :] / DI + EPSILON)
            slope = inv * inv * inv * dots[r, :] / DI
            use = usable_of(info, i)
            scan = y_scan[r, here]
            x = xs[r, :].astype(F32)
            y = scan + d_skip[...] * x
            zf = z[r, :].astype(F32)
            sg = sigmoid(zf)
            sz = zf * sg
            gated = y * sz
            qf = q[r, :].astype(F32) * use
            scaled = gated * inv
            normed[r, :] = (scaled * inner_gain[...] * use).astype(BF)
            gain_sum = gain_sum + jnp.sum(qf * scaled, axis=0, keepdims=True)
            gg = inv * qf * inner_gain[...] - gated * slope
            dz[r, :] = (gg * y * (sg + sz * (1.0 - sg))).astype(BF)
            dy = gg * sz
            low = dy.astype(BF)
            dyr[r, :] = low
            product[r, :] = low.astype(F32) * scan
            skip_sum = skip_sum + jnp.sum(dy * x, axis=0, keepdims=True)
            back = (dot(small[r, :], table[...]) * dy).astype(BF)
            dye[r, :] = back
            d_enter[i] = dot_tn(cs[r, :], back).astype(BF)
        gain_part[...] = gain_sum
        skip_part[...] = skip_sum


def run_gate(info, a, pieces, y_intra, z, q, inner_gain, d_skip, table):
    rows = z.shape[0]
    nb = rows // CH

    def early(p, c):
        return jnp.where(p == 0, c, GNW - 1)

    def both(p, c):
        return c

    def late(p, c):
        return jnp.where(p == 0, 0, c)

    ins = [(info, in_smem())]
    ins += [(v, columns_g(v, early)) for v in pieces]
    ins += [(v, pl.BlockSpec((nb, 16, LANES), lambda p, c: (0, 0, DI // LANES))) for v in pieces]
    ins += [(y_intra, columns_g(y_intra, early))]
    ins += [(a[k], whole(a[k])) for k in ("cs", "cum")]
    ins += [(v, columns_g(v, both)) for v in (a["xs"], z, q, inner_gain, d_skip, table)]
    wide = shape((rows, DI), BF)
    wide_f = shape((rows, DI), F32)
    row = shape((1, DI), F32)
    state = shape((nb, NS, DI), BF)
    outs = [(state, columns_g(state, early))]
    outs += [(v, columns_g(v, late)) for v in (wide, row, wide, wide, wide, wide_f, row, state)]
    scratch = [
        pltpu.VMEM((rows, DI), F32), pltpu.VMEM((rows, 2 * LANES), BF),
        pltpu.VMEM((nb * nb * len(pieces), 2 * LANES), BF), pltpu.VMEM((rows, 1), F32),
        pltpu.VMEM((rows, 1), F32),
    ]
    return call(
        functools.partial(gate_kernel, len(pieces)), 16, (2, GNW), ins, outs, scratch, VMEM_ASK,
    )


def intra_back_kernel(
    bs, cs, xt, cum, cum_t, dyr, dye, enter, normed, wo, tok, dxt, db, dc, mixed, scores, top, bottom,
    total,
):
    c = pl.program_id(0)
    nb = bs.shape[0] // CH
    low = iota((CH, LANES), 1) < HD
    keep = iota((HALF, HALF), 1) >= iota((HALF, HALF), 0)

    @pl.when(c == 0)
    def _():
        for i in range(nb):
            r = slice(i * CH, (i + 1) * CH)
            scores[i] = dot_nt(bs[r, :], cs[r, :])
        top[...] = jnp.zeros_like(top)
        bottom[...] = jnp.zeros_like(bottom)
        dc[...] = jnp.zeros_like(dc)
        total[...] = tok[...].astype(F32)

    total[...] += dot(normed[...], wo[...])

    for i in range(nb):
        r = slice(i * CH, (i + 1) * CH)
        cols = chunk_heads(cum[r, :], c * PER)
        dc[r, :] += dot_nt(dye[r, :], enter[i])
        top_sum, bottom_sum = top[i], bottom[i]
        for p in range(PER // 2):
            lanes = slice(p * LANES, (p + 1) * LANES)
            x, dy = xt[r, lanes], dyr[r, lanes]
            got = []
            for k in range(2):
                h = 2 * p + k
                col = cols[:, h : h + 1]
                row = cum_t[pl.ds(c * PER + h, 1), r]
                a, b = col[:HALF], col[HALF:]
                s, t = row[:, :HALF], row[:, HALF:]
                left = jnp.where(keep, jnp.exp(s - a), 0.0)
                right = jnp.exp(t - a)
                last = jnp.where(keep, jnp.exp(t - b), 0.0)
                dec = jnp.concatenate([left, right], axis=1)
                got.append(
                    jnp.concatenate(
                        [
                            dot((dec * scores[i, :HALF, :]).astype(BF), dy),
                            dot((last * scores[i, HALF:, HALF:]).astype(BF), dy[HALF:, :]),
                        ],
                        axis=0,
                    )
                )
                own = jnp.where(low, x, 0) if k == 0 else jnp.where(low, 0, x)
                top_sum = top_sum + dot_nt(own[:HALF, :], dy) * dec
                bottom_sum = bottom_sum + dot_nt(own[HALF:, :], dy[HALF:, :]) * last
            dxt[r, lanes] = jnp.where(low, got[0], got[1])
        top[i], bottom[i] = top_sum, bottom_sum

    @pl.when(c == NCW - 1)
    def _():
        for i in range(nb):
            r = slice(i * CH, (i + 1) * CH)
            up, down = top[i].astype(BF), bottom[i].astype(BF)
            down = jnp.concatenate([jnp.zeros((HALF, HALF), BF), down], axis=1)
            both = jnp.concatenate([up, down], axis=0)
            db[r, :] = dot(both, cs[r, :])
            dc[r, :] += dot_tn(both, bs[r, :])
        mixed[...] = total[...].astype(BF)


def run_intra_back(a, dyr, dye, enter, normed, wo, tok):
    rows = dyr.shape[0]
    nb = rows // CH

    def same(c):
        return c

    ins = [(a[k], whole(a[k])) for k in ("bs", "cs")]
    ins += [(a["xt"], columns(a["xt"], same))]
    ins += [(a[k], whole(a[k])) for k in ("cum", "cum_t")]
    ins += [(v, columns(v, same)) for v in (dyr, dye, enter, normed)]
    ins += [(wo, pl.BlockSpec((CW, DM), lambda c: (c, 0))), (tok, whole(tok))]
    full, small, mixed = shape((rows, DI), F32), shape((rows, NS), F32), shape((rows, DM), BF)
    return call(
        intra_back_kernel, 1, (NCW,), ins,
        [(full, columns(full, same))] + [(v, whole(v)) for v in (small, small, mixed)],
        [
            pltpu.VMEM((nb, CH, CH), F32), pltpu.VMEM((nb, HALF, CH), F32),
            pltpu.VMEM((nb, HALF, HALF), F32), pltpu.VMEM((rows, DM), F32),
        ],
    )


def back_kernel(n_pieces, *refs):
    info = refs[0]
    pieces = refs[1 : 1 + n_pieces]
    ends = refs[1 + n_pieces : 1 + 2 * n_pieces]
    (
        dx_intra, db_in, dc_in, xbc, slope, xs, xt, bs, raw, cum, enter, product, dyr, conv_w,
        a_log, d_skip, table, narrow, gain_part, skip_part,
        d_a, sums,
        grad, small, d_bs, heads, weights,
    ) = refs[1 + 2 * n_pieces :]
    step = pl.program_id(0)
    rows = xs.shape[0]
    nb = rows // CH
    n_all = n_pieces * nb

    @pl.when(step == 0)
    def _():
        weights[...] = carry_weights(info, clast_rows(ends, nb), nb, True)
        dt_all = softplus(raw[...])
        for i in range(nb):
            r = slice(i * CH, (i + 1) * CH)
            last = cum[(i + 1) * CH - 1 : (i + 1) * CH, :]
            small[i, 0] = jnp.concatenate(pieces2(dt_all[r, :]), axis=1)
            small[i, 1] = jnp.concatenate(pieces2(jnp.exp(last - cum[r, :])), axis=1)
            grad[i, :HALO, :] = jnp.zeros((HALO, CW), F32)
            grad[i, HALO + CH :, :] = jnp.zeros((HALO, CW), F32)
        d_bs[...] = db_in[...]
        heads[...] = jnp.zeros_like(heads)

    def put_rows(at, row):
        for j in range(row.shape[1] // LANES):
            sums[pl.ds(at + j, 1), :] = row[:, j * LANES : (j + 1) * LANES]

    def convolve_back(dacts, width):
        offset_sum = jnp.zeros((1, width), F32)
        tap_sums = [jnp.zeros((1, width), F32) for _ in range(KC)]
        all_heads = xbc[rows:, :width].astype(F32)
        head_grads = []
        for i in range(nb):
            r = slice(i * CH, (i + 1) * CH)
            dpre = dacts[i] * slope[r, :width].astype(F32)
            offset_sum = offset_sum + jnp.sum(dpre, axis=0, keepdims=True)
            grad[i, HALO : HALO + CH, :width] = dpre
            body = xbc[r, :width].astype(F32)
            head = all_heads[i * HALO : (i + 1) * HALO, :]
            total = jnp.zeros((CH, width), F32)
            total_head = jnp.zeros((HALO, width), F32)
            for lag in range(KC):
                tap = conv_w[KC - 1 - lag : KC - lag, :width]
                later = grad[i, HALO + lag : HALO + lag + CH, :width]
                later_head = grad[i, lag : lag + HALO, :width]
                total = total + tap * later
                total_head = total_head + tap * later_head
                tap_sums[KC - 1 - lag] = (
                    tap_sums[KC - 1 - lag]
                    + jnp.sum(later * body, axis=0, keepdims=True)
                    + jnp.sum(later_head * head, axis=0, keepdims=True)
                )
            d_a[r, :width] = (total * usable_of(info, i)).astype(BF)
            head_grads.append(total_head * halo_used(info, i))
        d_a[rows:, :width] = jnp.concatenate(head_grads, axis=0).astype(BF)
        for k, row in enumerate(tap_sums + [offset_sum]):
            put_rows(k * (XBC // LANES) + step * (CW // LANES), row)

    @pl.when(step < NCW)
    def _():
        wide_w = dot(weights[...], table[...])
        totals = [jnp.zeros((NS, CW), F32) for _ in range(nb)]
        for j in range(n_all):
            piece = pieces[j // nb][j % nb].astype(F32)
            for i in range(nb):
                totals[i] = totals[i] + wide_w[i * n_all + j : i * n_all + j + 1, :] * piece
        select = narrow[...]
        dacts = []
        for i in range(nb):
            r = slice(i * CH, (i + 1) * CH)
            low = totals[i].astype(BF)
            fade = jnp.sum(low.astype(F32) * enter[i].astype(F32), axis=0, keepdims=True)
            end_w = dot(small[i, 1], table[...])
            x_dt = xt[r, :].astype(F32)
            inter = end_w * dot(bs[r, :], low)
            d_bs[r, :] += dot_nt((x_dt * end_w).astype(BF), low)
            dxt = dx_intra[r, :] + inter
            flow = jnp.sum(x_dt * inter, axis=0, keepdims=True)
            hi, mid, lo = pieces3(product[r, :] - x_dt * dxt)
            heads[0, r, :] += dot(hi, select) + dot(mid, select) + dot(lo, select)
            heads[1, r, :] += dot((xs[r, :].astype(F32) * dxt).astype(BF), select)
            hi, mid, lo = pieces3(jnp.concatenate([flow, fade, jnp.zeros((6, CW), F32)], axis=0))
            heads[2, i * 8 : (i + 1) * 8, :] += dot(hi, select) + dot(mid, select) + dot(lo, select)
            dacts.append(
                dot(small[i, 0], table[...]) * dxt + d_skip[...] * dyr[r, :].astype(F32)
            )
        convolve_back(dacts, CW)
        put_rows(SUM_GAIN + step * (CW // LANES), gain_part[...])
        put_rows(SUM_SKIP + step * (CW // LANES), skip_part[...])

    @pl.when(step == NCW)
    def _():
        dacts = []
        for i in range(nb):
            r = slice(i * CH, (i + 1) * CH)
            dacts.append(jnp.concatenate([d_bs[r, :], dc_in[r, :]], axis=1))
        convolve_back(dacts, 2 * NS)
        rate = jnp.exp(a_log[...])
        anti = (iota((CH, CH), 0) <= iota((CH, CH), 1)).astype(F32).astype(BF)
        bias_sum = jnp.zeros((1, LANES), F32)
        rate_sum = jnp.zeros((1, LANES), F32)
        for i in range(nb):
            r = slice(i * CH, (i + 1) * CH)
            last = cum[(i + 1) * CH - 1 : (i + 1) * CH, :]
            flow, fade = heads[2, i * 8 : i * 8 + 1, :], heads[2, i * 8 + 1 : i * 8 + 2, :]
            parts = dot(anti, jnp.concatenate(pieces3(heads[0, r, :]), axis=1))
            d_log = parts[:, :LANES] + parts[:, LANES : 2 * LANES] + parts[:, 2 * LANES :]
            d_log = d_log + (flow + jnp.exp(last) * fade)
            start = raw[r, :]
            d_raw = (heads[1, r, :] - d_log * rate) * sigmoid(start)
            d_raw = jnp.where(iota((CH, LANES), 1) < NH, d_raw, 0.0)
            bias_sum = bias_sum + jnp.sum(d_raw, axis=0, keepdims=True)
            rate_sum = rate_sum - jnp.sum(d_log * softplus(start), axis=0, keepdims=True) * rate
            d_a[r, 2 * NS :] = d_raw.astype(BF)
        d_a[rows:, 2 * NS :] = jnp.zeros((nb * HALO, CW - 2 * NS), BF)
        put_rows(SUM_HEADS, bias_sum)
        put_rows(SUM_HEADS + 1, rate_sum)


def run_back(
    info, a, pieces, ends, dx_intra, db, dc, enter, product, dyr, conv_w, a_log, d_skip, table,
    narrow, gain_part, skip_part,
):
    rows = dyr.shape[0]
    nb = rows // CH
    ext_rows = rows + nb * HALO

    def chunk(s):
        return jnp.minimum(s, NCW - 1)

    def same(s):
        return s

    ins = [(info, in_smem())]
    ins += [(v, columns(v, chunk)) for v in pieces]
    ins += [(v, pl.BlockSpec((nb, 16, LANES), lambda s: (0, 0, DI // LANES))) for v in ends]
    ins += [(dx_intra, columns(dx_intra, chunk)), (db, whole(db)), (dc, whole(dc))]
    ins += [(a["xbc"], columns(a["xbc"], same)), (a["slope"], columns(a["slope"], same))]
    ins += [(a["xs"], columns(a["xs"], chunk)), (a["xt"], columns(a["xt"], chunk))]
    ins += [(a[k], whole(a[k])) for k in ("bs", "raw", "cum")]
    ins += [(v, columns(v, chunk)) for v in (enter, product, dyr)]
    ins += [(conv_w, columns(conv_w, same)), (a_log, whole(a_log)), (d_skip, columns(d_skip, chunk))]
    ins += [(table, columns(table, chunk))]
    ins += [(narrow, pl.BlockSpec((CW, LANES), lambda s: (chunk(s), 0)))]
    ins += [(v, columns(v, chunk)) for v in (gain_part, skip_part)]
    wide, sums = shape((ext_rows, WA), BF), shape((SUM_ROWS, LANES), F32)
    outs = [(wide, columns(wide, same)), (sums, whole(sums))]
    scratch = [
        pltpu.VMEM((nb, CH + 2 * HALO, CW), F32), pltpu.VMEM((nb, 2, CH, 2 * LANES), BF),
        pltpu.VMEM((rows, NS), F32), pltpu.VMEM((3, rows, LANES), F32),
        pltpu.VMEM((nb * nb * len(pieces), 2 * LANES), BF),
    ]
    return call(
        functools.partial(back_kernel, len(pieces)), 2, (NCW + 1,), ins, outs, scratch, VMEM_ASK,
    )


def unit(rows):
    f = rows.astype(F32)
    inv = lax.rsqrt(jnp.mean(f * f, axis=1, keepdims=True) + EPSILON)
    return f * inv, inv


def norm_back(normal_grad, rows, gain):
    u, inv = unit(rows)
    g = normal_grad * gain[None, :]
    return inv * (g - u * jnp.mean(g * u, axis=1, keepdims=True))


def shards(
    tokens, norm_gain, in_weight, conv_weight, conv_bias, dt_bias, a_log, d_skip, inner_gain,
    out_weight, block_place, seq_length, cotangent,
):
    n_head, n_shard = lax.axis_size("head"), lax.axis_size("shard")
    half = n_head // 2
    head_at, shard_at = lax.axis_index("head"), lax.axis_index("shard")
    rows = tokens.shape[0]
    nb = rows // CH
    group_blocks = nb * n_head
    k_rows = in_weight.shape[0]
    stay = (head_at // half) == (shard_at & 1)

    piece_a = jnp.concatenate(
        [in_weight[:, DI:], norm_gain[:, None], jnp.zeros((k_rows, WA - XBC - NH - 1), BF)], axis=1
    )
    numbers = jnp.concatenate([block_place, seq_length], axis=1)
    numbers_got = trade(numbers, "shard", 1)
    me = jnp.int32(0) if k_rows % 32 else shard_at.astype(jnp.int32)
    def block_tails(v):
        return v.reshape(nb, CH, DM)[:, CH - HALO :].reshape(nb * HALO, DM)

    tok_got = move_home(tokens)
    tails = jnp.where(stay, block_tails(tokens), block_tails(tok_got))

    numbers = jnp.where(stay, numbers, numbers_got)[0]
    lengths = [numbers[group_blocks + k] for k in range(seq_length.shape[1])]

    def order_from(core_at):
        ids = []
        for core in (0, 1):
            for z in range(half):
                device = (head_at % half ^ z) + (core_at ^ core) * half
                ids += [device * nb + b for b in range(nb)]
        return jnp.stack(ids)

    ids, home_order = order_from(shard_at & 1), order_from(head_at // half)
    places = jnp.sum(
        jnp.where(ids[:, None] == jnp.arange(group_blocks)[None, :], numbers[None, :group_blocks], 0),
        axis=1,
    )
    first, in_seq, begin = jnp.zeros_like(places), jnp.zeros_like(places), 0
    for length in lengths:
        first = jnp.where(places >= begin, begin, first)
        in_seq = jnp.where(places >= begin, length, in_seq)
        begin = begin + (length + CH - 1) // CH
    info = jnp.concatenate(
        [
            jnp.stack([me, stay.astype(jnp.int32)]),
            jnp.stack([places, first, in_seq], axis=1).reshape(-1),
        ]
    ).astype(jnp.int32)

    far_a = gather_far(piece_a)
    conv_weight, conv_bias, dt_bias, a_log, d_skip, inner_gain, none = after_all(
        [conv_weight, conv_bias, dt_bias, a_log, d_skip, inner_gain, jnp.int32(0)], far_a[0]
    )
    table = spread_table(none)

    def head_row(v):
        return jnp.pad(v, (0, LANES - NH))[None]

    narrow = narrow_table(none)
    gain_row = inner_gain[None]
    at = shard_at.astype(jnp.int32).reshape(1)
    taps = jnp.pad(conv_weight, ((0, 0), (0, WA - XBC)))
    rate_row = head_row(a_log)
    skip_row = jnp.repeat(d_skip, HD)[None]
    taps, rate_row, skip_row, bias_row, step_row, gain_row, narrow, table = after_all(
        [
            taps, rate_row, skip_row, jnp.pad(conv_bias, (0, WA - XBC))[None], head_row(dt_bias),
            gain_row, narrow, table,
        ]
    )
    prepared = [taps, rate_row, skip_row, bias_row, step_row, gain_row, narrow, table]
    parts_a = gather_near(piece_a, far_a)
    if k_rows % 32:
        parts_a = [(join_pieces(parts_a).reshape(DM, WA), 0)]
    z_own, o_own = after_all([in_weight[:, :DI], out_weight], numbers_got)
    piece_zo = jnp.concatenate([z_own, o_own[:k_rows], o_own[k_rows:]], axis=1)
    far_zo = gather_far(piece_zo)
    tails = group_spread(after(tails, info, *[v for v, _ in parts_a[1:]], *prepared))
    cot_got = move_home(after(cotangent, *tails))
    a = run_project(info, parts_a, tails, tokens, tok_got, taps, bias_row, step_row, rate_row, table)
    wa, tok, normal = a["wa"], a["tok"], a["normal"]
    state_by_head = head_pieces(a["states"])
    state_by_core = trade(a["states"], "shard", 1)
    y_intra = run_intra(a)
    parts_zo = gather_near(after(piece_zo, y_intra), after_all(far_zo, y_intra))
    if k_rows % 32:
        zo = join_pieces(parts_zo)
        wz, wo = zo[:, :, :DI].reshape(DM, DI), zo[:, :, DI:]
        wo = wo.reshape(n_shard, k_rows, 2, DM).swapaxes(1, 2).reshape(DI, DM)
        cot = jnp.where(stay, cotangent, cot_got)
        z, q = dot(normal[:rows], wz).astype(BF), dot_nt(cot, wo).astype(BF)
    else:
        cot_got = after(cot_got, y_intra)
        z, q, cot, wz, wo = run_open(
            at, parts_zo, normal, cotangent, cot_got, stay.astype(jnp.int32).reshape(1)
        )
    state_by_head = [after(v, z) for v in state_by_head]
    all_states = (
        [a["states"]] + state_by_head + [state_by_core] + [trade(v, "shard", 1) for v in state_by_head]
    )
    enter, normed, gain_part, dz, dyr, dye, product, skip_part, d_enter = run_gate(
        info, a, all_states, y_intra, z, q, gain_row, skip_row, table
    )
    enter_by_head = head_pieces(d_enter)
    enter_by_core = trade(d_enter, "shard", 1)
    if k_rows % 32:
        z_term = dot_tn(normal[:rows], dz).astype(BF).reshape(n_shard, k_rows, DI)
        out_term = dot_tn(normed, cot).astype(BF).reshape(n_shard, 2, k_rows, DM)
        zo_keep, zo_give = core_give([z_term, out_term[:, 0], out_term[:, 1]])
        zo_give = [zo_give[p] for p in range(n_shard // 2)]
    else:
        zo_keep, zo_give = run_terms(at, a["normal_t"], dz, normed, cot, n_shard)
    zo_got = [trade(v, "shard", 1) for v in zo_give]
    dx_intra, db, dc, mixed = run_intra_back(a, after(dyr, *zo_give), dye, enter, normed, wo, tok)
    arrived = after_all(enter_by_head + zo_got, dx_intra)
    enter_by_head, zo_got = arrived[: len(enter_by_head)], arrived[len(enter_by_head) :]
    zo_pairs = chip_pairs(zo_keep, jnp.stack(zo_got))
    zo_far = chip_send(zo_pairs)
    enter_by_head = [after(v, *zo_pairs) for v in enter_by_head]
    all_enter = (
        [d_enter] + enter_by_head + [enter_by_core] + [trade(v, "shard", 1) for v in enter_by_head]
    )
    mixed_got = move_home(after(mixed, all_enter[-1]))
    d_a_all, small = run_back(
        info, a, all_enter, all_states, dx_intra, db, dc, enter, product, dyr, taps,
        rate_row, skip_row, table, narrow, gain_part, skip_part,
    )
    d_a_all = after(d_a_all, mixed_got)
    a_term = dot_tn(normal, d_a_all).astype(BF).reshape(n_shard, k_rows, WA)
    a_keep, a_give = core_give([a_term])
    a_got = trade(a_give, "shard", 1)

    small_got = trade(after(small, a_give), "shard", 1)
    zo_own = chip_sum(zo_pairs[0], after_all(zo_far, a_give))
    zo_keep, zo_give = head_split(zo_own)
    zo_got = trade(zo_give, "head", 1)
    d_a_all, dz, tok, tok_halo, wa = after_all(
        [d_a_all, dz, tok, a["tok_halo"], wa], a_give, zo_give
    )
    gain = wa[:, XBC + NH].astype(F32)
    from_a = dot_nt(d_a_all, wa)
    normal_grad = dot_nt(dz, wz) + from_a[:rows]
    token_grad = (cot.astype(F32) + norm_back(normal_grad, tok, gain)).astype(BF)

    a_got, small_got = after_all([a_got, small_got], token_grad)
    if k_rows % 32:
        parts = split2((small + small_got).reshape(k_rows, -1))
        a_pairs = [jnp.concatenate([v, parts], axis=1) for v in chip_pairs(a_keep, a_got)]
    else:
        a_pairs = run_pair_small(at, a_term, a_got, small, small_got)
    a_far = chip_send(a_pairs)
    token_got = move_home(after(token_grad, a_pairs[0]))
    zo_half = head_add(zo_keep, after(zo_got, a_pairs[0]))
    zo_got = trade(zo_half, "head", 2)
    halo_part = norm_back(after(from_a, a_pairs[0])[rows:], tok_halo, gain)
    halo_part = halo_part.reshape(nb, HALO, DM)[:, HALO - KC :].astype(BF).reshape(k_rows, -1)
    halos = [halo_part, trade(halo_part, "shard", 1)]
    *a_far, zo_got, halos[1] = after_all(a_far + [zo_got, halos[1]])
    a_own = chip_sum(a_pairs[0][:, :WA], [v[:, :WA] for v in a_far])
    sums = [join2(v[:, WA:]) for v in [a_pairs[0]] + a_far]
    while len(sums) > 1:
        sums = [sums[k] + sums[k + 1] for k in range(0, len(sums), 2)]
    small = sums[0]
    a_keep, a_give = head_split(a_own)
    cut, edge = a_keep.shape[1], a_keep.shape[1] + 2 * small.shape[1]
    total = a_keep.astype(F32)
    bits = [b for b in (1, 2, 4, 8, 16) if b < n_head]
    for bit in bits:
        if bit > 1:
            a_give = total.astype(BF)
            total = a_give.astype(F32)
        parts = split2(small)
        sent = jnp.concatenate([a_give, parts] + (halos if bit < half else []), axis=1)
        sent = trade(sent, "head", bit)
        if bit == 1:
            sent, token_got, zo_got = after_all([sent, token_got, zo_got])
            zo_half = head_add(zo_half, zo_got)
            for more in bits[2:]:
                zo_half = head_add(zo_half, trade(zo_half, "head", more))
            zo_other = trade(zo_half, "head", 1)
        if bit < half:
            halos = halos + jnp.split(sent[:, edge:], len(halos), axis=1)
        total = total + sent[:, :cut].astype(F32)
        small = join2(parts) + join2(sent[:, cut:edge])
    low = total.astype(BF)
    other = trade(low, "head", 1)
    halos, small, zo_other = after_all([jnp.concatenate(halos, axis=1), small, zo_other], low)
    zo_grad = head_join(zo_half, zo_other).astype(F32)
    halos = jnp.where(stay, halos, move_home(halos))
    halos = jnp.split(halos, group_blocks // nb, axis=1)
    other = after(other, *halos)
    a_grad = head_join(low, other).astype(F32)
    small = small.reshape(SUM_ROWS, LANES)

    all_halo = jnp.concatenate(halos[0::2] + halos[1::2]).reshape(group_blocks, KC, DM).astype(F32)
    own_numbers = jnp.concatenate([block_place, seq_length], axis=1)[0]
    own_places = jnp.sum(
        jnp.where(
            home_order[:, None] == jnp.arange(group_blocks), own_numbers[None, :group_blocks], 0
        ),
        axis=1,
    )
    home_ids = head_at * nb + jnp.arange(nb)
    home_places = jnp.sum(
        jnp.where(
            home_ids[:, None] == jnp.arange(group_blocks), own_numbers[None, :group_blocks], 0
        ),
        axis=1,
    )
    goes_on, begin = home_places < 0, 0
    for k in range(seq_length.shape[1]):
        end = begin + (own_numbers[group_blocks + k] + CH - 1) // CH
        goes_on = goes_on | ((home_places >= begin) & (home_places + 1 < end))
        begin = end
    is_next = (own_places[None, :] == home_places[:, None] + 1) & goes_on[:, None]
    halo_back = jnp.sum(jnp.where(is_next[:, :, None, None], all_halo[None], 0.0), axis=1)
    token_grad = jnp.where(stay, token_grad, token_got).reshape(nb, CH, DM)
    token_grad = token_grad.at[:, CH - KC :].set(
        (token_grad[:, CH - KC :].astype(F32) + halo_back).astype(BF)
    ).reshape(rows, DM)
    mixed = jnp.where(stay, mixed, after(mixed_got, a_own))

    in_grad = jnp.concatenate([zo_grad[:, :DI], a_grad[:, : XBC + NH]], axis=1)
    out_grad = jnp.concatenate([zo_grad[:, DI : DI + DM], zo_grad[:, DI + DM :]], axis=0)
    gain_grad = jnp.sum(in_grad * in_weight.astype(F32), axis=1) / norm_gain.astype(F32)

    return (
        mixed, token_grad, gain_grad, in_grad, small[: KC * XBC // LANES].reshape(KC, XBC),
        small[KC * XBC // LANES : SUM_GAIN].reshape(XBC), small[SUM_HEADS, :NH],
        small[SUM_HEADS + 1, :NH], jnp.sum(small[SUM_SKIP:SUM_HEADS].reshape(NH, HD), axis=1),
        small[SUM_GAIN:SUM_SKIP].reshape(DI), out_grad,
    )


def solution(mesh):
    return jax.shard_map(
        shards,
        mesh=mesh,
        in_specs=(
            P(("head", "shard"), None), P("shard"), P("shard", None), P(), P(), P(), P(), P(), P(),
            P("shard", None), P("shard", None), P("shard", None), P(("head", "shard"), None),
        ),
        out_specs=(
            P(("head", "shard"), None), P(("head", "shard"), None), P("shard"), P("shard", None),
            P(), P(), P(), P(), P(), P(), P("shard", None),
        ),
        check_vma=False,
    )
```

```python
import functools

import jax
import jax.numpy as jnp
from jax import lax
from jax.experimental import pallas as pl
from jax.experimental.pallas import tpu as pltpu
from jax.sharding import PartitionSpec as P

NH = 24
HD = 64
NS = 128
KC = 4
CH = 256
DI = 1536
DM = 768
XBC = DI + 2 * NS
WA = 1920
HALO = 8
EPSILON = 1e-05
F32 = jnp.float32
BF = jnp.bfloat16
LANES = 128
CW = 384
NCW = DI // CW
VMEM_ASK = 56 * 2**20
VMEM_ROOM = 56 * 2**20
VMEM_LESS = 44 * 2**20
VMEM_LITTLE = 24 * 2**20
COST_SCALE = 0.4


def trade(value, axis, bit):
    size = lax.axis_size(axis)
    return lax.ppermute(value, axis, [(i, i ^ bit) for i in range(size)])


def after(value, *others):
    return lax.optimization_barrier((value,) + others)[0]


def move_home(value):
    n_head, n_shard = lax.axis_size("head"), lax.axis_size("shard")
    half = n_head // 2
    pairs = []
    for h in range(n_head):
        for s in range(n_shard):
            upper, core = h // half, s & 1
            if upper != core:
                there = (h % half + core * half) * n_shard + (s - core + upper)
                pairs.append((h * n_shard + s, there))
    return lax.ppermute(value, ("head", "shard"), pairs)


def swap_home(value, stay):
    return jnp.where(stay, value, move_home(value))


def group_spread(value):
    n_head, n_shard = lax.axis_size("head"), lax.axis_size("shard")
    pieces = [value]
    for core in (0, 1):
        for low in range(n_head // 2):
            if core or low:
                pairs = [
                    (h * n_shard + s, (h ^ low) * n_shard + (s ^ core))
                    for h in range(n_head)
                    for s in range(n_shard)
                ]
                pieces.append(lax.ppermute(value, ("head", "shard"), pairs))
    return pieces


def group_gather(value):
    half = lax.axis_size("head") // 2
    pieces = [value]
    bit = 1
    while bit < half:
        pieces = pieces + [trade(v, "head", bit) for v in pieces]
        bit *= 2
    return pieces + [trade(v, "shard", 1) for v in pieces]


def gather_far(piece):
    bits = range(2, lax.axis_size("shard"), 2)
    return [trade(piece, "shard", bit) for bit in sorted(bits, reverse=True)]


def gather_near(piece, far):
    held = [piece] + far
    offsets = [0] + sorted(range(2, lax.axis_size("shard"), 2), reverse=True)
    near = [trade(v, "shard", 1) for v in held]
    return list(zip(held + near, offsets + [k ^ 1 for k in offsets]))


def join_pieces(parts):
    me, n_shard = lax.axis_index("shard"), lax.axis_size("shard")
    joined = jnp.zeros((n_shard,) + parts[0][0].shape, parts[0][0].dtype)
    for v, k in parts:
        joined = lax.dynamic_update_slice(joined, v[None], (me ^ k, 0, 0))
    return joined


def head_pieces(value):
    pieces = [value]
    bit = 1
    while bit < lax.axis_size("head") // 2:
        pieces = pieces + [trade(v, "head", bit) for v in pieces]
        bit *= 2
    return pieces[1:]


def core_give(blocks):
    n_shard = lax.axis_size("shard")
    core = lax.axis_index("shard") % 2

    def half(which):
        parts = []
        for v in blocks:
            split = v.reshape((n_shard // 2, 2) + v.shape[1:])
            parts.append(lax.dynamic_index_in_dim(split, which, 1, False))
        return jnp.concatenate(parts, axis=2) if len(parts) > 1 else parts[0]

    return half(core), half(1 - core)


def chip_pairs(keep, got):
    pair = (keep.astype(F32) + got.astype(F32)).astype(BF)
    chip = lax.axis_index("shard") // 2
    return [lax.dynamic_index_in_dim(pair, chip ^ k, 0, False) for k in range(pair.shape[0])]


def after_all(values, *others):
    return list(lax.optimization_barrier((*values, *others)))[: len(values)]


def chip_send(pairs):
    return [trade(v, "shard", 2 * k) for k, v in enumerate(pairs) if k]


def chip_sum(own, got):
    total = own.astype(F32)
    for v in got:
        total = total + v.astype(F32)
    return total.astype(BF)


def split2(v):
    high = lax.reduce_precision(v, 8, 7)
    return jnp.concatenate([high.astype(BF), (v - high).astype(BF)], axis=1)


def join2(parts):
    high, low = jnp.split(parts, 2, axis=1)
    return high.astype(F32) + low.astype(F32)


def head_split(value):
    cut = value.shape[1] // 2
    odd = lax.axis_index("head") % 2
    return [lax.dynamic_slice_in_dim(value, at * cut, cut, 1) for at in (odd, 1 - odd)]


def head_add(keep, got):
    return (keep.astype(F32) + got.astype(F32)).astype(BF)


def head_join(half, other):
    odd = lax.axis_index("head") % 2
    return jnp.concatenate([jnp.where(odd, other, half), jnp.where(odd, half, other)], axis=1)


def dot(a, b):
    return jnp.dot(a, b, preferred_element_type=F32)


def dot_nt(a, b):
    return lax.dot_general(a, b, (((1,), (1,)), ((), ())), preferred_element_type=F32)


def dot_tn(a, b):
    return lax.dot_general(a, b, (((0,), (0,)), ((), ())), preferred_element_type=F32)


def spread_table(none):
    row = jnp.arange(2 * LANES)[:, None] % LANES + none
    return (row == jnp.arange(DI)[None, :] // HD).astype(BF)


def narrow_table(none):
    return (jnp.arange(DI)[:, None] // HD == jnp.arange(LANES)[None, :] + none).astype(BF)


def pieces2(v):
    hi = v.astype(BF)
    return hi, (v - hi.astype(F32)).astype(BF)


def pieces3(v):
    hi = v.astype(BF)
    rest = v - hi.astype(F32)
    mid = rest.astype(BF)
    return hi, mid, (rest - mid.astype(F32)).astype(BF)


def softplus(v):
    return jnp.maximum(v, 0.0) + jnp.log1p(jnp.exp(-jnp.abs(v)))


sigmoid = jax.nn.sigmoid


def shape(dims, dtype):
    return jax.ShapeDtypeStruct(dims, dtype)


def whole(arr):
    return pl.BlockSpec(arr.shape, lambda *g: (0,) * len(arr.shape))


def columns(arr, at, width=None):
    dims = arr.shape[:-1] + (width or CW,)
    return pl.BlockSpec(dims, lambda *g: (0,) * (len(dims) - 1) + (at(*g),))


def in_hbm():
    return pl.BlockSpec(memory_space=pl.ANY)


def in_smem():
    return pl.BlockSpec(memory_space=pltpu.SMEM)


def call(kernel, micros, grid, ins, outs, scratch, room=VMEM_ROOM):
    return pl.pallas_call(
        kernel,
        grid=grid,
        out_shape=[o for o, _ in outs],
        in_specs=[s for _, s in ins],
        out_specs=[s for _, s in outs],
        scratch_shapes=scratch,
        compiler_params=pltpu.CompilerParams(vmem_limit_bytes=room),
        cost_estimate=pl.CostEstimate(
            flops=1, bytes_accessed=int(micros * COST_SCALE * 3.7e6), transcendentals=0
        ),
    )(*[a for a, _ in ins])


def iota(dims, axis):
    return lax.broadcasted_iota(jnp.int32, dims, axis)


def place_of(info, q):
    return info[2 + 3 * q]


def first_of(info, q):
    return info[3 + 3 * q]


def usable_of(info, i):
    begin = (place_of(info, i) - first_of(info, i)) * CH
    return (iota((CH, 1), 0) + begin < info[4 + 3 * i]).astype(F32)


def halo_used(info, i):
    has_prev = place_of(info, i) > first_of(info, i)
    return (iota((HALO, 1), 0) + jnp.where(has_prev, 0, -HALO) > HALO - KC).astype(F32)


def clast_rows(refs, nb):
    rows = []
    for ref in refs:
        for b in range(nb):
            part = ref[b].astype(F32)
            rows.append(part[0:1, :] + part[1:2, :] + part[2:3, :])
    return rows


def carry_weights(info, ends, nb, into):
    n_all = len(ends)
    row = iota((n_all, 1), 0)
    place = jnp.zeros((n_all, 1), jnp.int32)
    first = jnp.zeros((n_all, 1), jnp.int32)
    for j in range(n_all):
        place = jnp.where(row == j, place_of(info, j), place)
        first = jnp.where(row == j, first_of(info, j), first)
    parts = []
    for i in range(nb):
        own = place_of(info, i)
        total = jnp.zeros((n_all, LANES), F32)
        for k in range(n_all):
            at = place_of(info, k)
            if into:
                between = (place > at) & (at > own)
            else:
                between = (place < at) & (at < own)
            total = total + jnp.where(between, ends[k], 0.0)
        if into:
            reach = (first <= own) & (place > own)
        else:
            reach = (place >= first_of(info, i)) & (place < own)
        parts.append(jnp.where(reach, jnp.exp(total), 0.0))
    return jnp.concatenate(pieces2(jnp.concatenate(parts, axis=0)), axis=1)


def normal_rows(rows, gain):
    f = rows.astype(F32)
    inv = lax.rsqrt(jnp.sum(f * f, axis=1, keepdims=True) / DM + EPSILON)
    return (f * inv * gain).astype(BF)


def project_kernel(layout, n_halo, *refs):
    info = refs[0]
    pieces = refs[1 : 1 + len(layout)]
    halos = refs[1 + len(layout) : 1 + len(layout) + n_halo]
    (
        tok_own, tok_got, conv_w, conv_b, dt_bias, a_log, table,
        wa_out, tok_out, tok_halo, normal_out, normal_t_out, xbc, slope, xs, xt, bs_out, cs_out,
        raw_out, cum_out, cum_t_out, states,
        wa, ext, small, sems, out_sems, tok, normal, normal_t, bs, cs, raw, cum, cum_t,
    ) = refs[1 + len(layout) + n_halo :]
    step = pl.program_id(0)
    rows = tok_own.shape[0]
    nb = rows // CH
    me = info[0]

    def project(at, width):
        proj = dot(normal[...], wa[:, pl.ds(at, width)]).astype(BF).astype(F32)
        acts, heads = [], []
        for i in range(nb):
            head = proj[rows + i * HALO : rows + (i + 1) * HALO, :] * halo_used(info, i)
            body = proj[i * CH : (i + 1) * CH, :] * usable_of(info, i)
            heads.append(head)
            ext[i, :HALO, :width] = head
            ext[i, HALO:, :width] = body
            xbc[i * CH : (i + 1) * CH, :width] = body.astype(BF)
            pre = conv_b[:, pl.ds(at, width)]
            for lag in range(KC):
                tap = conv_w[KC - 1 - lag : KC - lag, pl.ds(at, width)]
                pre = pre + tap * ext[i, HALO - lag : HALO - lag + CH, :width]
            sg = sigmoid(pre)
            act = pre * sg
            slope[i * CH : (i + 1) * CH, :width] = (sg + act * (1.0 - sg)).astype(BF)
            acts.append(act)
        xbc[rows:, :width] = jnp.concatenate(heads, axis=0).astype(BF)
        return acts

    def leaving():
        moves = [(wa, wa_out), (tok, tok_out), (normal, normal_out), (normal_t, normal_t_out)]
        moves += [(bs, bs_out), (cs, cs_out), (raw, raw_out), (cum, cum_out), (cum_t, cum_t_out)]
        return [pltpu.make_async_copy(v, there, out_sems.at[n]) for n, (v, there) in enumerate(moves)]

    @pl.when(step == 0)
    def _():
        def copy_of(n):
            at = pl.multiple_of((me ^ layout[n]) * pieces[n].shape[0], 16)
            return pltpu.make_async_copy(
                pieces[n], wa.at[pl.ds(at, pieces[n].shape[0]), :], sems.at[n]
            )

        for n in range(len(layout)):
            copy_of(n).start()
        stay = info[1] > 0
        tok[...] = jnp.where(stay, tok_own[...], tok_got[...])
        found = []
        for i in range(nb):
            own, has_prev = place_of(info, i), place_of(info, i) > first_of(info, i)
            total = jnp.zeros((HALO, DM), F32)
            for o in range(n_halo):
                part = halos[o][...].astype(F32)
                for b in range(nb):
                    hit = (place_of(info, o * nb + b) == own - 1) & has_prev
                    total = total + jnp.where(hit, part[b * HALO : (b + 1) * HALO, :], 0.0)
            found.append(total)
        tok_halo[...] = jnp.concatenate(found, axis=0).astype(BF)
        for n in range(len(layout)):
            copy_of(n).wait()
        for copy in leaving()[:2]:
            copy.start()
        gain = wa[:, XBC : XBC + LANES].astype(F32).T[NH : NH + 1, :]
        normal[:rows, :] = normal_rows(tok[...], gain)
        normal_t[...] = normal[:rows, :].T
        normal[rows:, :] = normal_rows(tok_halo[...], gain)
        for i, act in enumerate(project(DI, 2 * NS)):
            bs[i * CH : (i + 1) * CH, :] = act[:, :NS].astype(BF)
            cs[i * CH : (i + 1) * CH, :] = act[:, NS:].astype(BF)
        xbc[:, 2 * NS :] = jnp.zeros((xbc.shape[0], CW - 2 * NS), BF)
        slope[:, 2 * NS :] = jnp.zeros((rows, CW - 2 * NS), BF)
        first = dot(normal[:rows, :], wa[:, XBC : XBC + LANES]).astype(BF).astype(F32) + dt_bias[...]
        raw[...] = first
        dt_all = softplus(first)
        rate = jnp.exp(a_log[...])
        causal = (iota((CH, CH), 0) >= iota((CH, CH), 1)).astype(F32).astype(BF)
        states[:, :, DI:] = jnp.zeros((nb, NS, LANES), BF)
        for i in range(nb):
            dt = dt_all[i * CH : (i + 1) * CH, :]
            parts = dot(causal, jnp.concatenate(pieces3(-dt * rate), axis=1))
            run = parts[:, :LANES] + parts[:, LANES : 2 * LANES] + parts[:, 2 * LANES :]
            cum[i * CH : (i + 1) * CH, :] = run
            cum_t[:, i * CH : (i + 1) * CH] = run.T
            last = run[CH - 1 : CH, :]
            ends = jnp.concatenate(pieces3(last) + (jnp.zeros((13, LANES), BF),), axis=0)
            states[i, :16, DI:] = ends
            small[i, 0] = jnp.concatenate(pieces2(dt), axis=1)
            small[i, 1] = jnp.concatenate(pieces2(jnp.exp(last - run) * dt), axis=1)
        for copy in leaving()[2:]:
            copy.start()

    @pl.when(step > 0)
    def _():
        at = pl.multiple_of((step - 1) * CW, CW)
        for i, act in enumerate(project(at, CW)):
            r = slice(i * CH, (i + 1) * CH)
            xs[r, :] = act.astype(BF)
            xt[r, :] = (act * dot(small[i, 0], table[...])).astype(BF)
            weighted = (act * dot(small[i, 1], table[...])).astype(BF)
            states[i, :, pl.ds(at, CW)] = dot_tn(bs[r, :], weighted).astype(BF)

    @pl.when(step == NCW)
    def _():
        for copy in leaving():
            copy.wait()


def run_project(info, parts, halos, tok_own, tok_got, conv_w, conv_b, dt_bias, a_log, table):
    rows = tok_own.shape[0]
    nb = rows // CH
    ext_rows = rows + nb * HALO
    layout = [offset for _, offset in parts]

    def before(s):
        return jnp.maximum(s - 1, 0)

    def tail_first(s):
        return jnp.where(s == 0, NCW, s - 1)

    ins = [(info, in_smem())] + [(v, in_hbm()) for v, _ in parts]
    ins += [(v, whole(v)) for v in halos]
    ins += [(v, whole(v)) for v in (tok_own, tok_got, conv_w, conv_b, dt_bias, a_log)]
    ins += [(table, columns(table, before))]
    outs = {
        "wa": (shape((DM, WA), BF), in_hbm()),
        "tok": (shape((rows, DM), BF), in_hbm()),
        "tok_halo": (shape((nb * HALO, DM), BF), whole),
        "normal": (shape((ext_rows, DM), BF), in_hbm()),
        "normal_t": (shape((DM, rows), BF), in_hbm()),
        "xbc": (shape((ext_rows, WA), BF), lambda v: columns(v, tail_first)),
        "slope": (shape((rows, WA), BF), lambda v: columns(v, tail_first)),
        "xs": (shape((rows, DI), BF), lambda v: columns(v, before)),
        "xt": (shape((rows, DI), BF), lambda v: columns(v, before)),
        "bs": (shape((rows, NS), BF), in_hbm()),
        "cs": (shape((rows, NS), BF), in_hbm()),
        "raw": (shape((rows, LANES), F32), in_hbm()),
        "cum": (shape((rows, LANES), F32), in_hbm()),
        "cum_t": (shape((LANES, rows), F32), in_hbm()),
        "states": (shape((nb, NS, DI + LANES), BF), whole),
    }
    out_list = [(o, s(o) if callable(s) else s) for o, s in outs.values()]
    scratch = [
        pltpu.VMEM((DM, WA), BF), pltpu.VMEM((nb, HALO + CH, CW), F32),
        pltpu.VMEM((nb, 2, CH, 2 * LANES), BF), pltpu.SemaphoreType.DMA((len(parts),)),
        pltpu.SemaphoreType.DMA((9,)),
    ]
    kept = ("tok", "normal", "normal_t", "bs", "cs", "raw", "cum", "cum_t")
    scratch += [pltpu.VMEM(outs[k][0].shape, outs[k][0].dtype) for k in kept]
    got = call(
        functools.partial(project_kernel, layout, len(halos)), 14, (NCW + 1,), ins, out_list, scratch, VMEM_ASK,
    )
    return dict(zip(outs, got))


SUM_GAIN = (KC + 1) * XBC // LANES
SUM_SKIP = SUM_GAIN + DI // LANES
SUM_HEADS = SUM_SKIP + DI // LANES
SUM_ROWS = SUM_HEADS + 2
OUT_ROWS = CW // 4
PER = CW // HD
HALF = CH // 2


def chunk_heads(cum, first):
    return pltpu.roll(cum, lax.rem(LANES - first, LANES), axis=1)


def intra_kernel(bs, cs, xt, cum, cum_t, out, scores):
    c = pl.program_id(0)
    nb = bs.shape[0] // CH
    low = iota((CH, LANES), 1) < HD
    keep = iota((HALF, HALF), 0) >= iota((HALF, HALF), 1)

    @pl.when(c == 0)
    def _():
        for i in range(nb):
            r = slice(i * CH, (i + 1) * CH)
            scores[i] = dot_nt(cs[r, :], bs[r, :])

    for i in range(nb):
        r = slice(i * CH, (i + 1) * CH)
        cols = chunk_heads(cum[r, :], c * PER)
        for p in range(PER // 2):
            lanes = slice(p * LANES, (p + 1) * LANES)
            both = xt[r, lanes]
            got = []
            for k in range(2):
                h = 2 * p + k
                col = cols[:, h : h + 1]
                row = cum_t[pl.ds(c * PER + h, 1), r]
                a, b = col[:HALF], col[HALF:]
                s, t = row[:, :HALF], row[:, HALF:]
                upper = jnp.where(keep, jnp.exp(a - s), 0.0) * scores[i, :HALF, :HALF]
                left = jnp.exp(b - s) * scores[i, HALF:, :HALF]
                right = jnp.where(keep, jnp.exp(b - t), 0.0) * scores[i, HALF:, HALF:]
                lower = jnp.concatenate([left.astype(BF), right.astype(BF)], axis=1)
                got.append(
                    jnp.concatenate([dot(upper.astype(BF), both[:HALF, :]), dot(lower, both)], axis=0)
                )
            out[r, lanes] = jnp.where(low, got[0], got[1])


def run_intra(a):
    rows = a["bs"].shape[0]
    nb = rows // CH
    ins = [(a[k], whole(a[k])) for k in ("bs", "cs")]
    ins += [(a["xt"], columns(a["xt"], lambda c: c))]
    ins += [(a[k], whole(a[k])) for k in ("cum", "cum_t")]
    out = shape((rows, DI), F32)
    return call(
        intra_kernel, 6, (NCW,), ins, [(out, columns(out, lambda c: c))],
        [pltpu.VMEM((nb, CH, CH), F32)],
    )[0]


OW = 768
ONW = DI // OW


def open_kernel(layout, at, *refs):
    pieces = refs[: len(layout)]
    normal, cot_own, cot_got, stay, z, q, cot, wz_out, wo_out, wz, wo, sems, out_sems = refs[
        len(layout) :
    ]
    c = pl.program_id(0)
    k_rows = pieces[0].shape[0]

    def copies(n):
        shard = at[0] ^ layout[n]
        parts = [(wz, shard * k_rows, slice(0, DI))]
        for j in range(2):
            lanes = slice(DI + j * DM, DI + (j + 1) * DM)
            parts.append((wo, (2 * shard + j) * k_rows, lanes))
        return [
            pltpu.make_async_copy(
                pieces[n].at[:, lanes],
                ref.at[pl.ds(pl.multiple_of(begin, 16), k_rows), :],
                sems.at[3 * n + k],
            )
            for k, (ref, begin, lanes) in enumerate(parts)
        ]

    def leaving():
        return [
            pltpu.make_async_copy(wz, wz_out, out_sems.at[0]),
            pltpu.make_async_copy(wo, wo_out, out_sems.at[1]),
        ]

    @pl.when(c == 0)
    def _():
        for n in range(len(layout)):
            for copy in copies(n):
                copy.start()
        cot[...] = jnp.where(stay[0] > 0, cot_own[...], cot_got[...])
        for n in range(len(layout)):
            for copy in copies(n):
                copy.wait()
        for copy in leaving():
            copy.start()

    here = pl.ds(pl.multiple_of(c * OW, OW), OW)
    z[...] = dot(normal[...], wz[:, here]).astype(BF)
    q[...] = dot_nt(cot[...], wo[here, :]).astype(BF)

    @pl.when(c == ONW - 1)
    def _():
        for copy in leaving():
            copy.wait()


def run_open(at, parts, normal, cot_own, cot_got, stay):
    rows = cot_own.shape[0]
    layout = [offset for _, offset in parts]
    ins = [(at, in_smem())] + [(v, in_hbm()) for v, _ in parts]
    ins += [(normal, pl.BlockSpec((rows, DM), lambda c: (0, 0)))]
    ins += [(cot_own, whole(cot_own)), (cot_got, whole(cot_got)), (stay, in_smem())]
    wide = shape((rows, DI), BF)
    outs = [(wide, columns(wide, lambda c: c, OW))] * 2
    outs += [(v, whole(v)) for v in (shape((rows, DM), BF),)]
    outs += [(v, in_hbm()) for v in (shape((DM, DI), BF), shape((DI, DM), BF))]
    return call(
        functools.partial(open_kernel, layout), 1, (ONW,), ins, outs,
        [
            pltpu.VMEM((DM, DI), BF), pltpu.VMEM((DI, DM), BF),
            pltpu.SemaphoreType.DMA((3 * len(parts),)), pltpu.SemaphoreType.DMA((2,)),
        ],
        VMEM_LESS,
    )


def terms_kernel(at, normal_t, dz, normed, cot, keep, *refs):
    *give, z_part, o_part = refs
    p = pl.program_id(0)
    unit = give[0].shape[0]
    even = at[0] % 2 == 0
    z_part[...] = dot(normal_t[...], dz[...])
    o_part[...] = dot_tn(normed[...], cot[...])

    def rows_of(which):
        parts = [(z_part[which * unit : (which + 1) * unit, :], slice(0, DI))]
        for j in range(2):
            rows = o_part[(2 * which + j) * unit : (2 * which + j + 1) * unit, :]
            parts.append((rows, slice(DI + j * DM, DI + (j + 1) * DM)))
        return parts

    for (first, lanes), (second, _) in zip(rows_of(0), rows_of(1)):
        keep[0, :, lanes] = jnp.where(even, first, second).astype(BF)
        other = jnp.where(even, second, first).astype(BF)
        for k, ref in enumerate(give):

            @pl.when(p == k)
            def _(ref=ref, other=other, lanes=lanes):
                ref[:, lanes] = other


def run_terms(at, normal_t, dz, normed, cot, n_shard):
    rows = dz.shape[0]
    n, unit = n_shard // 2, DM // n_shard
    give = shape((unit, DI + 2 * DM), BF)
    keep = shape((n,) + give.shape, BF)
    got = call(
        terms_kernel, 1, (n,),
        [
            (at, in_smem()), (normal_t, pl.BlockSpec((2 * unit, rows), lambda p: (p, 0))),
            (dz, whole(dz)), (normed, columns(normed, lambda p: p, 4 * unit)), (cot, whole(cot)),
        ],
        [(keep, pl.BlockSpec((1,) + give.shape, lambda p: (p, 0, 0)))] + [(give, whole(give))] * n,
        [pltpu.VMEM((2 * unit, DI), F32), pltpu.VMEM((4 * unit, DM), F32)],
    )
    return got[0], list(got[1:])


def pair_small_kernel(at, term, got, small, small_got, *outs):
    cols = got.shape[-1]
    chip, core = at[0] // 2, at[0] % 2
    total = small[...] + small_got[...]
    parts = jnp.concatenate(pieces2(total), axis=1)
    for k, out in enumerate(outs):
        kept = term[2 * (chip ^ k) + core]
        out[:, :cols] = (kept.astype(F32) + got[chip ^ k].astype(F32)).astype(BF)
        out[:, cols:] = parts


def run_pair_small(at, term, got, small, small_got):
    n, rows, cols = got.shape
    out = shape((rows, cols + 2 * small.shape[1]), BF)
    args = [term, got, small, small_got]
    return call(
        pair_small_kernel, 1, (1,), [(at, in_smem())] + [(v, whole(v)) for v in args],
        [(out, whole(out))] * n, [], VMEM_LITTLE,
    )


def chip_sum_kernel(odd, *refs):
    n = len(refs) - 5
    terms, halos, (sent, keep, small_sum) = refs[:n], refs[n : n + 2], refs[n + 2 :]
    total = terms[0][:, :WA].astype(F32)
    for term in terms[1:]:
        total = total + term[:, :WA].astype(F32)
    low = total.astype(BF)
    cut = WA // 2
    right_kept = odd[0] > 0
    sent[:, :cut] = jnp.where(right_kept, low[:, :cut], low[:, cut:])
    keep[...] = jnp.where(right_kept, low[:, cut:], low[:, :cut])
    sums = [t[:, WA : WA + LANES].astype(F32) + t[:, WA + LANES :].astype(F32) for t in terms]
    while len(sums) > 1:
        sums = [sums[k] + sums[k + 1] for k in range(0, len(sums), 2)]
    high, rest = pieces2(sums[0])
    small_sum[...] = high.astype(F32) + rest.astype(F32)
    sent[:, cut:] = jnp.concatenate([high, rest] + [v[...] for v in halos], axis=1)


def run_chip_sum(odd, terms, halos):
    rows = terms[0].shape[0]
    width = WA // 2 + 2 * LANES + 2 * halos[0].shape[1]
    outs = [shape((rows, width), BF), shape((rows, WA // 2), BF), shape((rows, LANES), F32)]
    return call(
        chip_sum_kernel, 1, (1,),
        [(odd, in_smem())] + [(v, whole(v)) for v in list(terms) + halos],
        [(v, whole(v)) for v in outs], [], VMEM_LITTLE,
    )


GW = 768
GNW = DI // GW


def columns_g(arr, at):
    return columns(arr, at, GW)


def gate_kernel(n_pieces, *refs):
    info = refs[0]
    pieces = refs[1 : 1 + n_pieces]
    ends = refs[1 + n_pieces : 1 + 2 * n_pieces]
    (
        y_intra, cs, cum, xs, z, q, inner_gain, d_skip, table,
        enter, normed, gain_part, dz, dyr, dye, product, skip_part, d_enter,
        y_scan, small, weights, squares, dots,
    ) = refs[1 + 2 * n_pieces :]
    phase, c = pl.program_id(0), pl.program_id(1)
    rows = cs.shape[0]
    nb = rows // CH
    n_all = n_pieces * nb
    here = pl.ds(pl.multiple_of(c * GW, GW), GW)

    @pl.when((phase == 0) & (c == 0))
    def _():
        weights[...] = carry_weights(info, clast_rows(ends, nb), nb, False)
        squares[...] = jnp.zeros_like(squares)
        dots[...] = jnp.zeros_like(dots)
        for i in range(nb):
            r = slice(i * CH, (i + 1) * CH)
            small[r, :] = jnp.concatenate(pieces2(jnp.exp(cum[r, :])), axis=1)

    @pl.when(phase == 0)
    def _():
        wide_w = dot(weights[...], table[...])
        totals = [jnp.zeros((NS, GW), F32) for _ in range(nb)]
        for j in range(n_all):
            piece = pieces[j // nb][j % nb].astype(F32)
            for i in range(nb):
                totals[i] = totals[i] + wide_w[i * n_all + j : i * n_all + j + 1, :] * piece
        for i in range(nb):
            r = slice(i * CH, (i + 1) * CH)
            low = totals[i].astype(BF)
            enter[i] = low
            scan = y_intra[r, :] + dot(small[r, :], table[...]) * dot(cs[r, :], low)
            y_scan[r, here] = scan
            y = scan + d_skip[...] * xs[r, :].astype(F32)
            zf = z[r, :].astype(F32)
            gated = y * (zf * sigmoid(zf))
            qg = q[r, :].astype(F32) * inner_gain[...] * usable_of(info, i)
            squares[r, :] += jnp.sum(gated * gated, axis=1, keepdims=True)
            dots[r, :] += jnp.sum(qg * gated, axis=1, keepdims=True)

    @pl.when(phase == 1)
    def _():
        gain_sum = jnp.zeros((1, GW), F32)
        skip_sum = jnp.zeros((1, GW), F32)
        for i in range(nb):
            r = slice(i * CH, (i + 1) * CH)
            inv = lax.rsqrt(squares[r, :] / DI + EPSILON)
            slope = inv * inv * inv * dots[r, :] / DI
            use = usable_of(info, i)
            scan = y_scan[r, here]
            x = xs[r, :].astype(F32)
            y = scan + d_skip[...] * x
            zf = z[r, :].astype(F32)
            sg = sigmoid(zf)
            sz = zf * sg
            gated = y * sz
            qf = q[r, :].astype(F32) * use
            scaled = gated * inv
            normed[r, :] = (scaled * inner_gain[...] * use).astype(BF)
            gain_sum = gain_sum + jnp.sum(qf * scaled, axis=0, keepdims=True)
            gg = inv * qf * inner_gain[...] - gated * slope
            dz[r, :] = (gg * y * (sg + sz * (1.0 - sg))).astype(BF)
            dy = gg * sz
            low = dy.astype(BF)
            dyr[r, :] = low
            product[r, :] = low.astype(F32) * scan
            skip_sum = skip_sum + jnp.sum(dy * x, axis=0, keepdims=True)
            back = (dot(small[r, :], table[...]) * dy).astype(BF)
            dye[r, :] = back
            d_enter[i] = dot_tn(cs[r, :], back).astype(BF)
        gain_part[...] = gain_sum
        skip_part[...] = skip_sum


def run_gate(info, a, pieces, y_intra, z, q, inner_gain, d_skip, table):
    rows = z.shape[0]
    nb = rows // CH

    def early(p, c):
        return jnp.where(p == 0, c, GNW - 1)

    def both(p, c):
        return c

    def late(p, c):
        return jnp.where(p == 0, 0, c)

    ins = [(info, in_smem())]
    ins += [(v, columns_g(v, early)) for v in pieces]
    ins += [(v, pl.BlockSpec((nb, 16, LANES), lambda p, c: (0, 0, DI // LANES))) for v in pieces]
    ins += [(y_intra, columns_g(y_intra, early))]
    ins += [(a[k], whole(a[k])) for k in ("cs", "cum")]
    ins += [(v, columns_g(v, both)) for v in (a["xs"], z, q, inner_gain, d_skip, table)]
    wide = shape((rows, DI), BF)
    wide_f = shape((rows, DI), F32)
    row = shape((1, DI), F32)
    state = shape((nb, NS, DI), BF)
    outs = [(state, columns_g(state, early))]
    outs += [(v, columns_g(v, late)) for v in (wide, row, wide, wide, wide, wide_f, row, state)]
    scratch = [
        pltpu.VMEM((rows, DI), F32), pltpu.VMEM((rows, 2 * LANES), BF),
        pltpu.VMEM((nb * nb * len(pieces), 2 * LANES), BF), pltpu.VMEM((rows, 1), F32),
        pltpu.VMEM((rows, 1), F32),
    ]
    return call(
        functools.partial(gate_kernel, len(pieces)), 16, (2, GNW), ins, outs, scratch, VMEM_ASK,
    )


def intra_back_kernel(
    bs, cs, xt, cum, cum_t, dyr, dye, enter, normed, wo, tok, dxt, db, dc, mixed, scores, top, bottom,
    total,
):
    c = pl.program_id(0)
    nb = bs.shape[0] // CH
    low = iota((CH, LANES), 1) < HD
    keep = iota((HALF, HALF), 1) >= iota((HALF, HALF), 0)

    @pl.when(c == 0)
    def _():
        for i in range(nb):
            r = slice(i * CH, (i + 1) * CH)
            scores[i] = dot_nt(bs[r, :], cs[r, :])
        top[...] = jnp.zeros_like(top)
        bottom[...] = jnp.zeros_like(bottom)
        dc[...] = jnp.zeros_like(dc)
        total[...] = tok[...].astype(F32)

    total[...] += dot(normed[...], wo[...])

    for i in range(nb):
        r = slice(i * CH, (i + 1) * CH)
        cols = chunk_heads(cum[r, :], c * PER)
        dc[r, :] += dot_nt(dye[r, :], enter[i])
        top_sum, bottom_sum = top[i], bottom[i]
        for p in range(PER // 2):
            lanes = slice(p * LANES, (p + 1) * LANES)
            x, dy = xt[r, lanes], dyr[r, lanes]
            got = []
            for k in range(2):
                h = 2 * p + k
                col = cols[:, h : h + 1]
                row = cum_t[pl.ds(c * PER + h, 1), r]
                a, b = col[:HALF], col[HALF:]
                s, t = row[:, :HALF], row[:, HALF:]
                left = jnp.where(keep, jnp.exp(s - a), 0.0)
                right = jnp.exp(t - a)
                last = jnp.where(keep, jnp.exp(t - b), 0.0)
                dec = jnp.concatenate([left, right], axis=1)
                got.append(
                    jnp.concatenate(
                        [
                            dot((dec * scores[i, :HALF, :]).astype(BF), dy),
                            dot((last * scores[i, HALF:, HALF:]).astype(BF), dy[HALF:, :]),
                        ],
                        axis=0,
                    )
                )
                own = jnp.where(low, x, 0) if k == 0 else jnp.where(low, 0, x)
                top_sum = top_sum + dot_nt(own[:HALF, :], dy) * dec
                bottom_sum = bottom_sum + dot_nt(own[HALF:, :], dy[HALF:, :]) * last
            dxt[r, lanes] = jnp.where(low, got[0], got[1])
        top[i], bottom[i] = top_sum, bottom_sum

    @pl.when(c == NCW - 1)
    def _():
        for i in range(nb):
            r = slice(i * CH, (i + 1) * CH)
            up, down = top[i].astype(BF), bottom[i].astype(BF)
            down = jnp.concatenate([jnp.zeros((HALF, HALF), BF), down], axis=1)
            both = jnp.concatenate([up, down], axis=0)
            db[r, :] = dot(both, cs[r, :])
            dc[r, :] += dot_tn(both, bs[r, :])
        mixed[...] = total[...].astype(BF)


def run_intra_back(a, dyr, dye, enter, normed, wo, tok):
    rows = dyr.shape[0]
    nb = rows // CH

    def same(c):
        return c

    ins = [(a[k], whole(a[k])) for k in ("bs", "cs")]
    ins += [(a["xt"], columns(a["xt"], same))]
    ins += [(a[k], whole(a[k])) for k in ("cum", "cum_t")]
    ins += [(v, columns(v, same)) for v in (dyr, dye, enter, normed)]
    ins += [(wo, pl.BlockSpec((CW, DM), lambda c: (c, 0))), (tok, whole(tok))]
    full, small, mixed = shape((rows, DI), F32), shape((rows, NS), F32), shape((rows, DM), BF)
    return call(
        intra_back_kernel, 1, (NCW,), ins,
        [(full, columns(full, same))] + [(v, whole(v)) for v in (small, small, mixed)],
        [
            pltpu.VMEM((nb, CH, CH), F32), pltpu.VMEM((nb, HALF, CH), F32),
            pltpu.VMEM((nb, HALF, HALF), F32), pltpu.VMEM((rows, DM), F32),
        ],
    )


def back_kernel(n_pieces, *refs):
    info = refs[0]
    pieces = refs[1 : 1 + n_pieces]
    ends = refs[1 + n_pieces : 1 + 2 * n_pieces]
    (
        dx_intra, db_in, dc_in, xbc, slope, xs, xt, bs, raw, cum, enter, product, dyr, conv_w,
        a_log, d_skip, table, narrow, gain_part, skip_part,
        d_a, sums,
        grad, small, d_bs, heads, weights,
    ) = refs[1 + 2 * n_pieces :]
    step = pl.program_id(0)
    rows = xs.shape[0]
    nb = rows // CH
    n_all = n_pieces * nb

    @pl.when(step == 0)
    def _():
        weights[...] = carry_weights(info, clast_rows(ends, nb), nb, True)
        dt_all = softplus(raw[...])
        for i in range(nb):
            r = slice(i * CH, (i + 1) * CH)
            last = cum[(i + 1) * CH - 1 : (i + 1) * CH, :]
            small[i, 0] = jnp.concatenate(pieces2(dt_all[r, :]), axis=1)
            small[i, 1] = jnp.concatenate(pieces2(jnp.exp(last - cum[r, :])), axis=1)
            grad[i, :HALO, :] = jnp.zeros((HALO, CW), F32)
            grad[i, HALO + CH :, :] = jnp.zeros((HALO, CW), F32)
        d_bs[...] = db_in[...]
        heads[...] = jnp.zeros_like(heads)

    def put_rows(at, row):
        for j in range(row.shape[1] // LANES):
            sums[pl.ds(at + j, 1), :] = row[:, j * LANES : (j + 1) * LANES]

    def convolve_back(dacts, width):
        offset_sum = jnp.zeros((1, width), F32)
        tap_sums = [jnp.zeros((1, width), F32) for _ in range(KC)]
        all_heads = xbc[rows:, :width].astype(F32)
        head_grads = []
        for i in range(nb):
            r = slice(i * CH, (i + 1) * CH)
            dpre = dacts[i] * slope[r, :width].astype(F32)
            offset_sum = offset_sum + jnp.sum(dpre, axis=0, keepdims=True)
            grad[i, HALO : HALO + CH, :width] = dpre
            body = xbc[r, :width].astype(F32)
            head = all_heads[i * HALO : (i + 1) * HALO, :]
            total = jnp.zeros((CH, width), F32)
            total_head = jnp.zeros((HALO, width), F32)
            for lag in range(KC):
                tap = conv_w[KC - 1 - lag : KC - lag, :width]
                later = grad[i, HALO + lag : HALO + lag + CH, :width]
                later_head = grad[i, lag : lag + HALO, :width]
                total = total + tap * later
                total_head = total_head + tap * later_head
                tap_sums[KC - 1 - lag] = (
                    tap_sums[KC - 1 - lag]
                    + jnp.sum(later * body, axis=0, keepdims=True)
                    + jnp.sum(later_head * head, axis=0, keepdims=True)
                )
            d_a[r, :width] = (total * usable_of(info, i)).astype(BF)
            head_grads.append(total_head * halo_used(info, i))
        d_a[rows:, :width] = jnp.concatenate(head_grads, axis=0).astype(BF)
        for k, row in enumerate(tap_sums + [offset_sum]):
            put_rows(k * (XBC // LANES) + step * (CW // LANES), row)

    @pl.when(step < NCW)
    def _():
        wide_w = dot(weights[...], table[...])
        totals = [jnp.zeros((NS, CW), F32) for _ in range(nb)]
        for j in range(n_all):
            piece = pieces[j // nb][j % nb].astype(F32)
            for i in range(nb):
                totals[i] = totals[i] + wide_w[i * n_all + j : i * n_all + j + 1, :] * piece
        select = narrow[...]
        dacts = []
        for i in range(nb):
            r = slice(i * CH, (i + 1) * CH)
            low = totals[i].astype(BF)
            fade = jnp.sum(low.astype(F32) * enter[i].astype(F32), axis=0, keepdims=True)
            end_w = dot(small[i, 1], table[...])
            x_dt = xt[r, :].astype(F32)
            inter = end_w * dot(bs[r, :], low)
            d_bs[r, :] += dot_nt((x_dt * end_w).astype(BF), low)
            dxt = dx_intra[r, :] + inter
            flow = jnp.sum(x_dt * inter, axis=0, keepdims=True)
            hi, mid, lo = pieces3(product[r, :] - x_dt * dxt)
            heads[0, r, :] += dot(hi, select) + dot(mid, select) + dot(lo, select)
            heads[1, r, :] += dot((xs[r, :].astype(F32) * dxt).astype(BF), select)
            hi, mid, lo = pieces3(jnp.concatenate([flow, fade, jnp.zeros((6, CW), F32)], axis=0))
            heads[2, i * 8 : (i + 1) * 8, :] += dot(hi, select) + dot(mid, select) + dot(lo, select)
            dacts.append(
                dot(small[i, 0], table[...]) * dxt + d_skip[...] * dyr[r, :].astype(F32)
            )
        convolve_back(dacts, CW)
        put_rows(SUM_GAIN + step * (CW // LANES), gain_part[...])
        put_rows(SUM_SKIP + step * (CW // LANES), skip_part[...])

    @pl.when(step == NCW)
    def _():
        dacts = []
        for i in range(nb):
            r = slice(i * CH, (i + 1) * CH)
            dacts.append(jnp.concatenate([d_bs[r, :], dc_in[r, :]], axis=1))
        convolve_back(dacts, 2 * NS)
        rate = jnp.exp(a_log[...])
        anti = (iota((CH, CH), 0) <= iota((CH, CH), 1)).astype(F32).astype(BF)
        bias_sum = jnp.zeros((1, LANES), F32)
        rate_sum = jnp.zeros((1, LANES), F32)
        for i in range(nb):
            r = slice(i * CH, (i + 1) * CH)
            last = cum[(i + 1) * CH - 1 : (i + 1) * CH, :]
            flow, fade = heads[2, i * 8 : i * 8 + 1, :], heads[2, i * 8 + 1 : i * 8 + 2, :]
            parts = dot(anti, jnp.concatenate(pieces3(heads[0, r, :]), axis=1))
            d_log = parts[:, :LANES] + parts[:, LANES : 2 * LANES] + parts[:, 2 * LANES :]
            d_log = d_log + (flow + jnp.exp(last) * fade)
            start = raw[r, :]
            d_raw = (heads[1, r, :] - d_log * rate) * sigmoid(start)
            d_raw = jnp.where(iota((CH, LANES), 1) < NH, d_raw, 0.0)
            bias_sum = bias_sum + jnp.sum(d_raw, axis=0, keepdims=True)
            rate_sum = rate_sum - jnp.sum(d_log * softplus(start), axis=0, keepdims=True) * rate
            d_a[r, 2 * NS :] = d_raw.astype(BF)
        d_a[rows:, 2 * NS :] = jnp.zeros((nb * HALO, CW - 2 * NS), BF)
        put_rows(SUM_HEADS, bias_sum)
        put_rows(SUM_HEADS + 1, rate_sum)


def run_back(
    info, a, pieces, ends, dx_intra, db, dc, enter, product, dyr, conv_w, a_log, d_skip, table,
    narrow, gain_part, skip_part,
):
    rows = dyr.shape[0]
    nb = rows // CH
    ext_rows = rows + nb * HALO

    def chunk(s):
        return jnp.minimum(s, NCW - 1)

    def same(s):
        return s

    ins = [(info, in_smem())]
    ins += [(v, columns(v, chunk)) for v in pieces]
    ins += [(v, pl.BlockSpec((nb, 16, LANES), lambda s: (0, 0, DI // LANES))) for v in ends]
    ins += [(dx_intra, columns(dx_intra, chunk)), (db, whole(db)), (dc, whole(dc))]
    ins += [(a["xbc"], columns(a["xbc"], same)), (a["slope"], columns(a["slope"], same))]
    ins += [(a["xs"], columns(a["xs"], chunk)), (a["xt"], columns(a["xt"], chunk))]
    ins += [(a[k], whole(a[k])) for k in ("bs", "raw", "cum")]
    ins += [(v, columns(v, chunk)) for v in (enter, product, dyr)]
    ins += [(conv_w, columns(conv_w, same)), (a_log, whole(a_log)), (d_skip, columns(d_skip, chunk))]
    ins += [(table, columns(table, chunk))]
    ins += [(narrow, pl.BlockSpec((CW, LANES), lambda s: (chunk(s), 0)))]
    ins += [(v, columns(v, chunk)) for v in (gain_part, skip_part)]
    wide, sums = shape((ext_rows, WA), BF), shape((SUM_ROWS, LANES), F32)
    outs = [(wide, columns(wide, same)), (sums, whole(sums))]
    scratch = [
        pltpu.VMEM((nb, CH + 2 * HALO, CW), F32), pltpu.VMEM((nb, 2, CH, 2 * LANES), BF),
        pltpu.VMEM((rows, NS), F32), pltpu.VMEM((3, rows, LANES), F32),
        pltpu.VMEM((nb * nb * len(pieces), 2 * LANES), BF),
    ]
    return call(
        functools.partial(back_kernel, len(pieces)), 2, (NCW + 1,), ins, outs, scratch, VMEM_ASK,
    )


def unit(rows):
    f = rows.astype(F32)
    inv = lax.rsqrt(jnp.mean(f * f, axis=1, keepdims=True) + EPSILON)
    return f * inv, inv


def norm_back(normal_grad, rows, gain):
    u, inv = unit(rows)
    g = normal_grad * gain[None, :]
    return inv * (g - u * jnp.mean(g * u, axis=1, keepdims=True))


def shards(
    tokens, norm_gain, in_weight, conv_weight, conv_bias, dt_bias, a_log, d_skip, inner_gain,
    out_weight, block_place, seq_length, cotangent,
):
    n_head, n_shard = lax.axis_size("head"), lax.axis_size("shard")
    half = n_head // 2
    head_at, shard_at = lax.axis_index("head"), lax.axis_index("shard")
    rows = tokens.shape[0]
    nb = rows // CH
    group_blocks = nb * n_head
    k_rows = in_weight.shape[0]
    stay = (head_at // half) == (shard_at & 1)

    piece_a = jnp.concatenate(
        [in_weight[:, DI:], norm_gain[:, None], jnp.zeros((k_rows, WA - XBC - NH - 1), BF)], axis=1
    )
    numbers = jnp.concatenate([block_place, seq_length], axis=1)
    numbers_got = trade(numbers, "shard", 1)
    me = jnp.int32(0) if k_rows % 32 else shard_at.astype(jnp.int32)
    def block_tails(v):
        return v.reshape(nb, CH, DM)[:, CH - HALO :].reshape(nb * HALO, DM)

    tok_got = move_home(tokens)
    tails = jnp.where(stay, block_tails(tokens), block_tails(tok_got))

    numbers = jnp.where(stay, numbers, numbers_got)[0]
    lengths = [numbers[group_blocks + k] for k in range(seq_length.shape[1])]

    def order_from(core_at):
        ids = []
        for core in (0, 1):
            for z in range(half):
                device = (head_at % half ^ z) + (core_at ^ core) * half
                ids += [device * nb + b for b in range(nb)]
        return jnp.stack(ids)

    ids, home_order = order_from(shard_at & 1), order_from(head_at // half)
    places = jnp.sum(
        jnp.where(ids[:, None] == jnp.arange(group_blocks)[None, :], numbers[None, :group_blocks], 0),
        axis=1,
    )
    first, in_seq, begin = jnp.zeros_like(places), jnp.zeros_like(places), 0
    for length in lengths:
        first = jnp.where(places >= begin, begin, first)
        in_seq = jnp.where(places >= begin, length, in_seq)
        begin = begin + (length + CH - 1) // CH
    info = jnp.concatenate(
        [
            jnp.stack([me, stay.astype(jnp.int32)]),
            jnp.stack([places, first, in_seq], axis=1).reshape(-1),
        ]
    ).astype(jnp.int32)

    far_a = gather_far(piece_a)
    conv_weight, conv_bias, dt_bias, a_log, d_skip, inner_gain, none = after_all(
        [conv_weight, conv_bias, dt_bias, a_log, d_skip, inner_gain, jnp.int32(0)], far_a[0]
    )
    table = spread_table(none)

    def head_row(v):
        return jnp.pad(v, (0, LANES - NH))[None]

    narrow = narrow_table(none)
    gain_row = inner_gain[None]
    at = shard_at.astype(jnp.int32).reshape(1)
    taps = jnp.pad(conv_weight, ((0, 0), (0, WA - XBC)))
    rate_row = head_row(a_log)
    skip_row = jnp.repeat(d_skip, HD)[None]
    taps, rate_row, skip_row, bias_row, step_row, gain_row, narrow, table = after_all(
        [
            taps, rate_row, skip_row, jnp.pad(conv_bias, (0, WA - XBC))[None], head_row(dt_bias),
            gain_row, narrow, table,
        ]
    )
    prepared = [taps, rate_row, skip_row, bias_row, step_row, gain_row, narrow, table]
    parts_a = gather_near(piece_a, far_a)
    if k_rows % 32:
        parts_a = [(join_pieces(parts_a).reshape(DM, WA), 0)]
    z_own, o_own = after_all([in_weight[:, :DI], out_weight], numbers_got)
    piece_zo = jnp.concatenate([z_own, o_own[:k_rows], o_own[k_rows:]], axis=1)
    far_zo = gather_far(piece_zo)
    tails = group_spread(after(tails, info, *[v for v, _ in parts_a[1:]], *prepared))
    cot_got = move_home(after(cotangent, *tails))
    a = run_project(info, parts_a, tails, tokens, tok_got, taps, bias_row, step_row, rate_row, table)
    wa, tok, normal = a["wa"], a["tok"], a["normal"]
    state_by_head = head_pieces(a["states"])
    state_by_core = trade(a["states"], "shard", 1)
    y_intra = run_intra(a)
    parts_zo = gather_near(after(piece_zo, y_intra), after_all(far_zo, y_intra))
    if k_rows % 32:
        zo = join_pieces(parts_zo)
        wz, wo = zo[:, :, :DI].reshape(DM, DI), zo[:, :, DI:]
        wo = wo.reshape(n_shard, k_rows, 2, DM).swapaxes(1, 2).reshape(DI, DM)
        cot = jnp.where(stay, cotangent, cot_got)
        z, q = dot(normal[:rows], wz).astype(BF), dot_nt(cot, wo).astype(BF)
    else:
        cot_got = after(cot_got, y_intra)
        z, q, cot, wz, wo = run_open(
            at, parts_zo, normal, cotangent, cot_got, stay.astype(jnp.int32).reshape(1)
        )
    state_by_head = [after(v, z) for v in state_by_head]
    all_states = (
        [a["states"]] + state_by_head + [state_by_core] + [trade(v, "shard", 1) for v in state_by_head]
    )
    enter, normed, gain_part, dz, dyr, dye, product, skip_part, d_enter = run_gate(
        info, a, all_states, y_intra, z, q, gain_row, skip_row, table
    )
    enter_by_head = head_pieces(d_enter)
    enter_by_core = trade(d_enter, "shard", 1)
    if k_rows % 32:
        z_term = dot_tn(normal[:rows], dz).astype(BF).reshape(n_shard, k_rows, DI)
        out_term = dot_tn(normed, cot).astype(BF).reshape(n_shard, 2, k_rows, DM)
        zo_keep, zo_give = core_give([z_term, out_term[:, 0], out_term[:, 1]])
        zo_give = [zo_give[p] for p in range(n_shard // 2)]
    else:
        zo_keep, zo_give = run_terms(at, a["normal_t"], dz, normed, cot, n_shard)
    zo_got = [trade(v, "shard", 1) for v in zo_give]
    dx_intra, db, dc, mixed = run_intra_back(a, after(dyr, *zo_give), dye, enter, normed, wo, tok)
    arrived = after_all(enter_by_head + zo_got, dx_intra)
    enter_by_head, zo_got = arrived[: len(enter_by_head)], arrived[len(enter_by_head) :]
    zo_pairs = chip_pairs(zo_keep, jnp.stack(zo_got))
    zo_far = chip_send(zo_pairs)
    enter_by_head = [after(v, *zo_pairs) for v in enter_by_head]
    all_enter = (
        [d_enter] + enter_by_head + [enter_by_core] + [trade(v, "shard", 1) for v in enter_by_head]
    )
    mixed_got = move_home(after(mixed, all_enter[-1]))
    d_a_all, small = run_back(
        info, a, all_enter, all_states, dx_intra, db, dc, enter, product, dyr, taps,
        rate_row, skip_row, table, narrow, gain_part, skip_part,
    )
    d_a_all = after(d_a_all, mixed_got)
    a_term = dot_tn(normal, d_a_all).astype(BF).reshape(n_shard, k_rows, WA)
    a_keep, a_give = core_give([a_term])
    a_got = trade(a_give, "shard", 1)

    small_got = trade(after(small, a_give), "shard", 1)
    zo_own = chip_sum(zo_pairs[0], after_all(zo_far, a_give))
    zo_keep, zo_give = head_split(zo_own)
    zo_got = trade(zo_give, "head", 1)
    d_a_all, dz, tok, tok_halo, wa = after_all(
        [d_a_all, dz, tok, a["tok_halo"], wa], a_give, zo_give
    )
    gain = wa[:, XBC + NH].astype(F32)
    from_a = dot_nt(d_a_all, wa)
    normal_grad = dot_nt(dz, wz) + from_a[:rows]
    token_grad = (cot.astype(F32) + norm_back(normal_grad, tok, gain)).astype(BF)

    a_got, small_got = after_all([a_got, small_got], token_grad)
    if k_rows % 32:
        parts = split2((small + small_got).reshape(k_rows, -1))
        a_pairs = [jnp.concatenate([v, parts], axis=1) for v in chip_pairs(a_keep, a_got)]
    else:
        a_pairs = run_pair_small(at, a_term, a_got, small, small_got)
    a_far = chip_send(a_pairs)
    token_got = move_home(after(token_grad, a_pairs[0]))
    zo_half = head_add(zo_keep, after(zo_got, a_pairs[0]))
    zo_got = trade(zo_half, "head", 2)
    halo_part = norm_back(after(from_a, a_pairs[0])[rows:], tok_halo, gain)
    halo_part = halo_part.reshape(nb, HALO, DM)[:, HALO - KC :].astype(BF).reshape(k_rows, -1)
    halos = [halo_part, trade(halo_part, "shard", 1)]
    *a_far, token_got, halos[1] = after_all(a_far + [token_got, halos[1]])
    cut, edge = WA // 2, WA // 2 + 2 * SUM_ROWS * LANES // k_rows
    if k_rows % 32:
        a_own = chip_sum(a_pairs[0][:, :WA], [v[:, :WA] for v in a_far])
        sums = [join2(v[:, WA:]) for v in [a_pairs[0]] + a_far]
        while len(sums) > 1:
            sums = [sums[k] + sums[k + 1] for k in range(0, len(sums), 2)]
        small = sums[0]
        total, a_give = head_split(a_own)
        parts = split2(small)
        sent = jnp.concatenate([a_give, parts] + (halos if half > 1 else []), axis=1)
        small = join2(parts)
    else:
        odd = (head_at % 2).astype(jnp.int32).reshape(1)
        sent, total, small = run_chip_sum(odd, [a_pairs[0]] + a_far, halos)
    own_total = total = total.astype(F32)
    bits = [b for b in (1, 2, 4, 8, 16) if b < n_head]
    for bit in bits:
        if bit > 1:
            a_give = total.astype(BF)
            total = a_give.astype(F32)
            parts = split2(small)
            small = join2(parts)
            sent = jnp.concatenate([a_give, parts] + (halos if bit < half else []), axis=1)
        sent = trade(sent, "head", bit)
        if bit == 1:
            sent, zo_got = after_all([sent, zo_got])
            zo_half = head_add(zo_half, zo_got)
            for more in bits[2:]:
                zo_half = head_add(zo_half, trade(zo_half, "head", more))
            zo_other = trade(zo_half, "head", 1)
        if bit < half:
            halos = halos + jnp.split(sent[:, edge:], len(halos), axis=1)
        total = total + sent[:, :cut].astype(F32)
        small = small + join2(sent[:, cut:edge])
    low = total.astype(BF)
    other = trade(low, "head", 1)
    halos, small, zo_other = after_all([jnp.concatenate(halos, axis=1), small, zo_other], low)
    zo_grad = head_join(zo_half, zo_other).astype(F32)
    halos = jnp.where(stay, halos, move_home(halos))
    halos = jnp.split(halos, group_blocks // nb, axis=1)
    other = after(other, *halos)
    a_grad = head_join(low, other).astype(F32)
    small = small.reshape(SUM_ROWS, LANES)

    all_halo = jnp.concatenate(halos[0::2] + halos[1::2]).reshape(group_blocks, KC, DM).astype(F32)
    own_numbers = jnp.concatenate([block_place, seq_length], axis=1)[0]
    own_places = jnp.sum(
        jnp.where(
            home_order[:, None] == jnp.arange(group_blocks), own_numbers[None, :group_blocks], 0
        ),
        axis=1,
    )
    home_ids = head_at * nb + jnp.arange(nb)
    home_places = jnp.sum(
        jnp.where(
            home_ids[:, None] == jnp.arange(group_blocks), own_numbers[None, :group_blocks], 0
        ),
        axis=1,
    )
    goes_on, begin = home_places < 0, 0
    for k in range(seq_length.shape[1]):
        end = begin + (own_numbers[group_blocks + k] + CH - 1) // CH
        goes_on = goes_on | ((home_places >= begin) & (home_places + 1 < end))
        begin = end
    is_next = (own_places[None, :] == home_places[:, None] + 1) & goes_on[:, None]
    halo_back = jnp.sum(jnp.where(is_next[:, :, None, None], all_halo[None], 0.0), axis=1)
    token_grad = jnp.where(stay, token_grad, token_got).reshape(nb, CH, DM)
    token_grad = token_grad.at[:, CH - KC :].set(
        (token_grad[:, CH - KC :].astype(F32) + halo_back).astype(BF)
    ).reshape(rows, DM)
    mixed = jnp.where(stay, mixed, after(mixed_got, own_total))

    in_grad = jnp.concatenate([zo_grad[:, :DI], a_grad[:, : XBC + NH]], axis=1)
    out_grad = jnp.concatenate([zo_grad[:, DI : DI + DM], zo_grad[:, DI + DM :]], axis=0)
    gain_grad = jnp.sum(in_grad * in_weight.astype(F32), axis=1) / norm_gain.astype(F32)

    return (
        mixed, token_grad, gain_grad, in_grad, small[: KC * XBC // LANES].reshape(KC, XBC),
        small[KC * XBC // LANES : SUM_GAIN].reshape(XBC), small[SUM_HEADS, :NH],
        small[SUM_HEADS + 1, :NH], jnp.sum(small[SUM_SKIP:SUM_HEADS].reshape(NH, HD), axis=1),
        small[SUM_GAIN:SUM_SKIP].reshape(DI), out_grad,
    )


def solution(mesh):
    return jax.shard_map(
        shards,
        mesh=mesh,
        in_specs=(
            P(("head", "shard"), None), P("shard"), P("shard", None), P(), P(), P(), P(), P(), P(),
            P("shard", None), P("shard", None), P("shard", None), P(("head", "shard"), None),
        ),
        out_specs=(
            P(("head", "shard"), None), P(("head", "shard"), None), P("shard"), P("shard", None),
            P(), P(), P(), P(), P(), P(), P("shard", None),
        ),
        check_vma=False,
    )
```

```python
import functools

import jax
import jax.numpy as jnp
from jax import lax
from jax.experimental import pallas as pl
from jax.experimental.pallas import tpu as pltpu
from jax.sharding import PartitionSpec as P

NH = 24
HD = 64
NS = 128
KC = 4
CH = 256
DI = 1536
DM = 768
XBC = DI + 2 * NS
WA = 1920
HALO = 8
EPSILON = 1e-05
F32 = jnp.float32
BF = jnp.bfloat16
LANES = 128
CW = 384
NCW = DI // CW
VMEM_ASK = 56 * 2**20
VMEM_ROOM = 56 * 2**20
VMEM_LESS = 44 * 2**20
VMEM_LITTLE = 24 * 2**20
COST_SCALE = 0.4


def trade(value, axis, bit):
    size = lax.axis_size(axis)
    return lax.ppermute(value, axis, [(i, i ^ bit) for i in range(size)])


def after(value, *others):
    return lax.optimization_barrier((value,) + others)[0]


def move_home(value):
    n_head, n_shard = lax.axis_size("head"), lax.axis_size("shard")
    half = n_head // 2
    pairs = []
    for h in range(n_head):
        for s in range(n_shard):
            upper, core = h // half, s & 1
            if upper != core:
                there = (h % half + core * half) * n_shard + (s - core + upper)
                pairs.append((h * n_shard + s, there))
    return lax.ppermute(value, ("head", "shard"), pairs)


def swap_home(value, stay):
    return jnp.where(stay, value, move_home(value))


def group_spread(value):
    n_head, n_shard = lax.axis_size("head"), lax.axis_size("shard")
    pieces = [value]
    for core in (0, 1):
        for low in range(n_head // 2):
            if core or low:
                pairs = [
                    (h * n_shard + s, (h ^ low) * n_shard + (s ^ core))
                    for h in range(n_head)
                    for s in range(n_shard)
                ]
                pieces.append(lax.ppermute(value, ("head", "shard"), pairs))
    return pieces


def group_gather(value):
    half = lax.axis_size("head") // 2
    pieces = [value]
    bit = 1
    while bit < half:
        pieces = pieces + [trade(v, "head", bit) for v in pieces]
        bit *= 2
    return pieces + [trade(v, "shard", 1) for v in pieces]


def gather_far(piece):
    bits = range(2, lax.axis_size("shard"), 2)
    return [trade(piece, "shard", bit) for bit in sorted(bits, reverse=True)]


def gather_near(piece, far):
    held = [piece] + far
    offsets = [0] + sorted(range(2, lax.axis_size("shard"), 2), reverse=True)
    near = [trade(v, "shard", 1) for v in held]
    return list(zip(held + near, offsets + [k ^ 1 for k in offsets]))


def join_pieces(parts):
    me, n_shard = lax.axis_index("shard"), lax.axis_size("shard")
    joined = jnp.zeros((n_shard,) + parts[0][0].shape, parts[0][0].dtype)
    for v, k in parts:
        joined = lax.dynamic_update_slice(joined, v[None], (me ^ k, 0, 0))
    return joined


def head_pieces(value):
    pieces = [value]
    bit = 1
    while bit < lax.axis_size("head") // 2:
        pieces = pieces + [trade(v, "head", bit) for v in pieces]
        bit *= 2
    return pieces[1:]


def core_give(blocks):
    n_shard = lax.axis_size("shard")
    core = lax.axis_index("shard") % 2

    def half(which):
        parts = []
        for v in blocks:
            split = v.reshape((n_shard // 2, 2) + v.shape[1:])
            parts.append(lax.dynamic_index_in_dim(split, which, 1, False))
        return jnp.concatenate(parts, axis=2) if len(parts) > 1 else parts[0]

    return half(core), half(1 - core)


def chip_pairs(keep, got):
    pair = (keep.astype(F32) + got.astype(F32)).astype(BF)
    chip = lax.axis_index("shard") // 2
    return [lax.dynamic_index_in_dim(pair, chip ^ k, 0, False) for k in range(pair.shape[0])]


def after_all(values, *others):
    return list(lax.optimization_barrier((*values, *others)))[: len(values)]


def chip_send(pairs):
    return [trade(v, "shard", 2 * k) for k, v in enumerate(pairs) if k]


def chip_sum(own, got):
    total = own.astype(F32)
    for v in got:
        total = total + v.astype(F32)
    return total.astype(BF)


def split2(v):
    high = lax.reduce_precision(v, 8, 7)
    return jnp.concatenate([high.astype(BF), (v - high).astype(BF)], axis=1)


def join2(parts):
    high, low = jnp.split(parts, 2, axis=1)
    return high.astype(F32) + low.astype(F32)


def head_split(value):
    cut = value.shape[1] // 2
    odd = lax.axis_index("head") % 2
    return [lax.dynamic_slice_in_dim(value, at * cut, cut, 1) for at in (odd, 1 - odd)]


def head_add(keep, got):
    return (keep.astype(F32) + got.astype(F32)).astype(BF)


def head_join(half, other):
    odd = lax.axis_index("head") % 2
    return jnp.concatenate([jnp.where(odd, other, half), jnp.where(odd, half, other)], axis=1)


def dot(a, b):
    return jnp.dot(a, b, preferred_element_type=F32)


def dot_nt(a, b):
    return lax.dot_general(a, b, (((1,), (1,)), ((), ())), preferred_element_type=F32)


def dot_tn(a, b):
    return lax.dot_general(a, b, (((0,), (0,)), ((), ())), preferred_element_type=F32)


def spread_table(none):
    row = jnp.arange(2 * LANES)[:, None] % LANES + none
    return (row == jnp.arange(DI)[None, :] // HD).astype(BF)


def narrow_table(none):
    return (jnp.arange(DI)[:, None] // HD == jnp.arange(LANES)[None, :] + none).astype(BF)


def pieces2(v):
    hi = v.astype(BF)
    return hi, (v - hi.astype(F32)).astype(BF)


def pieces3(v):
    hi = v.astype(BF)
    rest = v - hi.astype(F32)
    mid = rest.astype(BF)
    return hi, mid, (rest - mid.astype(F32)).astype(BF)


def softplus(v):
    return jnp.maximum(v, 0.0) + jnp.log1p(jnp.exp(-jnp.abs(v)))


sigmoid = jax.nn.sigmoid


def shape(dims, dtype):
    return jax.ShapeDtypeStruct(dims, dtype)


def whole(arr):
    return pl.BlockSpec(arr.shape, lambda *g: (0,) * len(arr.shape))


def columns(arr, at, width=None):
    dims = arr.shape[:-1] + (width or CW,)
    return pl.BlockSpec(dims, lambda *g: (0,) * (len(dims) - 1) + (at(*g),))


def in_hbm():
    return pl.BlockSpec(memory_space=pl.ANY)


def in_smem():
    return pl.BlockSpec(memory_space=pltpu.SMEM)


def call(kernel, micros, grid, ins, outs, scratch, room=VMEM_ROOM):
    return pl.pallas_call(
        kernel,
        grid=grid,
        out_shape=[o for o, _ in outs],
        in_specs=[s for _, s in ins],
        out_specs=[s for _, s in outs],
        scratch_shapes=scratch,
        compiler_params=pltpu.CompilerParams(vmem_limit_bytes=room),
        cost_estimate=pl.CostEstimate(
            flops=1, bytes_accessed=int(micros * COST_SCALE * 3.7e6), transcendentals=0
        ),
    )(*[a for a, _ in ins])


def iota(dims, axis):
    return lax.broadcasted_iota(jnp.int32, dims, axis)


def place_of(info, q):
    return info[2 + 3 * q]


def first_of(info, q):
    return info[3 + 3 * q]


def usable_of(info, i):
    begin = (place_of(info, i) - first_of(info, i)) * CH
    return (iota((CH, 1), 0) + begin < info[4 + 3 * i]).astype(F32)


def halo_used(info, i):
    has_prev = place_of(info, i) > first_of(info, i)
    return (iota((HALO, 1), 0) + jnp.where(has_prev, 0, -HALO) > HALO - KC).astype(F32)


def clast_rows(refs, nb):
    rows = []
    for ref in refs:
        for b in range(nb):
            part = ref[b].astype(F32)
            rows.append(part[0:1, :] + part[1:2, :] + part[2:3, :])
    return rows


def carry_weights(info, ends, nb, into):
    n_all = len(ends)
    row = iota((n_all, 1), 0)
    place = jnp.zeros((n_all, 1), jnp.int32)
    first = jnp.zeros((n_all, 1), jnp.int32)
    for j in range(n_all):
        place = jnp.where(row == j, place_of(info, j), place)
        first = jnp.where(row == j, first_of(info, j), first)
    parts = []
    for i in range(nb):
        own = place_of(info, i)
        total = jnp.zeros((n_all, LANES), F32)
        for k in range(n_all):
            at = place_of(info, k)
            if into:
                between = (place > at) & (at > own)
            else:
                between = (place < at) & (at < own)
            total = total + jnp.where(between, ends[k], 0.0)
        if into:
            reach = (first <= own) & (place > own)
        else:
            reach = (place >= first_of(info, i)) & (place < own)
        parts.append(jnp.where(reach, jnp.exp(total), 0.0))
    return jnp.concatenate(pieces2(jnp.concatenate(parts, axis=0)), axis=1)


def normal_rows(rows, gain):
    f = rows.astype(F32)
    inv = lax.rsqrt(jnp.sum(f * f, axis=1, keepdims=True) / DM + EPSILON)
    return (f * inv * gain).astype(BF)


def project_kernel(layout, n_halo, *refs):
    info = refs[0]
    pieces = refs[1 : 1 + len(layout)]
    halos = refs[1 + len(layout) : 1 + len(layout) + n_halo]
    (
        tok_own, tok_got, conv_w, conv_b, dt_bias, a_log, table,
        wa_out, tok_out, tok_halo, normal_out, normal_t_out, xbc, slope, xs, xt, bs_out, cs_out,
        raw_out, cum_out, cum_t_out, states,
        wa, ext, small, sems, out_sems, tok, normal, normal_t, bs, cs, raw, cum, cum_t,
    ) = refs[1 + len(layout) + n_halo :]
    step = pl.program_id(0)
    rows = tok_own.shape[0]
    nb = rows // CH
    me = info[0]

    def project(at, width):
        proj = dot(normal[...], wa[:, pl.ds(at, width)]).astype(BF).astype(F32)
        acts, heads = [], []
        for i in range(nb):
            head = proj[rows + i * HALO : rows + (i + 1) * HALO, :] * halo_used(info, i)
            body = proj[i * CH : (i + 1) * CH, :] * usable_of(info, i)
            heads.append(head)
            ext[i, :HALO, :width] = head
            ext[i, HALO:, :width] = body
            xbc[i * CH : (i + 1) * CH, :width] = body.astype(BF)
            pre = conv_b[:, pl.ds(at, width)]
            for lag in range(KC):
                tap = conv_w[KC - 1 - lag : KC - lag, pl.ds(at, width)]
                pre = pre + tap * ext[i, HALO - lag : HALO - lag + CH, :width]
            sg = sigmoid(pre)
            act = pre * sg
            slope[i * CH : (i + 1) * CH, :width] = (sg + act * (1.0 - sg)).astype(BF)
            acts.append(act)
        xbc[rows:, :width] = jnp.concatenate(heads, axis=0).astype(BF)
        return acts

    def leaving():
        moves = [(wa, wa_out), (tok, tok_out), (normal, normal_out), (normal_t, normal_t_out)]
        moves += [(bs, bs_out), (cs, cs_out), (raw, raw_out), (cum, cum_out), (cum_t, cum_t_out)]
        return [pltpu.make_async_copy(v, there, out_sems.at[n]) for n, (v, there) in enumerate(moves)]

    @pl.when(step == 0)
    def _():
        def copy_of(n):
            at = pl.multiple_of((me ^ layout[n]) * pieces[n].shape[0], 16)
            return pltpu.make_async_copy(
                pieces[n], wa.at[pl.ds(at, pieces[n].shape[0]), :], sems.at[n]
            )

        for n in range(len(layout)):
            copy_of(n).start()
        stay = info[1] > 0
        tok[...] = jnp.where(stay, tok_own[...], tok_got[...])
        found = []
        for i in range(nb):
            own, has_prev = place_of(info, i), place_of(info, i) > first_of(info, i)
            total = jnp.zeros((HALO, DM), F32)
            for o in range(n_halo):
                part = halos[o][...].astype(F32)
                for b in range(nb):
                    hit = (place_of(info, o * nb + b) == own - 1) & has_prev
                    total = total + jnp.where(hit, part[b * HALO : (b + 1) * HALO, :], 0.0)
            found.append(total)
        tok_halo[...] = jnp.concatenate(found, axis=0).astype(BF)
        for n in range(len(layout)):
            copy_of(n).wait()
        for copy in leaving()[:2]:
            copy.start()
        gain = wa[:, XBC : XBC + LANES].astype(F32).T[NH : NH + 1, :]
        normal[:rows, :] = normal_rows(tok[...], gain)
        normal_t[...] = normal[:rows, :].T
        normal[rows:, :] = normal_rows(tok_halo[...], gain)
        for i, act in enumerate(project(DI, 2 * NS)):
            bs[i * CH : (i + 1) * CH, :] = act[:, :NS].astype(BF)
            cs[i * CH : (i + 1) * CH, :] = act[:, NS:].astype(BF)
        xbc[:, 2 * NS :] = jnp.zeros((xbc.shape[0], CW - 2 * NS), BF)
        slope[:, 2 * NS :] = jnp.zeros((rows, CW - 2 * NS), BF)
        first = dot(normal[:rows, :], wa[:, XBC : XBC + LANES]).astype(BF).astype(F32) + dt_bias[...]
        raw[...] = first
        dt_all = softplus(first)
        rate = jnp.exp(a_log[...])
        causal = (iota((CH, CH), 0) >= iota((CH, CH), 1)).astype(F32).astype(BF)
        states[:, :, DI:] = jnp.zeros((nb, NS, LANES), BF)
        for i in range(nb):
            dt = dt_all[i * CH : (i + 1) * CH, :]
            parts = dot(causal, jnp.concatenate(pieces3(-dt * rate), axis=1))
            run = parts[:, :LANES] + parts[:, LANES : 2 * LANES] + parts[:, 2 * LANES :]
            cum[i * CH : (i + 1) * CH, :] = run
            cum_t[:, i * CH : (i + 1) * CH] = run.T
            last = run[CH - 1 : CH, :]
            ends = jnp.concatenate(pieces3(last) + (jnp.zeros((13, LANES), BF),), axis=0)
            states[i, :16, DI:] = ends
            small[i, 0] = jnp.concatenate(pieces2(dt), axis=1)
            small[i, 1] = jnp.concatenate(pieces2(jnp.exp(last - run) * dt), axis=1)
        for copy in leaving()[2:]:
            copy.start()

    @pl.when(step > 0)
    def _():
        at = pl.multiple_of((step - 1) * CW, CW)
        for i, act in enumerate(project(at, CW)):
            r = slice(i * CH, (i + 1) * CH)
            xs[r, :] = act.astype(BF)
            xt[r, :] = (act * dot(small[i, 0], table[...])).astype(BF)
            weighted = (act * dot(small[i, 1], table[...])).astype(BF)
            states[i, :, pl.ds(at, CW)] = dot_tn(bs[r, :], weighted).astype(BF)

    @pl.when(step == NCW)
    def _():
        for copy in leaving():
            copy.wait()


def run_project(info, parts, halos, tok_own, tok_got, conv_w, conv_b, dt_bias, a_log, table):
    rows = tok_own.shape[0]
    nb = rows // CH
    ext_rows = rows + nb * HALO
    layout = [offset for _, offset in parts]

    def before(s):
        return jnp.maximum(s - 1, 0)

    def tail_first(s):
        return jnp.where(s == 0, NCW, s - 1)

    ins = [(info, in_smem())] + [(v, in_hbm()) for v, _ in parts]
    ins += [(v, whole(v)) for v in halos]
    ins += [(v, whole(v)) for v in (tok_own, tok_got, conv_w, conv_b, dt_bias, a_log)]
    ins += [(table, columns(table, before))]
    outs = {
        "wa": (shape((DM, WA), BF), in_hbm()),
        "tok": (shape((rows, DM), BF), in_hbm()),
        "tok_halo": (shape((nb * HALO, DM), BF), whole),
        "normal": (shape((ext_rows, DM), BF), in_hbm()),
        "normal_t": (shape((DM, rows), BF), in_hbm()),
        "xbc": (shape((ext_rows, WA), BF), lambda v: columns(v, tail_first)),
        "slope": (shape((rows, WA), BF), lambda v: columns(v, tail_first)),
        "xs": (shape((rows, DI), BF), lambda v: columns(v, before)),
        "xt": (shape((rows, DI), BF), lambda v: columns(v, before)),
        "bs": (shape((rows, NS), BF), in_hbm()),
        "cs": (shape((rows, NS), BF), in_hbm()),
        "raw": (shape((rows, LANES), F32), in_hbm()),
        "cum": (shape((rows, LANES), F32), in_hbm()),
        "cum_t": (shape((LANES, rows), F32), in_hbm()),
        "states": (shape((nb, NS, DI + LANES), BF), whole),
    }
    out_list = [(o, s(o) if callable(s) else s) for o, s in outs.values()]
    scratch = [
        pltpu.VMEM((DM, WA), BF), pltpu.VMEM((nb, HALO + CH, CW), F32),
        pltpu.VMEM((nb, 2, CH, 2 * LANES), BF), pltpu.SemaphoreType.DMA((len(parts),)),
        pltpu.SemaphoreType.DMA((9,)),
    ]
    kept = ("tok", "normal", "normal_t", "bs", "cs", "raw", "cum", "cum_t")
    scratch += [pltpu.VMEM(outs[k][0].shape, outs[k][0].dtype) for k in kept]
    got = call(
        functools.partial(project_kernel, layout, len(halos)), 14, (NCW + 1,), ins, out_list, scratch, VMEM_ASK,
    )
    return dict(zip(outs, got))


SUM_GAIN = (KC + 1) * XBC // LANES
SUM_SKIP = SUM_GAIN + DI // LANES
SUM_HEADS = SUM_SKIP + DI // LANES
SUM_ROWS = SUM_HEADS + 2
OUT_ROWS = CW // 4
PER = CW // HD
HALF = CH // 2


def chunk_heads(cum, first):
    return pltpu.roll(cum, lax.rem(LANES - first, LANES), axis=1)


def intra_kernel(bs, cs, xt, cum, cum_t, out, scores):
    c = pl.program_id(0)
    nb = bs.shape[0] // CH
    low = iota((CH, LANES), 1) < HD
    keep = iota((HALF, HALF), 0) >= iota((HALF, HALF), 1)

    @pl.when(c == 0)
    def _():
        for i in range(nb):
            r = slice(i * CH, (i + 1) * CH)
            scores[i] = dot_nt(cs[r, :], bs[r, :])

    for i in range(nb):
        r = slice(i * CH, (i + 1) * CH)
        cols = chunk_heads(cum[r, :], c * PER)
        for p in range(PER // 2):
            lanes = slice(p * LANES, (p + 1) * LANES)
            both = xt[r, lanes]
            got = []
            for k in range(2):
                h = 2 * p + k
                col = cols[:, h : h + 1]
                row = cum_t[pl.ds(c * PER + h, 1), r]
                a, b = col[:HALF], col[HALF:]
                s, t = row[:, :HALF], row[:, HALF:]
                upper = jnp.where(keep, jnp.exp(a - s), 0.0) * scores[i, :HALF, :HALF]
                left = jnp.exp(b - s) * scores[i, HALF:, :HALF]
                right = jnp.where(keep, jnp.exp(b - t), 0.0) * scores[i, HALF:, HALF:]
                lower = jnp.concatenate([left.astype(BF), right.astype(BF)], axis=1)
                got.append(
                    jnp.concatenate([dot(upper.astype(BF), both[:HALF, :]), dot(lower, both)], axis=0)
                )
            out[r, lanes] = jnp.where(low, got[0], got[1])


def run_intra(a):
    rows = a["bs"].shape[0]
    nb = rows // CH
    ins = [(a[k], whole(a[k])) for k in ("bs", "cs")]
    ins += [(a["xt"], columns(a["xt"], lambda c: c))]
    ins += [(a[k], whole(a[k])) for k in ("cum", "cum_t")]
    out = shape((rows, DI), F32)
    return call(
        intra_kernel, 6, (NCW,), ins, [(out, columns(out, lambda c: c))],
        [pltpu.VMEM((nb, CH, CH), F32)],
    )[0]


OW = 768
ONW = DI // OW


def open_kernel(layout, at, *refs):
    pieces = refs[: len(layout)]
    normal, cot_own, cot_got, stay, z, q, cot, wz_out, wo_out, wz, wo, sems, out_sems = refs[
        len(layout) :
    ]
    c = pl.program_id(0)
    k_rows = pieces[0].shape[0]

    def copies(n):
        shard = at[0] ^ layout[n]
        parts = [(wz, shard * k_rows, slice(0, DI))]
        for j in range(2):
            lanes = slice(DI + j * DM, DI + (j + 1) * DM)
            parts.append((wo, (2 * shard + j) * k_rows, lanes))
        return [
            pltpu.make_async_copy(
                pieces[n].at[:, lanes],
                ref.at[pl.ds(pl.multiple_of(begin, 16), k_rows), :],
                sems.at[3 * n + k],
            )
            for k, (ref, begin, lanes) in enumerate(parts)
        ]

    def leaving():
        return [
            pltpu.make_async_copy(wz, wz_out, out_sems.at[0]),
            pltpu.make_async_copy(wo, wo_out, out_sems.at[1]),
        ]

    @pl.when(c == 0)
    def _():
        for n in range(len(layout)):
            for copy in copies(n):
                copy.start()
        cot[...] = jnp.where(stay[0] > 0, cot_own[...], cot_got[...])
        for n in range(len(layout)):
            for copy in copies(n):
                copy.wait()
        for copy in leaving():
            copy.start()

    here = pl.ds(pl.multiple_of(c * OW, OW), OW)
    z[...] = dot(normal[...], wz[:, here]).astype(BF)
    q[...] = dot_nt(cot[...], wo[here, :]).astype(BF)

    @pl.when(c == ONW - 1)
    def _():
        for copy in leaving():
            copy.wait()


def run_open(at, parts, normal, cot_own, cot_got, stay):
    rows = cot_own.shape[0]
    layout = [offset for _, offset in parts]
    ins = [(at, in_smem())] + [(v, in_hbm()) for v, _ in parts]
    ins += [(normal, pl.BlockSpec((rows, DM), lambda c: (0, 0)))]
    ins += [(cot_own, whole(cot_own)), (cot_got, whole(cot_got)), (stay, in_smem())]
    wide = shape((rows, DI), BF)
    outs = [(wide, columns(wide, lambda c: c, OW))] * 2
    outs += [(v, whole(v)) for v in (shape((rows, DM), BF),)]
    outs += [(v, in_hbm()) for v in (shape((DM, DI), BF), shape((DI, DM), BF))]
    return call(
        functools.partial(open_kernel, layout), 1, (ONW,), ins, outs,
        [
            pltpu.VMEM((DM, DI), BF), pltpu.VMEM((DI, DM), BF),
            pltpu.SemaphoreType.DMA((3 * len(parts),)), pltpu.SemaphoreType.DMA((2,)),
        ],
        VMEM_LESS,
    )


def terms_kernel(at, normal_t, dz, normed, cot, keep, *refs):
    *give, z_part, o_part = refs
    p = pl.program_id(0)
    unit = give[0].shape[0]
    even = at[0] % 2 == 0
    z_part[...] = dot(normal_t[...], dz[...])
    o_part[...] = dot_tn(normed[...], cot[...])

    def rows_of(which):
        parts = [(z_part[which * unit : (which + 1) * unit, :], slice(0, DI))]
        for j in range(2):
            rows = o_part[(2 * which + j) * unit : (2 * which + j + 1) * unit, :]
            parts.append((rows, slice(DI + j * DM, DI + (j + 1) * DM)))
        return parts

    for (first, lanes), (second, _) in zip(rows_of(0), rows_of(1)):
        keep[0, :, lanes] = jnp.where(even, first, second).astype(BF)
        other = jnp.where(even, second, first).astype(BF)
        for k, ref in enumerate(give):

            @pl.when(p == k)
            def _(ref=ref, other=other, lanes=lanes):
                ref[:, lanes] = other


def run_terms(at, normal_t, dz, normed, cot, n_shard):
    rows = dz.shape[0]
    n, unit = n_shard // 2, DM // n_shard
    give = shape((unit, DI + 2 * DM), BF)
    keep = shape((n,) + give.shape, BF)
    got = call(
        terms_kernel, 1, (n,),
        [
            (at, in_smem()), (normal_t, pl.BlockSpec((2 * unit, rows), lambda p: (p, 0))),
            (dz, whole(dz)), (normed, columns(normed, lambda p: p, 4 * unit)), (cot, whole(cot)),
        ],
        [(keep, pl.BlockSpec((1,) + give.shape, lambda p: (p, 0, 0)))] + [(give, whole(give))] * n,
        [pltpu.VMEM((2 * unit, DI), F32), pltpu.VMEM((4 * unit, DM), F32)],
    )
    return got[0], list(got[1:])


def pair_small_kernel(at, term, got, small, small_got, *outs):
    cols = got.shape[-1]
    chip, core = at[0] // 2, at[0] % 2
    total = small[...] + small_got[...]
    parts = jnp.concatenate(pieces2(total), axis=1)
    for k, out in enumerate(outs):
        kept = term[2 * (chip ^ k) + core]
        out[:, :cols] = (kept.astype(F32) + got[chip ^ k].astype(F32)).astype(BF)
        out[:, cols:] = parts


def run_pair_small(at, term, got, small, small_got):
    n, rows, cols = got.shape
    out = shape((rows, cols + 2 * small.shape[1]), BF)
    args = [term, got, small, small_got]
    return call(
        pair_small_kernel, 1, (1,), [(at, in_smem())] + [(v, whole(v)) for v in args],
        [(out, whole(out))] * n, [], VMEM_LITTLE,
    )


def chip_sum_kernel(odd, *refs):
    n = len(refs) - 5
    terms, halos, (sent, keep, small_sum) = refs[:n], refs[n : n + 2], refs[n + 2 :]
    total = terms[0][:, :WA].astype(F32)
    for term in terms[1:]:
        total = total + term[:, :WA].astype(F32)
    low = total.astype(BF)
    cut = WA // 2
    right_kept = odd[0] > 0
    sent[:, :cut] = jnp.where(right_kept, low[:, :cut], low[:, cut:])
    keep[...] = jnp.where(right_kept, low[:, cut:], low[:, :cut])
    sums = [t[:, WA : WA + LANES].astype(F32) + t[:, WA + LANES :].astype(F32) for t in terms]
    while len(sums) > 1:
        sums = [sums[k] + sums[k + 1] for k in range(0, len(sums), 2)]
    high, rest = pieces2(sums[0])
    small_sum[...] = high.astype(F32) + rest.astype(F32)
    sent[:, cut:] = jnp.concatenate([high, rest] + [v[...] for v in halos], axis=1)


def run_chip_sum(odd, terms, halos):
    rows = terms[0].shape[0]
    width = WA // 2 + 2 * LANES + 2 * halos[0].shape[1]
    outs = [shape((rows, width), BF), shape((rows, WA // 2), BF), shape((rows, LANES), F32)]
    return call(
        chip_sum_kernel, 1, (1,),
        [(odd, in_smem())] + [(v, whole(v)) for v in list(terms) + halos],
        [(v, whole(v)) for v in outs], [], VMEM_LITTLE,
    )


GW = 768
GNW = DI // GW


def columns_g(arr, at):
    return columns(arr, at, GW)


def gate_kernel(n_pieces, *refs):
    info = refs[0]
    pieces = refs[1 : 1 + n_pieces]
    ends = refs[1 + n_pieces : 1 + 2 * n_pieces]
    (
        y_intra, cs, cum, xs, z, q, inner_gain, d_skip, table,
        enter, normed, gain_part, dz, dyr, dye, product, skip_part, d_enter,
        y_scan, small, weights, squares, dots,
    ) = refs[1 + 2 * n_pieces :]
    phase, c = pl.program_id(0), pl.program_id(1)
    rows = cs.shape[0]
    nb = rows // CH
    n_all = n_pieces * nb
    here = pl.ds(pl.multiple_of(c * GW, GW), GW)

    @pl.when((phase == 0) & (c == 0))
    def _():
        weights[...] = carry_weights(info, clast_rows(ends, nb), nb, False)
        squares[...] = jnp.zeros_like(squares)
        dots[...] = jnp.zeros_like(dots)
        for i in range(nb):
            r = slice(i * CH, (i + 1) * CH)
            small[r, :] = jnp.concatenate(pieces2(jnp.exp(cum[r, :])), axis=1)

    @pl.when(phase == 0)
    def _():
        wide_w = dot(weights[...], table[...])
        totals = [jnp.zeros((NS, GW), F32) for _ in range(nb)]
        for j in range(n_all):
            piece = pieces[j // nb][j % nb].astype(F32)
            for i in range(nb):
                totals[i] = totals[i] + wide_w[i * n_all + j : i * n_all + j + 1, :] * piece
        for i in range(nb):
            r = slice(i * CH, (i + 1) * CH)
            low = totals[i].astype(BF)
            enter[i] = low
            scan = y_intra[r, :] + dot(small[r, :], table[...]) * dot(cs[r, :], low)
            y_scan[r, here] = scan
            y = scan + d_skip[...] * xs[r, :].astype(F32)
            zf = z[r, :].astype(F32)
            gated = y * (zf * sigmoid(zf))
            qg = q[r, :].astype(F32) * inner_gain[...] * usable_of(info, i)
            squares[r, :] += jnp.sum(gated * gated, axis=1, keepdims=True)
            dots[r, :] += jnp.sum(qg * gated, axis=1, keepdims=True)

    @pl.when(phase == 1)
    def _():
        gain_sum = jnp.zeros((1, GW), F32)
        skip_sum = jnp.zeros((1, GW), F32)
        for i in range(nb):
            r = slice(i * CH, (i + 1) * CH)
            inv = lax.rsqrt(squares[r, :] / DI + EPSILON)
            slope = inv * inv * inv * dots[r, :] / DI
            use = usable_of(info, i)
            scan = y_scan[r, here]
            x = xs[r, :].astype(F32)
            y = scan + d_skip[...] * x
            zf = z[r, :].astype(F32)
            sg = sigmoid(zf)
            sz = zf * sg
            gated = y * sz
            qf = q[r, :].astype(F32) * use
            scaled = gated * inv
            normed[r, :] = (scaled * inner_gain[...] * use).astype(BF)
            gain_sum = gain_sum + jnp.sum(qf * scaled, axis=0, keepdims=True)
            gg = inv * qf * inner_gain[...] - gated * slope
            dz[r, :] = (gg * y * (sg + sz * (1.0 - sg))).astype(BF)
            dy = gg * sz
            low = dy.astype(BF)
            dyr[r, :] = low
            product[r, :] = low.astype(F32) * scan
            skip_sum = skip_sum + jnp.sum(dy * x, axis=0, keepdims=True)
            back = (dot(small[r, :], table[...]) * dy).astype(BF)
            dye[r, :] = back
            d_enter[i] = dot_tn(cs[r, :], back).astype(BF)
        gain_part[...] = gain_sum
        skip_part[...] = skip_sum


def run_gate(info, a, pieces, y_intra, z, q, inner_gain, d_skip, table):
    rows = z.shape[0]
    nb = rows // CH

    def early(p, c):
        return jnp.where(p == 0, c, GNW - 1)

    def both(p, c):
        return c

    def late(p, c):
        return jnp.where(p == 0, 0, c)

    ins = [(info, in_smem())]
    ins += [(v, columns_g(v, early)) for v in pieces]
    ins += [(v, pl.BlockSpec((nb, 16, LANES), lambda p, c: (0, 0, DI // LANES))) for v in pieces]
    ins += [(y_intra, columns_g(y_intra, early))]
    ins += [(a[k], whole(a[k])) for k in ("cs", "cum")]
    ins += [(v, columns_g(v, both)) for v in (a["xs"], z, q, inner_gain, d_skip, table)]
    wide = shape((rows, DI), BF)
    wide_f = shape((rows, DI), F32)
    row = shape((1, DI), F32)
    state = shape((nb, NS, DI), BF)
    outs = [(state, columns_g(state, early))]
    outs += [(v, columns_g(v, late)) for v in (wide, row, wide, wide, wide, wide_f, row, state)]
    scratch = [
        pltpu.VMEM((rows, DI), F32), pltpu.VMEM((rows, 2 * LANES), BF),
        pltpu.VMEM((nb * nb * len(pieces), 2 * LANES), BF), pltpu.VMEM((rows, 1), F32),
        pltpu.VMEM((rows, 1), F32),
    ]
    return call(
        functools.partial(gate_kernel, len(pieces)), 16, (2, GNW), ins, outs, scratch, VMEM_ASK,
    )


def intra_back_kernel(
    bs, cs, xt, cum, cum_t, dyr, dye, enter, normed, wo, tok, dxt, db, dc, mixed, scores, top, bottom,
    total,
):
    c = pl.program_id(0)
    nb = bs.shape[0] // CH
    low = iota((CH, LANES), 1) < HD
    keep = iota((HALF, HALF), 1) >= iota((HALF, HALF), 0)

    @pl.when(c == 0)
    def _():
        for i in range(nb):
            r = slice(i * CH, (i + 1) * CH)
            scores[i] = dot_nt(bs[r, :], cs[r, :])
        top[...] = jnp.zeros_like(top)
        bottom[...] = jnp.zeros_like(bottom)
        dc[...] = jnp.zeros_like(dc)
        total[...] = tok[...].astype(F32)

    total[...] += dot(normed[...], wo[...])

    for i in range(nb):
        r = slice(i * CH, (i + 1) * CH)
        cols = chunk_heads(cum[r, :], c * PER)
        dc[r, :] += dot_nt(dye[r, :], enter[i])
        top_sum, bottom_sum = top[i], bottom[i]
        for p in range(PER // 2):
            lanes = slice(p * LANES, (p + 1) * LANES)
            x, dy = xt[r, lanes], dyr[r, lanes]
            got = []
            for k in range(2):
                h = 2 * p + k
                col = cols[:, h : h + 1]
                row = cum_t[pl.ds(c * PER + h, 1), r]
                a, b = col[:HALF], col[HALF:]
                s, t = row[:, :HALF], row[:, HALF:]
                left = jnp.where(keep, jnp.exp(s - a), 0.0)
                right = jnp.exp(t - a)
                last = jnp.where(keep, jnp.exp(t - b), 0.0)
                dec = jnp.concatenate([left, right], axis=1)
                got.append(
                    jnp.concatenate(
                        [
                            dot((dec * scores[i, :HALF, :]).astype(BF), dy),
                            dot((last * scores[i, HALF:, HALF:]).astype(BF), dy[HALF:, :]),
                        ],
                        axis=0,
                    )
                )
                own = jnp.where(low, x, 0) if k == 0 else jnp.where(low, 0, x)
                top_sum = top_sum + dot_nt(own[:HALF, :], dy) * dec
                bottom_sum = bottom_sum + dot_nt(own[HALF:, :], dy[HALF:, :]) * last
            dxt[r, lanes] = jnp.where(low, got[0], got[1])
        top[i], bottom[i] = top_sum, bottom_sum

    @pl.when(c == NCW - 1)
    def _():
        for i in range(nb):
            r = slice(i * CH, (i + 1) * CH)
            up, down = top[i].astype(BF), bottom[i].astype(BF)
            down = jnp.concatenate([jnp.zeros((HALF, HALF), BF), down], axis=1)
            both = jnp.concatenate([up, down], axis=0)
            db[r, :] = dot(both, cs[r, :])
            dc[r, :] += dot_tn(both, bs[r, :])
        mixed[...] = total[...].astype(BF)


def run_intra_back(a, dyr, dye, enter, normed, wo, tok):
    rows = dyr.shape[0]
    nb = rows // CH

    def same(c):
        return c

    ins = [(a[k], whole(a[k])) for k in ("bs", "cs")]
    ins += [(a["xt"], columns(a["xt"], same))]
    ins += [(a[k], whole(a[k])) for k in ("cum", "cum_t")]
    ins += [(v, columns(v, same)) for v in (dyr, dye, enter, normed)]
    ins += [(wo, pl.BlockSpec((CW, DM), lambda c: (c, 0))), (tok, whole(tok))]
    full, small, mixed = shape((rows, DI), F32), shape((rows, NS), F32), shape((rows, DM), BF)
    return call(
        intra_back_kernel, 1, (NCW,), ins,
        [(full, columns(full, same))] + [(v, whole(v)) for v in (small, small, mixed)],
        [
            pltpu.VMEM((nb, CH, CH), F32), pltpu.VMEM((nb, HALF, CH), F32),
            pltpu.VMEM((nb, HALF, HALF), F32), pltpu.VMEM((rows, DM), F32),
        ],
    )


def back_kernel(n_pieces, *refs):
    info = refs[0]
    pieces = refs[1 : 1 + n_pieces]
    ends = refs[1 + n_pieces : 1 + 2 * n_pieces]
    (
        dx_intra, db_in, dc_in, xbc, slope, xs, xt, bs, raw, cum, enter, product, dyr, conv_w,
        a_log, d_skip, table, narrow, gain_part, skip_part,
        d_a, sums,
        grad, small, d_bs, heads, weights,
    ) = refs[1 + 2 * n_pieces :]
    step = pl.program_id(0)
    rows = xs.shape[0]
    nb = rows // CH
    n_all = n_pieces * nb

    @pl.when(step == 0)
    def _():
        weights[...] = carry_weights(info, clast_rows(ends, nb), nb, True)
        dt_all = softplus(raw[...])
        for i in range(nb):
            r = slice(i * CH, (i + 1) * CH)
            last = cum[(i + 1) * CH - 1 : (i + 1) * CH, :]
            small[i, 0] = jnp.concatenate(pieces2(dt_all[r, :]), axis=1)
            small[i, 1] = jnp.concatenate(pieces2(jnp.exp(last - cum[r, :])), axis=1)
            grad[i, :HALO, :] = jnp.zeros((HALO, CW), F32)
            grad[i, HALO + CH :, :] = jnp.zeros((HALO, CW), F32)
        d_bs[...] = db_in[...]
        heads[...] = jnp.zeros_like(heads)

    def put_rows(at, row):
        for j in range(row.shape[1] // LANES):
            sums[pl.ds(at + j, 1), :] = row[:, j * LANES : (j + 1) * LANES]

    def convolve_back(dacts, width):
        offset_sum = jnp.zeros((1, width), F32)
        tap_sums = [jnp.zeros((1, width), F32) for _ in range(KC)]
        all_heads = xbc[rows:, :width].astype(F32)
        head_grads = []
        for i in range(nb):
            r = slice(i * CH, (i + 1) * CH)
            dpre = dacts[i] * slope[r, :width].astype(F32)
            offset_sum = offset_sum + jnp.sum(dpre, axis=0, keepdims=True)
            grad[i, HALO : HALO + CH, :width] = dpre
            body = xbc[r, :width].astype(F32)
            head = all_heads[i * HALO : (i + 1) * HALO, :]
            total = jnp.zeros((CH, width), F32)
            total_head = jnp.zeros((HALO, width), F32)
            for lag in range(KC):
                tap = conv_w[KC - 1 - lag : KC - lag, :width]
                later = grad[i, HALO + lag : HALO + lag + CH, :width]
                later_head = grad[i, lag : lag + HALO, :width]
                total = total + tap * later
                total_head = total_head + tap * later_head
                tap_sums[KC - 1 - lag] = (
                    tap_sums[KC - 1 - lag]
                    + jnp.sum(later * body, axis=0, keepdims=True)
                    + jnp.sum(later_head * head, axis=0, keepdims=True)
                )
            d_a[r, :width] = (total * usable_of(info, i)).astype(BF)
            head_grads.append(total_head * halo_used(info, i))
        d_a[rows:, :width] = jnp.concatenate(head_grads, axis=0).astype(BF)
        for k, row in enumerate(tap_sums + [offset_sum]):
            put_rows(k * (XBC // LANES) + step * (CW // LANES), row)

    @pl.when(step < NCW)
    def _():
        wide_w = dot(weights[...], table[...])
        totals = [jnp.zeros((NS, CW), F32) for _ in range(nb)]
        for j in range(n_all):
            piece = pieces[j // nb][j % nb].astype(F32)
            for i in range(nb):
                totals[i] = totals[i] + wide_w[i * n_all + j : i * n_all + j + 1, :] * piece
        select = narrow[...]
        dacts = []
        for i in range(nb):
            r = slice(i * CH, (i + 1) * CH)
            low = totals[i].astype(BF)
            fade = jnp.sum(low.astype(F32) * enter[i].astype(F32), axis=0, keepdims=True)
            end_w = dot(small[i, 1], table[...])
            x_dt = xt[r, :].astype(F32)
            inter = end_w * dot(bs[r, :], low)
            d_bs[r, :] += dot_nt((x_dt * end_w).astype(BF), low)
            dxt = dx_intra[r, :] + inter
            flow = jnp.sum(x_dt * inter, axis=0, keepdims=True)
            hi, mid, lo = pieces3(product[r, :] - x_dt * dxt)
            heads[0, r, :] += dot(hi, select) + dot(mid, select) + dot(lo, select)
            heads[1, r, :] += dot((xs[r, :].astype(F32) * dxt).astype(BF), select)
            hi, mid, lo = pieces3(jnp.concatenate([flow, fade, jnp.zeros((6, CW), F32)], axis=0))
            heads[2, i * 8 : (i + 1) * 8, :] += dot(hi, select) + dot(mid, select) + dot(lo, select)
            dacts.append(
                dot(small[i, 0], table[...]) * dxt + d_skip[...] * dyr[r, :].astype(F32)
            )
        convolve_back(dacts, CW)
        put_rows(SUM_GAIN + step * (CW // LANES), gain_part[...])
        put_rows(SUM_SKIP + step * (CW // LANES), skip_part[...])

    @pl.when(step == NCW)
    def _():
        dacts = []
        for i in range(nb):
            r = slice(i * CH, (i + 1) * CH)
            dacts.append(jnp.concatenate([d_bs[r, :], dc_in[r, :]], axis=1))
        convolve_back(dacts, 2 * NS)
        rate = jnp.exp(a_log[...])
        anti = (iota((CH, CH), 0) <= iota((CH, CH), 1)).astype(F32).astype(BF)
        bias_sum = jnp.zeros((1, LANES), F32)
        rate_sum = jnp.zeros((1, LANES), F32)
        for i in range(nb):
            r = slice(i * CH, (i + 1) * CH)
            last = cum[(i + 1) * CH - 1 : (i + 1) * CH, :]
            flow, fade = heads[2, i * 8 : i * 8 + 1, :], heads[2, i * 8 + 1 : i * 8 + 2, :]
            parts = dot(anti, jnp.concatenate(pieces3(heads[0, r, :]), axis=1))
            d_log = parts[:, :LANES] + parts[:, LANES : 2 * LANES] + parts[:, 2 * LANES :]
            d_log = d_log + (flow + jnp.exp(last) * fade)
            start = raw[r, :]
            d_raw = (heads[1, r, :] - d_log * rate) * sigmoid(start)
            d_raw = jnp.where(iota((CH, LANES), 1) < NH, d_raw, 0.0)
            bias_sum = bias_sum + jnp.sum(d_raw, axis=0, keepdims=True)
            rate_sum = rate_sum - jnp.sum(d_log * softplus(start), axis=0, keepdims=True) * rate
            d_a[r, 2 * NS :] = d_raw.astype(BF)
        d_a[rows:, 2 * NS :] = jnp.zeros((nb * HALO, CW - 2 * NS), BF)
        put_rows(SUM_HEADS, bias_sum)
        put_rows(SUM_HEADS + 1, rate_sum)


def run_back(
    info, a, pieces, ends, dx_intra, db, dc, enter, product, dyr, conv_w, a_log, d_skip, table,
    narrow, gain_part, skip_part,
):
    rows = dyr.shape[0]
    nb = rows // CH
    ext_rows = rows + nb * HALO

    def chunk(s):
        return jnp.minimum(s, NCW - 1)

    def same(s):
        return s

    ins = [(info, in_smem())]
    ins += [(v, columns(v, chunk)) for v in pieces]
    ins += [(v, pl.BlockSpec((nb, 16, LANES), lambda s: (0, 0, DI // LANES))) for v in ends]
    ins += [(dx_intra, columns(dx_intra, chunk)), (db, whole(db)), (dc, whole(dc))]
    ins += [(a["xbc"], columns(a["xbc"], same)), (a["slope"], columns(a["slope"], same))]
    ins += [(a["xs"], columns(a["xs"], chunk)), (a["xt"], columns(a["xt"], chunk))]
    ins += [(a[k], whole(a[k])) for k in ("bs", "raw", "cum")]
    ins += [(v, columns(v, chunk)) for v in (enter, product, dyr)]
    ins += [(conv_w, columns(conv_w, same)), (a_log, whole(a_log)), (d_skip, columns(d_skip, chunk))]
    ins += [(table, columns(table, chunk))]
    ins += [(narrow, pl.BlockSpec((CW, LANES), lambda s: (chunk(s), 0)))]
    ins += [(v, columns(v, chunk)) for v in (gain_part, skip_part)]
    wide, sums = shape((ext_rows, WA), BF), shape((SUM_ROWS, LANES), F32)
    outs = [(wide, columns(wide, same)), (sums, whole(sums))]
    scratch = [
        pltpu.VMEM((nb, CH + 2 * HALO, CW), F32), pltpu.VMEM((nb, 2, CH, 2 * LANES), BF),
        pltpu.VMEM((rows, NS), F32), pltpu.VMEM((3, rows, LANES), F32),
        pltpu.VMEM((nb * nb * len(pieces), 2 * LANES), BF),
    ]
    return call(
        functools.partial(back_kernel, len(pieces)), 2, (NCW + 1,), ins, outs, scratch, VMEM_ASK,
    )


def unit(rows):
    f = rows.astype(F32)
    inv = lax.rsqrt(jnp.mean(f * f, axis=1, keepdims=True) + EPSILON)
    return f * inv, inv


def norm_back(normal_grad, rows, gain):
    u, inv = unit(rows)
    g = normal_grad * gain[None, :]
    return inv * (g - u * jnp.mean(g * u, axis=1, keepdims=True))


def shards(
    tokens, norm_gain, in_weight, conv_weight, conv_bias, dt_bias, a_log, d_skip, inner_gain,
    out_weight, block_place, seq_length, cotangent,
):
    n_head, n_shard = lax.axis_size("head"), lax.axis_size("shard")
    half = n_head // 2
    head_at, shard_at = lax.axis_index("head"), lax.axis_index("shard")
    rows = tokens.shape[0]
    nb = rows // CH
    group_blocks = nb * n_head
    k_rows = in_weight.shape[0]
    stay = (head_at // half) == (shard_at & 1)

    piece_a = jnp.concatenate(
        [in_weight[:, DI:], norm_gain[:, None], jnp.zeros((k_rows, WA - XBC - NH - 1), BF)], axis=1
    )
    numbers = jnp.concatenate([block_place, seq_length], axis=1)
    numbers_got = trade(numbers, "shard", 1)
    me = jnp.int32(0) if k_rows % 32 else shard_at.astype(jnp.int32)
    def block_tails(v):
        return v.reshape(nb, CH, DM)[:, CH - HALO :].reshape(nb * HALO, DM)

    tok_got = move_home(tokens)
    tails = jnp.where(stay, block_tails(tokens), block_tails(tok_got))

    numbers = jnp.where(stay, numbers, numbers_got)[0]
    lengths = [numbers[group_blocks + k] for k in range(seq_length.shape[1])]

    def order_from(core_at):
        ids = []
        for core in (0, 1):
            for z in range(half):
                device = (head_at % half ^ z) + (core_at ^ core) * half
                ids += [device * nb + b for b in range(nb)]
        return jnp.stack(ids)

    ids, home_order = order_from(shard_at & 1), order_from(head_at // half)
    places = jnp.sum(
        jnp.where(ids[:, None] == jnp.arange(group_blocks)[None, :], numbers[None, :group_blocks], 0),
        axis=1,
    )
    first, in_seq, begin = jnp.zeros_like(places), jnp.zeros_like(places), 0
    for length in lengths:
        first = jnp.where(places >= begin, begin, first)
        in_seq = jnp.where(places >= begin, length, in_seq)
        begin = begin + (length + CH - 1) // CH
    info = jnp.concatenate(
        [
            jnp.stack([me, stay.astype(jnp.int32)]),
            jnp.stack([places, first, in_seq], axis=1).reshape(-1),
        ]
    ).astype(jnp.int32)

    far_a = gather_far(piece_a)
    conv_weight, conv_bias, dt_bias, a_log, d_skip, inner_gain, none = after_all(
        [conv_weight, conv_bias, dt_bias, a_log, d_skip, inner_gain, jnp.int32(0)], far_a[0]
    )
    table = spread_table(none)

    def head_row(v):
        return jnp.pad(v, (0, LANES - NH))[None]

    narrow = narrow_table(none)
    gain_row = inner_gain[None]
    at = shard_at.astype(jnp.int32).reshape(1)
    taps = jnp.pad(conv_weight, ((0, 0), (0, WA - XBC)))
    rate_row = head_row(a_log)
    skip_row = jnp.repeat(d_skip, HD)[None]
    taps, rate_row, skip_row, bias_row, step_row, gain_row, narrow, table = after_all(
        [
            taps, rate_row, skip_row, jnp.pad(conv_bias, (0, WA - XBC))[None], head_row(dt_bias),
            gain_row, narrow, table,
        ]
    )
    prepared = [taps, rate_row, skip_row, bias_row, step_row, gain_row, narrow, table]
    parts_a = gather_near(piece_a, far_a)
    if k_rows % 32:
        parts_a = [(join_pieces(parts_a).reshape(DM, WA), 0)]
    z_own, o_own = after_all([in_weight[:, :DI], out_weight], numbers_got)
    piece_zo = jnp.concatenate([z_own, o_own[:k_rows], o_own[k_rows:]], axis=1)
    far_zo = gather_far(piece_zo)
    tails = group_spread(after(tails, info, *[v for v, _ in parts_a[1:]], *prepared))
    cot_got = move_home(after(cotangent, *tails))
    a = run_project(info, parts_a, tails, tokens, tok_got, taps, bias_row, step_row, rate_row, table)
    wa, tok, normal = a["wa"], a["tok"], a["normal"]
    state_by_head = head_pieces(a["states"])
    state_by_core = trade(a["states"], "shard", 1)
    y_intra = run_intra(a)
    parts_zo = gather_near(after(piece_zo, y_intra), after_all(far_zo, y_intra))
    if k_rows % 32:
        zo = join_pieces(parts_zo)
        wz, wo = zo[:, :, :DI].reshape(DM, DI), zo[:, :, DI:]
        wo = wo.reshape(n_shard, k_rows, 2, DM).swapaxes(1, 2).reshape(DI, DM)
        cot = jnp.where(stay, cotangent, cot_got)
        z, q = dot(normal[:rows], wz).astype(BF), dot_nt(cot, wo).astype(BF)
    else:
        cot_got = after(cot_got, y_intra)
        z, q, cot, wz, wo = run_open(
            at, parts_zo, normal, cotangent, cot_got, stay.astype(jnp.int32).reshape(1)
        )
    state_by_head = [after(v, z) for v in state_by_head]
    all_states = (
        [a["states"]] + state_by_head + [state_by_core] + [trade(v, "shard", 1) for v in state_by_head]
    )
    enter, normed, gain_part, dz, dyr, dye, product, skip_part, d_enter = run_gate(
        info, a, all_states, y_intra, z, q, gain_row, skip_row, table
    )
    enter_by_head = head_pieces(d_enter)
    enter_by_core = trade(d_enter, "shard", 1)
    if k_rows % 32:
        z_term = dot_tn(normal[:rows], dz).astype(BF).reshape(n_shard, k_rows, DI)
        out_term = dot_tn(normed, cot).astype(BF).reshape(n_shard, 2, k_rows, DM)
        zo_keep, zo_give = core_give([z_term, out_term[:, 0], out_term[:, 1]])
        zo_give = [zo_give[p] for p in range(n_shard // 2)]
    else:
        zo_keep, zo_give = run_terms(at, a["normal_t"], dz, normed, cot, n_shard)
    zo_got = [trade(v, "shard", 1) for v in zo_give]
    dx_intra, db, dc, mixed = run_intra_back(a, after(dyr, *zo_give), dye, enter, normed, wo, tok)
    arrived = after_all(enter_by_head + zo_got, dx_intra)
    enter_by_head, zo_got = arrived[: len(enter_by_head)], arrived[len(enter_by_head) :]
    zo_pairs = chip_pairs(zo_keep, jnp.stack(zo_got))
    zo_far = chip_send(zo_pairs)
    enter_by_head = [after(v, *zo_pairs) for v in enter_by_head]
    all_enter = (
        [d_enter] + enter_by_head + [enter_by_core] + [trade(v, "shard", 1) for v in enter_by_head]
    )
    mixed_got = move_home(after(mixed, all_enter[-1]))
    d_a_all, small = run_back(
        info, a, all_enter, all_states, dx_intra, db, dc, enter, product, dyr, taps,
        rate_row, skip_row, table, narrow, gain_part, skip_part,
    )
    d_a_all = after(d_a_all, mixed_got)
    a_term = dot_tn(normal, d_a_all).astype(BF).reshape(n_shard, k_rows, WA)
    a_keep, a_give = core_give([a_term])
    a_got = trade(a_give, "shard", 1)

    small_got = trade(after(small, a_give), "shard", 1)
    zo_own = chip_sum(zo_pairs[0], after_all(zo_far, a_give))
    zo_keep, zo_give = head_split(zo_own)
    zo_got = trade(zo_give, "head", 1)
    d_a_all, dz, tok, tok_halo, wa = after_all(
        [d_a_all, dz, tok, a["tok_halo"], wa], a_give, zo_give
    )
    gain = wa[:, XBC + NH].astype(F32)
    from_a = dot_nt(d_a_all, wa)
    normal_grad = dot_nt(dz, wz) + from_a[:rows]
    token_grad = (cot.astype(F32) + norm_back(normal_grad, tok, gain)).astype(BF)

    a_got, small_got = after_all([a_got, small_got], token_grad)
    if k_rows % 32:
        parts = split2((small + small_got).reshape(k_rows, -1))
        a_pairs = [jnp.concatenate([v, parts], axis=1) for v in chip_pairs(a_keep, a_got)]
    else:
        a_pairs = run_pair_small(at, a_term, a_got, small, small_got)
    a_far = chip_send(a_pairs)
    token_got = move_home(after(token_grad, a_pairs[0]))
    zo_half = head_add(zo_keep, after(zo_got, a_pairs[0]))
    zo_parts = jnp.split(zo_half, 2, axis=1)
    zo_first = trade(zo_parts[0], "head", 2)
    halo_part = norm_back(after(from_a, a_pairs[0])[rows:], tok_halo, gain)
    halo_part = halo_part.reshape(nb, HALO, DM)[:, HALO - KC :].astype(BF).reshape(k_rows, -1)
    halos = [halo_part, trade(halo_part, "shard", 1)]
    *a_far, token_got, halos[1] = after_all(a_far + [token_got, halos[1]])
    cut, edge = WA // 2, WA // 2 + 2 * SUM_ROWS * LANES // k_rows
    if k_rows % 32:
        a_own = chip_sum(a_pairs[0][:, :WA], [v[:, :WA] for v in a_far])
        sums = [join2(v[:, WA:]) for v in [a_pairs[0]] + a_far]
        while len(sums) > 1:
            sums = [sums[k] + sums[k + 1] for k in range(0, len(sums), 2)]
        small = sums[0]
        total, a_give = head_split(a_own)
        parts = split2(small)
        sent = jnp.concatenate([a_give, parts] + (halos if half > 1 else []), axis=1)
        small = join2(parts)
    else:
        odd = (head_at % 2).astype(jnp.int32).reshape(1)
        sent, total, small = run_chip_sum(odd, [a_pairs[0]] + a_far, halos)
    zo_second = after(zo_parts[1], sent)
    own_total = total = total.astype(F32)
    bits = [b for b in (1, 2, 4, 8, 16) if b < n_head]
    for bit in bits:
        if bit > 1:
            a_give = total.astype(BF)
            total = a_give.astype(F32)
            parts = split2(small)
            small = join2(parts)
            sent = jnp.concatenate([a_give, parts] + (halos if bit < half else []), axis=1)
        sent = trade(sent, "head", bit)
        if bit == 1:
            sent, zo_first = after_all([sent, zo_first])
            zo_got = jnp.concatenate([zo_first, trade(zo_second, "head", 2)], axis=1)
            zo_half = head_add(zo_half, zo_got)
            for more in bits[2:]:
                zo_half = head_add(zo_half, trade(zo_half, "head", more))
            zo_other = trade(zo_half, "head", 1)
        if bit < half:
            halos = halos + jnp.split(sent[:, edge:], len(halos), axis=1)
        total = total + sent[:, :cut].astype(F32)
        small = small + join2(sent[:, cut:edge])
    low = total.astype(BF)
    other = trade(low, "head", 1)
    halos, small = after_all([jnp.concatenate(halos, axis=1), small], low)
    halos = jnp.where(stay, halos, move_home(halos))
    halos = jnp.split(halos, group_blocks // nb, axis=1)
    other, zo_other = after_all([other, zo_other], *halos)
    zo_grad = head_join(zo_half, zo_other).astype(F32)
    a_grad = head_join(low, other).astype(F32)
    small = small.reshape(SUM_ROWS, LANES)

    all_halo = jnp.concatenate(halos[0::2] + halos[1::2]).reshape(group_blocks, KC, DM).astype(F32)
    own_numbers = jnp.concatenate([block_place, seq_length], axis=1)[0]
    own_places = jnp.sum(
        jnp.where(
            home_order[:, None] == jnp.arange(group_blocks), own_numbers[None, :group_blocks], 0
        ),
        axis=1,
    )
    home_ids = head_at * nb + jnp.arange(nb)
    home_places = jnp.sum(
        jnp.where(
            home_ids[:, None] == jnp.arange(group_blocks), own_numbers[None, :group_blocks], 0
        ),
        axis=1,
    )
    goes_on, begin = home_places < 0, 0
    for k in range(seq_length.shape[1]):
        end = begin + (own_numbers[group_blocks + k] + CH - 1) // CH
        goes_on = goes_on | ((home_places >= begin) & (home_places + 1 < end))
        begin = end
    is_next = (own_places[None, :] == home_places[:, None] + 1) & goes_on[:, None]
    halo_back = jnp.sum(jnp.where(is_next[:, :, None, None], all_halo[None], 0.0), axis=1)
    token_grad = jnp.where(stay, token_grad, token_got).reshape(nb, CH, DM)
    token_grad = token_grad.at[:, CH - KC :].set(
        (token_grad[:, CH - KC :].astype(F32) + halo_back).astype(BF)
    ).reshape(rows, DM)
    mixed = jnp.where(stay, mixed, after(mixed_got, own_total))

    in_grad = jnp.concatenate([zo_grad[:, :DI], a_grad[:, : XBC + NH]], axis=1)
    out_grad = jnp.concatenate([zo_grad[:, DI : DI + DM], zo_grad[:, DI + DM :]], axis=0)
    gain_grad = jnp.sum(in_grad * in_weight.astype(F32), axis=1) / norm_gain.astype(F32)

    return (
        mixed, token_grad, gain_grad, in_grad, small[: KC * XBC // LANES].reshape(KC, XBC),
        small[KC * XBC // LANES : SUM_GAIN].reshape(XBC), small[SUM_HEADS, :NH],
        small[SUM_HEADS + 1, :NH], jnp.sum(small[SUM_SKIP:SUM_HEADS].reshape(NH, HD), axis=1),
        small[SUM_GAIN:SUM_SKIP].reshape(DI), out_grad,
    )


def solution(mesh):
    return jax.shard_map(
        shards,
        mesh=mesh,
        in_specs=(
            P(("head", "shard"), None), P("shard"), P("shard", None), P(), P(), P(), P(), P(), P(),
            P("shard", None), P("shard", None), P("shard", None), P(("head", "shard"), None),
        ),
        out_specs=(
            P(("head", "shard"), None), P(("head", "shard"), None), P("shard"), P("shard", None),
            P(), P(), P(), P(), P(), P(), P("shard", None),
        ),
        check_vma=False,
    )
```

```python
import functools

import jax
import jax.numpy as jnp
from jax import lax
from jax.experimental import pallas as pl
from jax.experimental.pallas import tpu as pltpu
from jax.sharding import PartitionSpec as P

NH = 24
HD = 64
NS = 128
KC = 4
CH = 256
DI = 1536
DM = 768
XBC = DI + 2 * NS
WA = 1920
HALO = 8
EPSILON = 1e-05
F32 = jnp.float32
BF = jnp.bfloat16
LANES = 128
CW = 384
NCW = DI // CW
VMEM_ASK = 56 * 2**20
VMEM_ROOM = 56 * 2**20
VMEM_LESS = 44 * 2**20
VMEM_LITTLE = 24 * 2**20
COST_SCALE = 0.4


def trade(value, axis, bit):
    size = lax.axis_size(axis)
    return lax.ppermute(value, axis, [(i, i ^ bit) for i in range(size)])


def after(value, *others):
    return lax.optimization_barrier((value,) + others)[0]


def move_home(value):
    n_head, n_shard = lax.axis_size("head"), lax.axis_size("shard")
    half = n_head // 2
    pairs = []
    for h in range(n_head):
        for s in range(n_shard):
            upper, core = h // half, s & 1
            if upper != core:
                there = (h % half + core * half) * n_shard + (s - core + upper)
                pairs.append((h * n_shard + s, there))
    return lax.ppermute(value, ("head", "shard"), pairs)


def swap_home(value, stay):
    return jnp.where(stay, value, move_home(value))


def group_spread(value):
    n_head, n_shard = lax.axis_size("head"), lax.axis_size("shard")
    pieces = [value]
    for core in (0, 1):
        for low in range(n_head // 2):
            if core or low:
                pairs = [
                    (h * n_shard + s, (h ^ low) * n_shard + (s ^ core))
                    for h in range(n_head)
                    for s in range(n_shard)
                ]
                pieces.append(lax.ppermute(value, ("head", "shard"), pairs))
    return pieces


def group_gather(value):
    half = lax.axis_size("head") // 2
    pieces = [value]
    bit = 1
    while bit < half:
        pieces = pieces + [trade(v, "head", bit) for v in pieces]
        bit *= 2
    return pieces + [trade(v, "shard", 1) for v in pieces]


def gather_far(piece):
    bits = range(2, lax.axis_size("shard"), 2)
    return [trade(piece, "shard", bit) for bit in sorted(bits, reverse=True)]


def gather_near(piece, far):
    held = [piece] + far
    offsets = [0] + sorted(range(2, lax.axis_size("shard"), 2), reverse=True)
    near = [trade(v, "shard", 1) for v in held]
    return list(zip(held + near, offsets + [k ^ 1 for k in offsets]))


def join_pieces(parts):
    me, n_shard = lax.axis_index("shard"), lax.axis_size("shard")
    joined = jnp.zeros((n_shard,) + parts[0][0].shape, parts[0][0].dtype)
    for v, k in parts:
        joined = lax.dynamic_update_slice(joined, v[None], (me ^ k, 0, 0))
    return joined


def head_pieces(value):
    pieces = [value]
    bit = 1
    while bit < lax.axis_size("head") // 2:
        pieces = pieces + [trade(v, "head", bit) for v in pieces]
        bit *= 2
    return pieces[1:]


def core_give(blocks):
    n_shard = lax.axis_size("shard")
    core = lax.axis_index("shard") % 2

    def half(which):
        parts = []
        for v in blocks:
            split = v.reshape((n_shard // 2, 2) + v.shape[1:])
            parts.append(lax.dynamic_index_in_dim(split, which, 1, False))
        return jnp.concatenate(parts, axis=2) if len(parts) > 1 else parts[0]

    return half(core), half(1 - core)


def chip_pairs(keep, got):
    pair = (keep.astype(F32) + got.astype(F32)).astype(BF)
    chip = lax.axis_index("shard") // 2
    return [lax.dynamic_index_in_dim(pair, chip ^ k, 0, False) for k in range(pair.shape[0])]


def after_all(values, *others):
    return list(lax.optimization_barrier((*values, *others)))[: len(values)]


def chip_send(pairs):
    return [trade(v, "shard", 2 * k) for k, v in enumerate(pairs) if k]


def chip_sum(own, got):
    total = own.astype(F32)
    for v in got:
        total = total + v.astype(F32)
    return total.astype(BF)


def split2(v):
    high = lax.reduce_precision(v, 8, 7)
    return jnp.concatenate([high.astype(BF), (v - high).astype(BF)], axis=1)


def join2(parts):
    high, low = jnp.split(parts, 2, axis=1)
    return high.astype(F32) + low.astype(F32)


def head_split(value):
    cut = value.shape[1] // 2
    odd = lax.axis_index("head") % 2
    return [lax.dynamic_slice_in_dim(value, at * cut, cut, 1) for at in (odd, 1 - odd)]


def head_add(keep, got):
    return (keep.astype(F32) + got.astype(F32)).astype(BF)


def head_join(half, other):
    odd = lax.axis_index("head") % 2
    return jnp.concatenate([jnp.where(odd, other, half), jnp.where(odd, half, other)], axis=1)


def dot(a, b):
    return jnp.dot(a, b, preferred_element_type=F32)


def dot_nt(a, b):
    return lax.dot_general(a, b, (((1,), (1,)), ((), ())), preferred_element_type=F32)


def dot_tn(a, b):
    return lax.dot_general(a, b, (((0,), (0,)), ((), ())), preferred_element_type=F32)


def spread_table(none):
    row = jnp.arange(2 * LANES)[:, None] % LANES + none
    return (row == jnp.arange(DI)[None, :] // HD).astype(BF)


def narrow_table(none):
    return (jnp.arange(DI)[:, None] // HD == jnp.arange(LANES)[None, :] + none).astype(BF)


def pieces2(v):
    hi = v.astype(BF)
    return hi, (v - hi.astype(F32)).astype(BF)


def pieces3(v):
    hi = v.astype(BF)
    rest = v - hi.astype(F32)
    mid = rest.astype(BF)
    return hi, mid, (rest - mid.astype(F32)).astype(BF)


def softplus(v):
    return jnp.maximum(v, 0.0) + jnp.log1p(jnp.exp(-jnp.abs(v)))


sigmoid = jax.nn.sigmoid


def shape(dims, dtype):
    return jax.ShapeDtypeStruct(dims, dtype)


def whole(arr):
    return pl.BlockSpec(arr.shape, lambda *g: (0,) * len(arr.shape))


def columns(arr, at, width=None):
    dims = arr.shape[:-1] + (width or CW,)
    return pl.BlockSpec(dims, lambda *g: (0,) * (len(dims) - 1) + (at(*g),))


def in_hbm():
    return pl.BlockSpec(memory_space=pl.ANY)


def in_smem():
    return pl.BlockSpec(memory_space=pltpu.SMEM)


def call(kernel, micros, grid, ins, outs, scratch, room=VMEM_ROOM):
    return pl.pallas_call(
        kernel,
        grid=grid,
        out_shape=[o for o, _ in outs],
        in_specs=[s for _, s in ins],
        out_specs=[s for _, s in outs],
        scratch_shapes=scratch,
        compiler_params=pltpu.CompilerParams(vmem_limit_bytes=room),
        cost_estimate=pl.CostEstimate(
            flops=1, bytes_accessed=int(micros * COST_SCALE * 3.7e6), transcendentals=0
        ),
    )(*[a for a, _ in ins])


def iota(dims, axis):
    return lax.broadcasted_iota(jnp.int32, dims, axis)


def place_of(info, q):
    return info[2 + 3 * q]


def first_of(info, q):
    return info[3 + 3 * q]


def usable_of(info, i):
    begin = (place_of(info, i) - first_of(info, i)) * CH
    return (iota((CH, 1), 0) + begin < info[4 + 3 * i]).astype(F32)


def halo_used(info, i):
    has_prev = place_of(info, i) > first_of(info, i)
    return (iota((HALO, 1), 0) + jnp.where(has_prev, 0, -HALO) > HALO - KC).astype(F32)


def clast_rows(refs, nb):
    rows = []
    for ref in refs:
        for b in range(nb):
            part = ref[b].astype(F32)
            rows.append(part[0:1, :] + part[1:2, :] + part[2:3, :])
    return rows


def carry_weights(info, ends, nb, into):
    n_all = len(ends)
    row = iota((n_all, 1), 0)
    place = jnp.zeros((n_all, 1), jnp.int32)
    first = jnp.zeros((n_all, 1), jnp.int32)
    for j in range(n_all):
        place = jnp.where(row == j, place_of(info, j), place)
        first = jnp.where(row == j, first_of(info, j), first)
    parts = []
    for i in range(nb):
        own = place_of(info, i)
        total = jnp.zeros((n_all, LANES), F32)
        for k in range(n_all):
            at = place_of(info, k)
            if into:
                between = (place > at) & (at > own)
            else:
                between = (place < at) & (at < own)
            total = total + jnp.where(between, ends[k], 0.0)
        if into:
            reach = (first <= own) & (place > own)
        else:
            reach = (place >= first_of(info, i)) & (place < own)
        parts.append(jnp.where(reach, jnp.exp(total), 0.0))
    return jnp.concatenate(pieces2(jnp.concatenate(parts, axis=0)), axis=1)


def normal_rows(rows, gain):
    f = rows.astype(F32)
    inv = lax.rsqrt(jnp.sum(f * f, axis=1, keepdims=True) / DM + EPSILON)
    return (f * inv * gain).astype(BF)


def project_kernel(layout, n_halo, *refs):
    info = refs[0]
    pieces = refs[1 : 1 + len(layout)]
    halos = refs[1 + len(layout) : 1 + len(layout) + n_halo]
    (
        tok_own, tok_got, conv_w, conv_b, dt_bias, a_log, table,
        wa_out, tok_out, tok_halo, normal_out, normal_t_out, xbc, slope, xs, xt, bs_out, cs_out,
        raw_out, cum_out, cum_t_out, states,
        wa, ext, small, sems, out_sems, tok, normal, normal_t, bs, cs, raw, cum, cum_t,
    ) = refs[1 + len(layout) + n_halo :]
    step = pl.program_id(0)
    rows = tok_own.shape[0]
    nb = rows // CH
    me = info[0]

    def project(at, width):
        proj = dot(normal[...], wa[:, pl.ds(at, width)]).astype(BF).astype(F32)
        acts, heads = [], []
        for i in range(nb):
            head = proj[rows + i * HALO : rows + (i + 1) * HALO, :] * halo_used(info, i)
            body = proj[i * CH : (i + 1) * CH, :] * usable_of(info, i)
            heads.append(head)
            ext[i, :HALO, :width] = head
            ext[i, HALO:, :width] = body
            xbc[i * CH : (i + 1) * CH, :width] = body.astype(BF)
            pre = conv_b[:, pl.ds(at, width)]
            for lag in range(KC):
                tap = conv_w[KC - 1 - lag : KC - lag, pl.ds(at, width)]
                pre = pre + tap * ext[i, HALO - lag : HALO - lag + CH, :width]
            sg = sigmoid(pre)
            act = pre * sg
            slope[i * CH : (i + 1) * CH, :width] = (sg + act * (1.0 - sg)).astype(BF)
            acts.append(act)
        xbc[rows:, :width] = jnp.concatenate(heads, axis=0).astype(BF)
        return acts

    def leaving():
        moves = [(wa, wa_out), (tok, tok_out), (normal, normal_out), (normal_t, normal_t_out)]
        moves += [(bs, bs_out), (cs, cs_out), (raw, raw_out), (cum, cum_out), (cum_t, cum_t_out)]
        return [pltpu.make_async_copy(v, there, out_sems.at[n]) for n, (v, there) in enumerate(moves)]

    @pl.when(step == 0)
    def _():
        def copy_of(n):
            at = pl.multiple_of((me ^ layout[n]) * pieces[n].shape[0], 16)
            return pltpu.make_async_copy(
                pieces[n], wa.at[pl.ds(at, pieces[n].shape[0]), :], sems.at[n]
            )

        for n in range(len(layout)):
            copy_of(n).start()
        stay = info[1] > 0
        tok[...] = jnp.where(stay, tok_own[...], tok_got[...])
        found = []
        for i in range(nb):
            own, has_prev = place_of(info, i), place_of(info, i) > first_of(info, i)
            total = jnp.zeros((HALO, DM), F32)
            for o in range(n_halo):
                part = halos[o][...].astype(F32)
                for b in range(nb):
                    hit = (place_of(info, o * nb + b) == own - 1) & has_prev
                    total = total + jnp.where(hit, part[b * HALO : (b + 1) * HALO, :], 0.0)
            found.append(total)
        tok_halo[...] = jnp.concatenate(found, axis=0).astype(BF)
        for n in range(len(layout)):
            copy_of(n).wait()
        for copy in leaving()[:2]:
            copy.start()
        gain = wa[:, XBC : XBC + LANES].astype(F32).T[NH : NH + 1, :]
        normal[:rows, :] = normal_rows(tok[...], gain)
        normal_t[...] = normal[:rows, :].T
        normal[rows:, :] = normal_rows(tok_halo[...], gain)
        for i, act in enumerate(project(DI, 2 * NS)):
            bs[i * CH : (i + 1) * CH, :] = act[:, :NS].astype(BF)
            cs[i * CH : (i + 1) * CH, :] = act[:, NS:].astype(BF)
        xbc[:, 2 * NS :] = jnp.zeros((xbc.shape[0], CW - 2 * NS), BF)
        slope[:, 2 * NS :] = jnp.zeros((rows, CW - 2 * NS), BF)
        first = dot(normal[:rows, :], wa[:, XBC : XBC + LANES]).astype(BF).astype(F32) + dt_bias[...]
        raw[...] = first
        dt_all = softplus(first)
        rate = jnp.exp(a_log[...])
        causal = (iota((CH, CH), 0) >= iota((CH, CH), 1)).astype(F32).astype(BF)
        states[:, :, DI:] = jnp.zeros((nb, NS, LANES), BF)
        for i in range(nb):
            dt = dt_all[i * CH : (i + 1) * CH, :]
            parts = dot(causal, jnp.concatenate(pieces3(-dt * rate), axis=1))
            run = parts[:, :LANES] + parts[:, LANES : 2 * LANES] + parts[:, 2 * LANES :]
            cum[i * CH : (i + 1) * CH, :] = run
            cum_t[:, i * CH : (i + 1) * CH] = run.T
            last = run[CH - 1 : CH, :]
            ends = jnp.concatenate(pieces3(last) + (jnp.zeros((13, LANES), BF),), axis=0)
            states[i, :16, DI:] = ends
            small[i, 0] = jnp.concatenate(pieces2(dt), axis=1)
            small[i, 1] = jnp.concatenate(pieces2(jnp.exp(last - run) * dt), axis=1)
        for copy in leaving()[2:]:
            copy.start()

    @pl.when(step > 0)
    def _():
        at = pl.multiple_of((step - 1) * CW, CW)
        for i, act in enumerate(project(at, CW)):
            r = slice(i * CH, (i + 1) * CH)
            xs[r, :] = act.astype(BF)
            xt[r, :] = (act * dot(small[i, 0], table[...])).astype(BF)
            weighted = (act * dot(small[i, 1], table[...])).astype(BF)
            states[i, :, pl.ds(at, CW)] = dot_tn(bs[r, :], weighted).astype(BF)

    @pl.when(step == NCW)
    def _():
        for copy in leaving():
            copy.wait()


def run_project(info, parts, halos, tok_own, tok_got, conv_w, conv_b, dt_bias, a_log, table):
    rows = tok_own.shape[0]
    nb = rows // CH
    ext_rows = rows + nb * HALO
    layout = [offset for _, offset in parts]

    def before(s):
        return jnp.maximum(s - 1, 0)

    def tail_first(s):
        return jnp.where(s == 0, NCW, s - 1)

    ins = [(info, in_smem())] + [(v, in_hbm()) for v, _ in parts]
    ins += [(v, whole(v)) for v in halos]
    ins += [(v, whole(v)) for v in (tok_own, tok_got, conv_w, conv_b, dt_bias, a_log)]
    ins += [(table, columns(table, before))]
    outs = {
        "wa": (shape((DM, WA), BF), in_hbm()),
        "tok": (shape((rows, DM), BF), in_hbm()),
        "tok_halo": (shape((nb * HALO, DM), BF), whole),
        "normal": (shape((ext_rows, DM), BF), in_hbm()),
        "normal_t": (shape((DM, rows), BF), in_hbm()),
        "xbc": (shape((ext_rows, WA), BF), lambda v: columns(v, tail_first)),
        "slope": (shape((rows, WA), BF), lambda v: columns(v, tail_first)),
        "xs": (shape((rows, DI), BF), lambda v: columns(v, before)),
        "xt": (shape((rows, DI), BF), lambda v: columns(v, before)),
        "bs": (shape((rows, NS), BF), in_hbm()),
        "cs": (shape((rows, NS), BF), in_hbm()),
        "raw": (shape((rows, LANES), F32), in_hbm()),
        "cum": (shape((rows, LANES), F32), in_hbm()),
        "cum_t": (shape((LANES, rows), F32), in_hbm()),
        "states": (shape((nb, NS, DI + LANES), BF), whole),
    }
    out_list = [(o, s(o) if callable(s) else s) for o, s in outs.values()]
    scratch = [
        pltpu.VMEM((DM, WA), BF), pltpu.VMEM((nb, HALO + CH, CW), F32),
        pltpu.VMEM((nb, 2, CH, 2 * LANES), BF), pltpu.SemaphoreType.DMA((len(parts),)),
        pltpu.SemaphoreType.DMA((9,)),
    ]
    kept = ("tok", "normal", "normal_t", "bs", "cs", "raw", "cum", "cum_t")
    scratch += [pltpu.VMEM(outs[k][0].shape, outs[k][0].dtype) for k in kept]
    got = call(
        functools.partial(project_kernel, layout, len(halos)), 14, (NCW + 1,), ins, out_list, scratch, VMEM_ASK,
    )
    return dict(zip(outs, got))


SUM_GAIN = (KC + 1) * XBC // LANES
SUM_SKIP = SUM_GAIN + DI // LANES
SUM_HEADS = SUM_SKIP + DI // LANES
SUM_ROWS = SUM_HEADS + 2
OUT_ROWS = CW // 4
PER = CW // HD
HALF = CH // 2


def chunk_heads(cum, first):
    return pltpu.roll(cum, lax.rem(LANES - first, LANES), axis=1)


def intra_kernel(bs, cs, xt, cum, cum_t, out, scores):
    c = pl.program_id(0)
    nb = bs.shape[0] // CH
    low = iota((CH, LANES), 1) < HD
    keep = iota((HALF, HALF), 0) >= iota((HALF, HALF), 1)

    @pl.when(c == 0)
    def _():
        for i in range(nb):
            r = slice(i * CH, (i + 1) * CH)
            scores[i] = dot_nt(cs[r, :], bs[r, :])

    for i in range(nb):
        r = slice(i * CH, (i + 1) * CH)
        cols = chunk_heads(cum[r, :], c * PER)
        for p in range(PER // 2):
            lanes = slice(p * LANES, (p + 1) * LANES)
            both = xt[r, lanes]
            got = []
            for k in range(2):
                h = 2 * p + k
                col = cols[:, h : h + 1]
                row = cum_t[pl.ds(c * PER + h, 1), r]
                a, b = col[:HALF], col[HALF:]
                s, t = row[:, :HALF], row[:, HALF:]
                upper = jnp.where(keep, jnp.exp(a - s), 0.0) * scores[i, :HALF, :HALF]
                left = jnp.exp(b - s) * scores[i, HALF:, :HALF]
                right = jnp.where(keep, jnp.exp(b - t), 0.0) * scores[i, HALF:, HALF:]
                lower = jnp.concatenate([left.astype(BF), right.astype(BF)], axis=1)
                got.append(
                    jnp.concatenate([dot(upper.astype(BF), both[:HALF, :]), dot(lower, both)], axis=0)
                )
            out[r, lanes] = jnp.where(low, got[0], got[1])


def run_intra(a):
    rows = a["bs"].shape[0]
    nb = rows // CH
    ins = [(a[k], whole(a[k])) for k in ("bs", "cs")]
    ins += [(a["xt"], columns(a["xt"], lambda c: c))]
    ins += [(a[k], whole(a[k])) for k in ("cum", "cum_t")]
    out = shape((rows, DI), F32)
    return call(
        intra_kernel, 6, (NCW,), ins, [(out, columns(out, lambda c: c))],
        [pltpu.VMEM((nb, CH, CH), F32)],
    )[0]


OW = 768
ONW = DI // OW


def open_kernel(layout, at, *refs):
    pieces = refs[: len(layout)]
    normal, cot_own, cot_got, stay, z, q, cot, wz_out, wo_out, wz, wo, sems, out_sems = refs[
        len(layout) :
    ]
    c = pl.program_id(0)
    k_rows = pieces[0].shape[0]

    def copies(n):
        shard = at[0] ^ layout[n]
        parts = [(wz, shard * k_rows, slice(0, DI))]
        for j in range(2):
            lanes = slice(DI + j * DM, DI + (j + 1) * DM)
            parts.append((wo, (2 * shard + j) * k_rows, lanes))
        return [
            pltpu.make_async_copy(
                pieces[n].at[:, lanes],
                ref.at[pl.ds(pl.multiple_of(begin, 16), k_rows), :],
                sems.at[3 * n + k],
            )
            for k, (ref, begin, lanes) in enumerate(parts)
        ]

    def leaving():
        return [
            pltpu.make_async_copy(wz, wz_out, out_sems.at[0]),
            pltpu.make_async_copy(wo, wo_out, out_sems.at[1]),
        ]

    @pl.when(c == 0)
    def _():
        for n in range(len(layout)):
            for copy in copies(n):
                copy.start()
        cot[...] = jnp.where(stay[0] > 0, cot_own[...], cot_got[...])
        for n in range(len(layout)):
            for copy in copies(n):
                copy.wait()
        for copy in leaving():
            copy.start()

    here = pl.ds(pl.multiple_of(c * OW, OW), OW)
    z[...] = dot(normal[...], wz[:, here]).astype(BF)
    q[...] = dot_nt(cot[...], wo[here, :]).astype(BF)

    @pl.when(c == ONW - 1)
    def _():
        for copy in leaving():
            copy.wait()


def run_open(at, parts, normal, cot_own, cot_got, stay):
    rows = cot_own.shape[0]
    layout = [offset for _, offset in parts]
    ins = [(at, in_smem())] + [(v, in_hbm()) for v, _ in parts]
    ins += [(normal, pl.BlockSpec((rows, DM), lambda c: (0, 0)))]
    ins += [(cot_own, whole(cot_own)), (cot_got, whole(cot_got)), (stay, in_smem())]
    wide = shape((rows, DI), BF)
    outs = [(wide, columns(wide, lambda c: c, OW))] * 2
    outs += [(v, whole(v)) for v in (shape((rows, DM), BF),)]
    outs += [(v, in_hbm()) for v in (shape((DM, DI), BF), shape((DI, DM), BF))]
    return call(
        functools.partial(open_kernel, layout), 1, (ONW,), ins, outs,
        [
            pltpu.VMEM((DM, DI), BF), pltpu.VMEM((DI, DM), BF),
            pltpu.SemaphoreType.DMA((3 * len(parts),)), pltpu.SemaphoreType.DMA((2,)),
        ],
        VMEM_LESS,
    )


def terms_kernel(at, normal_t, dz, normed, cot, keep, *refs):
    *give, z_part, o_part = refs
    p = pl.program_id(0)
    unit = give[0].shape[0]
    even = at[0] % 2 == 0
    z_part[...] = dot(normal_t[...], dz[...])
    o_part[...] = dot_tn(normed[...], cot[...])

    def rows_of(which):
        parts = [(z_part[which * unit : (which + 1) * unit, :], slice(0, DI))]
        for j in range(2):
            rows = o_part[(2 * which + j) * unit : (2 * which + j + 1) * unit, :]
            parts.append((rows, slice(DI + j * DM, DI + (j + 1) * DM)))
        return parts

    for (first, lanes), (second, _) in zip(rows_of(0), rows_of(1)):
        keep[0, :, lanes] = jnp.where(even, first, second).astype(BF)
        other = jnp.where(even, second, first).astype(BF)
        for k, ref in enumerate(give):

            @pl.when(p == k)
            def _(ref=ref, other=other, lanes=lanes):
                ref[:, lanes] = other


def run_terms(at, normal_t, dz, normed, cot, n_shard):
    rows = dz.shape[0]
    n, unit = n_shard // 2, DM // n_shard
    give = shape((unit, DI + 2 * DM), BF)
    keep = shape((n,) + give.shape, BF)
    got = call(
        terms_kernel, 1, (n,),
        [
            (at, in_smem()), (normal_t, pl.BlockSpec((2 * unit, rows), lambda p: (p, 0))),
            (dz, whole(dz)), (normed, columns(normed, lambda p: p, 4 * unit)), (cot, whole(cot)),
        ],
        [(keep, pl.BlockSpec((1,) + give.shape, lambda p: (p, 0, 0)))] + [(give, whole(give))] * n,
        [pltpu.VMEM((2 * unit, DI), F32), pltpu.VMEM((4 * unit, DM), F32)],
    )
    return got[0], list(got[1:])


def pair_small_kernel(at, term, got, small, small_got, *outs):
    cols = got.shape[-1]
    chip, core = at[0] // 2, at[0] % 2
    total = small[...] + small_got[...]
    parts = jnp.concatenate(pieces2(total), axis=1)
    for k, out in enumerate(outs):
        kept = term[2 * (chip ^ k) + core]
        out[:, :cols] = (kept.astype(F32) + got[chip ^ k].astype(F32)).astype(BF)
        out[:, cols:] = parts


def run_pair_small(at, term, got, small, small_got):
    n, rows, cols = got.shape
    out = shape((rows, cols + 2 * small.shape[1]), BF)
    args = [term, got, small, small_got]
    return call(
        pair_small_kernel, 1, (1,), [(at, in_smem())] + [(v, whole(v)) for v in args],
        [(out, whole(out))] * n, [], VMEM_LITTLE,
    )


def chip_sum_kernel(odd, *refs):
    n = len(refs) - 5
    terms, halos, (sent, keep, small_sum) = refs[:n], refs[n : n + 2], refs[n + 2 :]
    total = terms[0][:, :WA].astype(F32)
    for term in terms[1:]:
        total = total + term[:, :WA].astype(F32)
    low = total.astype(BF)
    cut = WA // 2
    right_kept = odd[0] > 0
    sent[:, :cut] = jnp.where(right_kept, low[:, :cut], low[:, cut:])
    keep[...] = jnp.where(right_kept, low[:, cut:], low[:, :cut])
    sums = [t[:, WA : WA + LANES].astype(F32) + t[:, WA + LANES :].astype(F32) for t in terms]
    while len(sums) > 1:
        sums = [sums[k] + sums[k + 1] for k in range(0, len(sums), 2)]
    high, rest = pieces2(sums[0])
    small_sum[...] = high.astype(F32) + rest.astype(F32)
    sent[:, cut:] = jnp.concatenate([high, rest] + [v[...] for v in halos], axis=1)


def run_chip_sum(odd, terms, halos):
    rows = terms[0].shape[0]
    width = WA // 2 + 2 * LANES + 2 * halos[0].shape[1]
    outs = [shape((rows, width), BF), shape((rows, WA // 2), BF), shape((rows, LANES), F32)]
    return call(
        chip_sum_kernel, 1, (1,),
        [(odd, in_smem())] + [(v, whole(v)) for v in list(terms) + halos],
        [(v, whole(v)) for v in outs], [], VMEM_LITTLE,
    )


GW = 768
GNW = DI // GW


def columns_g(arr, at):
    return columns(arr, at, GW)


def gate_kernel(n_pieces, *refs):
    info = refs[0]
    pieces = refs[1 : 1 + n_pieces]
    ends = refs[1 + n_pieces : 1 + 2 * n_pieces]
    (
        y_intra, cs, cum, xs, z, q, inner_gain, d_skip, table,
        enter, normed, gain_part, dz, dyr, dye, product, skip_part, d_enter,
        y_scan, small, weights, squares, dots,
    ) = refs[1 + 2 * n_pieces :]
    phase, c = pl.program_id(0), pl.program_id(1)
    rows = cs.shape[0]
    nb = rows // CH
    n_all = n_pieces * nb
    here = pl.ds(pl.multiple_of(c * GW, GW), GW)

    @pl.when((phase == 0) & (c == 0))
    def _():
        weights[...] = carry_weights(info, clast_rows(ends, nb), nb, False)
        squares[...] = jnp.zeros_like(squares)
        dots[...] = jnp.zeros_like(dots)
        for i in range(nb):
            r = slice(i * CH, (i + 1) * CH)
            small[r, :] = jnp.concatenate(pieces2(jnp.exp(cum[r, :])), axis=1)

    @pl.when(phase == 0)
    def _():
        wide_w = dot(weights[...], table[...])
        totals = [jnp.zeros((NS, GW), F32) for _ in range(nb)]
        for j in range(n_all):
            piece = pieces[j // nb][j % nb].astype(F32)
            for i in range(nb):
                totals[i] = totals[i] + wide_w[i * n_all + j : i * n_all + j + 1, :] * piece
        for i in range(nb):
            r = slice(i * CH, (i + 1) * CH)
            low = totals[i].astype(BF)
            enter[i] = low
            scan = y_intra[r, :] + dot(small[r, :], table[...]) * dot(cs[r, :], low)
            y_scan[r, here] = scan
            y = scan + d_skip[...] * xs[r, :].astype(F32)
            zf = z[r, :].astype(F32)
            gated = y * (zf * sigmoid(zf))
            qg = q[r, :].astype(F32) * inner_gain[...] * usable_of(info, i)
            squares[r, :] += jnp.sum(gated * gated, axis=1, keepdims=True)
            dots[r, :] += jnp.sum(qg * gated, axis=1, keepdims=True)

    @pl.when(phase == 1)
    def _():
        gain_sum = jnp.zeros((1, GW), F32)
        skip_sum = jnp.zeros((1, GW), F32)
        for i in range(nb):
            r = slice(i * CH, (i + 1) * CH)
            inv = lax.rsqrt(squares[r, :] / DI + EPSILON)
            slope = inv * inv * inv * dots[r, :] / DI
            use = usable_of(info, i)
            scan = y_scan[r, here]
            x = xs[r, :].astype(F32)
            y = scan + d_skip[...] * x
            zf = z[r, :].astype(F32)
            sg = sigmoid(zf)
            sz = zf * sg
            gated = y * sz
            qf = q[r, :].astype(F32) * use
            scaled = gated * inv
            normed[r, :] = (scaled * inner_gain[...] * use).astype(BF)
            gain_sum = gain_sum + jnp.sum(qf * scaled, axis=0, keepdims=True)
            gg = inv * qf * inner_gain[...] - gated * slope
            dz[r, :] = (gg * y * (sg + sz * (1.0 - sg))).astype(BF)
            dy = gg * sz
            low = dy.astype(BF)
            dyr[r, :] = low
            product[r, :] = low.astype(F32) * scan
            skip_sum = skip_sum + jnp.sum(dy * x, axis=0, keepdims=True)
            back = (dot(small[r, :], table[...]) * dy).astype(BF)
            dye[r, :] = back
            d_enter[i] = dot_tn(cs[r, :], back).astype(BF)
        gain_part[...] = gain_sum
        skip_part[...] = skip_sum


def run_gate(info, a, pieces, y_intra, z, q, inner_gain, d_skip, table):
    rows = z.shape[0]
    nb = rows // CH

    def early(p, c):
        return jnp.where(p == 0, c, GNW - 1)

    def both(p, c):
        return c

    def late(p, c):
        return jnp.where(p == 0, 0, c)

    ins = [(info, in_smem())]
    ins += [(v, columns_g(v, early)) for v in pieces]
    ins += [(v, pl.BlockSpec((nb, 16, LANES), lambda p, c: (0, 0, DI // LANES))) for v in pieces]
    ins += [(y_intra, columns_g(y_intra, early))]
    ins += [(a[k], whole(a[k])) for k in ("cs", "cum")]
    ins += [(v, columns_g(v, both)) for v in (a["xs"], z, q, inner_gain, d_skip, table)]
    wide = shape((rows, DI), BF)
    wide_f = shape((rows, DI), F32)
    row = shape((1, DI), F32)
    state = shape((nb, NS, DI), BF)
    outs = [(state, columns_g(state, early))]
    outs += [(v, columns_g(v, late)) for v in (wide, row, wide, wide, wide, wide_f, row, state)]
    scratch = [
        pltpu.VMEM((rows, DI), F32), pltpu.VMEM((rows, 2 * LANES), BF),
        pltpu.VMEM((nb * nb * len(pieces), 2 * LANES), BF), pltpu.VMEM((rows, 1), F32),
        pltpu.VMEM((rows, 1), F32),
    ]
    return call(
        functools.partial(gate_kernel, len(pieces)), 16, (2, GNW), ins, outs, scratch, VMEM_ASK,
    )


def intra_back_kernel(
    bs, cs, xt, cum, cum_t, dyr, dye, enter, normed, wo, tok, dxt, db, dc, mixed, scores, top, bottom,
    total,
):
    c = pl.program_id(0)
    nb = bs.shape[0] // CH
    low = iota((CH, LANES), 1) < HD
    keep = iota((HALF, HALF), 1) >= iota((HALF, HALF), 0)

    @pl.when(c == 0)
    def _():
        for i in range(nb):
            r = slice(i * CH, (i + 1) * CH)
            scores[i] = dot_nt(bs[r, :], cs[r, :])
        top[...] = jnp.zeros_like(top)
        bottom[...] = jnp.zeros_like(bottom)
        dc[...] = jnp.zeros_like(dc)
        total[...] = tok[...].astype(F32)

    total[...] += dot(normed[...], wo[...])

    for i in range(nb):
        r = slice(i * CH, (i + 1) * CH)
        cols = chunk_heads(cum[r, :], c * PER)
        dc[r, :] += dot_nt(dye[r, :], enter[i])
        top_sum, bottom_sum = top[i], bottom[i]
        for p in range(PER // 2):
            lanes = slice(p * LANES, (p + 1) * LANES)
            x, dy = xt[r, lanes], dyr[r, lanes]
            got = []
            for k in range(2):
                h = 2 * p + k
                col = cols[:, h : h + 1]
                row = cum_t[pl.ds(c * PER + h, 1), r]
                a, b = col[:HALF], col[HALF:]
                s, t = row[:, :HALF], row[:, HALF:]
                left = jnp.where(keep, jnp.exp(s - a), 0.0)
                right = jnp.exp(t - a)
                last = jnp.where(keep, jnp.exp(t - b), 0.0)
                dec = jnp.concatenate([left, right], axis=1)
                got.append(
                    jnp.concatenate(
                        [
                            dot((dec * scores[i, :HALF, :]).astype(BF), dy),
                            dot((last * scores[i, HALF:, HALF:]).astype(BF), dy[HALF:, :]),
                        ],
                        axis=0,
                    )
                )
                own = jnp.where(low, x, 0) if k == 0 else jnp.where(low, 0, x)
                top_sum = top_sum + dot_nt(own[:HALF, :], dy) * dec
                bottom_sum = bottom_sum + dot_nt(own[HALF:, :], dy[HALF:, :]) * last
            dxt[r, lanes] = jnp.where(low, got[0], got[1])
        top[i], bottom[i] = top_sum, bottom_sum

    @pl.when(c == NCW - 1)
    def _():
        for i in range(nb):
            r = slice(i * CH, (i + 1) * CH)
            up, down = top[i].astype(BF), bottom[i].astype(BF)
            down = jnp.concatenate([jnp.zeros((HALF, HALF), BF), down], axis=1)
            both = jnp.concatenate([up, down], axis=0)
            db[r, :] = dot(both, cs[r, :])
            dc[r, :] += dot_tn(both, bs[r, :])
        mixed[...] = total[...].astype(BF)


def run_intra_back(a, dyr, dye, enter, normed, wo, tok):
    rows = dyr.shape[0]
    nb = rows // CH

    def same(c):
        return c

    ins = [(a[k], whole(a[k])) for k in ("bs", "cs")]
    ins += [(a["xt"], columns(a["xt"], same))]
    ins += [(a[k], whole(a[k])) for k in ("cum", "cum_t")]
    ins += [(v, columns(v, same)) for v in (dyr, dye, enter, normed)]
    ins += [(wo, pl.BlockSpec((CW, DM), lambda c: (c, 0))), (tok, whole(tok))]
    full, small, mixed = shape((rows, DI), F32), shape((rows, NS), F32), shape((rows, DM), BF)
    return call(
        intra_back_kernel, 1, (NCW,), ins,
        [(full, columns(full, same))] + [(v, whole(v)) for v in (small, small, mixed)],
        [
            pltpu.VMEM((nb, CH, CH), F32), pltpu.VMEM((nb, HALF, CH), F32),
            pltpu.VMEM((nb, HALF, HALF), F32), pltpu.VMEM((rows, DM), F32),
        ],
    )


def back_kernel(n_pieces, *refs):
    info = refs[0]
    pieces = refs[1 : 1 + n_pieces]
    ends = refs[1 + n_pieces : 1 + 2 * n_pieces]
    (
        dx_intra, db_in, dc_in, xbc, slope, xs, xt, bs, raw, cum, enter, product, dyr, conv_w,
        a_log, d_skip, table, narrow, gain_part, skip_part,
        d_a, sums,
        grad, small, d_bs, heads, weights,
    ) = refs[1 + 2 * n_pieces :]
    step = pl.program_id(0)
    rows = xs.shape[0]
    nb = rows // CH
    n_all = n_pieces * nb

    @pl.when(step == 0)
    def _():
        weights[...] = carry_weights(info, clast_rows(ends, nb), nb, True)
        dt_all = softplus(raw[...])
        for i in range(nb):
            r = slice(i * CH, (i + 1) * CH)
            last = cum[(i + 1) * CH - 1 : (i + 1) * CH, :]
            small[i, 0] = jnp.concatenate(pieces2(dt_all[r, :]), axis=1)
            small[i, 1] = jnp.concatenate(pieces2(jnp.exp(last - cum[r, :])), axis=1)
            grad[i, :HALO, :] = jnp.zeros((HALO, CW), F32)
            grad[i, HALO + CH :, :] = jnp.zeros((HALO, CW), F32)
        d_bs[...] = db_in[...]
        heads[...] = jnp.zeros_like(heads)

    def put_rows(at, row):
        for j in range(row.shape[1] // LANES):
            sums[pl.ds(at + j, 1), :] = row[:, j * LANES : (j + 1) * LANES]

    def convolve_back(dacts, width):
        offset_sum = jnp.zeros((1, width), F32)
        tap_sums = [jnp.zeros((1, width), F32) for _ in range(KC)]
        all_heads = xbc[rows:, :width].astype(F32)
        head_grads = []
        for i in range(nb):
            r = slice(i * CH, (i + 1) * CH)
            dpre = dacts[i] * slope[r, :width].astype(F32)
            offset_sum = offset_sum + jnp.sum(dpre, axis=0, keepdims=True)
            grad[i, HALO : HALO + CH, :width] = dpre
            body = xbc[r, :width].astype(F32)
            head = all_heads[i * HALO : (i + 1) * HALO, :]
            total = jnp.zeros((CH, width), F32)
            total_head = jnp.zeros((HALO, width), F32)
            for lag in range(KC):
                tap = conv_w[KC - 1 - lag : KC - lag, :width]
                later = grad[i, HALO + lag : HALO + lag + CH, :width]
                later_head = grad[i, lag : lag + HALO, :width]
                total = total + tap * later
                total_head = total_head + tap * later_head
                tap_sums[KC - 1 - lag] = (
                    tap_sums[KC - 1 - lag]
                    + jnp.sum(later * body, axis=0, keepdims=True)
                    + jnp.sum(later_head * head, axis=0, keepdims=True)
                )
            d_a[r, :width] = (total * usable_of(info, i)).astype(BF)
            head_grads.append(total_head * halo_used(info, i))
        d_a[rows:, :width] = jnp.concatenate(head_grads, axis=0).astype(BF)
        for k, row in enumerate(tap_sums + [offset_sum]):
            put_rows(k * (XBC // LANES) + step * (CW // LANES), row)

    @pl.when(step < NCW)
    def _():
        wide_w = dot(weights[...], table[...])
        totals = [jnp.zeros((NS, CW), F32) for _ in range(nb)]
        for j in range(n_all):
            piece = pieces[j // nb][j % nb].astype(F32)
            for i in range(nb):
                totals[i] = totals[i] + wide_w[i * n_all + j : i * n_all + j + 1, :] * piece
        select = narrow[...]
        dacts = []
        for i in range(nb):
            r = slice(i * CH, (i + 1) * CH)
            low = totals[i].astype(BF)
            fade = jnp.sum(low.astype(F32) * enter[i].astype(F32), axis=0, keepdims=True)
            end_w = dot(small[i, 1], table[...])
            x_dt = xt[r, :].astype(F32)
            inter = end_w * dot(bs[r, :], low)
            d_bs[r, :] += dot_nt((x_dt * end_w).astype(BF), low)
            dxt = dx_intra[r, :] + inter
            flow = jnp.sum(x_dt * inter, axis=0, keepdims=True)
            hi, mid, lo = pieces3(product[r, :] - x_dt * dxt)
            heads[0, r, :] += dot(hi, select) + dot(mid, select) + dot(lo, select)
            heads[1, r, :] += dot((xs[r, :].astype(F32) * dxt).astype(BF), select)
            hi, mid, lo = pieces3(jnp.concatenate([flow, fade, jnp.zeros((6, CW), F32)], axis=0))
            heads[2, i * 8 : (i + 1) * 8, :] += dot(hi, select) + dot(mid, select) + dot(lo, select)
            dacts.append(
                dot(small[i, 0], table[...]) * dxt + d_skip[...] * dyr[r, :].astype(F32)
            )
        convolve_back(dacts, CW)
        put_rows(SUM_GAIN + step * (CW // LANES), gain_part[...])
        put_rows(SUM_SKIP + step * (CW // LANES), skip_part[...])

    @pl.when(step == NCW)
    def _():
        dacts = []
        for i in range(nb):
            r = slice(i * CH, (i + 1) * CH)
            dacts.append(jnp.concatenate([d_bs[r, :], dc_in[r, :]], axis=1))
        convolve_back(dacts, 2 * NS)
        rate = jnp.exp(a_log[...])
        anti = (iota((CH, CH), 0) <= iota((CH, CH), 1)).astype(F32).astype(BF)
        bias_sum = jnp.zeros((1, LANES), F32)
        rate_sum = jnp.zeros((1, LANES), F32)
        for i in range(nb):
            r = slice(i * CH, (i + 1) * CH)
            last = cum[(i + 1) * CH - 1 : (i + 1) * CH, :]
            flow, fade = heads[2, i * 8 : i * 8 + 1, :], heads[2, i * 8 + 1 : i * 8 + 2, :]
            parts = dot(anti, jnp.concatenate(pieces3(heads[0, r, :]), axis=1))
            d_log = parts[:, :LANES] + parts[:, LANES : 2 * LANES] + parts[:, 2 * LANES :]
            d_log = d_log + (flow + jnp.exp(last) * fade)
            start = raw[r, :]
            d_raw = (heads[1, r, :] - d_log * rate) * sigmoid(start)
            d_raw = jnp.where(iota((CH, LANES), 1) < NH, d_raw, 0.0)
            bias_sum = bias_sum + jnp.sum(d_raw, axis=0, keepdims=True)
            rate_sum = rate_sum - jnp.sum(d_log * softplus(start), axis=0, keepdims=True) * rate
            d_a[r, 2 * NS :] = d_raw.astype(BF)
        d_a[rows:, 2 * NS :] = jnp.zeros((nb * HALO, CW - 2 * NS), BF)
        put_rows(SUM_HEADS, bias_sum)
        put_rows(SUM_HEADS + 1, rate_sum)


def run_back(
    info, a, pieces, ends, dx_intra, db, dc, enter, product, dyr, conv_w, a_log, d_skip, table,
    narrow, gain_part, skip_part,
):
    rows = dyr.shape[0]
    nb = rows // CH
    ext_rows = rows + nb * HALO

    def chunk(s):
        return jnp.minimum(s, NCW - 1)

    def same(s):
        return s

    ins = [(info, in_smem())]
    ins += [(v, columns(v, chunk)) for v in pieces]
    ins += [(v, pl.BlockSpec((nb, 16, LANES), lambda s: (0, 0, DI // LANES))) for v in ends]
    ins += [(dx_intra, columns(dx_intra, chunk)), (db, whole(db)), (dc, whole(dc))]
    ins += [(a["xbc"], columns(a["xbc"], same)), (a["slope"], columns(a["slope"], same))]
    ins += [(a["xs"], columns(a["xs"], chunk)), (a["xt"], columns(a["xt"], chunk))]
    ins += [(a[k], whole(a[k])) for k in ("bs", "raw", "cum")]
    ins += [(v, columns(v, chunk)) for v in (enter, product, dyr)]
    ins += [(conv_w, columns(conv_w, same)), (a_log, whole(a_log)), (d_skip, columns(d_skip, chunk))]
    ins += [(table, columns(table, chunk))]
    ins += [(narrow, pl.BlockSpec((CW, LANES), lambda s: (chunk(s), 0)))]
    ins += [(v, columns(v, chunk)) for v in (gain_part, skip_part)]
    wide, sums = shape((ext_rows, WA), BF), shape((SUM_ROWS, LANES), F32)
    outs = [(wide, columns(wide, same)), (sums, whole(sums))]
    scratch = [
        pltpu.VMEM((nb, CH + 2 * HALO, CW), F32), pltpu.VMEM((nb, 2, CH, 2 * LANES), BF),
        pltpu.VMEM((rows, NS), F32), pltpu.VMEM((3, rows, LANES), F32),
        pltpu.VMEM((nb * nb * len(pieces), 2 * LANES), BF),
    ]
    return call(
        functools.partial(back_kernel, len(pieces)), 2, (NCW + 1,), ins, outs, scratch, VMEM_ASK,
    )


def unit(rows):
    f = rows.astype(F32)
    inv = lax.rsqrt(jnp.mean(f * f, axis=1, keepdims=True) + EPSILON)
    return f * inv, inv


def norm_back(normal_grad, rows, gain):
    u, inv = unit(rows)
    g = normal_grad * gain[None, :]
    return inv * (g - u * jnp.mean(g * u, axis=1, keepdims=True))


def shards(
    tokens, norm_gain, in_weight, conv_weight, conv_bias, dt_bias, a_log, d_skip, inner_gain,
    out_weight, block_place, seq_length, cotangent,
):
    n_head, n_shard = lax.axis_size("head"), lax.axis_size("shard")
    half = n_head // 2
    head_at, shard_at = lax.axis_index("head"), lax.axis_index("shard")
    rows = tokens.shape[0]
    nb = rows // CH
    group_blocks = nb * n_head
    k_rows = in_weight.shape[0]
    stay = (head_at // half) == (shard_at & 1)

    piece_a = jnp.concatenate(
        [in_weight[:, DI:], norm_gain[:, None], jnp.zeros((k_rows, WA - XBC - NH - 1), BF)], axis=1
    )
    numbers = jnp.concatenate([block_place, seq_length], axis=1)
    numbers_got = trade(numbers, "shard", 1)
    me = jnp.int32(0) if k_rows % 32 else shard_at.astype(jnp.int32)
    def block_tails(v):
        return v.reshape(nb, CH, DM)[:, CH - HALO :].reshape(nb * HALO, DM)

    tok_got = move_home(tokens)
    tails = jnp.where(stay, block_tails(tokens), block_tails(tok_got))

    numbers = jnp.where(stay, numbers, numbers_got)[0]
    lengths = [numbers[group_blocks + k] for k in range(seq_length.shape[1])]

    def order_from(core_at):
        ids = []
        for core in (0, 1):
            for z in range(half):
                device = (head_at % half ^ z) + (core_at ^ core) * half
                ids += [device * nb + b for b in range(nb)]
        return jnp.stack(ids)

    ids, home_order = order_from(shard_at & 1), order_from(head_at // half)
    places = jnp.sum(
        jnp.where(ids[:, None] == jnp.arange(group_blocks)[None, :], numbers[None, :group_blocks], 0),
        axis=1,
    )
    first, in_seq, begin = jnp.zeros_like(places), jnp.zeros_like(places), 0
    for length in lengths:
        first = jnp.where(places >= begin, begin, first)
        in_seq = jnp.where(places >= begin, length, in_seq)
        begin = begin + (length + CH - 1) // CH
    info = jnp.concatenate(
        [
            jnp.stack([me, stay.astype(jnp.int32)]),
            jnp.stack([places, first, in_seq], axis=1).reshape(-1),
        ]
    ).astype(jnp.int32)

    far_a = gather_far(piece_a)
    conv_weight, conv_bias, dt_bias, a_log, d_skip, inner_gain, none = after_all(
        [conv_weight, conv_bias, dt_bias, a_log, d_skip, inner_gain, jnp.int32(0)], far_a[0]
    )
    table = spread_table(none)

    def head_row(v):
        return jnp.pad(v, (0, LANES - NH))[None]

    narrow = narrow_table(none)
    gain_row = inner_gain[None]
    at = shard_at.astype(jnp.int32).reshape(1)
    taps = jnp.pad(conv_weight, ((0, 0), (0, WA - XBC)))
    rate_row = head_row(a_log)
    skip_row = jnp.repeat(d_skip, HD)[None]
    taps, rate_row, skip_row, bias_row, step_row, gain_row, narrow, table = after_all(
        [
            taps, rate_row, skip_row, jnp.pad(conv_bias, (0, WA - XBC))[None], head_row(dt_bias),
            gain_row, narrow, table,
        ]
    )
    prepared = [taps, rate_row, skip_row, bias_row, step_row, gain_row, narrow, table]
    parts_a = gather_near(piece_a, far_a)
    if k_rows % 32:
        parts_a = [(join_pieces(parts_a).reshape(DM, WA), 0)]
    z_own, o_own = after_all([in_weight[:, :DI], out_weight], numbers_got)
    piece_zo = jnp.concatenate([z_own, o_own[:k_rows], o_own[k_rows:]], axis=1)
    far_zo = gather_far(piece_zo)
    tails = group_spread(after(tails, info, *[v for v, _ in parts_a[1:]], *prepared))
    cot_got = move_home(after(cotangent, *tails))
    a = run_project(info, parts_a, tails, tokens, tok_got, taps, bias_row, step_row, rate_row, table)
    wa, tok, normal = a["wa"], a["tok"], a["normal"]
    state_by_head = head_pieces(a["states"])
    state_by_core = trade(a["states"], "shard", 1)
    y_intra = run_intra(a)
    parts_zo = gather_near(after(piece_zo, y_intra), after_all(far_zo, y_intra))
    if k_rows % 32:
        zo = join_pieces(parts_zo)
        wz, wo = zo[:, :, :DI].reshape(DM, DI), zo[:, :, DI:]
        wo = wo.reshape(n_shard, k_rows, 2, DM).swapaxes(1, 2).reshape(DI, DM)
        cot = jnp.where(stay, cotangent, cot_got)
        z, q = dot(normal[:rows], wz).astype(BF), dot_nt(cot, wo).astype(BF)
    else:
        cot_got = after(cot_got, y_intra)
        z, q, cot, wz, wo = run_open(
            at, parts_zo, normal, cotangent, cot_got, stay.astype(jnp.int32).reshape(1)
        )
    state_by_head = [after(v, z) for v in state_by_head]
    all_states = (
        [a["states"]] + state_by_head + [state_by_core] + [trade(v, "shard", 1) for v in state_by_head]
    )
    enter, normed, gain_part, dz, dyr, dye, product, skip_part, d_enter = run_gate(
        info, a, all_states, y_intra, z, q, gain_row, skip_row, table
    )
    enter_by_head = head_pieces(d_enter)
    enter_by_core = trade(d_enter, "shard", 1)
    if k_rows % 32:
        z_term = dot_tn(normal[:rows], dz).astype(BF).reshape(n_shard, k_rows, DI)
        out_term = dot_tn(normed, cot).astype(BF).reshape(n_shard, 2, k_rows, DM)
        zo_keep, zo_give = core_give([z_term, out_term[:, 0], out_term[:, 1]])
        zo_give = [zo_give[p] for p in range(n_shard // 2)]
    else:
        zo_keep, zo_give = run_terms(at, a["normal_t"], dz, normed, cot, n_shard)
    zo_got = [trade(v, "shard", 1) for v in zo_give]
    dx_intra, db, dc, mixed = run_intra_back(a, after(dyr, *zo_give), dye, enter, normed, wo, tok)
    arrived = after_all(enter_by_head + zo_got, dx_intra)
    enter_by_head, zo_got = arrived[: len(enter_by_head)], arrived[len(enter_by_head) :]
    zo_pairs = chip_pairs(zo_keep, jnp.stack(zo_got))
    zo_far = chip_send(zo_pairs)
    enter_by_head = [after(v, *zo_pairs) for v in enter_by_head]
    all_enter = (
        [d_enter] + enter_by_head + [enter_by_core] + [trade(v, "shard", 1) for v in enter_by_head]
    )
    mixed_got = move_home(after(mixed, all_enter[-1]))
    d_a_all, small = run_back(
        info, a, all_enter, all_states, dx_intra, db, dc, enter, product, dyr, taps,
        rate_row, skip_row, table, narrow, gain_part, skip_part,
    )
    d_a_all = after(d_a_all, mixed_got)
    a_term = dot_tn(normal, d_a_all).astype(BF).reshape(n_shard, k_rows, WA)
    a_keep, a_give = core_give([a_term])
    a_got = trade(a_give, "shard", 1)

    small_got = trade(after(small, a_give), "shard", 1)
    zo_own = chip_sum(zo_pairs[0], after_all(zo_far, a_give))
    zo_keep, zo_give = head_split(zo_own)
    zo_got = trade(zo_give, "head", 1)
    d_a_all, dz, tok, tok_halo, wa = after_all(
        [d_a_all, dz, tok, a["tok_halo"], wa], a_give, zo_give
    )
    gain = wa[:, XBC + NH].astype(F32)
    from_a = dot_nt(d_a_all, wa)
    normal_grad = dot_nt(dz, wz) + from_a[:rows]
    token_grad = (cot.astype(F32) + norm_back(normal_grad, tok, gain)).astype(BF)

    a_got, small_got = after_all([a_got, small_got], token_grad)
    if k_rows % 32:
        parts = split2((small + small_got).reshape(k_rows, -1))
        a_pairs = [jnp.concatenate([v, parts], axis=1) for v in chip_pairs(a_keep, a_got)]
    else:
        a_pairs = run_pair_small(at, a_term, a_got, small, small_got)
    a_far = chip_send(a_pairs)
    token_got = move_home(after(token_grad, a_pairs[0]))
    zo_half = head_add(zo_keep, after(zo_got, a_pairs[0]))
    zo_parts = jnp.split(zo_half, 2, axis=1)
    zo_first = trade(zo_parts[0], "head", 2)
    halo_part = norm_back(after(from_a, a_pairs[0])[rows:], tok_halo, gain)
    halo_part = halo_part.reshape(nb, HALO, DM)[:, HALO - KC :].astype(BF).reshape(k_rows, -1)
    halos = [halo_part, trade(halo_part, "shard", 1)]
    *a_far, token_got, halos[1] = after_all(a_far + [token_got, halos[1]])
    cut, edge = WA // 2, WA // 2 + 2 * SUM_ROWS * LANES // k_rows
    if k_rows % 32:
        a_own = chip_sum(a_pairs[0][:, :WA], [v[:, :WA] for v in a_far])
        sums = [join2(v[:, WA:]) for v in [a_pairs[0]] + a_far]
        while len(sums) > 1:
            sums = [sums[k] + sums[k + 1] for k in range(0, len(sums), 2)]
        small = sums[0]
        total, a_give = head_split(a_own)
        parts = split2(small)
        sent = jnp.concatenate([a_give, parts] + (halos if half > 1 else []), axis=1)
        small = join2(parts)
    else:
        odd = (head_at % 2).astype(jnp.int32).reshape(1)
        sent, total, small = run_chip_sum(odd, [a_pairs[0]] + a_far, halos)
    zo_second = after(zo_parts[1], sent)
    own_total = total = total.astype(F32)
    bits = [b for b in (1, 2, 4, 8, 16) if b < n_head]
    for bit in bits:
        if bit > 1:
            a_give = total.astype(BF)
            total = a_give.astype(F32)
            parts = split2(small)
            small = join2(parts)
            sent = jnp.concatenate([a_give, parts] + (halos if bit < half else []), axis=1)
        sent = trade(sent, "head", bit)
        if bit == 1:
            sent, zo_first = after_all([sent, zo_first])
            zo_got = jnp.concatenate([zo_first, trade(zo_second, "head", 2)], axis=1)
            zo_half = head_add(zo_half, zo_got)
            for more in bits[2:]:
                zo_half = head_add(zo_half, trade(zo_half, "head", more))
            zo_other = trade(zo_half, "head", 1)
        if bit < half:
            halos = halos + jnp.split(sent[:, edge:], len(halos), axis=1)
        total = total + sent[:, :cut].astype(F32)
        small = small + join2(sent[:, cut:edge])
    low = total.astype(BF)
    other = trade(low, "head", 1)
    halos, small = after_all([jnp.concatenate(halos, axis=1), small], low)
    halos = jnp.where(stay, halos, move_home(halos))
    halos = jnp.split(halos, group_blocks // nb, axis=1)
    zo_other = after(zo_other, *halos)
    zo_grad = head_join(zo_half, zo_other).astype(F32)
    other = after(other, zo_other)
    a_grad = head_join(low, other).astype(F32)
    small = small.reshape(SUM_ROWS, LANES)

    all_halo = jnp.concatenate(halos[0::2] + halos[1::2]).reshape(group_blocks, KC, DM).astype(F32)
    own_numbers = jnp.concatenate([block_place, seq_length], axis=1)[0]
    own_places = jnp.sum(
        jnp.where(
            home_order[:, None] == jnp.arange(group_blocks), own_numbers[None, :group_blocks], 0
        ),
        axis=1,
    )
    home_ids = head_at * nb + jnp.arange(nb)
    home_places = jnp.sum(
        jnp.where(
            home_ids[:, None] == jnp.arange(group_blocks), own_numbers[None, :group_blocks], 0
        ),
        axis=1,
    )
    goes_on, begin = home_places < 0, 0
    for k in range(seq_length.shape[1]):
        end = begin + (own_numbers[group_blocks + k] + CH - 1) // CH
        goes_on = goes_on | ((home_places >= begin) & (home_places + 1 < end))
        begin = end
    is_next = (own_places[None, :] == home_places[:, None] + 1) & goes_on[:, None]
    halo_back = jnp.sum(jnp.where(is_next[:, :, None, None], all_halo[None], 0.0), axis=1)
    token_grad = jnp.where(stay, token_grad, token_got).reshape(nb, CH, DM)
    token_grad = token_grad.at[:, CH - KC :].set(
        (token_grad[:, CH - KC :].astype(F32) + halo_back).astype(BF)
    ).reshape(rows, DM)
    mixed = jnp.where(stay, mixed, after(mixed_got, own_total))

    in_grad = jnp.concatenate([zo_grad[:, :DI], a_grad[:, : XBC + NH]], axis=1)
    out_grad = jnp.concatenate([zo_grad[:, DI : DI + DM], zo_grad[:, DI + DM :]], axis=0)
    gain_grad = jnp.sum(in_grad * in_weight.astype(F32), axis=1) / norm_gain.astype(F32)

    return (
        mixed, token_grad, gain_grad, in_grad, small[: KC * XBC // LANES].reshape(KC, XBC),
        small[KC * XBC // LANES : SUM_GAIN].reshape(XBC), small[SUM_HEADS, :NH],
        small[SUM_HEADS + 1, :NH], jnp.sum(small[SUM_SKIP:SUM_HEADS].reshape(NH, HD), axis=1),
        small[SUM_GAIN:SUM_SKIP].reshape(DI), out_grad,
    )


def solution(mesh):
    return jax.shard_map(
        shards,
        mesh=mesh,
        in_specs=(
            P(("head", "shard"), None), P("shard"), P("shard", None), P(), P(), P(), P(), P(), P(),
            P("shard", None), P("shard", None), P("shard", None), P(("head", "shard"), None),
        ),
        out_specs=(
            P(("head", "shard"), None), P(("head", "shard"), None), P("shard"), P("shard", None),
            P(), P(), P(), P(), P(), P(), P("shard", None),
        ),
        check_vma=False,
    )
```
